32 devices in a mesh: dp: 8 (over z, x), tensor: 4 (over y, core).
Axes of the slice: x: 2, y: 2, z: 4, core: 2. Of those that a mesh axis runs over, the one named last changes fastest.
Arguments:
- latent: bfloat16 [8, 16, 1280, 128], P('dp', None, 'tensor'), may hold values from -6 to 6
- clip_flags: int32 [8], P('dp'), may hold values 0 or 1
- cotangent: bfloat16 [8, 16, 1280, 128], P('dp', None, 'tensor'), may hold values from -6 to 6
- norm_gain: float32 [4, 1280], P(None, 'tensor'), may hold values from 0.5 to 1.5
- norm_shift: float32 [4, 1280], P(None, 'tensor'), may hold values from -3 to 3
- channel_bias: float32 [5, 1280], P(None, 'tensor'), may hold values from -3 to 3
- hidden_bias: float32 [5120], P('tensor'), may hold values from -3 to 3
- weight_in: bfloat16 [1280, 1280], P('dp', 'tensor'), may hold values from -0.15625 to 0.15625
- weight_qkv: bfloat16 [2, 1280, 3, 1280], P(None, 'dp', None, 'tensor'), may hold values from -0.15625 to 0.15625
- weight_out: bfloat16 [2, 1280, 1280], P(None, 'tensor', 'dp'), may hold values from -0.5 to 0.5
- weight_up: bfloat16 [1280, 5120], P('dp', 'tensor'), may hold values from -0.15625 to 0.15625
- weight_down: bfloat16 [5120, 1280], P('tensor', 'dp'), may hold values from -0.078125 to 0.078125
- weight_proj: bfloat16 [1280, 1280], P('dp', 'tensor'), may hold values from -0.15625 to 0.15625
Outputs:
- output: bfloat16 [8, 16, 1280, 128], P('dp', None, 'tensor')
- latent_grad: float32 [8, 16, 1280, 128], P('dp', None, 'tensor')
- gain_grad: float32 [4, 1280], P(None, 'tensor')
- shift_grad: float32 [4, 1280], P(None, 'tensor')
- channel_bias_grad: float32 [5, 1280], P(None, 'tensor')
- hidden_bias_grad: float32 [5120], P('tensor')
- weight_in_grad: float32 [1280, 1280], P('dp', 'tensor')
- weight_qkv_grad: float32 [2, 1280, 3, 1280], P(None, 'dp', None, 'tensor')
- weight_out_grad: float32 [2, 1280, 1280], P(None, 'tensor', 'dp')
- weight_up_grad: float32 [1280, 5120], P('dp', 'tensor')
- weight_down_grad: float32 [5120, 1280], P('tensor', 'dp')
- weight_proj_grad: float32 [1280, 1280], P('dp', 'tensor')
The draws below stay inside these ranges and needn't reach their ends.
Inputs may be any that keep to these rules, and one draw needn't show every extreme that they name: `clip_flags`: 1 marks a slot holding one clip of 16 frames, 0 a slot of 16 unrelated still images that bypass the module.
All inputs are finite; a program needn't handle non-finite values. No bound on the sum of `clip_flags` on one device may be relied on, other than what follows from the above.
Results may differ from the reference program's by a relative error of at most 0.025.
Values may be sent and summed in bfloat16 or wider, within the bound.
A program may use at most 256 MiB of HBM per device.

```python
import math
import jax
import jax.numpy as jnp
from jax import lax

C = 1280
HEADS = 8
FF = 5120
GROUPS = 32
FRAMES = 16
PIX = 128
HEAD = 160
SLOTS = 8
N_TENSOR = 4


def touch_ends(drawn, key, low, high):
    longest = drawn.shape.index(max(drawn.shape))
    spots = []
    for shift in (0, 1):
        where = [jax.random.randint(jax.random.fold_in(key, axis), (), 0, length) for axis, length in enumerate(drawn.shape)]
        where[longest] = (where[longest] + shift) % drawn.shape[longest]
        spots.append(tuple(where))
    return drawn.at[spots[0]].set(low).at[spots[1]].set(high)


def steps_of(stream_key, shape, cuts, low, largest):
    def one(axis_at, blocks):
        heights = jax.random.uniform(jax.random.fold_in(jax.random.fold_in(stream_key, 6), axis_at), (blocks,), jnp.float32, low / len(cuts), largest / len(cuts))
        return jnp.repeat(jnp.exp(heights), shape[axis_at] // blocks).reshape((-1,) + (1,) * (len(shape) - axis_at - 1))

    factor_of = one(*cuts[0])
    for cut in cuts[1:]:
        factor_of = factor_of * one(*cut)
    return factor_of


def scatter_about(stream_key, extent, scale, most, cuts=(), dtype=jnp.bfloat16):
    entries = scale * jax.random.normal(stream_key, extent, jnp.float32)
    if cuts:
        entries = entries * steps_of(stream_key, extent, cuts, -0.22, 0.18)
    return jnp.clip(entries, -most, most).astype(dtype)


def setup_inputs(seed: int = 0) -> dict:
    seeds = jax.random.split(jax.random.key(seed), 14)
    return {
        "latent": scatter_about(seeds[0], (SLOTS, FRAMES, C, PIX), 1.0, 6.0, ((0, 8), (2, 4))),
        "clip_flags": touch_ends((jax.random.randint(seeds[1], (SLOTS,), 0, 4) < 3).astype(jnp.int32), jax.random.fold_in(seeds[1], 1), 0, 1),
        "cotangent": scatter_about(seeds[2], (SLOTS, FRAMES, C, PIX), 1.0, 6.0, ((0, 8), (2, 4))),
        "norm_gain": jnp.clip(1.0 + 0.1 * jax.random.normal(seeds[3], (4, C), jnp.float32), 0.5, 1.5),
        "norm_shift": scatter_about(seeds[4], (4, C), 0.5, 3.0, ((1, 4),), jnp.float32),
        "channel_bias": scatter_about(seeds[5], (5, C), 0.5, 3.0, ((1, 4),), jnp.float32),
        "hidden_bias": scatter_about(seeds[6], (FF,), 0.5, 3.0, ((0, 4),), jnp.float32),
        "weight_in": scatter_about(seeds[7], (C, C), C ** -0.5, 0.15625, ((0, 8), (1, 4))),
        "weight_qkv": scatter_about(seeds[8], (2, C, 3, C), C ** -0.5, 0.15625, ((1, 8), (3, 4))),
        "weight_out": scatter_about(seeds[9], (2, C, C), (C // 8) ** -0.5, 0.5, ((1, 4), (2, 8))),
        "weight_up": scatter_about(seeds[10], (C, FF), C ** -0.5, 0.15625, ((0, 8), (1, 4))),
        "weight_down": scatter_about(seeds[11], (FF, C), FF ** -0.5, 0.078125, ((0, 4), (1, 8))),
        "weight_proj": scatter_about(seeds[12], (C, C), C ** -0.5, 0.15625, ((0, 8), (1, 4))),
    }


@jax.custom_vjp
def low(v):
    return lax.optimization_barrier(v.astype(jnp.bfloat16)).astype(jnp.float32)

@jax.custom_vjp
def low_back(v):
    return v

def low_keep(v):
    return (low(v), None)

def low_pass(kept, grad):
    return (grad,)

def back_keep(v):
    return (v, None)

def back_low(kept, grad):
    return (low(grad),)
low.defvjp(low_keep, low_pass)
low_back.defvjp(back_keep, back_low)

def matmul(left_side, right_side):
    return jnp.dot(left_side, right_side, precision=lax.Precision.HIGHEST, preferred_element_type=jnp.float32)

def split_product(source, matrices):
    span_cols = matrices[0].shape[1] // N_TENSOR
    collected = [[] for matrix in matrices]
    for portion in range(N_TENSOR):
        joined = jnp.concatenate([matrix[:, portion * span_cols:(portion + 1) * span_cols] for matrix in matrices], axis=1)
        product = matmul(low_back(source), joined)
        for number in range(len(matrices)):
            collected[number].append(product[:, number * span_cols:(number + 1) * span_cols])
    return [jnp.concatenate(pieces, axis=1) for pieces in collected]

def group_sum(source, matrix):
    span_rows = matrix.shape[0] // N_TENSOR
    summed = jnp.zeros((source.shape[0], matrix.shape[1]), jnp.float32)
    for portion in range(N_TENSOR):
        lower_edge = portion * span_rows
        summed = summed + low(matmul(source[:, lower_edge:lower_edge + span_rows], matrix[lower_edge:lower_edge + span_rows]))
    return low_back(summed)

def positions():
    frame_ids = jnp.arange(FRAMES).astype(jnp.float32)[:, None]
    channel_ids = jnp.arange(C)
    pair_rate = jnp.exp((channel_ids // 2).astype(jnp.float32) * (-2.0 * math.log(10000.0) / C))
    angles = frame_ids * pair_rate[None, :]
    return jnp.where(channel_ids[None, :] % 2 == 0, jnp.sin(angles), jnp.cos(angles))

def group_norm(stream, gain, shift):
    rows_slot = stream.shape[0]
    grouped = stream.reshape(rows_slot, GROUPS, C // GROUPS)
    centre = lax.optimization_barrier(jnp.mean(grouped, axis=(0, 2), keepdims=True))
    offset = grouped - centre
    spread = lax.optimization_barrier(jnp.mean(offset * offset, axis=(0, 2), keepdims=True))
    return (offset * lax.rsqrt(spread + 1e-06)).reshape(rows_slot, C) * gain + shift

def layer_norm(stream, gain, shift):
    centre = lax.optimization_barrier(jnp.mean(stream, axis=-1, keepdims=True))
    offset = stream - centre
    spread = lax.optimization_barrier(jnp.mean(offset * offset, axis=-1, keepdims=True))
    return offset * lax.rsqrt(spread + 1e-05) * gain + shift

def module(slot_in, params):
    norm_gain, norm_shift, channel_bias, hidden_bias, weight_in, weight_qkv, weight_out, weight_up, weight_down, weight_proj = params
    position_table = positions()
    score_scale = 1.0 / math.sqrt(HEAD)
    normed = group_norm(slot_in, norm_gain[0], norm_shift[0])
    stream = low_back(split_product(low(normed), [weight_in])[0]) + channel_bias[0]
    for sub_block in range(2):
        lifted = layer_norm(stream, norm_gain[1 + sub_block], norm_shift[1 + sub_block])
        lifted = (lifted.reshape(FRAMES, PIX, C) + position_table[:, None, :]).reshape(FRAMES * PIX, C)
        matrices = [weight_qkv[sub_block, :, member, :] for member in range(3)]
        query_heads, key_heads, value_heads = [low(low_back(projected)).reshape(FRAMES, PIX, HEADS, HEAD) for projected in split_product(low(lifted), matrices)]
        raw_scores = jnp.einsum('fphd,gphd->phfg', query_heads, key_heads, precision=lax.Precision.HIGHEST)
        attention_probs = jax.nn.softmax(low_back(raw_scores) * score_scale, axis=-1)
        attended = jnp.einsum('phfg,gphd->fphd', low(attention_probs), value_heads, precision=lax.Precision.HIGHEST)
        attended = low(low_back(attended)).reshape(FRAMES * PIX, C)
        stream = stream + group_sum(attended, weight_out[sub_block]) + channel_bias[1 + sub_block]
    normed = layer_norm(stream, norm_gain[3], norm_shift[3])
    pre_act = low_back(split_product(low(normed), [weight_up])[0]) + hidden_bias
    hidden = low(jax.nn.gelu(pre_act, approximate=False))
    stream = stream + group_sum(hidden, weight_down) + channel_bias[3]
    projected_out = low_back(split_product(low(stream), [weight_proj])[0]) + channel_bias[4]
    return slot_in + projected_out

def forward(latent_float, params, clip_flags):
    slot_rows = jnp.transpose(latent_float, (0, 1, 3, 2)).reshape(SLOTS, FRAMES * PIX, C)
    checked = jax.checkpoint(module)

    def advance(carried, slot_pair):
        slot_in, flag_value = slot_pair
        return (carried, jnp.where(flag_value > 0, checked(slot_in, params), slot_in))
    unused, outputs = lax.scan(advance, jnp.zeros((), jnp.float32), (slot_rows, clip_flags))
    return jnp.transpose(outputs.reshape(SLOTS, FRAMES, PIX, C), (0, 1, 3, 2))

def reference(latent, clip_flags, cotangent, norm_gain, norm_shift, channel_bias, hidden_bias, weight_in, weight_qkv, weight_out, weight_up, weight_down, weight_proj):
    params = tuple((member.astype(jnp.float32) for member in (norm_gain, norm_shift, channel_bias, hidden_bias, weight_in, weight_qkv, weight_out, weight_up, weight_down, weight_proj)))

    def wrapped(inputs, weights):
        return forward(inputs, weights, clip_flags)
    result, pullback = jax.vjp(wrapped, latent.astype(jnp.float32), params)
    latent_grad, grads = pullback(cotangent.astype(jnp.float32))
    gain_grad, shift_grad, channel_bias_grad, hidden_bias_grad, weight_in_grad, weight_qkv_grad, weight_out_grad, weight_up_grad, weight_down_grad, weight_proj_grad = grads
    return (result.astype(jnp.bfloat16), latent_grad, gain_grad, shift_grad, channel_bias_grad, hidden_bias_grad, weight_in_grad, weight_qkv_grad, weight_out_grad, weight_up_grad, weight_down_grad, weight_proj_grad)
```

```python
from functools import partial
import math

import jax
import jax.numpy as jnp
from jax import lax
from jax.experimental import pallas as pl
from jax.experimental.pallas import tpu as pltpu
from jax.sharding import PartitionSpec as P

C = 1280
GROUPS = 32
FRAMES = 16
HEAD = 160
BLOCK = 128
MIXED = ("tensor", "dp")


def spread(rows, weight):
    return jnp.einsum("rk,tkn->trn", rows, weight, preferred_element_type=jnp.float32)


def collapse(parts, weight):
    return jnp.einsum("trn,tkn->rk", parts, weight, preferred_element_type=jnp.float32)


def weight_grad(rows, parts):
    return jnp.einsum("rk,trn->tkn", rows, parts, preferred_element_type=jnp.float32)


def make_positions():
    channel_ids = jnp.arange(C)
    pair_rate = jnp.exp((channel_ids // 2).astype(jnp.float32) * (-2.0 * math.log(10000.0) / C))
    angles = jnp.arange(FRAMES).astype(jnp.float32)[:, None] * pair_rate[None, :]
    return jnp.where(channel_ids[None, :] % 2 == 0, jnp.sin(angles), jnp.cos(angles))


def layer_stats(stream):
    centre = jnp.mean(stream, axis=1, keepdims=True)
    offset = stream - centre
    inverse = lax.rsqrt(jnp.mean(offset * offset, axis=1, keepdims=True) + 1e-05)
    return offset * inverse, inverse


def layer_back(grad_out, normal_part, inverse, gain):
    scaled = grad_out * gain
    first = jnp.mean(scaled, axis=1, keepdims=True)
    second = jnp.mean(scaled * normal_part, axis=1, keepdims=True)
    grad_in = inverse * (scaled - first - normal_part * second)
    return grad_in, jnp.sum(grad_out * normal_part, 0), jnp.sum(grad_out, 0)


def dot_rows(left, right):
    return lax.dot_general(left, right, (((1,), (1,)), ((), ())), preferred_element_type=jnp.float32)


def dot_plain(left, right):
    return lax.dot_general(left, right, (((1,), (0,)), ((), ())), preferred_element_type=jnp.float32)


def dot_first(left, right):
    return lax.dot_general(left, right, (((0,), (0,)), ((), ())), preferred_element_type=jnp.float32)


def same_pixel(block):
    row = lax.broadcasted_iota(jnp.int32, (block, block), 0) // FRAMES
    col = lax.broadcasted_iota(jnp.int32, (block, block), 1) // FRAMES
    return row == col


def head_probs(query, key, same, scale):
    scores = jnp.where(same, dot_rows(query, key) * scale, -1e30)
    top = jnp.max(scores, axis=1, keepdims=True)
    weights = jnp.where(same, jnp.exp(scores - top), 0.0)
    return weights / jnp.sum(weights, axis=1, keepdims=True)


def attend_kernel(scale, qkv_ref, out_ref):
    rows, width = out_ref.shape[1], out_ref.shape[2]
    block = min(BLOCK, rows)
    same = same_pixel(block)
    for start in range(0, rows, block):
        for head in range(width // HEAD):
            low = head * HEAD
            query = qkv_ref[0, start : start + block, low : low + HEAD]
            key = qkv_ref[0, start : start + block, width + low : width + low + HEAD]
            value = qkv_ref[0, start : start + block, 2 * width + low : 2 * width + low + HEAD]
            probs = head_probs(query, key, same, scale).astype(jnp.bfloat16)
            out_ref[0, start : start + block, low : low + HEAD] = dot_plain(probs, value).astype(
                jnp.bfloat16
            )


def attend(qkv):
    parts, rows, wide = qkv.shape
    width = wide // 3
    return pl.pallas_call(
        partial(attend_kernel, 1.0 / math.sqrt(HEAD)),
        grid=(parts,),
        in_specs=[pl.BlockSpec((1, rows, wide), lambda t: (t, 0, 0))],
        out_specs=pl.BlockSpec((1, rows, width), lambda t: (t, 0, 0)),
        out_shape=jax.ShapeDtypeStruct((parts, rows, width), jnp.bfloat16),
        compiler_params=pltpu.CompilerParams(vmem_limit_bytes=32 << 20),
    )(qkv)


def attend_back_kernel(scale, qkv_ref, grad_ref, out_ref):
    rows, width = grad_ref.shape[1], grad_ref.shape[2]
    block = min(BLOCK, rows)
    same = same_pixel(block)
    for start in range(0, rows, block):
        for head in range(width // HEAD):
            low = head * HEAD
            here = slice(start, start + block)
            query = qkv_ref[0, here, low : low + HEAD]
            key = qkv_ref[0, here, width + low : width + low + HEAD]
            value = qkv_ref[0, here, 2 * width + low : 2 * width + low + HEAD]
            grad = grad_ref[0, here, low : low + HEAD]
            probs = head_probs(query, key, same, scale)
            grad_probs = dot_rows(grad, value)
            centred = jnp.sum(probs * grad_probs, axis=1, keepdims=True)
            grad_raw = (probs * (grad_probs - centred) * scale).astype(jnp.bfloat16)
            out_ref[0, here, low : low + HEAD] = dot_plain(grad_raw, key).astype(jnp.bfloat16)
            out_ref[0, here, width + low : width + low + HEAD] = dot_first(grad_raw, query).astype(
                jnp.bfloat16
            )
            out_ref[0, here, 2 * width + low : 2 * width + low + HEAD] = dot_first(
                probs.astype(jnp.bfloat16), grad
            ).astype(jnp.bfloat16)


def attend_back(qkv, grad):
    parts, rows, wide = qkv.shape
    width = wide // 3
    return pl.pallas_call(
        partial(attend_back_kernel, 1.0 / math.sqrt(HEAD)),
        grid=(parts,),
        in_specs=[
            pl.BlockSpec((1, rows, wide), lambda t: (t, 0, 0)),
            pl.BlockSpec((1, rows, width), lambda t: (t, 0, 0)),
        ],
        out_specs=pl.BlockSpec((1, rows, wide), lambda t: (t, 0, 0)),
        out_shape=jax.ShapeDtypeStruct((parts, rows, wide), jnp.bfloat16),
        compiler_params=pltpu.CompilerParams(vmem_limit_bytes=32 << 20),
    )(qkv, grad)


def gather_weight(shard):
    tensor_size = lax.axis_size("tensor")
    whole = lax.all_gather(shard, MIXED, axis=0, tiled=True)
    return whole.reshape(tensor_size, C, shard.shape[1])


def reduce_weight(grad):
    parts, rows, width = grad.shape
    flat = grad.astype(jnp.bfloat16).reshape(parts * rows, width)
    return lax.psum_scatter(flat, MIXED, scatter_dimension=0, tiled=True).astype(jnp.float32)


def to_pixels(values, tensor_size):
    slots, frames, width, pixels = values.shape
    own = pixels // tensor_size
    turned = jnp.transpose(values, (3, 0, 1, 2)).reshape(tensor_size, own * slots * frames, width)
    return lax.all_to_all(turned, "tensor", 0, 0, tiled=True)


def to_channels(values, slots, pixels):
    tensor_size, rows, width = values.shape
    arrived = lax.all_to_all(values, "tensor", 0, 0, tiled=True)
    return jnp.transpose(arrived.reshape(pixels, slots, FRAMES, width), (1, 2, 3, 0))


def body(
    latent,
    clip_flags,
    cotangent,
    norm_gain,
    norm_shift,
    channel_bias,
    hidden_bias,
    weight_in,
    weight_qkv,
    weight_out,
    weight_up,
    weight_down,
    weight_proj,
):
    tensor_size = lax.axis_size("tensor")
    slots, frames, width, pixels = latent.shape
    share = weight_in.shape[0]
    hidden_width = hidden_bias.shape[0]
    flags = (clip_flags > 0)[:, None, None, None]

    full_in = gather_weight(weight_in)
    full_qkv, full_out = [], []
    for block in range(2):
        full_qkv.append(gather_weight(weight_qkv[block].reshape(share, 3 * width)))
        full_out.append(gather_weight(weight_out[block].T))
    full_up = gather_weight(weight_up)
    full_down = gather_weight(weight_down.T)
    full_proj = gather_weight(weight_proj)

    packed = jnp.concatenate([norm_gain, norm_shift, channel_bias], 0)
    packed = lax.all_gather(
        jnp.concatenate([packed.reshape(-1), hidden_bias]), "tensor", axis=0, tiled=False
    )
    channel_params = packed[:, : 13 * width].reshape(tensor_size, 13, width)
    channel_params = jnp.transpose(channel_params, (1, 0, 2)).reshape(13, C)
    gains, shifts, biases = channel_params[:4], channel_params[4:8], channel_params[8:]
    hidden_full = packed[:, 13 * width :]

    start = latent.astype(jnp.float32)
    cot = cotangent.astype(jnp.float32)
    group_width = C // GROUPS
    grouped = start.reshape(slots, frames, width // group_width, group_width, pixels)
    group_centre = jnp.mean(grouped, axis=(1, 3, 4), keepdims=True)
    offset = grouped - group_centre
    group_inverse = lax.rsqrt(jnp.mean(offset * offset, axis=(1, 3, 4), keepdims=True) + 1e-06)
    group_hat = (offset * group_inverse).reshape(start.shape)
    normed = group_hat * norm_gain[0][:, None] + norm_shift[0][:, None]
    arrived = to_pixels(normed.astype(jnp.bfloat16), tensor_size)
    rows = arrived.shape[1]
    inputs_in = jnp.transpose(arrived, (1, 0, 2)).reshape(rows, C)

    grad_moved_local = jnp.where(flags, cot, 0.0)
    bias_moved = jnp.sum(grad_moved_local, axis=(0, 1, 3))
    grad_moved = to_pixels(grad_moved_local.astype(jnp.bfloat16), tensor_size)

    def join(parts):
        return jnp.transpose(parts, (1, 0, 2)).reshape(rows, parts.shape[0] * parts.shape[2])

    stream = join(spread(inputs_in, full_in)) + biases[0]
    position = jnp.tile(make_positions(), (rows // FRAMES, 1))
    kept = []
    for block in range(2):
        hat, inverse = layer_stats(stream)
        lifted = (hat * gains[1 + block] + shifts[1 + block] + position).astype(jnp.bfloat16)
        qkv = spread(lifted, full_qkv[block]).astype(jnp.bfloat16)
        attended = attend(qkv)
        stream = stream + collapse(attended, full_out[block]) + biases[1 + block]
        kept.append((hat, inverse, lifted, qkv, attended))
    hat_feed, inverse_feed = layer_stats(stream)
    inputs_up = (hat_feed * gains[3] + shifts[3]).astype(jnp.bfloat16)
    pre_act = spread(inputs_up, full_up) + hidden_full[:, None, :]
    hidden = jax.nn.gelu(pre_act, approximate=False).astype(jnp.bfloat16)
    stream = stream + collapse(hidden, full_down) + biases[3]
    inputs_proj = stream.astype(jnp.bfloat16)
    moved = spread(inputs_proj, full_proj) + biases[4].reshape(tensor_size, 1, width)
    moved_local = to_channels(moved.astype(jnp.bfloat16), slots, pixels).astype(jnp.float32)
    output = jnp.where(flags, start + moved_local, start).astype(jnp.bfloat16)

    bias_grads = [None] * 4
    gain_grads = [None] * 3
    shift_grads = [None] * 3
    qkv_grads = [None, None]
    out_grads = [None, None]
    proj_grad = reduce_weight(weight_grad(inputs_proj, grad_moved))
    grad_stream = collapse(grad_moved, full_proj)
    bias_grads[3] = jnp.sum(grad_stream, 0)
    grad_low = grad_stream.astype(jnp.bfloat16)
    down_grad = reduce_weight(weight_grad(grad_low, hidden))
    grad_hidden = spread(grad_low, full_down)
    unused, gelu_pull = jax.vjp(partial(jax.nn.gelu, approximate=False), pre_act)
    grad_pre = gelu_pull(grad_hidden)[0]
    hidden_grad = jnp.sum(grad_pre, 1)
    grad_pre_low = grad_pre.astype(jnp.bfloat16)
    up_grad = reduce_weight(weight_grad(inputs_up, grad_pre_low))
    grad_layer, gain_grads[2], shift_grads[2] = layer_back(
        collapse(grad_pre_low, full_up), hat_feed, inverse_feed, gains[3]
    )
    grad_stream = grad_stream + grad_layer
    for block in (1, 0):
        hat, inverse, lifted, qkv, attended = kept[block]
        bias_grads[1 + block] = jnp.sum(grad_stream, 0)
        grad_low = grad_stream.astype(jnp.bfloat16)
        out_grads[block] = reduce_weight(weight_grad(grad_low, attended)).T
        grad_attended = spread(grad_low, full_out[block]).astype(jnp.bfloat16)
        grad_qkv = attend_back(qkv, grad_attended)
        qkv_grads[block] = reduce_weight(weight_grad(lifted, grad_qkv)).reshape(share, 3, width)
        grad_layer, gain_grads[block], shift_grads[block] = layer_back(
            collapse(grad_qkv, full_qkv[block]), hat, inverse, gains[1 + block]
        )
        grad_stream = grad_stream + grad_layer
    bias_grads[0] = jnp.sum(grad_stream, 0)
    grad_low = grad_stream.astype(jnp.bfloat16)
    grad_low_parts = jnp.transpose(grad_low.reshape(rows, tensor_size, width), (1, 0, 2))
    in_grad = reduce_weight(weight_grad(inputs_in, grad_low_parts))
    grad_normed = collapse(grad_low_parts, full_in).astype(jnp.bfloat16)
    grad_normed = jnp.transpose(grad_normed.reshape(rows, tensor_size, width), (1, 0, 2))
    grad_normed = to_channels(grad_normed, slots, pixels).astype(jnp.float32)
    scaled = grad_normed * norm_gain[0][:, None]
    scaled_groups = scaled.reshape(grouped.shape)
    hat_groups = group_hat.reshape(grouped.shape)
    first = jnp.mean(scaled_groups, axis=(1, 3, 4), keepdims=True)
    second = jnp.mean(scaled_groups * hat_groups, axis=(1, 3, 4), keepdims=True)
    grad_group = group_inverse * (scaled_groups - first - hat_groups * second)
    latent_grad = cot + grad_group.reshape(start.shape)
    group_gain_grad = jnp.sum(grad_normed * group_hat, axis=(0, 1, 3))
    group_shift_grad = jnp.sum(grad_normed, axis=(0, 1, 3))

    vectors = jnp.stack(gain_grads + shift_grads + bias_grads, 0)
    vectors = jnp.transpose(vectors.reshape(10, tensor_size, width), (1, 0, 2))
    vectors = jnp.concatenate([vectors.reshape(tensor_size, 10 * width), hidden_grad], 1)
    vectors = lax.psum_scatter(vectors, "tensor", scatter_dimension=0, tiled=False)
    sums = lax.psum(
        jnp.concatenate([vectors, group_gain_grad, group_shift_grad, bias_moved]), "dp"
    )
    channel_sums = sums[: 10 * width].reshape(10, width)
    hidden_bias_grad = sums[10 * width : 10 * width + hidden_width]
    local_sums = sums[10 * width + hidden_width :].reshape(3, width)
    gain_grad = jnp.concatenate([local_sums[0:1], channel_sums[0:3]], 0)
    shift_grad = jnp.concatenate([local_sums[1:2], channel_sums[3:6]], 0)
    channel_bias_grad = jnp.concatenate([channel_sums[6:10], local_sums[2:3]], 0)
    return (
        output,
        latent_grad,
        gain_grad,
        shift_grad,
        channel_bias_grad,
        hidden_bias_grad,
        in_grad,
        jnp.stack(qkv_grads, 0),
        jnp.stack(out_grads, 0),
        up_grad,
        down_grad.T,
        proj_grad,
    )


def solution(mesh):
    placed = (
        P("dp", None, "tensor", None),
        P("dp"),
        P("dp", None, "tensor", None),
        P(None, "tensor"),
        P(None, "tensor"),
        P(None, "tensor"),
        P("tensor"),
        P("dp", "tensor"),
        P(None, "dp", None, "tensor"),
        P(None, "tensor", "dp"),
        P("dp", "tensor"),
        P("tensor", "dp"),
        P("dp", "tensor"),
    )
    return jax.shard_map(
        body,
        mesh=mesh,
        in_specs=placed,
        out_specs=(
            P("dp", None, "tensor", None),
            P("dp", None, "tensor", None),
            P(None, "tensor"),
            P(None, "tensor"),
            P(None, "tensor"),
            P("tensor"),
            P("dp", "tensor"),
            P(None, "dp", None, "tensor"),
            P(None, "tensor", "dp"),
            P("dp", "tensor"),
            P("tensor", "dp"),
            P("dp", "tensor"),
        ),
        check_vma=False,
    )
```

```python
from functools import partial
import math

import jax
import jax.numpy as jnp
from jax import lax
from jax.experimental import pallas as pl
from jax.experimental.pallas import tpu as pltpu
from jax.sharding import PartitionSpec as P

C = 1280
GROUPS = 32
FRAMES = 16
HEAD = 160
BLOCK = 128
MIXED = ("tensor", "dp")


def spread(rows, weight):
    return jnp.einsum("rk,tkn->trn", rows, weight, preferred_element_type=jnp.float32)


def collapse(parts, weight):
    return jnp.einsum("trn,tkn->rk", parts, weight, preferred_element_type=jnp.float32)


def make_positions():
    channel_ids = jnp.arange(C)
    pair_rate = jnp.exp((channel_ids // 2).astype(jnp.float32) * (-2.0 * math.log(10000.0) / C))
    angles = jnp.arange(FRAMES).astype(jnp.float32)[:, None] * pair_rate[None, :]
    return jnp.where(channel_ids[None, :] % 2 == 0, jnp.sin(angles), jnp.cos(angles))


def layer_stats(stream):
    centre = jnp.mean(stream, axis=1, keepdims=True)
    offset = stream - centre
    inverse = lax.rsqrt(jnp.mean(offset * offset, axis=1, keepdims=True) + 1e-05)
    return offset * inverse, inverse


def layer_back(grad_out, normal_part, inverse, gain):
    scaled = grad_out * gain
    first = jnp.mean(scaled, axis=1, keepdims=True)
    second = jnp.mean(scaled * normal_part, axis=1, keepdims=True)
    grad_in = inverse * (scaled - first - normal_part * second)
    return grad_in, jnp.sum(grad_out * normal_part, 0), jnp.sum(grad_out, 0)


def dot_rows(left, right):
    return lax.dot_general(left, right, (((1,), (1,)), ((), ())), preferred_element_type=jnp.float32)


def dot_plain(left, right):
    return lax.dot_general(left, right, (((1,), (0,)), ((), ())), preferred_element_type=jnp.float32)


def dot_first(left, right):
    return lax.dot_general(left, right, (((0,), (0,)), ((), ())), preferred_element_type=jnp.float32)


def same_pixel(block):
    row = lax.broadcasted_iota(jnp.int32, (block, block), 0) // FRAMES
    col = lax.broadcasted_iota(jnp.int32, (block, block), 1) // FRAMES
    return row == col


def head_probs(query, key, same, scale):
    scores = jnp.where(same, dot_rows(query, key) * scale, -1e30)
    top = jnp.max(scores, axis=1, keepdims=True)
    weights = jnp.where(same, jnp.exp(scores - top), 0.0)
    return weights / jnp.sum(weights, axis=1, keepdims=True)


def attend_kernel(scale, qk_ref, v_ref, out_ref):
    rows, width = out_ref.shape[1], out_ref.shape[2]
    block = min(BLOCK, rows)
    same = same_pixel(block)
    for start in range(0, rows, block):
        for head in range(width // HEAD):
            here, low = slice(start, start + block), head * HEAD
            query = qk_ref[0, here, low : low + HEAD]
            key = qk_ref[0, here, width + low : width + low + HEAD]
            value = v_ref[0, here, low : low + HEAD]
            probs = head_probs(query, key, same, scale).astype(jnp.bfloat16)
            out_ref[0, here, low : low + HEAD] = dot_plain(probs, value).astype(jnp.bfloat16)


def part_spec(array):
    return pl.BlockSpec((1,) + array.shape[1:], lambda t: (t, 0, 0))


def attend(qk, values):
    return pl.pallas_call(
        partial(attend_kernel, 1.0 / math.sqrt(HEAD)),
        grid=(qk.shape[0],),
        in_specs=[part_spec(qk), part_spec(values)],
        out_specs=part_spec(values),
        out_shape=jax.ShapeDtypeStruct(values.shape, jnp.bfloat16),
        compiler_params=pltpu.CompilerParams(vmem_limit_bytes=32 << 20),
    )(qk, values)


def attend_back_kernel(scale, qk_ref, v_ref, grad_ref, dqk_ref, dv_ref):
    rows, width = grad_ref.shape[1], grad_ref.shape[2]
    block = min(BLOCK, rows)
    same = same_pixel(block)
    for start in range(0, rows, block):
        for head in range(width // HEAD):
            here, low = slice(start, start + block), head * HEAD
            query = qk_ref[0, here, low : low + HEAD]
            key = qk_ref[0, here, width + low : width + low + HEAD]
            value = v_ref[0, here, low : low + HEAD]
            grad = grad_ref[0, here, low : low + HEAD]
            probs = head_probs(query, key, same, scale)
            grad_probs = dot_rows(grad, value)
            centred = jnp.sum(probs * grad_probs, axis=1, keepdims=True)
            grad_raw = (probs * (grad_probs - centred) * scale).astype(jnp.bfloat16)
            dqk_ref[0, here, low : low + HEAD] = dot_plain(grad_raw, key).astype(jnp.bfloat16)
            dqk_ref[0, here, width + low : width + low + HEAD] = dot_first(grad_raw, query).astype(
                jnp.bfloat16
            )
            dv_ref[0, here, low : low + HEAD] = dot_first(probs.astype(jnp.bfloat16), grad).astype(
                jnp.bfloat16
            )


def attend_back(qk, values, grad):
    return pl.pallas_call(
        partial(attend_back_kernel, 1.0 / math.sqrt(HEAD)),
        grid=(qk.shape[0],),
        in_specs=[part_spec(qk), part_spec(values), part_spec(values)],
        out_specs=[part_spec(qk), part_spec(values)],
        out_shape=[
            jax.ShapeDtypeStruct(qk.shape, jnp.bfloat16),
            jax.ShapeDtypeStruct(values.shape, jnp.bfloat16),
        ],
        compiler_params=pltpu.CompilerParams(vmem_limit_bytes=32 << 20),
    )(qk, values, grad)


UNITS = 9
WIDE = 640
SLOTS_IN_FLIGHT = 6
ROWS_A = 96
MESH_ID = pl.DeviceIdType.MESH


class Place:
    def __init__(self):
        dp, tn = lax.axis_index("dp"), lax.axis_index("tensor")
        self.z, self.x = dp // 2, dp % 2
        self.y, self.c = tn // 2, tn % 2
        self.far_x, self.far_y = 1 - self.x, 1 - self.y
        self.to = {
            "x": (self.z * 2 + self.far_x, tn),
            "y": (dp, self.far_y * 2 + self.c),
            "core": (dp, self.y * 2 + 1 - self.c),
            "up": (dp + 2, tn),
            "down": (dp - 2, tn),
        }
        self.has_up = self.z < 3
        self.has_down = self.z > 0

    def greet(self):
        barrier = pltpu.get_barrier_semaphore()

        def hello(name):
            pl.semaphore_signal(barrier, inc=1, device_id=self.to[name], device_id_type=MESH_ID)

        for name in ("x", "y", "core"):
            hello(name)
        pl.when(self.has_up)(lambda: hello("up"))
        pl.when(self.has_down)(lambda: hello("down"))
        pl.semaphore_wait(barrier, 3 + (6 - self.z) // 4 + (self.z + 3) // 4)


def await_bytes(ref, sem):
    pltpu.make_async_copy(ref, ref, sem).wait()


def gather_kernel(shard_ref, whole_ref, local_sem, send_sem, recv_sem, core_sem):
    at = Place()
    z, x, y, c = at.z, at.x, at.y, at.c
    share = shard_ref.shape[1]
    cut = (pl.ds(0, ROWS_A), pl.ds(ROWS_A, share - ROWS_A))
    kinds = {"up": 0, "down": 1, "x": 2, "y": 3, "core": 4}
    at.greet()

    def send(unit, colour, yy, zz, xx, kind, own=False):
        place = whole_ref.at[unit, yy, c, zz, xx, cut[colour]]
        pltpu.make_async_remote_copy(
            src_ref=shard_ref.at[unit, cut[colour]] if own else place,
            dst_ref=place,
            send_sem=send_sem.at[unit, colour, kinds[kind]],
            recv_sem=recv_sem.at[unit, colour, yy, zz, xx],
            device_id=at.to[kind],
            device_id_type=MESH_ID,
        ).start()

    def arrived(unit, colour, yy, zz, xx):
        await_bytes(
            whole_ref.at[unit, yy, c, zz, xx, cut[colour]], recv_sem.at[unit, colour, yy, zz, xx]
        )

    def own_copy(unit):
        return pltpu.make_async_copy(
            shard_ref.at[unit], whole_ref.at[unit, y, c, z, x], local_sem.at[unit]
        )

    def to_core(unit, part):
        if part == 2:
            place = whole_ref.at[unit, :, c, :, :, cut[1]]
        else:
            place = whole_ref.at[unit, y if part == 0 else at.far_y, c, :, :, cut[0]]
        return pltpu.make_async_remote_copy(
            src_ref=place,
            dst_ref=place,
            send_sem=send_sem.at[unit, part // 2, 4],
            recv_sem=core_sem.at[unit, part],
            device_id=at.to["core"],
            device_id_type=MESH_ID,
        )

    def from_z(unit, colour, step, yy):
        @pl.when(z >= step)
        def _():
            zz = z - step
            arrived(unit, colour, yy, zz, x)
            pl.when(at.has_up)(lambda: send(unit, colour, yy, zz, x, "up"))
            send(unit, colour, yy, zz, x, "x")
            if colour == 0:
                send(unit, colour, yy, zz, x, "y")

        @pl.when(z + step <= 3)
        def _():
            zz = z + step
            arrived(unit, colour, yy, zz, x)
            pl.when(at.has_down)(lambda: send(unit, colour, yy, zz, x, "down"))
            send(unit, colour, yy, zz, x, "x")
            if colour == 0:
                send(unit, colour, yy, zz, x, "y")

    def from_x(unit, step):
        def one(zz):
            arrived(unit, 0, y, zz, at.far_x)
            send(unit, 0, y, zz, at.far_x, "y")

        if step == 0:
            one(z)
        else:
            pl.when(z >= step)(lambda: one(z - step))
            pl.when(z + step <= 3)(lambda: one(z + step))

    def stage0(unit):
        own_copy(unit).start()
        pl.when(at.has_up)(lambda: send(unit, 0, y, z, x, "up", True))
        pl.when(at.has_down)(lambda: send(unit, 0, y, z, x, "down", True))
        send(unit, 1, y, z, x, "y", True)
        send(unit, 0, y, z, x, "x", True)
        pl.when(at.has_up)(lambda: send(unit, 1, y, z, x, "up", True))
        pl.when(at.has_down)(lambda: send(unit, 1, y, z, x, "down", True))
        send(unit, 0, y, z, x, "y", True)
        send(unit, 1, y, z, x, "x", True)

    def stage1(unit):
        from_z(unit, 0, 1, y)
        arrived(unit, 1, at.far_y, z, x)
        pl.when(at.has_up)(lambda: send(unit, 1, at.far_y, z, x, "up"))
        pl.when(at.has_down)(lambda: send(unit, 1, at.far_y, z, x, "down"))
        send(unit, 1, at.far_y, z, x, "x")
        from_z(unit, 1, 1, y)
        from_x(unit, 0)

    def stage2(unit):
        from_z(unit, 0, 2, y)
        from_z(unit, 1, 1, at.far_y)
        from_z(unit, 1, 2, y)
        from_x(unit, 1)

    def stage3(unit):
        from_z(unit, 0, 3, y)
        from_z(unit, 1, 2, at.far_y)
        from_z(unit, 1, 3, y)
        from_x(unit, 2)

    def stage4(unit):
        from_z(unit, 1, 3, at.far_y)
        from_x(unit, 3)
        own_copy(unit).wait()
        to_core(unit, 0).start()

    def stage5(unit):
        for zz in range(4):
            for xx in range(2):
                arrived(unit, 0, at.far_y, zz, xx)
        to_core(unit, 1).start()
        for zz in range(4):
            for yy in range(2):
                arrived(unit, 1, yy, zz, at.far_x)
        to_core(unit, 2).start()

    def stage6(unit):
        other = 1 - c
        await_bytes(whole_ref.at[unit, y, other, :, :, cut[0]], core_sem.at[unit, 0])
        await_bytes(whole_ref.at[unit, at.far_y, other, :, :, cut[0]], core_sem.at[unit, 1])
        await_bytes(whole_ref.at[unit, :, other, :, :, cut[1]], core_sem.at[unit, 2])
        for colour in range(2):
            rows = cut[colour]
            await_bytes(whole_ref.at[unit, :, c, :, :, rows], send_sem.at[unit, colour, 4])
            whole_x = whole_ref.at[unit, 0, c, :, 0, rows] if colour == 0 else None
            if colour == 0:
                await_bytes(whole_x, send_sem.at[unit, 0, 2])
                await_bytes(whole_ref.at[unit, 0, c, :, :, rows], send_sem.at[unit, 0, 3])
            else:
                await_bytes(whole_ref.at[unit, 0, c, :, :, rows], send_sem.at[unit, 1, 2])
                await_bytes(whole_ref.at[unit, 0, c, 0, 0, rows], send_sem.at[unit, 1, 3])
            for level in range(3):

                def ups(level=level):
                    if colour == 0:
                        ref = whole_ref.at[unit, 0, c, pl.ds(0, level + 1), 0, rows]
                    else:
                        ref = whole_ref.at[unit, :, c, pl.ds(0, level + 1), 0, rows]
                    return ref

                pl.when(z == level)(
                    lambda level=level: await_bytes(ups(level), send_sem.at[unit, colour, 0])
                )
                pl.when(z == 3 - level)(
                    lambda level=level: await_bytes(ups(level), send_sem.at[unit, colour, 1])
                )

    stages = (stage0, stage1, stage2, stage3, stage4, stage5, stage6)

    def advance(turn, carry):
        for number in reversed(range(len(stages))):
            unit = turn - number

            @pl.when((unit >= 0) & (unit < UNITS))
            def _(number=number, unit=unit):
                stages[number](unit)

        return carry

    lax.fori_loop(0, UNITS + len(stages) - 1, advance, 0)


def gather_all(shards):
    units, share, wide = shards.shape
    return pl.pallas_call(
        gather_kernel,
        in_specs=[pl.BlockSpec(memory_space=pl.ANY)],
        out_specs=pl.BlockSpec(memory_space=pl.ANY),
        out_shape=jax.ShapeDtypeStruct((units, 2, 2, 4, 2, share, wide), jnp.bfloat16),
        scratch_shapes=[
            pltpu.SemaphoreType.DMA((units,)),
            pltpu.SemaphoreType.DMA((units, 2, 5)),
            pltpu.SemaphoreType.DMA((units, 2, 2, 4, 2)),
            pltpu.SemaphoreType.DMA((units, 3)),
        ],
        compiler_params=pltpu.CompilerParams(
            collective_id=0, has_side_effects=True, vmem_limit_bytes=16 << 20
        ),
    )(shards)


def reduce_kernel(
    pt_ref,
    q_ref,
    out_ref,
    ptx_ref,
    qx_ref,
    p_buf,
    q_buf,
    dw,
    rya,
    rxa,
    rua,
    rda,
    rxb,
    rub,
    rdb,
    ryb,
    load_sem,
    give_sem,
    take_sem,
    send_sem,
    recv_sem,
    credit,
):
    at = Place()
    z, x, y, c = at.z, at.x, at.y, at.c
    far_x, far_y = at.far_x, at.far_y
    share = out_ref.shape[1]
    row_a, row_b = pl.ds(0, ROWS_A), pl.ds(ROWS_A, share - ROWS_A)
    count_p = pt_ref.shape[0]
    at.greet()

    def give_p(index):
        return pltpu.make_async_remote_copy(
            src_ref=pt_ref.at[index],
            dst_ref=ptx_ref.at[index],
            send_sem=give_sem.at[index],
            recv_sem=take_sem.at[index],
            device_id=at.to["core"],
            device_id_type=MESH_ID,
        )

    def give_q(index):
        return pltpu.make_async_remote_copy(
            src_ref=q_ref.at[index, :, 1 - c],
            dst_ref=qx_ref.at[index],
            send_sem=give_sem.at[count_p + index],
            recv_sem=take_sem.at[count_p + index],
            device_id=at.to["core"],
            device_id_type=MESH_ID,
        )

    for index in range(UNITS):
        if (index + index // 5) % 2 == 0:
            give_p((index + index // 5) // 2).start()
        give_q(index).start()
        if index in (4, 5, 7):
            extra = (index - 3) // 2
            give_p(5 + extra).start()
            give_q(UNITS + extra).start()

    names = ["ya0", "ya1", "xa", "ua0", "ua1", "ua2", "da0", "da1", "da2"]
    names += ["xb0", "xb1", "ub0", "ub1", "ub2", "db0", "db1", "db2", "yb"]
    number = {name: index for index, name in enumerate(names)}

    def copy(slot, name, src, dst, kind, shift=0):
        index = number[name] + shift
        return pltpu.make_async_remote_copy(
            src_ref=src,
            dst_ref=dst,
            send_sem=send_sem.at[slot, index],
            recv_sem=recv_sem.at[slot, index],
            device_id=at.to[kind],
            device_id_type=MESH_ID,
        )

    def ya(slot, part):
        side = far_x if part == 0 else x
        return copy(
            slot, f"ya{part}", dw.at[slot, far_y, :, side, row_a], rya.at[slot, part], "y"
        )

    def xa(slot):
        return copy(slot, "xa", dw.at[slot, y, :, far_x, row_a], rxa.at[slot], "x")

    def xb(slot, part):
        return copy(slot, f"xb{part}", dw.at[slot, part, :, far_x, row_b], rxb.at[slot, part], "x")

    def yb(slot):
        return copy(slot, "yb", dw.at[slot, far_y, z, x, row_b], ryb.at[slot], "y")

    def up(slot, colour, d):
        if colour == 0:
            return copy(slot, "ua0", dw.at[slot, y, d, x, row_a], rua.at[slot, d - 1], "up", d - 1)
        return copy(slot, "ub0", dw.at[slot, :, d, x, row_b], rub.at[slot, d - 1], "up", d - 1)

    def down(slot, colour, d):
        if colour == 0:
            return copy(slot, "da0", dw.at[slot, y, d, x, row_a], rda.at[slot, d], "down", d)
        return copy(slot, "db0", dw.at[slot, :, d, x, row_b], rdb.at[slot, d], "down", d)

    def add(place, got):
        total = place[...].astype(jnp.float32) + got[...].astype(jnp.float32)
        place[...] = total.astype(jnp.bfloat16)

    def products(slot, p_index, q_index, more):
        loads = [
            pltpu.make_async_copy(pt_ref.at[p_index], p_buf.at[0], load_sem.at[0]),
            pltpu.make_async_copy(ptx_ref.at[p_index], p_buf.at[1], load_sem.at[1]),
            pltpu.make_async_copy(q_ref.at[q_index, :, c], q_buf.at[0], load_sem.at[2]),
            pltpu.make_async_copy(qx_ref.at[q_index], q_buf.at[1], load_sem.at[3]),
        ]
        for load in loads:
            load.start()
        for load in loads:
            load.wait()

        def one(step, carry):
            side, zz = step // 4, step % 4
            yy = jnp.where(side == 0, far_y, y)
            rows = pl.ds(pl.multiple_of(zz * 2 * share, 2 * share), 2 * share)
            total = dot_plain(p_buf[0, rows, :], q_buf[0, yy]) + dot_plain(
                p_buf[1, rows, :], q_buf[1, yy]
            )
            total = total.reshape(2, share, WIDE)
            if more:
                total = total + dw[slot, yy, zz].astype(jnp.float32)
            dw[slot, yy, zz] = total.astype(jnp.bfloat16)
            return carry

        lax.fori_loop(0, 8, one, 0)

    def stage0(turn):
        slot = turn % SLOTS_IN_FLIGHT
        p_index = (turn + turn // 5) // 2

        @pl.when((turn + turn // 5) % 2 == 0)
        def _():
            give_p(p_index).wait_recv()

        give_q(turn).wait_recv()
        products(slot, p_index, turn, False)

        @pl.when((turn == 4) | (turn == 5) | (turn == 7))
        def _():
            extra = (turn - 3) // 2
            give_p(5 + extra).wait_recv()
            give_q(UNITS + extra).wait_recv()
            products(slot, 5 + extra, UNITS + extra, True)

        @pl.when(turn >= SLOTS_IN_FLIGHT)
        def _():
            pl.semaphore_wait(credit.at[0], 1)
            pl.semaphore_wait(credit.at[1], 1)
            pl.when(at.has_up)(lambda: pl.semaphore_wait(credit.at[2], 1))
            pl.when(at.has_down)(lambda: pl.semaphore_wait(credit.at[3], 1))

        ya(slot, 0).start()
        xb(slot, 0).start()
        ya(slot, 1).start()
        xb(slot, 1).start()

    def z_step(slot, colour, step):
        @pl.when(z <= step - 1)
        def _():
            d = z + 4 - step

            @pl.when(z >= 1)
            def _():
                up(slot, colour, d).wait_recv()
                if colour == 0:
                    add(dw.at[slot, y, d, x, row_a], rua.at[slot, d - 1])
                else:
                    add(dw.at[slot, 0, d, x, row_b], rub.at[slot, d - 1, 0])
                    add(dw.at[slot, 1, d, x, row_b], rub.at[slot, d - 1, 1])

            up(slot, colour, d).start()

        @pl.when(3 - z <= step - 1)
        def _():
            d = z - 4 + step

            @pl.when(z <= 2)
            def _():
                down(slot, colour, d).wait_recv()
                if colour == 0:
                    add(dw.at[slot, y, d, x, row_a], rda.at[slot, d])
                else:
                    add(dw.at[slot, 0, d, x, row_b], rdb.at[slot, d, 0])
                    add(dw.at[slot, 1, d, x, row_b], rdb.at[slot, d, 1])

            down(slot, colour, d).start()

    def stage1(turn):
        slot = turn % SLOTS_IN_FLIGHT
        for part in range(2):
            xb(slot, part).wait_recv()
            for zz in range(4):
                add(dw.at[slot, part, zz, x, row_b], rxb.at[slot, part, zz])
        z_step(slot, 1, 1)
        ya(slot, 0).wait_recv()
        for zz in range(4):
            add(dw.at[slot, y, zz, far_x, row_a], rya.at[slot, 0, zz])
        xa(slot).start()
        ya(slot, 1).wait_recv()
        for zz in range(4):
            add(dw.at[slot, y, zz, x, row_a], rya.at[slot, 1, zz])

    def stage2(turn):
        slot = turn % SLOTS_IN_FLIGHT
        z_step(slot, 1, 2)
        xa(slot).wait_recv()
        for zz in range(4):
            add(dw.at[slot, y, zz, x, row_a], rxa.at[slot, zz])
        z_step(slot, 0, 1)

    def stage3(turn):
        slot = turn % SLOTS_IN_FLIGHT
        z_step(slot, 1, 3)
        z_step(slot, 0, 2)

    def stage4(turn):
        slot = turn % SLOTS_IN_FLIGHT
        z_step(slot, 0, 3)

        @pl.when(z >= 1)
        def _():
            up(slot, 1, z).wait_recv()
            for yy in range(2):
                add(dw.at[slot, yy, z, x, row_b], rub.at[slot, z - 1, yy])

        @pl.when(z <= 2)
        def _():
            down(slot, 1, z).wait_recv()
            for yy in range(2):
                add(dw.at[slot, yy, z, x, row_b], rdb.at[slot, z, yy])

        yb(slot).start()

    def stage5(turn):
        slot = turn % SLOTS_IN_FLIGHT
        unit = UNITS - 1 - turn
        out_ref[unit, row_a, :] = dw[slot, y, z, x, row_a, :].astype(jnp.float32)

        @pl.when(z >= 1)
        def _():
            up(slot, 0, z).wait_recv()
            out_ref[unit, row_a, :] += rua[slot, z - 1].astype(jnp.float32)

        @pl.when(z <= 2)
        def _():
            down(slot, 0, z).wait_recv()
            out_ref[unit, row_a, :] += rda[slot, z].astype(jnp.float32)

        yb(slot).wait_recv()
        out_ref[unit, row_b, :] = dw[slot, y, z, x, row_b, :].astype(jnp.float32) + ryb[
            slot
        ].astype(jnp.float32)

        ya(slot, 0).wait_send()
        ya(slot, 1).wait_send()
        xa(slot).wait_send()
        xb(slot, 0).wait_send()
        xb(slot, 1).wait_send()
        yb(slot).wait_send()
        for colour in range(2):
            for step in range(1, 4):

                @pl.when(z <= step - 1)
                def _(colour=colour, step=step):
                    up(slot, colour, z + 4 - step).wait_send()

                @pl.when(3 - z <= step - 1)
                def _(colour=colour, step=step):
                    down(slot, colour, z - 4 + step).wait_send()

        @pl.when(turn + SLOTS_IN_FLIGHT < UNITS)
        def _():
            def grant(kind, index):
                pl.semaphore_signal(
                    credit.at[index], inc=1, device_id=at.to[kind], device_id_type=MESH_ID
                )

            grant("x", 0)
            grant("y", 1)
            pl.when(at.has_up)(lambda: grant("up", 3))
            pl.when(at.has_down)(lambda: grant("down", 2))

    stages = (stage0, stage1, stage2, stage3, stage4, stage5)

    def advance(now, carry):
        for step in range(len(stages)):
            turn = now - step

            @pl.when((turn >= 0) & (turn < UNITS))
            def _(step=step, turn=turn):
                stages[step](turn)

        return carry

    lax.fori_loop(0, UNITS + len(stages) - 1, advance, 0)
    for index in range(count_p):
        give_p(index).wait_send()
    for index in range(q_ref.shape[0]):
        give_q(index).wait_send()


def reduce_all(turned, parts, share):
    count_p, width, rows = turned.shape
    count_q = parts.shape[0]
    low = jnp.bfloat16
    slots, rest = SLOTS_IN_FLIGHT, share - ROWS_A
    return pl.pallas_call(
        reduce_kernel,
        in_specs=[pl.BlockSpec(memory_space=pl.ANY)] * 2,
        out_specs=[
            pl.BlockSpec(memory_space=pltpu.VMEM),
            pl.BlockSpec(memory_space=pl.ANY),
            pl.BlockSpec(memory_space=pl.ANY),
        ],
        out_shape=[
            jax.ShapeDtypeStruct((UNITS, share, WIDE), jnp.float32),
            jax.ShapeDtypeStruct((count_p, width, rows), low),
            jax.ShapeDtypeStruct((count_q, 2, rows, WIDE), low),
        ],
        scratch_shapes=[
            pltpu.VMEM((2, width, rows), low),
            pltpu.VMEM((2, 2, rows, WIDE), low),
            pltpu.VMEM((slots, 2, 4, 2, share, WIDE), low),
            pltpu.VMEM((slots, 2, 4, ROWS_A, WIDE), low),
            pltpu.VMEM((slots, 4, ROWS_A, WIDE), low),
            pltpu.VMEM((slots, 3, ROWS_A, WIDE), low),
            pltpu.VMEM((slots, 3, ROWS_A, WIDE), low),
            pltpu.VMEM((slots, 2, 4, rest, WIDE), low),
            pltpu.VMEM((slots, 3, 2, rest, WIDE), low),
            pltpu.VMEM((slots, 3, 2, rest, WIDE), low),
            pltpu.VMEM((slots, rest, WIDE), low),
            pltpu.SemaphoreType.DMA((4,)),
            pltpu.SemaphoreType.DMA((count_p + count_q,)),
            pltpu.SemaphoreType.DMA((count_p + count_q,)),
            pltpu.SemaphoreType.DMA((slots, 18)),
            pltpu.SemaphoreType.DMA((slots, 18)),
            pltpu.SemaphoreType.REGULAR((4,)),
        ],
        compiler_params=pltpu.CompilerParams(
            collective_id=1, has_side_effects=True, vmem_limit_bytes=60 << 20
        ),
    )(turned, parts)[0]


def gather_plain(shards):
    units, share, wide = shards.shape
    whole = lax.all_gather(shards, MIXED, axis=1, tiled=True)
    return whole.reshape(units, lax.axis_size("tensor"), C, wide)


def reduce_plain(turned, parts, share):
    reduced = []
    for turn in range(UNITS):
        whole = jnp.einsum(
            "kr,trn->tkn", turned[(turn + turn // 5) // 2], parts[turn],
            preferred_element_type=jnp.float32,
        )
        if turn in (4, 5, 7):
            extra = (turn - 3) // 2
            whole = whole + jnp.einsum(
                "kr,trn->tkn", turned[5 + extra], parts[UNITS + extra],
                preferred_element_type=jnp.float32,
            )
        whole = whole.astype(jnp.bfloat16).reshape(-1, whole.shape[2])
        reduced.append(
            lax.psum_scatter(whole, MIXED, scatter_dimension=0, tiled=True).astype(jnp.float32)
        )
    return jnp.stack(reduced[::-1], 0)


def to_pixels(values, tensor_size):
    slots, frames, width, pixels = values.shape
    own = pixels // tensor_size
    turned = jnp.transpose(values, (3, 0, 1, 2)).reshape(tensor_size, own * slots * frames, width)
    return lax.all_to_all(turned, "tensor", 0, 0, tiled=True)


def to_channels(values, slots, pixels):
    tensor_size, rows, width = values.shape
    arrived = lax.all_to_all(values, "tensor", 0, 0, tiled=True)
    return jnp.transpose(arrived.reshape(pixels, slots, FRAMES, width), (1, 2, 3, 0))


def body(
    by_kernel,
    latent,
    clip_flags,
    cotangent,
    norm_gain,
    norm_shift,
    channel_bias,
    hidden_bias,
    weight_in,
    weight_qkv,
    weight_out,
    weight_up,
    weight_down,
    weight_proj,
):
    tensor_size = lax.axis_size("tensor")
    slots, frames, width, pixels = latent.shape
    share = weight_in.shape[0]
    hidden_width = hidden_bias.shape[0]
    flags = (clip_flags > 0)[:, None, None, None]

    wide = 2 * width

    shards = []
    side = jnp.concatenate
    for block in range(2):
        shards.append(weight_qkv[block, :, :2].reshape(share, wide))
        other = weight_in if block == 0 else weight_out[0].T
        shards.append(side([weight_qkv[block, :, 2], other], 1))
    shards.append(side([weight_out[1].T, weight_proj], 1))
    shards += [weight_up[:, :wide], weight_up[:, wide:]]
    down_turned = weight_down.T
    shards += [down_turned[:, :wide], down_turned[:, wide:]]
    shards = jnp.stack(shards, 0)
    if by_kernel:
        whole = gather_all(shards).reshape(UNITS, tensor_size, C, wide)
    else:
        whole = gather_plain(shards)
    full_qk = (whole[0], whole[2])
    full_v = (whole[1, :, :, :width], whole[3, :, :, :width])
    full_in = whole[1, :, :, width:]
    full_out = (whole[3, :, :, width:], whole[4, :, :, :width])
    full_proj = whole[4, :, :, width:]
    full_up = (whole[5], whole[6])
    full_down = (whole[7], whole[8])

    packed = jnp.concatenate([norm_gain, norm_shift, channel_bias], 0)
    packed = lax.all_gather(
        jnp.concatenate([packed.reshape(-1), hidden_bias]), "tensor", axis=0, tiled=False
    )
    channel_params = packed[:, : 13 * width].reshape(tensor_size, 13, width)
    channel_params = jnp.transpose(channel_params, (1, 0, 2)).reshape(13, C)
    gains, shifts, biases = channel_params[:4], channel_params[4:8], channel_params[8:]
    hidden_full = packed[:, 13 * width :]

    start = latent.astype(jnp.float32)
    cot = cotangent.astype(jnp.float32)
    group_width = C // GROUPS
    grouped = start.reshape(slots, frames, width // group_width, group_width, pixels)
    group_centre = jnp.mean(grouped, axis=(1, 3, 4), keepdims=True)
    offset = grouped - group_centre
    group_inverse = lax.rsqrt(jnp.mean(offset * offset, axis=(1, 3, 4), keepdims=True) + 1e-06)
    group_hat = (offset * group_inverse).reshape(start.shape)
    normed = group_hat * norm_gain[0][:, None] + norm_shift[0][:, None]
    arrived = to_pixels(normed.astype(jnp.bfloat16), tensor_size)
    rows = arrived.shape[1]
    inputs_in = jnp.transpose(arrived, (1, 0, 2)).reshape(rows, C)

    grad_moved_local = jnp.where(flags, cot, 0.0)
    bias_moved = jnp.sum(grad_moved_local, axis=(0, 1, 3))
    grad_moved = to_pixels(grad_moved_local.astype(jnp.bfloat16), tensor_size)

    def join(parts):
        return jnp.transpose(parts, (1, 0, 2)).reshape(rows, parts.shape[0] * parts.shape[2])

    stream = join(spread(inputs_in, full_in)) + biases[0]
    position = jnp.tile(make_positions(), (rows // FRAMES, 1))
    kept = []
    for block in range(2):
        hat, inverse = layer_stats(stream)
        lifted = (hat * gains[1 + block] + shifts[1 + block] + position).astype(jnp.bfloat16)
        qk = spread(lifted, full_qk[block]).astype(jnp.bfloat16)
        values = spread(lifted, full_v[block]).astype(jnp.bfloat16)
        attended = attend(qk, values)
        stream = stream + collapse(attended, full_out[block]) + biases[1 + block]
        kept.append((hat, inverse, lifted, qk, values, attended))
    hat_feed, inverse_feed = layer_stats(stream)
    inputs_up = (hat_feed * gains[3] + shifts[3]).astype(jnp.bfloat16)
    pre_act = [
        spread(inputs_up, full_up[half])
        + hidden_full[:, None, half * wide : half * wide + wide]
        for half in range(2)
    ]
    hidden = [jax.nn.gelu(pre, approximate=False).astype(jnp.bfloat16) for pre in pre_act]
    stream = stream + collapse(hidden[0], full_down[0]) + collapse(hidden[1], full_down[1])
    stream = stream + biases[3]
    inputs_proj = stream.astype(jnp.bfloat16)
    moved = spread(inputs_proj, full_proj) + biases[4].reshape(tensor_size, 1, width)
    moved_local = to_channels(moved.astype(jnp.bfloat16), slots, pixels).astype(jnp.float32)
    output = jnp.where(flags, start + moved_local, start).astype(jnp.bfloat16)

    bias_grads = [None] * 4
    gain_grads = [None] * 3
    shift_grads = [None] * 3
    empty = jnp.zeros((tensor_size, rows, width), jnp.bfloat16)
    turned, parts = [None] * 8, [None] * 12
    turned[5] = inputs_proj.T
    parts[9] = side([empty, grad_moved], 2)
    grad_stream = collapse(grad_moved, full_proj)
    bias_grads[3] = jnp.sum(grad_stream, 0)
    grad_low = grad_stream.astype(jnp.bfloat16)
    turned[0] = grad_low.T
    parts[0], parts[1] = hidden[1], hidden[0]
    turned[1] = inputs_up.T
    hidden_grads = [None, None]
    grad_normed = 0.0
    for half in (1, 0):
        grad_hidden = spread(grad_low, full_down[half])
        unused, gelu_pull = jax.vjp(partial(jax.nn.gelu, approximate=False), pre_act[half])
        grad_pre = gelu_pull(grad_hidden)[0]
        hidden_grads[half] = jnp.sum(grad_pre, 1)
        parts[3 - half] = grad_pre.astype(jnp.bfloat16)
        grad_normed = grad_normed + collapse(parts[3 - half], full_up[half])
    hidden_grad = side(hidden_grads, 1)
    grad_layer, gain_grads[2], shift_grads[2] = layer_back(
        grad_normed, hat_feed, inverse_feed, gains[3]
    )
    grad_stream = grad_stream + grad_layer
    for block in (1, 0):
        hat, inverse, lifted, qk, values, attended = kept[block]
        bias_grads[1 + block] = jnp.sum(grad_stream, 0)
        grad_low = grad_stream.astype(jnp.bfloat16)
        turned[2 if block == 1 else 6] = grad_low.T
        pair = [attended, empty] if block == 1 else [empty, attended]
        parts[4 if block == 1 else 10] = side(pair, 2)
        grad_attended = spread(grad_low, full_out[block]).astype(jnp.bfloat16)
        grad_qk, grad_values = attend_back(qk, values, grad_attended)
        turned[3 if block == 1 else 4] = lifted.T
        parts[5 if block == 1 else 7] = side([grad_values, empty], 2)
        parts[6 if block == 1 else 8] = grad_qk
        grad_lifted = collapse(grad_qk, full_qk[block]) + collapse(grad_values, full_v[block])
        grad_layer, gain_grads[block], shift_grads[block] = layer_back(
            grad_lifted, hat, inverse, gains[1 + block]
        )
        grad_stream = grad_stream + grad_layer
    bias_grads[0] = jnp.sum(grad_stream, 0)
    grad_low = grad_stream.astype(jnp.bfloat16)
    grad_low_parts = jnp.transpose(grad_low.reshape(rows, tensor_size, width), (1, 0, 2))
    turned[7] = inputs_in.T
    parts[11] = side([empty, grad_low_parts], 2)
    turned, parts = jnp.stack(turned, 0), jnp.stack(parts, 0)
    if by_kernel:
        reduced = reduce_all(turned, parts.reshape(12, 2, 2, rows, wide), share)
    else:
        reduced = reduce_plain(turned, parts, share)
    qkv_grads = [
        side([reduced[2 * block], reduced[2 * block + 1, :, :width]], 1).reshape(share, 3, width)
        for block in range(2)
    ]
    out_grads = [reduced[3, :, width:].T, reduced[4, :, :width].T]
    in_grad, proj_grad = reduced[1, :, width:], reduced[4, :, width:]
    up_grad = side([reduced[5], reduced[6]], 1)
    down_grad = side([reduced[7], reduced[8]], 1)
    grad_normed = collapse(grad_low_parts, full_in).astype(jnp.bfloat16)
    grad_normed = jnp.transpose(grad_normed.reshape(rows, tensor_size, width), (1, 0, 2))
    grad_normed = to_channels(grad_normed, slots, pixels).astype(jnp.float32)
    scaled = grad_normed * norm_gain[0][:, None]
    scaled_groups = scaled.reshape(grouped.shape)
    hat_groups = group_hat.reshape(grouped.shape)
    first = jnp.mean(scaled_groups, axis=(1, 3, 4), keepdims=True)
    second = jnp.mean(scaled_groups * hat_groups, axis=(1, 3, 4), keepdims=True)
    grad_group = group_inverse * (scaled_groups - first - hat_groups * second)
    latent_grad = cot + grad_group.reshape(start.shape)
    group_gain_grad = jnp.sum(grad_normed * group_hat, axis=(0, 1, 3))
    group_shift_grad = jnp.sum(grad_normed, axis=(0, 1, 3))

    vectors = jnp.stack(gain_grads + shift_grads + bias_grads, 0)
    vectors = jnp.transpose(vectors.reshape(10, tensor_size, width), (1, 0, 2))
    vectors = jnp.concatenate([vectors.reshape(tensor_size, 10 * width), hidden_grad], 1)
    vectors = lax.psum_scatter(vectors, "tensor", scatter_dimension=0, tiled=False)
    sums = lax.psum(
        jnp.concatenate([vectors, group_gain_grad, group_shift_grad, bias_moved]), "dp"
    )
    channel_sums = sums[: 10 * width].reshape(10, width)
    hidden_bias_grad = sums[10 * width : 10 * width + hidden_width]
    local_sums = sums[10 * width + hidden_width :].reshape(3, width)
    gain_grad = jnp.concatenate([local_sums[0:1], channel_sums[0:3]], 0)
    shift_grad = jnp.concatenate([local_sums[1:2], channel_sums[3:6]], 0)
    channel_bias_grad = jnp.concatenate([channel_sums[6:10], local_sums[2:3]], 0)
    return (
        output,
        latent_grad,
        gain_grad,
        shift_grad,
        channel_bias_grad,
        hidden_bias_grad,
        in_grad,
        jnp.stack(qkv_grads, 0),
        jnp.stack(out_grads, 0),
        up_grad,
        down_grad.T,
        proj_grad,
    )


def solution(mesh):
    placed = (
        P("dp", None, "tensor", None),
        P("dp"),
        P("dp", None, "tensor", None),
        P(None, "tensor"),
        P(None, "tensor"),
        P(None, "tensor"),
        P("tensor"),
        P("dp", "tensor"),
        P(None, "dp", None, "tensor"),
        P(None, "tensor", "dp"),
        P("dp", "tensor"),
        P("tensor", "dp"),
        P("dp", "tensor"),
    )
    return jax.shard_map(
        partial(body, tuple(mesh.shape[name] for name in ("dp", "tensor")) == (8, 4)),
        mesh=mesh,
        in_specs=placed,
        out_specs=(
            P("dp", None, "tensor", None),
            P("dp", None, "tensor", None),
            P(None, "tensor"),
            P(None, "tensor"),
            P(None, "tensor"),
            P("tensor"),
            P("dp", "tensor"),
            P(None, "dp", None, "tensor"),
            P(None, "tensor", "dp"),
            P("dp", "tensor"),
            P("tensor", "dp"),
            P("dp", "tensor"),
        ),
        check_vma=False,
    )
```

```python
from functools import partial
import math

import jax
import jax.numpy as jnp
from jax import lax
from jax.experimental import pallas as pl
from jax.experimental.pallas import tpu as pltpu
from jax.sharding import PartitionSpec as P

C = 1280
GROUPS = 32
FRAMES = 16
HEAD = 160
BLOCK = 128
MIXED = ("tensor", "dp")


def spread(rows, weight):
    return jnp.einsum("rk,tkn->trn", rows, weight, preferred_element_type=jnp.float32)


def collapse(parts, weight):
    return jnp.einsum("trn,tkn->rk", parts, weight, preferred_element_type=jnp.float32)


def make_positions():
    channel_ids = jnp.arange(C)
    pair_rate = jnp.exp((channel_ids // 2).astype(jnp.float32) * (-2.0 * math.log(10000.0) / C))
    angles = jnp.arange(FRAMES).astype(jnp.float32)[:, None] * pair_rate[None, :]
    return jnp.where(channel_ids[None, :] % 2 == 0, jnp.sin(angles), jnp.cos(angles))


def layer_stats(stream):
    centre = jnp.mean(stream, axis=1, keepdims=True)
    offset = stream - centre
    inverse = lax.rsqrt(jnp.mean(offset * offset, axis=1, keepdims=True) + 1e-05)
    return offset * inverse, inverse


def layer_back(grad_out, normal_part, inverse, gain):
    scaled = grad_out * gain
    first = jnp.mean(scaled, axis=1, keepdims=True)
    second = jnp.mean(scaled * normal_part, axis=1, keepdims=True)
    grad_in = inverse * (scaled - first - normal_part * second)
    return grad_in, jnp.sum(grad_out * normal_part, 0), jnp.sum(grad_out, 0)


def dot_rows(left, right):
    return lax.dot_general(left, right, (((1,), (1,)), ((), ())), preferred_element_type=jnp.float32)


def dot_plain(left, right):
    return lax.dot_general(left, right, (((1,), (0,)), ((), ())), preferred_element_type=jnp.float32)


def dot_first(left, right):
    return lax.dot_general(left, right, (((0,), (0,)), ((), ())), preferred_element_type=jnp.float32)


def same_pixel(block):
    row = lax.broadcasted_iota(jnp.int32, (block, block), 0) // FRAMES
    col = lax.broadcasted_iota(jnp.int32, (block, block), 1) // FRAMES
    return row == col


def head_probs(query, key, same, scale):
    scores = jnp.where(same, dot_rows(query, key) * scale, -1e30)
    top = jnp.max(scores, axis=1, keepdims=True)
    weights = jnp.where(same, jnp.exp(scores - top), 0.0)
    return weights / jnp.sum(weights, axis=1, keepdims=True)


def attend_kernel(scale, qk_ref, v_ref, out_ref):
    rows, width = out_ref.shape[1], out_ref.shape[2]
    block = min(BLOCK, rows)
    same = same_pixel(block)
    for start in range(0, rows, block):
        for head in range(width // HEAD):
            here, low = slice(start, start + block), head * HEAD
            query = qk_ref[0, here, low : low + HEAD]
            key = qk_ref[0, here, width + low : width + low + HEAD]
            value = v_ref[0, here, low : low + HEAD]
            probs = head_probs(query, key, same, scale).astype(jnp.bfloat16)
            out_ref[0, here, low : low + HEAD] = dot_plain(probs, value).astype(jnp.bfloat16)


def part_spec(array):
    return pl.BlockSpec((1,) + array.shape[1:], lambda t: (t, 0, 0))


def attend(qk, values):
    return pl.pallas_call(
        partial(attend_kernel, 1.0 / math.sqrt(HEAD)),
        grid=(qk.shape[0],),
        in_specs=[part_spec(qk), part_spec(values)],
        out_specs=part_spec(values),
        out_shape=jax.ShapeDtypeStruct(values.shape, jnp.bfloat16),
        compiler_params=pltpu.CompilerParams(vmem_limit_bytes=32 << 20),
    )(qk, values)


def attend_back_kernel(scale, qk_ref, v_ref, grad_ref, dqk_ref, dv_ref):
    rows, width = grad_ref.shape[1], grad_ref.shape[2]
    block = min(BLOCK, rows)
    same = same_pixel(block)
    for start in range(0, rows, block):
        for head in range(width // HEAD):
            here, low = slice(start, start + block), head * HEAD
            query = qk_ref[0, here, low : low + HEAD]
            key = qk_ref[0, here, width + low : width + low + HEAD]
            value = v_ref[0, here, low : low + HEAD]
            grad = grad_ref[0, here, low : low + HEAD]
            probs = head_probs(query, key, same, scale)
            grad_probs = dot_rows(grad, value)
            centred = jnp.sum(probs * grad_probs, axis=1, keepdims=True)
            grad_raw = (probs * (grad_probs - centred) * scale).astype(jnp.bfloat16)
            dqk_ref[0, here, low : low + HEAD] = dot_plain(grad_raw, key).astype(jnp.bfloat16)
            dqk_ref[0, here, width + low : width + low + HEAD] = dot_first(grad_raw, query).astype(
                jnp.bfloat16
            )
            dv_ref[0, here, low : low + HEAD] = dot_first(probs.astype(jnp.bfloat16), grad).astype(
                jnp.bfloat16
            )


def attend_back(qk, values, grad):
    return pl.pallas_call(
        partial(attend_back_kernel, 1.0 / math.sqrt(HEAD)),
        grid=(qk.shape[0],),
        in_specs=[part_spec(qk), part_spec(values), part_spec(values)],
        out_specs=[part_spec(qk), part_spec(values)],
        out_shape=[
            jax.ShapeDtypeStruct(qk.shape, jnp.bfloat16),
            jax.ShapeDtypeStruct(values.shape, jnp.bfloat16),
        ],
        compiler_params=pltpu.CompilerParams(vmem_limit_bytes=32 << 20),
    )(qk, values, grad)


UNITS = 9
WIDE = 640
SLOTS_IN_FLIGHT = 6
ROWS_A = 96
MESH_ID = pl.DeviceIdType.MESH


class Place:
    def __init__(self):
        dp, tn = lax.axis_index("dp"), lax.axis_index("tensor")
        self.z, self.x = dp // 2, dp % 2
        self.y, self.c = tn // 2, tn % 2
        self.far_x, self.far_y = 1 - self.x, 1 - self.y
        self.to = {
            "x": (self.z * 2 + self.far_x, tn),
            "y": (dp, self.far_y * 2 + self.c),
            "core": (dp, self.y * 2 + 1 - self.c),
            "up": (dp + 2, tn),
            "down": (dp - 2, tn),
        }
        self.has_up = self.z < 3
        self.has_down = self.z > 0

    def greet(self):
        barrier = pltpu.get_barrier_semaphore()

        def hello(name):
            pl.semaphore_signal(barrier, inc=1, device_id=self.to[name], device_id_type=MESH_ID)

        for name in ("x", "y", "core"):
            hello(name)
        pl.when(self.has_up)(lambda: hello("up"))
        pl.when(self.has_down)(lambda: hello("down"))
        pl.semaphore_wait(barrier, 3 + (6 - self.z) // 4 + (self.z + 3) // 4)


def await_bytes(ref, sem):
    pltpu.make_async_copy(ref, ref, sem).wait()


def forward_kernel(
    shard_ref,
    x_ref,
    gains_ref,
    shifts_ref,
    biases_ref,
    out_bias_ref,
    hidden_bias_ref,
    position_ref,
    moved_part_ref,
    whole_ref,
    q_ref,
    pt_ref,
    stream_out_ref,
    qk_ref,
    v_ref,
    slope_ref,
    moved_ref,
    stream,
    xb,
    ptb,
    qkb,
    vb,
    attb,
    hid,
    slopeb,
    wb,
    tile_sem,
    save_sem,
    local_sem,
    send_sem,
    recv_sem,
    core_sem,
):
    at = Place()
    z, x, y, c = at.z, at.x, at.y, at.c
    share = shard_ref.shape[1]
    cut = (pl.ds(0, ROWS_A), pl.ds(ROWS_A, share - ROWS_A))
    kinds = {"up": 0, "down": 1, "x": 2, "y": 3, "core": 4}
    at.greet()

    def send(unit, colour, yy, zz, xx, kind, own=False):
        place = whole_ref.at[unit, yy, c, zz, xx, cut[colour]]
        pltpu.make_async_remote_copy(
            src_ref=shard_ref.at[unit, cut[colour]] if own else place,
            dst_ref=place,
            send_sem=send_sem.at[unit, colour, kinds[kind]],
            recv_sem=recv_sem.at[unit, colour, yy, zz, xx],
            device_id=at.to[kind],
            device_id_type=MESH_ID,
        ).start()

    def arrived(unit, colour, yy, zz, xx):
        await_bytes(
            whole_ref.at[unit, yy, c, zz, xx, cut[colour]], recv_sem.at[unit, colour, yy, zz, xx]
        )

    def own_copy(unit):
        return pltpu.make_async_copy(
            shard_ref.at[unit], whole_ref.at[unit, y, c, z, x], local_sem.at[unit]
        )

    def to_core(unit, part):
        if part == 2:
            place = whole_ref.at[unit, :, c, :, :, cut[1]]
        else:
            place = whole_ref.at[unit, y if part == 0 else at.far_y, c, :, :, cut[0]]
        return pltpu.make_async_remote_copy(
            src_ref=place,
            dst_ref=place,
            send_sem=send_sem.at[unit, part // 2, 4],
            recv_sem=core_sem.at[unit, part],
            device_id=at.to["core"],
            device_id_type=MESH_ID,
        )

    def from_z(unit, colour, step, yy):
        @pl.when(z >= step)
        def _():
            zz = z - step
            arrived(unit, colour, yy, zz, x)
            pl.when(at.has_up)(lambda: send(unit, colour, yy, zz, x, "up"))
            send(unit, colour, yy, zz, x, "x")
            if colour == 0:
                send(unit, colour, yy, zz, x, "y")

        @pl.when(z + step <= 3)
        def _():
            zz = z + step
            arrived(unit, colour, yy, zz, x)
            pl.when(at.has_down)(lambda: send(unit, colour, yy, zz, x, "down"))
            send(unit, colour, yy, zz, x, "x")
            if colour == 0:
                send(unit, colour, yy, zz, x, "y")

    def from_x(unit, step):
        def one(zz):
            arrived(unit, 0, y, zz, at.far_x)
            send(unit, 0, y, zz, at.far_x, "y")

        if step == 0:
            one(z)
        else:
            pl.when(z >= step)(lambda: one(z - step))
            pl.when(z + step <= 3)(lambda: one(z + step))

    def stage0(unit):
        own_copy(unit).start()
        pl.when(at.has_up)(lambda: send(unit, 0, y, z, x, "up", True))
        pl.when(at.has_down)(lambda: send(unit, 0, y, z, x, "down", True))
        send(unit, 1, y, z, x, "y", True)
        send(unit, 0, y, z, x, "x", True)
        pl.when(at.has_up)(lambda: send(unit, 1, y, z, x, "up", True))
        pl.when(at.has_down)(lambda: send(unit, 1, y, z, x, "down", True))
        send(unit, 0, y, z, x, "y", True)
        send(unit, 1, y, z, x, "x", True)

    def stage1(unit):
        from_z(unit, 0, 1, y)
        arrived(unit, 1, at.far_y, z, x)
        pl.when(at.has_up)(lambda: send(unit, 1, at.far_y, z, x, "up"))
        pl.when(at.has_down)(lambda: send(unit, 1, at.far_y, z, x, "down"))
        send(unit, 1, at.far_y, z, x, "x")
        from_z(unit, 1, 1, y)
        from_x(unit, 0)

    def stage2(unit):
        from_z(unit, 0, 2, y)
        from_z(unit, 1, 1, at.far_y)
        from_z(unit, 1, 2, y)
        from_x(unit, 1)

    def stage3(unit):
        from_z(unit, 0, 3, y)
        from_z(unit, 1, 2, at.far_y)
        from_z(unit, 1, 3, y)
        from_x(unit, 2)

    def stage4(unit):
        from_z(unit, 1, 3, at.far_y)
        from_x(unit, 3)
        own_copy(unit).wait()
        to_core(unit, 0).start()

    def stage5(unit):
        for zz in range(4):
            for xx in range(2):
                arrived(unit, 0, at.far_y, zz, xx)
        to_core(unit, 1).start()
        for zz in range(4):
            for yy in range(2):
                arrived(unit, 1, yy, zz, at.far_x)
        to_core(unit, 2).start()

    def stage6(unit):
        other = 1 - c
        await_bytes(whole_ref.at[unit, y, other, :, :, cut[0]], core_sem.at[unit, 0])
        await_bytes(whole_ref.at[unit, at.far_y, other, :, :, cut[0]], core_sem.at[unit, 1])
        await_bytes(whole_ref.at[unit, :, other, :, :, cut[1]], core_sem.at[unit, 2])
        for colour in range(2):
            rows = cut[colour]
            await_bytes(whole_ref.at[unit, :, c, :, :, rows], send_sem.at[unit, colour, 4])
            whole_x = whole_ref.at[unit, 0, c, :, 0, rows] if colour == 0 else None
            if colour == 0:
                await_bytes(whole_x, send_sem.at[unit, 0, 2])
                await_bytes(whole_ref.at[unit, 0, c, :, :, rows], send_sem.at[unit, 0, 3])
            else:
                await_bytes(whole_ref.at[unit, 0, c, :, :, rows], send_sem.at[unit, 1, 2])
                await_bytes(whole_ref.at[unit, 0, c, 0, 0, rows], send_sem.at[unit, 1, 3])
            for level in range(3):

                def ups(level=level):
                    if colour == 0:
                        ref = whole_ref.at[unit, 0, c, pl.ds(0, level + 1), 0, rows]
                    else:
                        ref = whole_ref.at[unit, :, c, pl.ds(0, level + 1), 0, rows]
                    return ref

                pl.when(z == level)(
                    lambda level=level: await_bytes(ups(level), send_sem.at[unit, colour, 0])
                )
                pl.when(z == 3 - level)(
                    lambda level=level: await_bytes(ups(level), send_sem.at[unit, colour, 1])
                )

    stages = (stage0, stage1, stage2, stage3, stage4, stage5, stage6)

    rows_all = x_ref.shape[0]
    width = v_ref.shape[3]
    half_rows = rows_all // 2
    scale = 1.0 / math.sqrt(HEAD)

    def save(source, target):
        copy = pltpu.make_async_copy(source, target, save_sem.at[0])
        copy.start()
        copy.wait()

    def tile_load(unit, t):
        return pltpu.make_async_copy(
            whole_ref.at[unit, t // 2, t % 2], wb.at[t % 2], tile_sem.at[t % 2]
        )

    def each_tile(unit, use):
        tile_load(unit, 0).start()

        def one(t, carry):
            pl.when(t < 3)(lambda: tile_load(unit, t + 1).start())
            tile_load(unit, t).wait()
            use(t, t % 2)
            return carry

        lax.fori_loop(0, 4, one, 0)

    def tile(slot, first, last):
        return wb[slot, :, :, :, first:last].reshape(C, last - first)

    def spread_tile(source, slot, first, last, sink):
        def one(step, carry):
            rows = pl.ds(pl.multiple_of(step * half_rows, half_rows), half_rows)
            sink(rows, dot_plain(source[rows, :], tile(slot, first, last)))
            return carry

        lax.fori_loop(0, 2, one, 0)

    def collapse_tile(source, t, slot, first, last):
        def one(step, carry):
            rows = pl.ds(pl.multiple_of(step * half_rows, half_rows), half_rows)
            stream[rows, :] += dot_rows(source[t, rows, first:last], tile(slot, first, last))
            return carry

        lax.fori_loop(0, 2, one, 0)

    def turn_to(source, index):
        def one(step, carry):
            lanes = pl.ds(pl.multiple_of(step * 128, 128), 128)
            ptb[lanes, :] = source[:, lanes].T
            return carry

        lax.fori_loop(0, C // 128, one, 0)
        save(ptb, pt_ref.at[index])

    chunk = 4 * FRAMES

    def normalise(bias, norm, positions):
        def one(step, carry):
            rows = pl.ds(pl.multiple_of(step * chunk, chunk), chunk)
            values = stream[rows, :] + biases_ref[bias : bias + 1, :]
            stream[rows, :] = values
            centre = jnp.mean(values, axis=1, keepdims=True)
            offset = values - centre
            inverse = lax.rsqrt(jnp.mean(offset * offset, axis=1, keepdims=True) + 1e-05)
            normed = offset * inverse * gains_ref[norm : norm + 1, :] + shifts_ref[norm : norm + 1, :]
            if positions:
                normed = normed.reshape(chunk // FRAMES, FRAMES, C) + position_ref[...][None]
                normed = normed.reshape(chunk, C)
            xb[rows, :] = normed.astype(jnp.bfloat16)
            return carry

        lax.fori_loop(0, rows_all // chunk, one, 0)

    def attention(place):
        same = same_pixel(BLOCK)

        def one(step, carry):
            t, block = step // (rows_all // BLOCK), step % (rows_all // BLOCK)
            rows = pl.ds(pl.multiple_of(block * BLOCK, BLOCK), BLOCK)
            for head in range(width // HEAD):
                low = head * HEAD
                query = qkb[t, rows, low : low + HEAD]
                key = qkb[t, rows, width + low : width + low + HEAD]
                value = vb[t, rows, low : low + HEAD]
                probs = head_probs(query, key, same, scale).astype(jnp.bfloat16)
                attb[t, rows, place + low : place + low + HEAD] = dot_plain(probs, value).astype(
                    jnp.bfloat16
                )
            return carry

        lax.fori_loop(0, 4 * (rows_all // BLOCK), one, 0)

    def attention_block(block):
        normalise(block, 1 + block, True)
        save(stream, stream_out_ref.at[block])

        def qk_tile(t, slot):
            def sink(rows, total):
                qkb[t, rows, :] = total.astype(jnp.bfloat16)

            spread_tile(xb, slot, 0, WIDE, sink)

        def v_tile(t, slot):
            def sink(rows, total):
                vb[t, rows, :] = total[:, :width].astype(jnp.bfloat16)

            spread_tile(xb, slot, 0, 384, sink)

        each_tile(2 * block, qk_tile)
        each_tile(2 * block + 1, v_tile)
        attb[...] = jnp.zeros_like(attb)
        attention((1 - block) * width)
        save(attb, q_ref.at[10 if block == 0 else 4])
        save(qkb, qk_ref.at[block])
        save(vb, v_ref.at[block])
        turn_to(xb, 4 - block)

    def before_units():
        turn_to(x_ref, 7)
        save(moved_part_ref, q_ref.at[9])

    def after_1():
        for t in range(4):
            tile_load(1, t).start()
            tile_load(1, t).wait()

            def sink(rows, total, t=t):
                stream[rows, t * width : (t + 1) * width] = total[:, 64:384]

            spread_tile(x_ref, t % 2, 256, WIDE, sink)
        attention_block(0)

    def after_3():
        each_tile(3, lambda t, slot: collapse_tile(attb, t, slot, 256, WIDE))
        attention_block(1)

    def after_4():
        each_tile(4, lambda t, slot: collapse_tile(attb, t, slot, 0, 384))
        normalise(2, 3, False)
        save(stream, stream_out_ref.at[2])
        turn_to(xb, 1)

    def after_up(half):
        def up_tile(t, slot):
            def sink(rows, total):
                pre = total + hidden_bias_ref[t, half]
                below = 0.5 * (1.0 + lax.erf(pre * math.sqrt(0.5)))
                hid[half, t, rows, :] = (pre * below).astype(jnp.bfloat16)
                density = jnp.exp(-0.5 * pre * pre) * (1.0 / math.sqrt(2.0 * math.pi))
                slopeb[t, rows, :] = (below + pre * density).astype(jnp.bfloat16)

            spread_tile(xb, slot, 0, WIDE, sink)

        each_tile(5 + half, up_tile)
        save(hid.at[half], q_ref.at[1 - half])
        save(slopeb, slope_ref.at[half])

    def after_down(half):
        each_tile(7 + half, lambda t, slot: collapse_tile(hid.at[half], t, slot, 0, WIDE))
        if half == 0:
            return

        def finish(step, carry):
            rows = pl.ds(pl.multiple_of(step * chunk, chunk), chunk)
            xb[rows, :] = (stream[rows, :] + biases_ref[3:4, :]).astype(jnp.bfloat16)
            return carry

        lax.fori_loop(0, rows_all // chunk, finish, 0)

        def moved_tile(t, slot):
            def sink(rows, total):
                moved_ref[t, rows, :] = (total[:, 64:384] + out_bias_ref[t]).astype(jnp.bfloat16)

            spread_tile(xb, slot, 256, WIDE, sink)

        each_tile(4, moved_tile)
        turn_to(xb, 5)

    unit_work = {
        1: after_1,
        3: after_3,
        4: after_4,
        5: lambda: after_up(0),
        6: lambda: after_up(1),
        7: lambda: after_down(0),
        8: lambda: after_down(1),
    }

    def advance(turn, carry):
        for number in reversed(range(len(stages))):
            unit = turn - number

            @pl.when((unit >= 0) & (unit < UNITS))
            def _(number=number, unit=unit):
                stages[number](unit)

        pl.when(turn == 1)(before_units)
        ready = turn - (len(stages) - 1)
        for unit, work in unit_work.items():
            pl.when(ready == unit)(work)
        return carry

    lax.fori_loop(0, UNITS + len(stages) - 1, advance, 0)


def forward_all(shards, rows_in, gains, shifts, biases, hidden_bias, position, moved_part):
    units, share, wide = shards.shape
    rows, width = rows_in.shape[0], wide // 2
    low = jnp.bfloat16
    out_bias = biases[4].reshape(4, 1, width)
    hidden_bias = hidden_bias.reshape(4, 2, 1, wide)
    anywhere, near = pl.BlockSpec(memory_space=pl.ANY), pl.BlockSpec(memory_space=pltpu.VMEM)
    return pl.pallas_call(
        forward_kernel,
        in_specs=[anywhere] + [near] * 7 + [anywhere],
        out_specs=[anywhere] * 7 + [near],
        out_shape=[
            jax.ShapeDtypeStruct((units, 2, 2, 4, 2, share, wide), low),
            jax.ShapeDtypeStruct((12, 4, rows, wide), low),
            jax.ShapeDtypeStruct((8, C, rows), low),
            jax.ShapeDtypeStruct((3, rows, C), jnp.float32),
            jax.ShapeDtypeStruct((2, 4, rows, wide), low),
            jax.ShapeDtypeStruct((2, 4, rows, width), low),
            jax.ShapeDtypeStruct((2, 4, rows, wide), low),
            jax.ShapeDtypeStruct((4, rows, width), low),
        ],
        scratch_shapes=[
            pltpu.VMEM((rows, C), jnp.float32),
            pltpu.VMEM((rows, C), low),
            pltpu.VMEM((C, rows), low),
            pltpu.VMEM((4, rows, wide), low),
            pltpu.VMEM((4, rows, width), low),
            pltpu.VMEM((4, rows, wide), low),
            pltpu.VMEM((2, 4, rows, wide), low),
            pltpu.VMEM((4, rows, wide), low),
            pltpu.VMEM((2, 4, 2, share, wide), low),
            pltpu.SemaphoreType.DMA((2,)),
            pltpu.SemaphoreType.DMA((1,)),
            pltpu.SemaphoreType.DMA((units,)),
            pltpu.SemaphoreType.DMA((units, 2, 5)),
            pltpu.SemaphoreType.DMA((units, 2, 2, 4, 2)),
            pltpu.SemaphoreType.DMA((units, 3)),
        ],
        compiler_params=pltpu.CompilerParams(
            collective_id=0, has_side_effects=True, vmem_limit_bytes=58 << 20
        ),
    )(shards, rows_in, gains, shifts, biases, out_bias, hidden_bias, position, moved_part)


def reduce_kernel(
    pt_ref,
    q_ref,
    out_ref,
    ptx_ref,
    qx_ref,
    p_buf,
    q_buf,
    dw,
    rya,
    rxa,
    rua,
    rda,
    rxb,
    rub,
    rdb,
    ryb,
    load_sem,
    give_sem,
    take_sem,
    send_sem,
    recv_sem,
    credit,
):
    at = Place()
    z, x, y, c = at.z, at.x, at.y, at.c
    far_x, far_y = at.far_x, at.far_y
    share = out_ref.shape[1]
    row_a, row_b = pl.ds(0, ROWS_A), pl.ds(ROWS_A, share - ROWS_A)
    count_p = pt_ref.shape[0]
    at.greet()

    def give_p(index):
        return pltpu.make_async_remote_copy(
            src_ref=pt_ref.at[index],
            dst_ref=ptx_ref.at[index],
            send_sem=give_sem.at[index],
            recv_sem=take_sem.at[index],
            device_id=at.to["core"],
            device_id_type=MESH_ID,
        )

    def give_q(index):
        return pltpu.make_async_remote_copy(
            src_ref=q_ref.at[index, :, 1 - c],
            dst_ref=qx_ref.at[index],
            send_sem=give_sem.at[count_p + index],
            recv_sem=take_sem.at[count_p + index],
            device_id=at.to["core"],
            device_id_type=MESH_ID,
        )

    for index in range(UNITS):
        if (index + index // 5) % 2 == 0:
            give_p((index + index // 5) // 2).start()
        give_q(index).start()
        if index in (4, 5, 7):
            extra = (index - 3) // 2
            give_p(5 + extra).start()
            give_q(UNITS + extra).start()

    names = ["ya0", "ya1", "xa", "ua0", "ua1", "ua2", "da0", "da1", "da2"]
    names += ["xb0", "xb1", "ub0", "ub1", "ub2", "db0", "db1", "db2", "yb"]
    number = {name: index for index, name in enumerate(names)}

    def copy(slot, name, src, dst, kind, shift=0):
        index = number[name] + shift
        return pltpu.make_async_remote_copy(
            src_ref=src,
            dst_ref=dst,
            send_sem=send_sem.at[slot, index],
            recv_sem=recv_sem.at[slot, index],
            device_id=at.to[kind],
            device_id_type=MESH_ID,
        )

    def ya(slot, part):
        side = far_x if part == 0 else x
        return copy(
            slot, f"ya{part}", dw.at[slot, far_y, :, side, row_a], rya.at[slot, part], "y"
        )

    def xa(slot):
        return copy(slot, "xa", dw.at[slot, y, :, far_x, row_a], rxa.at[slot], "x")

    def xb(slot, part):
        return copy(slot, f"xb{part}", dw.at[slot, part, :, far_x, row_b], rxb.at[slot, part], "x")

    def yb(slot):
        return copy(slot, "yb", dw.at[slot, far_y, z, x, row_b], ryb.at[slot], "y")

    def up(slot, colour, d):
        if colour == 0:
            return copy(slot, "ua0", dw.at[slot, y, d, x, row_a], rua.at[slot, d - 1], "up", d - 1)
        return copy(slot, "ub0", dw.at[slot, :, d, x, row_b], rub.at[slot, d - 1], "up", d - 1)

    def down(slot, colour, d):
        if colour == 0:
            return copy(slot, "da0", dw.at[slot, y, d, x, row_a], rda.at[slot, d], "down", d)
        return copy(slot, "db0", dw.at[slot, :, d, x, row_b], rdb.at[slot, d], "down", d)

    def add(place, got):
        total = place[...].astype(jnp.float32) + got[...].astype(jnp.float32)
        place[...] = total.astype(jnp.bfloat16)

    def products(slot, p_index, q_index, more):
        loads = [
            pltpu.make_async_copy(pt_ref.at[p_index], p_buf.at[0], load_sem.at[0]),
            pltpu.make_async_copy(ptx_ref.at[p_index], p_buf.at[1], load_sem.at[1]),
            pltpu.make_async_copy(q_ref.at[q_index, :, c], q_buf.at[0], load_sem.at[2]),
            pltpu.make_async_copy(qx_ref.at[q_index], q_buf.at[1], load_sem.at[3]),
        ]
        for load in loads:
            load.start()
        for load in loads:
            load.wait()

        def one(step, carry):
            side, zz = step // 4, step % 4
            yy = jnp.where(side == 0, far_y, y)
            rows = pl.ds(pl.multiple_of(zz * 2 * share, 2 * share), 2 * share)
            total = dot_plain(p_buf[0, rows, :], q_buf[0, yy]) + dot_plain(
                p_buf[1, rows, :], q_buf[1, yy]
            )
            total = total.reshape(2, share, WIDE)
            if more:
                total = total + dw[slot, yy, zz].astype(jnp.float32)
            dw[slot, yy, zz] = total.astype(jnp.bfloat16)
            return carry

        lax.fori_loop(0, 8, one, 0)

    def stage0(turn):
        slot = turn % SLOTS_IN_FLIGHT
        p_index = (turn + turn // 5) // 2

        @pl.when((turn + turn // 5) % 2 == 0)
        def _():
            give_p(p_index).wait_recv()

        give_q(turn).wait_recv()
        products(slot, p_index, turn, False)

        @pl.when((turn == 4) | (turn == 5) | (turn == 7))
        def _():
            extra = (turn - 3) // 2
            give_p(5 + extra).wait_recv()
            give_q(UNITS + extra).wait_recv()
            products(slot, 5 + extra, UNITS + extra, True)

        @pl.when(turn >= SLOTS_IN_FLIGHT)
        def _():
            pl.semaphore_wait(credit.at[0], 1)
            pl.semaphore_wait(credit.at[1], 1)
            pl.when(at.has_up)(lambda: pl.semaphore_wait(credit.at[2], 1))
            pl.when(at.has_down)(lambda: pl.semaphore_wait(credit.at[3], 1))

        ya(slot, 0).start()
        xb(slot, 0).start()
        ya(slot, 1).start()
        xb(slot, 1).start()

    def z_step(slot, colour, step):
        @pl.when(z <= step - 1)
        def _():
            d = z + 4 - step

            @pl.when(z >= 1)
            def _():
                up(slot, colour, d).wait_recv()
                if colour == 0:
                    add(dw.at[slot, y, d, x, row_a], rua.at[slot, d - 1])
                else:
                    add(dw.at[slot, 0, d, x, row_b], rub.at[slot, d - 1, 0])
                    add(dw.at[slot, 1, d, x, row_b], rub.at[slot, d - 1, 1])

            up(slot, colour, d).start()

        @pl.when(3 - z <= step - 1)
        def _():
            d = z - 4 + step

            @pl.when(z <= 2)
            def _():
                down(slot, colour, d).wait_recv()
                if colour == 0:
                    add(dw.at[slot, y, d, x, row_a], rda.at[slot, d])
                else:
                    add(dw.at[slot, 0, d, x, row_b], rdb.at[slot, d, 0])
                    add(dw.at[slot, 1, d, x, row_b], rdb.at[slot, d, 1])

            down(slot, colour, d).start()

    def stage1(turn):
        slot = turn % SLOTS_IN_FLIGHT
        for part in range(2):
            xb(slot, part).wait_recv()
            for zz in range(4):
                add(dw.at[slot, part, zz, x, row_b], rxb.at[slot, part, zz])
        z_step(slot, 1, 1)
        ya(slot, 0).wait_recv()
        for zz in range(4):
            add(dw.at[slot, y, zz, far_x, row_a], rya.at[slot, 0, zz])
        xa(slot).start()
        ya(slot, 1).wait_recv()
        for zz in range(4):
            add(dw.at[slot, y, zz, x, row_a], rya.at[slot, 1, zz])

    def stage2(turn):
        slot = turn % SLOTS_IN_FLIGHT
        z_step(slot, 1, 2)
        xa(slot).wait_recv()
        for zz in range(4):
            add(dw.at[slot, y, zz, x, row_a], rxa.at[slot, zz])
        z_step(slot, 0, 1)

    def stage3(turn):
        slot = turn % SLOTS_IN_FLIGHT
        z_step(slot, 1, 3)
        z_step(slot, 0, 2)

    def stage4(turn):
        slot = turn % SLOTS_IN_FLIGHT
        z_step(slot, 0, 3)

        @pl.when(z >= 1)
        def _():
            up(slot, 1, z).wait_recv()
            for yy in range(2):
                add(dw.at[slot, yy, z, x, row_b], rub.at[slot, z - 1, yy])

        @pl.when(z <= 2)
        def _():
            down(slot, 1, z).wait_recv()
            for yy in range(2):
                add(dw.at[slot, yy, z, x, row_b], rdb.at[slot, z, yy])

        yb(slot).start()

    def stage5(turn):
        slot = turn % SLOTS_IN_FLIGHT
        unit = UNITS - 1 - turn
        out_ref[unit, row_a, :] = dw[slot, y, z, x, row_a, :].astype(jnp.float32)

        @pl.when(z >= 1)
        def _():
            up(slot, 0, z).wait_recv()
            out_ref[unit, row_a, :] += rua[slot, z - 1].astype(jnp.float32)

        @pl.when(z <= 2)
        def _():
            down(slot, 0, z).wait_recv()
            out_ref[unit, row_a, :] += rda[slot, z].astype(jnp.float32)

        yb(slot).wait_recv()
        out_ref[unit, row_b, :] = dw[slot, y, z, x, row_b, :].astype(jnp.float32) + ryb[
            slot
        ].astype(jnp.float32)

        ya(slot, 0).wait_send()
        ya(slot, 1).wait_send()
        xa(slot).wait_send()
        xb(slot, 0).wait_send()
        xb(slot, 1).wait_send()
        yb(slot).wait_send()
        for colour in range(2):
            for step in range(1, 4):

                @pl.when(z <= step - 1)
                def _(colour=colour, step=step):
                    up(slot, colour, z + 4 - step).wait_send()

                @pl.when(3 - z <= step - 1)
                def _(colour=colour, step=step):
                    down(slot, colour, z - 4 + step).wait_send()

        @pl.when(turn + SLOTS_IN_FLIGHT < UNITS)
        def _():
            def grant(kind, index):
                pl.semaphore_signal(
                    credit.at[index], inc=1, device_id=at.to[kind], device_id_type=MESH_ID
                )

            grant("x", 0)
            grant("y", 1)
            pl.when(at.has_up)(lambda: grant("up", 3))
            pl.when(at.has_down)(lambda: grant("down", 2))

    stages = (stage0, stage1, stage2, stage3, stage4, stage5)

    def advance(now, carry):
        for step in range(len(stages)):
            turn = now - step

            @pl.when((turn >= 0) & (turn < UNITS))
            def _(step=step, turn=turn):
                stages[step](turn)

        return carry

    lax.fori_loop(0, UNITS + len(stages) - 1, advance, 0)
    for index in range(count_p):
        give_p(index).wait_send()
    for index in range(q_ref.shape[0]):
        give_q(index).wait_send()


def reduce_all(turned, parts, share):
    count_p, width, rows = turned.shape
    count_q = parts.shape[0]
    low = jnp.bfloat16
    slots, rest = SLOTS_IN_FLIGHT, share - ROWS_A
    return pl.pallas_call(
        reduce_kernel,
        in_specs=[pl.BlockSpec(memory_space=pl.ANY)] * 2,
        out_specs=[
            pl.BlockSpec(memory_space=pltpu.VMEM),
            pl.BlockSpec(memory_space=pl.ANY),
            pl.BlockSpec(memory_space=pl.ANY),
        ],
        out_shape=[
            jax.ShapeDtypeStruct((UNITS, share, WIDE), jnp.float32),
            jax.ShapeDtypeStruct((count_p, width, rows), low),
            jax.ShapeDtypeStruct((count_q, 2, rows, WIDE), low),
        ],
        scratch_shapes=[
            pltpu.VMEM((2, width, rows), low),
            pltpu.VMEM((2, 2, rows, WIDE), low),
            pltpu.VMEM((slots, 2, 4, 2, share, WIDE), low),
            pltpu.VMEM((slots, 2, 4, ROWS_A, WIDE), low),
            pltpu.VMEM((slots, 4, ROWS_A, WIDE), low),
            pltpu.VMEM((slots, 3, ROWS_A, WIDE), low),
            pltpu.VMEM((slots, 3, ROWS_A, WIDE), low),
            pltpu.VMEM((slots, 2, 4, rest, WIDE), low),
            pltpu.VMEM((slots, 3, 2, rest, WIDE), low),
            pltpu.VMEM((slots, 3, 2, rest, WIDE), low),
            pltpu.VMEM((slots, rest, WIDE), low),
            pltpu.SemaphoreType.DMA((4,)),
            pltpu.SemaphoreType.DMA((count_p + count_q,)),
            pltpu.SemaphoreType.DMA((count_p + count_q,)),
            pltpu.SemaphoreType.DMA((slots, 18)),
            pltpu.SemaphoreType.DMA((slots, 18)),
            pltpu.SemaphoreType.REGULAR((4,)),
        ],
        compiler_params=pltpu.CompilerParams(
            collective_id=1, has_side_effects=True, vmem_limit_bytes=60 << 20
        ),
    )(turned, parts)[0]
def gather_plain(shards):
    units, share, wide = shards.shape
    whole = lax.all_gather(shards, MIXED, axis=1, tiled=True)
    return whole.reshape(units, lax.axis_size("tensor"), C, wide)


def reduce_plain(turned, parts, share):
    reduced = []
    for turn in range(UNITS):
        whole = jnp.einsum(
            "kr,trn->tkn", turned[(turn + turn // 5) // 2], parts[turn],
            preferred_element_type=jnp.float32,
        )
        if turn in (4, 5, 7):
            extra = (turn - 3) // 2
            whole = whole + jnp.einsum(
                "kr,trn->tkn", turned[5 + extra], parts[UNITS + extra],
                preferred_element_type=jnp.float32,
            )
        whole = whole.astype(jnp.bfloat16).reshape(-1, whole.shape[2])
        reduced.append(
            lax.psum_scatter(whole, MIXED, scatter_dimension=0, tiled=True).astype(jnp.float32)
        )
    return jnp.stack(reduced[::-1], 0)


def to_pixels(values, tensor_size):
    slots, frames, width, pixels = values.shape
    own = pixels // tensor_size
    turned = jnp.transpose(values, (3, 0, 1, 2)).reshape(tensor_size, own * slots * frames, width)
    return lax.all_to_all(turned, "tensor", 0, 0, tiled=True)


def to_channels(values, slots, pixels):
    tensor_size, rows, width = values.shape
    arrived = lax.all_to_all(values, "tensor", 0, 0, tiled=True)
    return jnp.transpose(arrived.reshape(pixels, slots, FRAMES, width), (1, 2, 3, 0))


def body(
    by_kernel,
    latent,
    clip_flags,
    cotangent,
    norm_gain,
    norm_shift,
    channel_bias,
    hidden_bias,
    weight_in,
    weight_qkv,
    weight_out,
    weight_up,
    weight_down,
    weight_proj,
):
    tensor_size = lax.axis_size("tensor")
    slots, frames, width, pixels = latent.shape
    share = weight_in.shape[0]
    hidden_width = hidden_bias.shape[0]
    flags = (clip_flags > 0)[:, None, None, None]

    wide = 2 * width

    shards = []
    side = jnp.concatenate
    for block in range(2):
        shards.append(weight_qkv[block, :, :2].reshape(share, wide))
        other = weight_in if block == 0 else weight_out[0].T
        shards.append(side([weight_qkv[block, :, 2], other], 1))
    shards.append(side([weight_out[1].T, weight_proj], 1))
    shards += [weight_up[:, :wide], weight_up[:, wide:]]
    down_turned = weight_down.T
    shards += [down_turned[:, :wide], down_turned[:, wide:]]
    shards = jnp.stack(shards, 0)
    packed = jnp.concatenate([norm_gain, norm_shift, channel_bias], 0)
    packed = lax.all_gather(
        jnp.concatenate([packed.reshape(-1), hidden_bias]), "tensor", axis=0, tiled=False
    )
    channel_params = packed[:, : 13 * width].reshape(tensor_size, 13, width)
    channel_params = jnp.transpose(channel_params, (1, 0, 2)).reshape(13, C)
    gains, shifts, biases = channel_params[:4], channel_params[4:8], channel_params[8:]
    hidden_full = packed[:, 13 * width :]

    start = latent.astype(jnp.float32)
    cot = cotangent.astype(jnp.float32)
    group_width = C // GROUPS
    grouped = start.reshape(slots, frames, width // group_width, group_width, pixels)
    group_centre = jnp.mean(grouped, axis=(1, 3, 4), keepdims=True)
    offset = grouped - group_centre
    group_inverse = lax.rsqrt(jnp.mean(offset * offset, axis=(1, 3, 4), keepdims=True) + 1e-06)
    group_hat = (offset * group_inverse).reshape(start.shape)
    normed = group_hat * norm_gain[0][:, None] + norm_shift[0][:, None]
    arrived = to_pixels(normed.astype(jnp.bfloat16), tensor_size)
    rows = arrived.shape[1]
    inputs_in = jnp.transpose(arrived, (1, 0, 2)).reshape(rows, C)

    grad_moved_local = jnp.where(flags, cot, 0.0)
    bias_moved = jnp.sum(grad_moved_local, axis=(0, 1, 3))
    grad_moved = to_pixels(grad_moved_local.astype(jnp.bfloat16), tensor_size)

    if by_kernel:
        empty = jnp.zeros((tensor_size, rows, width), jnp.bfloat16)
        whole, q_all, pt_all, streams, qk_all, v_all, slopes, moved = forward_all(
            shards,
            inputs_in,
            gains,
            shifts,
            biases,
            hidden_full,
            make_positions(),
            side([empty, grad_moved], 2),
        )
        whole = whole.reshape(UNITS, tensor_size, C, wide)
    else:
        whole = gather_plain(shards)
    full_qk = (whole[0], whole[2])
    full_v = (whole[1, :, :, :width], whole[3, :, :, :width])
    full_in = whole[1, :, :, width:]
    full_out = (whole[3, :, :, width:], whole[4, :, :, :width])
    full_proj = whole[4, :, :, width:]
    full_up = (whole[5], whole[6])
    full_down = (whole[7], whole[8])

    if by_kernel:
        kept = []
        for block in range(2):
            hat, inverse = layer_stats(streams[block])
            kept.append((hat, inverse, pt_all[4 - block], qk_all[block], v_all[block], None))
        hat_feed, inverse_feed = layer_stats(streams[2])
    else:
        def join(parts):
            return jnp.transpose(parts, (1, 0, 2)).reshape(rows, parts.shape[0] * parts.shape[2])

        stream = join(spread(inputs_in, full_in)) + biases[0]
        position = jnp.tile(make_positions(), (rows // FRAMES, 1))
        kept = []
        for block in range(2):
            hat, inverse = layer_stats(stream)
            lifted = (hat * gains[1 + block] + shifts[1 + block] + position).astype(jnp.bfloat16)
            qk = spread(lifted, full_qk[block]).astype(jnp.bfloat16)
            values = spread(lifted, full_v[block]).astype(jnp.bfloat16)
            attended = attend(qk, values)
            stream = stream + collapse(attended, full_out[block]) + biases[1 + block]
            kept.append((hat, inverse, lifted.T, qk, values, attended))
        hat_feed, inverse_feed = layer_stats(stream)
        inputs_up = (hat_feed * gains[3] + shifts[3]).astype(jnp.bfloat16)
        pre_act = [
            spread(inputs_up, full_up[half])
            + hidden_full[:, None, half * wide : half * wide + wide]
            for half in range(2)
        ]
        slopes = [
            jax.vjp(partial(jax.nn.gelu, approximate=False), pre)[1](jnp.ones_like(pre))[0]
            for pre in pre_act
        ]
        hidden = [jax.nn.gelu(pre, approximate=False).astype(jnp.bfloat16) for pre in pre_act]
        stream = stream + collapse(hidden[0], full_down[0]) + collapse(hidden[1], full_down[1])
        stream = stream + biases[3]
        inputs_proj = stream.astype(jnp.bfloat16)
        moved = spread(inputs_proj, full_proj) + biases[4].reshape(tensor_size, 1, width)
        moved = moved.astype(jnp.bfloat16)

    moved_local = to_channels(moved, slots, pixels).astype(jnp.float32)
    output = jnp.where(flags, start + moved_local, start).astype(jnp.bfloat16)

    bias_grads = [None] * 4
    gain_grads = [None] * 3
    shift_grads = [None] * 3
    empty = jnp.zeros((tensor_size, rows, width), jnp.bfloat16)
    turned, parts = [None] * 8, [None] * 12
    if by_kernel:
        turned[1], turned[5], turned[7] = pt_all[1], pt_all[5], pt_all[7]
        for index in (0, 1, 4, 9, 10):
            parts[index] = q_all[index]
    else:
        turned[1], turned[5], turned[7] = inputs_up.T, inputs_proj.T, inputs_in.T
        parts[9] = side([empty, grad_moved], 2)
        parts[0], parts[1] = hidden[1], hidden[0]
    grad_stream = collapse(grad_moved, full_proj)
    bias_grads[3] = jnp.sum(grad_stream, 0)
    grad_low = grad_stream.astype(jnp.bfloat16)
    turned[0] = grad_low.T
    hidden_grads = [None, None]
    grad_normed = 0.0
    for half in (1, 0):
        grad_hidden = spread(grad_low, full_down[half])
        grad_pre = grad_hidden * slopes[half]
        hidden_grads[half] = jnp.sum(grad_pre, 1)
        parts[3 - half] = grad_pre.astype(jnp.bfloat16)
        grad_normed = grad_normed + collapse(parts[3 - half], full_up[half])
    hidden_grad = side(hidden_grads, 1)
    grad_layer, gain_grads[2], shift_grads[2] = layer_back(
        grad_normed, hat_feed, inverse_feed, gains[3]
    )
    grad_stream = grad_stream + grad_layer
    for block in (1, 0):
        hat, inverse, lifted_turned, qk, values, attended = kept[block]
        bias_grads[1 + block] = jnp.sum(grad_stream, 0)
        grad_low = grad_stream.astype(jnp.bfloat16)
        turned[2 if block == 1 else 6] = grad_low.T
        if not by_kernel:
            pair = [attended, empty] if block == 1 else [empty, attended]
            parts[4 if block == 1 else 10] = side(pair, 2)
        grad_attended = spread(grad_low, full_out[block]).astype(jnp.bfloat16)
        grad_qk, grad_values = attend_back(qk, values, grad_attended)
        turned[3 if block == 1 else 4] = lifted_turned
        parts[5 if block == 1 else 7] = side([grad_values, empty], 2)
        parts[6 if block == 1 else 8] = grad_qk
        grad_lifted = collapse(grad_qk, full_qk[block]) + collapse(grad_values, full_v[block])
        grad_layer, gain_grads[block], shift_grads[block] = layer_back(
            grad_lifted, hat, inverse, gains[1 + block]
        )
        grad_stream = grad_stream + grad_layer
    bias_grads[0] = jnp.sum(grad_stream, 0)
    grad_low = grad_stream.astype(jnp.bfloat16)
    grad_low_parts = jnp.transpose(grad_low.reshape(rows, tensor_size, width), (1, 0, 2))
    parts[11] = side([empty, grad_low_parts], 2)
    turned, parts = jnp.stack(turned, 0), jnp.stack(parts, 0)
    if by_kernel:
        reduced = reduce_all(turned, parts.reshape(12, 2, 2, rows, wide), share)
    else:
        reduced = reduce_plain(turned, parts, share)
    qkv_grads = [
        side([reduced[2 * block], reduced[2 * block + 1, :, :width]], 1).reshape(share, 3, width)
        for block in range(2)
    ]
    out_grads = [reduced[3, :, width:].T, reduced[4, :, :width].T]
    in_grad, proj_grad = reduced[1, :, width:], reduced[4, :, width:]
    up_grad = side([reduced[5], reduced[6]], 1)
    down_grad = side([reduced[7], reduced[8]], 1)
    grad_normed = collapse(grad_low_parts, full_in).astype(jnp.bfloat16)
    grad_normed = jnp.transpose(grad_normed.reshape(rows, tensor_size, width), (1, 0, 2))
    grad_normed = to_channels(grad_normed, slots, pixels).astype(jnp.float32)
    scaled = grad_normed * norm_gain[0][:, None]
    scaled_groups = scaled.reshape(grouped.shape)
    hat_groups = group_hat.reshape(grouped.shape)
    first = jnp.mean(scaled_groups, axis=(1, 3, 4), keepdims=True)
    second = jnp.mean(scaled_groups * hat_groups, axis=(1, 3, 4), keepdims=True)
    grad_group = group_inverse * (scaled_groups - first - hat_groups * second)
    latent_grad = cot + grad_group.reshape(start.shape)
    group_gain_grad = jnp.sum(grad_normed * group_hat, axis=(0, 1, 3))
    group_shift_grad = jnp.sum(grad_normed, axis=(0, 1, 3))

    vectors = jnp.stack(gain_grads + shift_grads + bias_grads, 0)
    vectors = jnp.transpose(vectors.reshape(10, tensor_size, width), (1, 0, 2))
    vectors = jnp.concatenate([vectors.reshape(tensor_size, 10 * width), hidden_grad], 1)
    vectors = lax.psum_scatter(vectors, "tensor", scatter_dimension=0, tiled=False)
    sums = lax.psum(
        jnp.concatenate([vectors, group_gain_grad, group_shift_grad, bias_moved]), "dp"
    )
    channel_sums = sums[: 10 * width].reshape(10, width)
    hidden_bias_grad = sums[10 * width : 10 * width + hidden_width]
    local_sums = sums[10 * width + hidden_width :].reshape(3, width)
    gain_grad = jnp.concatenate([local_sums[0:1], channel_sums[0:3]], 0)
    shift_grad = jnp.concatenate([local_sums[1:2], channel_sums[3:6]], 0)
    channel_bias_grad = jnp.concatenate([channel_sums[6:10], local_sums[2:3]], 0)
    return (
        output,
        latent_grad,
        gain_grad,
        shift_grad,
        channel_bias_grad,
        hidden_bias_grad,
        in_grad,
        jnp.stack(qkv_grads, 0),
        jnp.stack(out_grads, 0),
        up_grad,
        down_grad.T,
        proj_grad,
    )


def solution(mesh):
    placed = (
        P("dp", None, "tensor", None),
        P("dp"),
        P("dp", None, "tensor", None),
        P(None, "tensor"),
        P(None, "tensor"),
        P(None, "tensor"),
        P("tensor"),
        P("dp", "tensor"),
        P(None, "dp", None, "tensor"),
        P(None, "tensor", "dp"),
        P("dp", "tensor"),
        P("tensor", "dp"),
        P("dp", "tensor"),
    )
    return jax.shard_map(
        partial(body, tuple(mesh.shape[name] for name in ("dp", "tensor")) == (8, 4)),
        mesh=mesh,
        in_specs=placed,
        out_specs=(
            P("dp", None, "tensor", None),
            P("dp", None, "tensor", None),
            P(None, "tensor"),
            P(None, "tensor"),
            P(None, "tensor"),
            P("tensor"),
            P("dp", "tensor"),
            P(None, "dp", None, "tensor"),
            P(None, "tensor", "dp"),
            P("dp", "tensor"),
            P("tensor", "dp"),
            P("dp", "tensor"),
        ),
        check_vma=False,
    )
```

```python
from functools import partial
import math

import jax
import jax.numpy as jnp
from jax import lax
from jax.experimental import pallas as pl
from jax.experimental.pallas import tpu as pltpu
from jax.sharding import PartitionSpec as P

C = 1280
GROUPS = 32
FRAMES = 16
HEAD = 160
BLOCK = 128
MIXED = ("tensor", "dp")


def spread(rows, weight):
    return jnp.einsum("rk,tkn->trn", rows, weight, preferred_element_type=jnp.float32)


def collapse(parts, weight):
    return jnp.einsum("trn,tkn->rk", parts, weight, preferred_element_type=jnp.float32)


def make_positions():
    channel_ids = jnp.arange(C)
    pair_rate = jnp.exp((channel_ids // 2).astype(jnp.float32) * (-2.0 * math.log(10000.0) / C))
    angles = jnp.arange(FRAMES).astype(jnp.float32)[:, None] * pair_rate[None, :]
    return jnp.where(channel_ids[None, :] % 2 == 0, jnp.sin(angles), jnp.cos(angles))


def layer_stats(stream):
    centre = jnp.mean(stream, axis=1, keepdims=True)
    offset = stream - centre
    inverse = lax.rsqrt(jnp.mean(offset * offset, axis=1, keepdims=True) + 1e-05)
    return offset * inverse, inverse


def layer_back(grad_out, normal_part, inverse, gain):
    scaled = grad_out * gain
    first = jnp.mean(scaled, axis=1, keepdims=True)
    second = jnp.mean(scaled * normal_part, axis=1, keepdims=True)
    grad_in = inverse * (scaled - first - normal_part * second)
    return grad_in, jnp.sum(grad_out * normal_part, 0), jnp.sum(grad_out, 0)


def dot_rows(left, right):
    return lax.dot_general(left, right, (((1,), (1,)), ((), ())), preferred_element_type=jnp.float32)


def dot_plain(left, right):
    return lax.dot_general(left, right, (((1,), (0,)), ((), ())), preferred_element_type=jnp.float32)


def dot_first(left, right):
    return lax.dot_general(left, right, (((0,), (0,)), ((), ())), preferred_element_type=jnp.float32)


def same_pixel(block):
    row = lax.broadcasted_iota(jnp.int32, (block, block), 0) // FRAMES
    col = lax.broadcasted_iota(jnp.int32, (block, block), 1) // FRAMES
    return row == col


def head_probs(query, key, same, scale):
    scores = jnp.where(same, dot_rows(query, key) * scale, -1e30)
    top = jnp.max(scores, axis=1, keepdims=True)
    weights = jnp.where(same, jnp.exp(scores - top), 0.0)
    return weights / jnp.sum(weights, axis=1, keepdims=True)


def attend_kernel(scale, qk_ref, v_ref, out_ref):
    rows, width = out_ref.shape[1], out_ref.shape[2]
    block = min(BLOCK, rows)
    same = same_pixel(block)
    for start in range(0, rows, block):
        for head in range(width // HEAD):
            here, low = slice(start, start + block), head * HEAD
            query = qk_ref[0, here, low : low + HEAD]
            key = qk_ref[0, here, width + low : width + low + HEAD]
            value = v_ref[0, here, low : low + HEAD]
            probs = head_probs(query, key, same, scale).astype(jnp.bfloat16)
            out_ref[0, here, low : low + HEAD] = dot_plain(probs, value).astype(jnp.bfloat16)


def part_spec(array):
    return pl.BlockSpec((1,) + array.shape[1:], lambda t: (t, 0, 0))


def attend(qk, values):
    return pl.pallas_call(
        partial(attend_kernel, 1.0 / math.sqrt(HEAD)),
        grid=(qk.shape[0],),
        in_specs=[part_spec(qk), part_spec(values)],
        out_specs=part_spec(values),
        out_shape=jax.ShapeDtypeStruct(values.shape, jnp.bfloat16),
        compiler_params=pltpu.CompilerParams(vmem_limit_bytes=32 << 20),
    )(qk, values)


def attend_back_kernel(scale, qk_ref, v_ref, grad_ref, dqk_ref, dv_ref):
    rows, width = grad_ref.shape[1], grad_ref.shape[2]
    block = min(BLOCK, rows)
    same = same_pixel(block)
    for start in range(0, rows, block):
        for head in range(width // HEAD):
            here, low = slice(start, start + block), head * HEAD
            query = qk_ref[0, here, low : low + HEAD]
            key = qk_ref[0, here, width + low : width + low + HEAD]
            value = v_ref[0, here, low : low + HEAD]
            grad = grad_ref[0, here, low : low + HEAD]
            probs = head_probs(query, key, same, scale)
            grad_probs = dot_rows(grad, value)
            centred = jnp.sum(probs * grad_probs, axis=1, keepdims=True)
            grad_raw = (probs * (grad_probs - centred) * scale).astype(jnp.bfloat16)
            dqk_ref[0, here, low : low + HEAD] = dot_plain(grad_raw, key).astype(jnp.bfloat16)
            dqk_ref[0, here, width + low : width + low + HEAD] = dot_first(grad_raw, query).astype(
                jnp.bfloat16
            )
            dv_ref[0, here, low : low + HEAD] = dot_first(probs.astype(jnp.bfloat16), grad).astype(
                jnp.bfloat16
            )


def attend_back(qk, values, grad):
    return pl.pallas_call(
        partial(attend_back_kernel, 1.0 / math.sqrt(HEAD)),
        grid=(qk.shape[0],),
        in_specs=[part_spec(qk), part_spec(values), part_spec(values)],
        out_specs=[part_spec(qk), part_spec(values)],
        out_shape=[
            jax.ShapeDtypeStruct(qk.shape, jnp.bfloat16),
            jax.ShapeDtypeStruct(values.shape, jnp.bfloat16),
        ],
        compiler_params=pltpu.CompilerParams(vmem_limit_bytes=32 << 20),
    )(qk, values, grad)


UNITS = 9
WIDE = 640
SLOTS_IN_FLIGHT = 6
ROWS_A = 96
MESH_ID = pl.DeviceIdType.MESH


class Place:
    def __init__(self):
        dp, tn = lax.axis_index("dp"), lax.axis_index("tensor")
        self.z, self.x = dp // 2, dp % 2
        self.y, self.c = tn // 2, tn % 2
        self.far_x, self.far_y = 1 - self.x, 1 - self.y
        self.to = {
            "x": (self.z * 2 + self.far_x, tn),
            "y": (dp, self.far_y * 2 + self.c),
            "core": (dp, self.y * 2 + 1 - self.c),
            "cross": (dp, self.far_y * 2 + 1 - self.c),
            "up": (dp + 2, tn),
            "down": (dp - 2, tn),
        }
        self.has_up = self.z < 3
        self.has_down = self.z > 0

    def greet(self):
        barrier = pltpu.get_barrier_semaphore()

        def hello(name):
            pl.semaphore_signal(barrier, inc=1, device_id=self.to[name], device_id_type=MESH_ID)

        for name in ("x", "y", "core", "cross"):
            hello(name)
        pl.when(self.has_up)(lambda: hello("up"))
        pl.when(self.has_down)(lambda: hello("down"))
        pl.semaphore_wait(barrier, 4 + (6 - self.z) // 4 + (self.z + 3) // 4)


def await_bytes(ref, sem):
    pltpu.make_async_copy(ref, ref, sem).wait()


def forward_kernel(
    shard_ref,
    x_ref,
    params_ref,
    position_ref,
    whole_ref,
    q_ref,
    pt_ref,
    stream_out_ref,
    qk_ref,
    v_ref,
    slope_ref,
    moved_ref,
    joined_ref,
    stream,
    xb,
    ptb,
    x_got,
    params_got,
    hidden_bias,
    qkb,
    vb,
    attb,
    hid,
    slopeb,
    wb,
    tile_sem,
    save_sem,
    peer_send,
    peer_recv,
    local_sem,
    send_sem,
    recv_sem,
    core_sem,
):
    at = Place()
    z, x, y, c = at.z, at.x, at.y, at.c
    share = shard_ref.shape[1]
    cut = (pl.ds(0, ROWS_A), pl.ds(ROWS_A, share - ROWS_A))
    kinds = {"up": 0, "down": 1, "x": 2, "y": 3, "core": 4}
    at.greet()

    def send(unit, colour, yy, zz, xx, kind, own=False):
        place = whole_ref.at[unit, yy, c, zz, xx, cut[colour]]
        pltpu.make_async_remote_copy(
            src_ref=shard_ref.at[unit, cut[colour]] if own else place,
            dst_ref=place,
            send_sem=send_sem.at[unit, colour, kinds[kind]],
            recv_sem=recv_sem.at[unit, colour, yy, zz, xx],
            device_id=at.to[kind],
            device_id_type=MESH_ID,
        ).start()

    def arrived(unit, colour, yy, zz, xx):
        await_bytes(
            whole_ref.at[unit, yy, c, zz, xx, cut[colour]], recv_sem.at[unit, colour, yy, zz, xx]
        )

    def own_copy(unit):
        return pltpu.make_async_copy(
            shard_ref.at[unit], whole_ref.at[unit, y, c, z, x], local_sem.at[unit]
        )

    def to_core(unit, part):
        if part == 2:
            place = whole_ref.at[unit, :, c, :, :, cut[1]]
        else:
            place = whole_ref.at[unit, y if part == 0 else at.far_y, c, :, :, cut[0]]
        return pltpu.make_async_remote_copy(
            src_ref=place,
            dst_ref=place,
            send_sem=send_sem.at[unit, part // 2, 4],
            recv_sem=core_sem.at[unit, part],
            device_id=at.to["core"],
            device_id_type=MESH_ID,
        )

    def from_z(unit, colour, step, yy):
        @pl.when(z >= step)
        def _():
            zz = z - step
            arrived(unit, colour, yy, zz, x)
            pl.when(at.has_up)(lambda: send(unit, colour, yy, zz, x, "up"))
            send(unit, colour, yy, zz, x, "x")
            if colour == 0:
                send(unit, colour, yy, zz, x, "y")

        @pl.when(z + step <= 3)
        def _():
            zz = z + step
            arrived(unit, colour, yy, zz, x)
            pl.when(at.has_down)(lambda: send(unit, colour, yy, zz, x, "down"))
            send(unit, colour, yy, zz, x, "x")
            if colour == 0:
                send(unit, colour, yy, zz, x, "y")

    def from_x(unit, step):
        def one(zz):
            arrived(unit, 0, y, zz, at.far_x)
            send(unit, 0, y, zz, at.far_x, "y")

        if step == 0:
            one(z)
        else:
            pl.when(z >= step)(lambda: one(z - step))
            pl.when(z + step <= 3)(lambda: one(z + step))

    def stage0(unit):
        own_copy(unit).start()
        pl.when(at.has_up)(lambda: send(unit, 0, y, z, x, "up", True))
        pl.when(at.has_down)(lambda: send(unit, 0, y, z, x, "down", True))
        send(unit, 1, y, z, x, "y", True)
        send(unit, 0, y, z, x, "x", True)
        pl.when(at.has_up)(lambda: send(unit, 1, y, z, x, "up", True))
        pl.when(at.has_down)(lambda: send(unit, 1, y, z, x, "down", True))
        send(unit, 0, y, z, x, "y", True)
        send(unit, 1, y, z, x, "x", True)

    def stage1(unit):
        from_z(unit, 0, 1, y)
        arrived(unit, 1, at.far_y, z, x)
        pl.when(at.has_up)(lambda: send(unit, 1, at.far_y, z, x, "up"))
        pl.when(at.has_down)(lambda: send(unit, 1, at.far_y, z, x, "down"))
        send(unit, 1, at.far_y, z, x, "x")
        from_z(unit, 1, 1, y)
        from_x(unit, 0)

    def stage2(unit):
        from_z(unit, 0, 2, y)
        from_z(unit, 1, 1, at.far_y)
        from_z(unit, 1, 2, y)
        from_x(unit, 1)

    def stage3(unit):
        from_z(unit, 0, 3, y)
        from_z(unit, 1, 2, at.far_y)
        from_z(unit, 1, 3, y)
        from_x(unit, 2)

    def stage4(unit):
        from_z(unit, 1, 3, at.far_y)
        from_x(unit, 3)
        own_copy(unit).wait()
        to_core(unit, 0).start()

    def stage5(unit):
        for zz in range(4):
            for xx in range(2):
                arrived(unit, 0, at.far_y, zz, xx)
        to_core(unit, 1).start()
        for zz in range(4):
            for yy in range(2):
                arrived(unit, 1, yy, zz, at.far_x)
        to_core(unit, 2).start()

    def stage6(unit):
        other = 1 - c
        await_bytes(whole_ref.at[unit, y, other, :, :, cut[0]], core_sem.at[unit, 0])
        await_bytes(whole_ref.at[unit, at.far_y, other, :, :, cut[0]], core_sem.at[unit, 1])
        await_bytes(whole_ref.at[unit, :, other, :, :, cut[1]], core_sem.at[unit, 2])
        for colour in range(2):
            rows = cut[colour]
            await_bytes(whole_ref.at[unit, :, c, :, :, rows], send_sem.at[unit, colour, 4])
            whole_x = whole_ref.at[unit, 0, c, :, 0, rows] if colour == 0 else None
            if colour == 0:
                await_bytes(whole_x, send_sem.at[unit, 0, 2])
                await_bytes(whole_ref.at[unit, 0, c, :, :, rows], send_sem.at[unit, 0, 3])
            else:
                await_bytes(whole_ref.at[unit, 0, c, :, :, rows], send_sem.at[unit, 1, 2])
                await_bytes(whole_ref.at[unit, 0, c, 0, 0, rows], send_sem.at[unit, 1, 3])
            for level in range(3):

                def ups(level=level):
                    if colour == 0:
                        ref = whole_ref.at[unit, 0, c, pl.ds(0, level + 1), 0, rows]
                    else:
                        ref = whole_ref.at[unit, :, c, pl.ds(0, level + 1), 0, rows]
                    return ref

                pl.when(z == level)(
                    lambda level=level: await_bytes(ups(level), send_sem.at[unit, colour, 0])
                )
                pl.when(z == 3 - level)(
                    lambda level=level: await_bytes(ups(level), send_sem.at[unit, colour, 1])
                )

    stages = (stage0, stage1, stage2, stage3, stage4, stage5, stage6)

    rows_all, width = x_ref.shape[1], x_ref.shape[2]
    half_rows = rows_all // 2
    scale = 1.0 / math.sqrt(HEAD)
    own_t = y * 2 + c
    pending = []

    def save(source, target):
        copy = pltpu.make_async_copy(source, target, save_sem.at[len(pending)])
        pending.append(copy)
        state = [False]

        def begin():
            copy.start()

        def wait():
            if not state[0]:
                state[0] = True
                copy.wait()

        return begin, wait

    peers = (("y", at.far_y * 2 + c), ("core", y * 2 + 1 - c), ("cross", at.far_y * 2 + 1 - c))

    def peer_copies(index):
        kind, t = peers[index]
        target = {"device_id": at.to[kind], "device_id_type": MESH_ID}
        return (
            pltpu.make_async_remote_copy(
                src_ref=params_ref,
                dst_ref=params_got.at[own_t],
                send_sem=peer_send.at[0, index],
                recv_sem=peer_recv.at[0, index],
                **target,
            ),
            pltpu.make_async_remote_copy(
                src_ref=x_ref.at[t],
                dst_ref=x_got.at[own_t],
                send_sem=peer_send.at[1, index],
                recv_sem=peer_recv.at[1, index],
                **target,
            ),
        )

    own_peer = (
        pltpu.make_async_copy(params_ref, params_got.at[own_t], peer_send.at[0, 3]),
        pltpu.make_async_copy(x_ref.at[own_t], x_got.at[own_t], peer_send.at[1, 3]),
    )
    for index in range(3):
        for copy in peer_copies(index):
            copy.start()
    for copy in own_peer:
        copy.start()

    def tile_pieces(uses):
        def load(index):
            unit, t, use = uses[index]
            return pltpu.make_async_copy(
                whole_ref.at[unit, t // 2, t % 2], wb.at[index % 2], tile_sem.at[index % 2]
            )

        def piece(index):
            def run():
                if index == 0:
                    load(0).start()
                if index + 1 < len(uses):
                    load(index + 1).start()
                load(index).wait()
                uses[index][2](uses[index][1], index % 2)

            return run

        return [piece(index) for index in range(len(uses))]

    def tile(slot, first, last):
        return wb[slot, :, :, :, first:last].reshape(C, last - first)

    def spread_tile(source, slot, first, last, sink):
        def one(step, carry):
            rows = pl.ds(pl.multiple_of(step * half_rows, half_rows), half_rows)
            sink(rows, dot_plain(source[rows, :], tile(slot, first, last)))
            return carry

        lax.fori_loop(0, 2, one, 0)

    def collapse_tile(source, t, slot, first, last):
        def one(step, carry):
            rows = pl.ds(pl.multiple_of(step * half_rows, half_rows), half_rows)
            stream[rows, :] += dot_rows(source[t, rows, first:last], tile(slot, first, last))
            return carry

        lax.fori_loop(0, 2, one, 0)

    turned_before = [None]

    def turn_to(source, index):
        begin, wait = save(ptb, pt_ref.at[index])
        earlier, turned_before[0] = turned_before[0], wait

        def run():
            if earlier is not None:
                earlier()

            def one(step, carry):
                lanes = pl.ds(pl.multiple_of(step * 128, 128), 128)
                ptb[lanes, :] = source[:, lanes].T
                return carry

            lax.fori_loop(0, C // 128, one, 0)
            begin()

        return run

    chunk = 4 * FRAMES

    def normalise(bias, norm, positions):
        def one(step, carry):
            rows = pl.ds(pl.multiple_of(step * chunk, chunk), chunk)
            values = stream[rows, :] + joined_ref[8 + bias : 9 + bias, :]
            stream[rows, :] = values
            centre = jnp.mean(values, axis=1, keepdims=True)
            offset = values - centre
            inverse = lax.rsqrt(jnp.mean(offset * offset, axis=1, keepdims=True) + 1e-05)
            normed = offset * inverse * joined_ref[norm : norm + 1, :]
            normed = normed + joined_ref[4 + norm : 5 + norm, :]
            if positions:
                normed = normed.reshape(chunk // FRAMES, FRAMES, C) + position_ref[...][None]
                normed = normed.reshape(chunk, C)
            xb[rows, :] = normed.astype(jnp.bfloat16)
            return carry

        def run():
            lax.fori_loop(0, rows_all // chunk, one, 0)

        return run

    def attention(block, t):
        place = (1 - block) * width

        def run():
            same = same_pixel(BLOCK)
            for start in range(0, rows_all, BLOCK):
                here = slice(start, start + BLOCK)
                for head in range(width // HEAD):
                    low = head * HEAD
                    query = qkb[block, t, here, low : low + HEAD]
                    key = qkb[block, t, here, width + low : width + low + HEAD]
                    value = vb[block, t, here, low : low + HEAD]
                    probs = head_probs(query, key, same, scale).astype(jnp.bfloat16)
                    attb[block, t, here, place + low : place + low + HEAD] = dot_plain(
                        probs, value
                    ).astype(jnp.bfloat16)
            empty = pl.ds(0, width) if block == 0 else pl.ds(width, width)
            attb[block, t, :, empty] = jnp.zeros((rows_all, width), jnp.bfloat16)

        return run

    def join_input():
        for index in range(3):
            for copy in peer_copies(index):
                copy.wait_recv()
        for copy in own_peer:
            copy.wait()
        for t in range(4):
            lanes = slice(t * width, (t + 1) * width)
            joined_ref[:, lanes] = params_got[t, 0:16, :]
            xb[:, lanes] = x_got[t]
            for half in range(2):
                for part in range(2):
                    row = 16 + 2 * half + part
                    hidden_bias[t, half : half + 1, part * width : (part + 1) * width] = params_got[
                        t, row : row + 1, :
                    ]

    def in_tile(t, slot):
        def sink(rows, total):
            stream[rows, t * width : (t + 1) * width] = total[:, 64:384]

        spread_tile(xb, slot, 256, WIDE, sink)

    def qk_tile(block):
        def use(t, slot):
            def sink(rows, total):
                qkb[block, t, rows, :] = total.astype(jnp.bfloat16)

            spread_tile(xb, slot, 0, WIDE, sink)

        return use

    def v_tile(block):
        def use(t, slot):
            def sink(rows, total):
                vb[block, t, rows, :] = total[:, :width].astype(jnp.bfloat16)

            spread_tile(xb, slot, 0, 384, sink)

        return use

    def up_tile(half):
        def use(t, slot):
            def sink(rows, total):
                pre = total + hidden_bias[t, half : half + 1, :]
                below = 0.5 * (1.0 + lax.erf(pre * math.sqrt(0.5)))
                hid[half, t, rows, :] = (pre * below).astype(jnp.bfloat16)
                density = jnp.exp(-0.5 * pre * pre) * (1.0 / math.sqrt(2.0 * math.pi))
                slopeb[half, t, rows, :] = (below + pre * density).astype(jnp.bfloat16)

            spread_tile(xb, slot, 0, WIDE, sink)

        return use

    def down_tile(half):
        return lambda t, slot: collapse_tile(hid.at[half], t, slot, 0, WIDE)

    def last_stream():
        def one(step, carry):
            rows = pl.ds(pl.multiple_of(step * chunk, chunk), chunk)
            xb[rows, :] = (stream[rows, :] + joined_ref[11:12, :]).astype(jnp.bfloat16)
            return carry

        lax.fori_loop(0, rows_all // chunk, one, 0)

    def moved_tile(t, slot):
        def sink(rows, total):
            moved_ref[t, rows, :] = (total[:, 64:384] + params_got[t, 12:13, :]).astype(
                jnp.bfloat16
            )

        spread_tile(xb, slot, 256, WIDE, sink)

    four = range(4)
    streams = [save(stream, stream_out_ref.at[index]) for index in range(3)]
    kept = [
        (
            save(attb.at[block], q_ref.at[10 if block == 0 else 4]),
            save(qkb.at[block], qk_ref.at[block]),
            save(vb.at[block], v_ref.at[block]),
        )
        for block in range(2)
    ]
    hid_save = [save(hid.at[half], q_ref.at[1 - half]) for half in range(2)]
    slope_save = [save(slopeb.at[half], slope_ref.at[half]) for half in range(2)]

    def start_saves(*saves):
        def run():
            for begin, wait in saves:
                begin()

        return run

    input_turn = turn_to(xb, 7)
    unit_work = {
        1: tile_pieces([(1, t, in_tile) for t in four])
        + [normalise(0, 1, True), start_saves(streams[0])]
        + tile_pieces([(0, t, qk_tile(0)) for t in four] + [(1, t, v_tile(0)) for t in four]),
        2: [turn_to(xb, 4)]
        + [attention(0, t) for t in four]
        + [start_saves(*kept[0]), streams[0][1]],
        3: tile_pieces(
            [(3, t, lambda t, slot: collapse_tile(attb.at[0], t, slot, 256, WIDE)) for t in four]
        )
        + [normalise(1, 2, True), start_saves(streams[1])]
        + tile_pieces([(2, t, qk_tile(1)) for t in four] + [(3, t, v_tile(1)) for t in four]),
        4: [turn_to(xb, 3)]
        + [attention(1, t) for t in four]
        + [start_saves(*kept[1]), streams[1][1]]
        + tile_pieces(
            [(4, t, lambda t, slot: collapse_tile(attb.at[1], t, slot, 0, 384)) for t in four]
        )
        + [normalise(2, 3, False), start_saves(streams[2])],
        5: [turn_to(xb, 1)]
        + tile_pieces([(5, t, up_tile(0)) for t in four])
        + [start_saves(hid_save[0], slope_save[0])],
        6: tile_pieces([(6, t, up_tile(1)) for t in four])
        + [start_saves(hid_save[1], slope_save[1]), streams[2][1]],
        7: tile_pieces([(7, t, down_tile(0)) for t in four]),
        8: tile_pieces([(8, t, down_tile(1)) for t in four])
        + [last_stream]
        + tile_pieces([(4, t, moved_tile) for t in four])
        + [turn_to(xb, 5)],
    }

    def advance(turn, carry):
        count = len(stages)
        ready = turn - (count - 1)
        for place, number in enumerate(reversed(range(count))):
            unit = turn - number

            @pl.when((unit >= 0) & (unit < UNITS))
            def _(number=number, unit=unit):
                stages[number](unit)

            for owner, pieces in unit_work.items():
                size = len(pieces)
                mine = pieces[size * place // count : size * (place + 1) // count]
                if mine:

                    @pl.when(ready == owner)
                    def _(mine=mine):
                        for piece in mine:
                            piece()

        @pl.when(turn == 2)
        def _():
            join_input()
            input_turn()

        return carry

    lax.fori_loop(0, UNITS + len(stages) - 1, advance, 0)
    for wait in (
        [turned_before[0]]
        + [entry[1] for group in kept for entry in group]
        + [entry[1] for entry in hid_save + slope_save]
    ):
        wait()
    for index in range(3):
        for copy in peer_copies(index):
            copy.wait_send()


def forward_all(shards, rows_in, params, position):
    units, share, wide = shards.shape
    rows, width = rows_in.shape[1], rows_in.shape[2]
    low = jnp.bfloat16
    anywhere, near = pl.BlockSpec(memory_space=pl.ANY), pl.BlockSpec(memory_space=pltpu.VMEM)
    return pl.pallas_call(
        forward_kernel,
        in_specs=[anywhere, anywhere, near, near],
        out_specs=[anywhere] * 7 + [near] * 2,
        out_shape=[
            jax.ShapeDtypeStruct((units, 2, 2, 4, 2, share, wide), low),
            jax.ShapeDtypeStruct((12, 4, rows, wide), low),
            jax.ShapeDtypeStruct((8, C, rows), low),
            jax.ShapeDtypeStruct((3, rows, C), jnp.float32),
            jax.ShapeDtypeStruct((2, 4, rows, wide), low),
            jax.ShapeDtypeStruct((2, 4, rows, width), low),
            jax.ShapeDtypeStruct((2, 4, rows, wide), low),
            jax.ShapeDtypeStruct((4, rows, width), low),
            jax.ShapeDtypeStruct((16, C), jnp.float32),
        ],
        scratch_shapes=[
            pltpu.VMEM((rows, C), jnp.float32),
            pltpu.VMEM((rows, C), low),
            pltpu.VMEM((C, rows), low),
            pltpu.VMEM((4, rows, width), low),
            pltpu.VMEM((4,) + params.shape, jnp.float32),
            pltpu.VMEM((4, 8, wide), jnp.float32),
            pltpu.VMEM((2, 4, rows, wide), low),
            pltpu.VMEM((2, 4, rows, width), low),
            pltpu.VMEM((2, 4, rows, wide), low),
            pltpu.VMEM((2, 4, rows, wide), low),
            pltpu.VMEM((2, 4, rows, wide), low),
            pltpu.VMEM((2, 4, 2, share, wide), low),
            pltpu.SemaphoreType.DMA((2,)),
            pltpu.SemaphoreType.DMA((24,)),
            pltpu.SemaphoreType.DMA((2, 4)),
            pltpu.SemaphoreType.DMA((2, 3)),
            pltpu.SemaphoreType.DMA((units,)),
            pltpu.SemaphoreType.DMA((units, 2, 5)),
            pltpu.SemaphoreType.DMA((units, 2, 2, 4, 2)),
            pltpu.SemaphoreType.DMA((units, 3)),
        ],
        compiler_params=pltpu.CompilerParams(
            collective_id=0, has_side_effects=True, vmem_limit_bytes=60 << 20
        ),
    )(shards, rows_in, params, position)


def reduce_kernel(
    pt_ref,
    q_ref,
    out_ref,
    ptx_ref,
    qx_ref,
    p_buf,
    q_buf,
    dw,
    rya,
    rxa,
    rua,
    rda,
    rxb,
    rub,
    rdb,
    ryb,
    load_sem,
    give_sem,
    take_sem,
    send_sem,
    recv_sem,
    credit,
):
    at = Place()
    z, x, y, c = at.z, at.x, at.y, at.c
    far_x, far_y = at.far_x, at.far_y
    share = out_ref.shape[1]
    row_a, row_b = pl.ds(0, ROWS_A), pl.ds(ROWS_A, share - ROWS_A)
    count_p = pt_ref.shape[0]
    at.greet()

    def give_p(index):
        return pltpu.make_async_remote_copy(
            src_ref=pt_ref.at[index],
            dst_ref=ptx_ref.at[index],
            send_sem=give_sem.at[index],
            recv_sem=take_sem.at[index],
            device_id=at.to["core"],
            device_id_type=MESH_ID,
        )

    def give_q(index):
        return pltpu.make_async_remote_copy(
            src_ref=q_ref.at[index, :, 1 - c],
            dst_ref=qx_ref.at[index],
            send_sem=give_sem.at[count_p + index],
            recv_sem=take_sem.at[count_p + index],
            device_id=at.to["core"],
            device_id_type=MESH_ID,
        )

    for index in range(UNITS):
        if (index + index // 5) % 2 == 0:
            give_p((index + index // 5) // 2).start()
        give_q(index).start()
        if index in (4, 5, 7):
            extra = (index - 3) // 2
            give_p(5 + extra).start()
            give_q(UNITS + extra).start()

    names = ["ya0", "ya1", "xa", "ua0", "ua1", "ua2", "da0", "da1", "da2"]
    names += ["xb0", "xb1", "ub0", "ub1", "ub2", "db0", "db1", "db2", "yb"]
    number = {name: index for index, name in enumerate(names)}

    def copy(slot, name, src, dst, kind, shift=0):
        index = number[name] + shift
        return pltpu.make_async_remote_copy(
            src_ref=src,
            dst_ref=dst,
            send_sem=send_sem.at[slot, index],
            recv_sem=recv_sem.at[slot, index],
            device_id=at.to[kind],
            device_id_type=MESH_ID,
        )

    def ya(slot, part):
        side = far_x if part == 0 else x
        return copy(
            slot, f"ya{part}", dw.at[slot, far_y, :, side, row_a], rya.at[slot, part], "y"
        )

    def xa(slot):
        return copy(slot, "xa", dw.at[slot, y, :, far_x, row_a], rxa.at[slot], "x")

    def xb(slot, part):
        return copy(slot, f"xb{part}", dw.at[slot, part, :, far_x, row_b], rxb.at[slot, part], "x")

    def yb(slot):
        return copy(slot, "yb", dw.at[slot, far_y, z, x, row_b], ryb.at[slot], "y")

    def up(slot, colour, d):
        if colour == 0:
            return copy(slot, "ua0", dw.at[slot, y, d, x, row_a], rua.at[slot, d - 1], "up", d - 1)
        return copy(slot, "ub0", dw.at[slot, :, d, x, row_b], rub.at[slot, d - 1], "up", d - 1)

    def down(slot, colour, d):
        if colour == 0:
            return copy(slot, "da0", dw.at[slot, y, d, x, row_a], rda.at[slot, d], "down", d)
        return copy(slot, "db0", dw.at[slot, :, d, x, row_b], rdb.at[slot, d], "down", d)

    def add(place, got):
        total = place[...].astype(jnp.float32) + got[...].astype(jnp.float32)
        place[...] = total.astype(jnp.bfloat16)

    def products(slot, p_index, q_index, more):
        loads = [
            pltpu.make_async_copy(pt_ref.at[p_index], p_buf.at[0], load_sem.at[0]),
            pltpu.make_async_copy(ptx_ref.at[p_index], p_buf.at[1], load_sem.at[1]),
            pltpu.make_async_copy(q_ref.at[q_index, :, c], q_buf.at[0], load_sem.at[2]),
            pltpu.make_async_copy(qx_ref.at[q_index], q_buf.at[1], load_sem.at[3]),
        ]
        for load in loads:
            load.start()
        for load in loads:
            load.wait()

        def one(step, carry):
            side, zz = step // 4, step % 4
            yy = jnp.where(side == 0, far_y, y)
            rows = pl.ds(pl.multiple_of(zz * 2 * share, 2 * share), 2 * share)
            total = dot_plain(p_buf[0, rows, :], q_buf[0, yy]) + dot_plain(
                p_buf[1, rows, :], q_buf[1, yy]
            )
            total = total.reshape(2, share, WIDE)
            if more:
                total = total + dw[slot, yy, zz].astype(jnp.float32)
            dw[slot, yy, zz] = total.astype(jnp.bfloat16)
            return carry

        lax.fori_loop(0, 8, one, 0)

    def stage0(turn):
        slot = turn % SLOTS_IN_FLIGHT
        p_index = (turn + turn // 5) // 2

        @pl.when((turn + turn // 5) % 2 == 0)
        def _():
            give_p(p_index).wait_recv()

        give_q(turn).wait_recv()
        products(slot, p_index, turn, False)

        @pl.when((turn == 4) | (turn == 5) | (turn == 7))
        def _():
            extra = (turn - 3) // 2
            give_p(5 + extra).wait_recv()
            give_q(UNITS + extra).wait_recv()
            products(slot, 5 + extra, UNITS + extra, True)

        @pl.when(turn >= SLOTS_IN_FLIGHT)
        def _():
            pl.semaphore_wait(credit.at[0], 1)
            pl.semaphore_wait(credit.at[1], 1)
            pl.when(at.has_up)(lambda: pl.semaphore_wait(credit.at[2], 1))
            pl.when(at.has_down)(lambda: pl.semaphore_wait(credit.at[3], 1))

        ya(slot, 0).start()
        xb(slot, 0).start()
        ya(slot, 1).start()
        xb(slot, 1).start()

    def z_step(slot, colour, step):
        @pl.when(z <= step - 1)
        def _():
            d = z + 4 - step

            @pl.when(z >= 1)
            def _():
                up(slot, colour, d).wait_recv()
                if colour == 0:
                    add(dw.at[slot, y, d, x, row_a], rua.at[slot, d - 1])
                else:
                    add(dw.at[slot, 0, d, x, row_b], rub.at[slot, d - 1, 0])
                    add(dw.at[slot, 1, d, x, row_b], rub.at[slot, d - 1, 1])

            up(slot, colour, d).start()

        @pl.when(3 - z <= step - 1)
        def _():
            d = z - 4 + step

            @pl.when(z <= 2)
            def _():
                down(slot, colour, d).wait_recv()
                if colour == 0:
                    add(dw.at[slot, y, d, x, row_a], rda.at[slot, d])
                else:
                    add(dw.at[slot, 0, d, x, row_b], rdb.at[slot, d, 0])
                    add(dw.at[slot, 1, d, x, row_b], rdb.at[slot, d, 1])

            down(slot, colour, d).start()

    def stage1(turn):
        slot = turn % SLOTS_IN_FLIGHT
        for part in range(2):
            xb(slot, part).wait_recv()
            for zz in range(4):
                add(dw.at[slot, part, zz, x, row_b], rxb.at[slot, part, zz])
        z_step(slot, 1, 1)
        ya(slot, 0).wait_recv()
        for zz in range(4):
            add(dw.at[slot, y, zz, far_x, row_a], rya.at[slot, 0, zz])
        xa(slot).start()
        ya(slot, 1).wait_recv()
        for zz in range(4):
            add(dw.at[slot, y, zz, x, row_a], rya.at[slot, 1, zz])

    def stage2(turn):
        slot = turn % SLOTS_IN_FLIGHT
        z_step(slot, 1, 2)
        xa(slot).wait_recv()
        for zz in range(4):
            add(dw.at[slot, y, zz, x, row_a], rxa.at[slot, zz])
        z_step(slot, 0, 1)

    def stage3(turn):
        slot = turn % SLOTS_IN_FLIGHT
        z_step(slot, 1, 3)
        z_step(slot, 0, 2)

    def stage4(turn):
        slot = turn % SLOTS_IN_FLIGHT
        z_step(slot, 0, 3)

        @pl.when(z >= 1)
        def _():
            up(slot, 1, z).wait_recv()
            for yy in range(2):
                add(dw.at[slot, yy, z, x, row_b], rub.at[slot, z - 1, yy])

        @pl.when(z <= 2)
        def _():
            down(slot, 1, z).wait_recv()
            for yy in range(2):
                add(dw.at[slot, yy, z, x, row_b], rdb.at[slot, z, yy])

        yb(slot).start()

    def stage5(turn):
        slot = turn % SLOTS_IN_FLIGHT
        unit = UNITS - 1 - turn
        out_ref[unit, row_a, :] = dw[slot, y, z, x, row_a, :].astype(jnp.float32)

        @pl.when(z >= 1)
        def _():
            up(slot, 0, z).wait_recv()
            out_ref[unit, row_a, :] += rua[slot, z - 1].astype(jnp.float32)

        @pl.when(z <= 2)
        def _():
            down(slot, 0, z).wait_recv()
            out_ref[unit, row_a, :] += rda[slot, z].astype(jnp.float32)

        yb(slot).wait_recv()
        out_ref[unit, row_b, :] = dw[slot, y, z, x, row_b, :].astype(jnp.float32) + ryb[
            slot
        ].astype(jnp.float32)

        ya(slot, 0).wait_send()
        ya(slot, 1).wait_send()
        xa(slot).wait_send()
        xb(slot, 0).wait_send()
        xb(slot, 1).wait_send()
        yb(slot).wait_send()
        for colour in range(2):
            for step in range(1, 4):

                @pl.when(z <= step - 1)
                def _(colour=colour, step=step):
                    up(slot, colour, z + 4 - step).wait_send()

                @pl.when(3 - z <= step - 1)
                def _(colour=colour, step=step):
                    down(slot, colour, z - 4 + step).wait_send()

        @pl.when(turn + SLOTS_IN_FLIGHT < UNITS)
        def _():
            def grant(kind, index):
                pl.semaphore_signal(
                    credit.at[index], inc=1, device_id=at.to[kind], device_id_type=MESH_ID
                )

            grant("x", 0)
            grant("y", 1)
            pl.when(at.has_up)(lambda: grant("up", 3))
            pl.when(at.has_down)(lambda: grant("down", 2))

    stages = (stage0, stage1, stage2, stage3, stage4, stage5)

    def advance(now, carry):
        for step in range(len(stages)):
            turn = now - step

            @pl.when((turn >= 0) & (turn < UNITS))
            def _(step=step, turn=turn):
                stages[step](turn)

        return carry

    lax.fori_loop(0, UNITS + len(stages) - 1, advance, 0)
    for index in range(count_p):
        give_p(index).wait_send()
    for index in range(q_ref.shape[0]):
        give_q(index).wait_send()


def reduce_all(turned, parts, share):
    count_p, width, rows = turned.shape
    count_q = parts.shape[0]
    low = jnp.bfloat16
    slots, rest = SLOTS_IN_FLIGHT, share - ROWS_A
    return pl.pallas_call(
        reduce_kernel,
        in_specs=[pl.BlockSpec(memory_space=pl.ANY)] * 2,
        out_specs=[
            pl.BlockSpec(memory_space=pltpu.VMEM),
            pl.BlockSpec(memory_space=pl.ANY),
            pl.BlockSpec(memory_space=pl.ANY),
        ],
        out_shape=[
            jax.ShapeDtypeStruct((UNITS, share, WIDE), jnp.float32),
            jax.ShapeDtypeStruct((count_p, width, rows), low),
            jax.ShapeDtypeStruct((count_q, 2, rows, WIDE), low),
        ],
        scratch_shapes=[
            pltpu.VMEM((2, width, rows), low),
            pltpu.VMEM((2, 2, rows, WIDE), low),
            pltpu.VMEM((slots, 2, 4, 2, share, WIDE), low),
            pltpu.VMEM((slots, 2, 4, ROWS_A, WIDE), low),
            pltpu.VMEM((slots, 4, ROWS_A, WIDE), low),
            pltpu.VMEM((slots, 3, ROWS_A, WIDE), low),
            pltpu.VMEM((slots, 3, ROWS_A, WIDE), low),
            pltpu.VMEM((slots, 2, 4, rest, WIDE), low),
            pltpu.VMEM((slots, 3, 2, rest, WIDE), low),
            pltpu.VMEM((slots, 3, 2, rest, WIDE), low),
            pltpu.VMEM((slots, rest, WIDE), low),
            pltpu.SemaphoreType.DMA((4,)),
            pltpu.SemaphoreType.DMA((count_p + count_q,)),
            pltpu.SemaphoreType.DMA((count_p + count_q,)),
            pltpu.SemaphoreType.DMA((slots, 18)),
            pltpu.SemaphoreType.DMA((slots, 18)),
            pltpu.SemaphoreType.REGULAR((4,)),
        ],
        compiler_params=pltpu.CompilerParams(
            collective_id=1, has_side_effects=True, vmem_limit_bytes=60 << 20
        ),
    )(turned, parts)[0]
def gather_plain(shards):
    units, share, wide = shards.shape
    whole = lax.all_gather(shards, MIXED, axis=1, tiled=True)
    return whole.reshape(units, lax.axis_size("tensor"), C, wide)


def reduce_plain(turned, parts, share):
    reduced = []
    for turn in range(UNITS):
        whole = jnp.einsum(
            "kr,trn->tkn", turned[(turn + turn // 5) // 2], parts[turn],
            preferred_element_type=jnp.float32,
        )
        if turn in (4, 5, 7):
            extra = (turn - 3) // 2
            whole = whole + jnp.einsum(
                "kr,trn->tkn", turned[5 + extra], parts[UNITS + extra],
                preferred_element_type=jnp.float32,
            )
        whole = whole.astype(jnp.bfloat16).reshape(-1, whole.shape[2])
        reduced.append(
            lax.psum_scatter(whole, MIXED, scatter_dimension=0, tiled=True).astype(jnp.float32)
        )
    return jnp.stack(reduced[::-1], 0)


def by_pixels(values, tensor_size):
    slots, frames, width, pixels = values.shape
    own = pixels // tensor_size
    return jnp.transpose(values, (3, 0, 1, 2)).reshape(tensor_size, own * slots * frames, width)


def exchange(parts):
    return lax.all_to_all(parts, "tensor", 0, 0, tiled=True)


def to_channels(values, slots, pixels):
    tensor_size, rows, width = values.shape
    arrived = lax.all_to_all(values, "tensor", 0, 0, tiled=True)
    return jnp.transpose(arrived.reshape(pixels, slots, FRAMES, width), (1, 2, 3, 0))


def body(
    by_kernel,
    latent,
    clip_flags,
    cotangent,
    norm_gain,
    norm_shift,
    channel_bias,
    hidden_bias,
    weight_in,
    weight_qkv,
    weight_out,
    weight_up,
    weight_down,
    weight_proj,
):
    tensor_size = lax.axis_size("tensor")
    slots, frames, width, pixels = latent.shape
    share = weight_in.shape[0]
    hidden_width = hidden_bias.shape[0]
    flags = (clip_flags > 0)[:, None, None, None]

    wide = 2 * width

    shards = []
    side = jnp.concatenate
    for block in range(2):
        shards.append(weight_qkv[block, :, :2].reshape(share, wide))
        other = weight_in if block == 0 else weight_out[0].T
        shards.append(side([weight_qkv[block, :, 2], other], 1))
    shards.append(side([weight_out[1].T, weight_proj], 1))
    shards += [weight_up[:, :wide], weight_up[:, wide:]]
    down_turned = weight_down.T
    shards += [down_turned[:, :wide], down_turned[:, wide:]]
    shards = jnp.stack(shards, 0)
    params = jnp.zeros((24, width), jnp.float32)
    params = params.at[:13].set(side([norm_gain, norm_shift, channel_bias], 0))
    params = params.at[16:20].set(hidden_bias.reshape(4, width))

    start = latent.astype(jnp.float32)
    cot = cotangent.astype(jnp.float32)
    group_width = C // GROUPS
    grouped = start.reshape(slots, frames, width // group_width, group_width, pixels)
    group_centre = jnp.mean(grouped, axis=(1, 3, 4), keepdims=True)
    offset = grouped - group_centre
    group_inverse = lax.rsqrt(jnp.mean(offset * offset, axis=(1, 3, 4), keepdims=True) + 1e-06)
    group_hat = (offset * group_inverse).reshape(start.shape)
    normed = group_hat * norm_gain[0][:, None] + norm_shift[0][:, None]
    sent = by_pixels(normed.astype(jnp.bfloat16), tensor_size)
    rows = sent.shape[1]

    grad_moved_local = jnp.where(flags, cot, 0.0)
    bias_moved = jnp.sum(grad_moved_local, axis=(0, 1, 3))
    grad_moved = exchange(by_pixels(grad_moved_local.astype(jnp.bfloat16), tensor_size))

    if by_kernel:
        whole, q_all, pt_all, streams, qk_all, v_all, slopes, moved, joined = forward_all(
            shards, sent, params, make_positions()
        )
        gains = joined[:4]
        whole = whole.reshape(UNITS, tensor_size, C, wide)
    else:
        arrived = exchange(sent)
        inputs_in = jnp.transpose(arrived, (1, 0, 2)).reshape(rows, C)
        packed = lax.all_gather(params, "tensor", axis=0, tiled=False)
        joined = jnp.transpose(packed[:, :13], (1, 0, 2)).reshape(13, C)
        gains, shifts, biases = joined[:4], joined[4:8], joined[8:]
        hidden_full = packed[:, 16:20].reshape(tensor_size, 2 * wide)
        whole = gather_plain(shards)
    full_qk = (whole[0], whole[2])
    full_v = (whole[1, :, :, :width], whole[3, :, :, :width])
    full_in = whole[1, :, :, width:]
    full_out = (whole[3, :, :, width:], whole[4, :, :, :width])
    full_proj = whole[4, :, :, width:]
    full_up = (whole[5], whole[6])
    full_down = (whole[7], whole[8])

    if by_kernel:
        kept = []
        for block in range(2):
            hat, inverse = layer_stats(streams[block])
            kept.append((hat, inverse, pt_all[4 - block], qk_all[block], v_all[block], None))
        hat_feed, inverse_feed = layer_stats(streams[2])
    else:
        def join(parts):
            return jnp.transpose(parts, (1, 0, 2)).reshape(rows, parts.shape[0] * parts.shape[2])

        stream = join(spread(inputs_in, full_in)) + biases[0]
        position = jnp.tile(make_positions(), (rows // FRAMES, 1))
        kept = []
        for block in range(2):
            hat, inverse = layer_stats(stream)
            lifted = (hat * gains[1 + block] + shifts[1 + block] + position).astype(jnp.bfloat16)
            qk = spread(lifted, full_qk[block]).astype(jnp.bfloat16)
            values = spread(lifted, full_v[block]).astype(jnp.bfloat16)
            attended = attend(qk, values)
            stream = stream + collapse(attended, full_out[block]) + biases[1 + block]
            kept.append((hat, inverse, lifted.T, qk, values, attended))
        hat_feed, inverse_feed = layer_stats(stream)
        inputs_up = (hat_feed * gains[3] + shifts[3]).astype(jnp.bfloat16)
        pre_act = [
            spread(inputs_up, full_up[half])
            + hidden_full[:, None, half * wide : half * wide + wide]
            for half in range(2)
        ]
        slopes = [
            jax.vjp(partial(jax.nn.gelu, approximate=False), pre)[1](jnp.ones_like(pre))[0]
            for pre in pre_act
        ]
        hidden = [jax.nn.gelu(pre, approximate=False).astype(jnp.bfloat16) for pre in pre_act]
        stream = stream + collapse(hidden[0], full_down[0]) + collapse(hidden[1], full_down[1])
        stream = stream + biases[3]
        inputs_proj = stream.astype(jnp.bfloat16)
        moved = spread(inputs_proj, full_proj) + biases[4].reshape(tensor_size, 1, width)
        moved = moved.astype(jnp.bfloat16)

    moved_local = to_channels(moved, slots, pixels).astype(jnp.float32)
    output = jnp.where(flags, start + moved_local, start).astype(jnp.bfloat16)

    bias_grads = [None] * 4
    gain_grads = [None] * 3
    shift_grads = [None] * 3
    empty = jnp.zeros((tensor_size, rows, width), jnp.bfloat16)
    turned, parts = [None] * 8, [None] * 12
    if by_kernel:
        turned[1], turned[5], turned[7] = pt_all[1], pt_all[5], pt_all[7]
        for index in (0, 1, 4, 10):
            parts[index] = q_all[index]
    else:
        turned[1], turned[5], turned[7] = inputs_up.T, inputs_proj.T, inputs_in.T
        parts[0], parts[1] = hidden[1], hidden[0]
    parts[9] = side([empty, grad_moved], 2)
    grad_stream = collapse(grad_moved, full_proj)
    bias_grads[3] = jnp.sum(grad_stream, 0)
    grad_low = grad_stream.astype(jnp.bfloat16)
    turned[0] = grad_low.T
    hidden_grads = [None, None]
    grad_normed = 0.0
    for half in (1, 0):
        grad_hidden = spread(grad_low, full_down[half])
        grad_pre = grad_hidden * slopes[half]
        hidden_grads[half] = jnp.sum(grad_pre, 1)
        parts[3 - half] = grad_pre.astype(jnp.bfloat16)
        grad_normed = grad_normed + collapse(parts[3 - half], full_up[half])
    hidden_grad = side(hidden_grads, 1)
    grad_layer, gain_grads[2], shift_grads[2] = layer_back(
        grad_normed, hat_feed, inverse_feed, gains[3]
    )
    grad_stream = grad_stream + grad_layer
    for block in (1, 0):
        hat, inverse, lifted_turned, qk, values, attended = kept[block]
        bias_grads[1 + block] = jnp.sum(grad_stream, 0)
        grad_low = grad_stream.astype(jnp.bfloat16)
        turned[2 if block == 1 else 6] = grad_low.T
        if not by_kernel:
            pair = [attended, empty] if block == 1 else [empty, attended]
            parts[4 if block == 1 else 10] = side(pair, 2)
        grad_attended = spread(grad_low, full_out[block]).astype(jnp.bfloat16)
        grad_qk, grad_values = attend_back(qk, values, grad_attended)
        turned[3 if block == 1 else 4] = lifted_turned
        parts[5 if block == 1 else 7] = side([grad_values, empty], 2)
        parts[6 if block == 1 else 8] = grad_qk
        grad_lifted = collapse(grad_qk, full_qk[block]) + collapse(grad_values, full_v[block])
        grad_layer, gain_grads[block], shift_grads[block] = layer_back(
            grad_lifted, hat, inverse, gains[1 + block]
        )
        grad_stream = grad_stream + grad_layer
    bias_grads[0] = jnp.sum(grad_stream, 0)
    grad_low = grad_stream.astype(jnp.bfloat16)
    grad_low_parts = jnp.transpose(grad_low.reshape(rows, tensor_size, width), (1, 0, 2))
    parts[11] = side([empty, grad_low_parts], 2)
    turned, parts = jnp.stack(turned, 0), jnp.stack(parts, 0)
    if by_kernel:
        reduced = reduce_all(turned, parts.reshape(12, 2, 2, rows, wide), share)
    else:
        reduced = reduce_plain(turned, parts, share)
    qkv_grads = [
        side([reduced[2 * block], reduced[2 * block + 1, :, :width]], 1).reshape(share, 3, width)
        for block in range(2)
    ]
    out_grads = [reduced[3, :, width:].T, reduced[4, :, :width].T]
    in_grad, proj_grad = reduced[1, :, width:], reduced[4, :, width:]
    up_grad = side([reduced[5], reduced[6]], 1)
    down_grad = side([reduced[7], reduced[8]], 1)
    grad_normed = collapse(grad_low_parts, full_in).astype(jnp.bfloat16)
    grad_normed = jnp.transpose(grad_normed.reshape(rows, tensor_size, width), (1, 0, 2))
    grad_normed = to_channels(grad_normed, slots, pixels).astype(jnp.float32)
    scaled = grad_normed * norm_gain[0][:, None]
    scaled_groups = scaled.reshape(grouped.shape)
    hat_groups = group_hat.reshape(grouped.shape)
    first = jnp.mean(scaled_groups, axis=(1, 3, 4), keepdims=True)
    second = jnp.mean(scaled_groups * hat_groups, axis=(1, 3, 4), keepdims=True)
    grad_group = group_inverse * (scaled_groups - first - hat_groups * second)
    latent_grad = cot + grad_group.reshape(start.shape)
    group_gain_grad = jnp.sum(grad_normed * group_hat, axis=(0, 1, 3))
    group_shift_grad = jnp.sum(grad_normed, axis=(0, 1, 3))

    vectors = jnp.stack(gain_grads + shift_grads + bias_grads, 0)
    vectors = jnp.transpose(vectors.reshape(10, tensor_size, width), (1, 0, 2))
    vectors = jnp.concatenate([vectors.reshape(tensor_size, 10 * width), hidden_grad], 1)
    vectors = lax.psum_scatter(vectors, "tensor", scatter_dimension=0, tiled=False)
    sums = lax.psum(
        jnp.concatenate([vectors, group_gain_grad, group_shift_grad, bias_moved]), "dp"
    )
    channel_sums = sums[: 10 * width].reshape(10, width)
    hidden_bias_grad = sums[10 * width : 10 * width + hidden_width]
    local_sums = sums[10 * width + hidden_width :].reshape(3, width)
    gain_grad = jnp.concatenate([local_sums[0:1], channel_sums[0:3]], 0)
    shift_grad = jnp.concatenate([local_sums[1:2], channel_sums[3:6]], 0)
    channel_bias_grad = jnp.concatenate([channel_sums[6:10], local_sums[2:3]], 0)
    return (
        output,
        latent_grad,
        gain_grad,
        shift_grad,
        channel_bias_grad,
        hidden_bias_grad,
        in_grad,
        jnp.stack(qkv_grads, 0),
        jnp.stack(out_grads, 0),
        up_grad,
        down_grad.T,
        proj_grad,
    )


def solution(mesh):
    placed = (
        P("dp", None, "tensor", None),
        P("dp"),
        P("dp", None, "tensor", None),
        P(None, "tensor"),
        P(None, "tensor"),
        P(None, "tensor"),
        P("tensor"),
        P("dp", "tensor"),
        P(None, "dp", None, "tensor"),
        P(None, "tensor", "dp"),
        P("dp", "tensor"),
        P("tensor", "dp"),
        P("dp", "tensor"),
    )
    return jax.shard_map(
        partial(body, tuple(mesh.shape[name] for name in ("dp", "tensor")) == (8, 4)),
        mesh=mesh,
        in_specs=placed,
        out_specs=(
            P("dp", None, "tensor", None),
            P("dp", None, "tensor", None),
            P(None, "tensor"),
            P(None, "tensor"),
            P(None, "tensor"),
            P("tensor"),
            P("dp", "tensor"),
            P(None, "dp", None, "tensor"),
            P(None, "tensor", "dp"),
            P("dp", "tensor"),
            P("tensor", "dp"),
            P("dp", "tensor"),
        ),
        check_vma=False,
    )
```

```python
from functools import partial
import math

import jax
import jax.numpy as jnp
from jax import lax
from jax.experimental import pallas as pl
from jax.experimental.pallas import tpu as pltpu
from jax.sharding import PartitionSpec as P

C = 1280
GROUPS = 32
FRAMES = 16
HEAD = 160
BLOCK = 128
MIXED = ("tensor", "dp")


def spread(rows, weight):
    return jnp.einsum("rk,tkn->trn", rows, weight, preferred_element_type=jnp.float32)


def collapse(parts, weight):
    return jnp.einsum("trn,tkn->rk", parts, weight, preferred_element_type=jnp.float32)


def make_positions():
    channel_ids = jnp.arange(C)
    pair_rate = jnp.exp((channel_ids // 2).astype(jnp.float32) * (-2.0 * math.log(10000.0) / C))
    angles = jnp.arange(FRAMES).astype(jnp.float32)[:, None] * pair_rate[None, :]
    return jnp.where(channel_ids[None, :] % 2 == 0, jnp.sin(angles), jnp.cos(angles))


def layer_stats(stream):
    centre = jnp.mean(stream, axis=1, keepdims=True)
    offset = stream - centre
    inverse = lax.rsqrt(jnp.mean(offset * offset, axis=1, keepdims=True) + 1e-05)
    return offset * inverse, inverse


def layer_back(grad_out, normal_part, inverse, gain):
    scaled = grad_out * gain
    first = jnp.mean(scaled, axis=1, keepdims=True)
    second = jnp.mean(scaled * normal_part, axis=1, keepdims=True)
    grad_in = inverse * (scaled - first - normal_part * second)
    return grad_in, jnp.sum(grad_out * normal_part, 0), jnp.sum(grad_out, 0)


def dot_rows(left, right):
    return lax.dot_general(left, right, (((1,), (1,)), ((), ())), preferred_element_type=jnp.float32)


def dot_plain(left, right):
    return lax.dot_general(left, right, (((1,), (0,)), ((), ())), preferred_element_type=jnp.float32)


def dot_first(left, right):
    return lax.dot_general(left, right, (((0,), (0,)), ((), ())), preferred_element_type=jnp.float32)


def same_pixel(block):
    row = lax.broadcasted_iota(jnp.int32, (block, block), 0) // FRAMES
    col = lax.broadcasted_iota(jnp.int32, (block, block), 1) // FRAMES
    return row == col


def head_probs(query, key, same, scale):
    scores = jnp.where(same, dot_rows(query, key) * scale, -1e30)
    top = jnp.max(scores, axis=1, keepdims=True)
    weights = jnp.where(same, jnp.exp(scores - top), 0.0)
    return weights / jnp.sum(weights, axis=1, keepdims=True)


def attend_kernel(scale, qk_ref, v_ref, out_ref):
    rows, width = out_ref.shape[1], out_ref.shape[2]
    block = min(BLOCK, rows)
    same = same_pixel(block)
    for start in range(0, rows, block):
        for head in range(width // HEAD):
            here, low = slice(start, start + block), head * HEAD
            query = qk_ref[0, here, low : low + HEAD]
            key = qk_ref[0, here, width + low : width + low + HEAD]
            value = v_ref[0, here, low : low + HEAD]
            probs = head_probs(query, key, same, scale).astype(jnp.bfloat16)
            out_ref[0, here, low : low + HEAD] = dot_plain(probs, value).astype(jnp.bfloat16)


def part_spec(array):
    return pl.BlockSpec((1,) + array.shape[1:], lambda t: (t, 0, 0))


def attend(qk, values):
    return pl.pallas_call(
        partial(attend_kernel, 1.0 / math.sqrt(HEAD)),
        grid=(qk.shape[0],),
        in_specs=[part_spec(qk), part_spec(values)],
        out_specs=part_spec(values),
        out_shape=jax.ShapeDtypeStruct(values.shape, jnp.bfloat16),
        compiler_params=pltpu.CompilerParams(vmem_limit_bytes=32 << 20),
    )(qk, values)


def attend_back_kernel(scale, qk_ref, v_ref, grad_ref, dqk_ref, dv_ref):
    rows, width = grad_ref.shape[1], grad_ref.shape[2]
    block = min(BLOCK, rows)
    same = same_pixel(block)
    for start in range(0, rows, block):
        for head in range(width // HEAD):
            here, low = slice(start, start + block), head * HEAD
            query = qk_ref[0, here, low : low + HEAD]
            key = qk_ref[0, here, width + low : width + low + HEAD]
            value = v_ref[0, here, low : low + HEAD]
            grad = grad_ref[0, here, low : low + HEAD]
            probs = head_probs(query, key, same, scale)
            grad_probs = dot_rows(grad, value)
            centred = jnp.sum(probs * grad_probs, axis=1, keepdims=True)
            grad_raw = (probs * (grad_probs - centred) * scale).astype(jnp.bfloat16)
            dqk_ref[0, here, low : low + HEAD] = dot_plain(grad_raw, key).astype(jnp.bfloat16)
            dqk_ref[0, here, width + low : width + low + HEAD] = dot_first(grad_raw, query).astype(
                jnp.bfloat16
            )
            dv_ref[0, here, low : low + HEAD] = dot_first(probs.astype(jnp.bfloat16), grad).astype(
                jnp.bfloat16
            )


def attend_back(qk, values, grad):
    return pl.pallas_call(
        partial(attend_back_kernel, 1.0 / math.sqrt(HEAD)),
        grid=(qk.shape[0],),
        in_specs=[part_spec(qk), part_spec(values), part_spec(values)],
        out_specs=[part_spec(qk), part_spec(values)],
        out_shape=[
            jax.ShapeDtypeStruct(qk.shape, jnp.bfloat16),
            jax.ShapeDtypeStruct(values.shape, jnp.bfloat16),
        ],
        compiler_params=pltpu.CompilerParams(vmem_limit_bytes=32 << 20),
    )(qk, values, grad)


UNITS = 9
WIDE = 640
SLOTS_IN_FLIGHT = 6
SLOTS_RECEIVED = 4
ROWS_A = 96
MESH_ID = pl.DeviceIdType.MESH


class Place:
    def __init__(self):
        dp, tn = lax.axis_index("dp"), lax.axis_index("tensor")
        self.z, self.x = dp // 2, dp % 2
        self.y, self.c = tn // 2, tn % 2
        self.far_x, self.far_y = 1 - self.x, 1 - self.y
        self.to = {
            "x": (self.z * 2 + self.far_x, tn),
            "y": (dp, self.far_y * 2 + self.c),
            "core": (dp, self.y * 2 + 1 - self.c),
            "cross": (dp, self.far_y * 2 + 1 - self.c),
            "up": (dp + 2, tn),
            "down": (dp - 2, tn),
        }
        self.has_up = self.z < 3
        self.has_down = self.z > 0

    def greet(self):
        barrier = pltpu.get_barrier_semaphore()

        def hello(name):
            pl.semaphore_signal(barrier, inc=1, device_id=self.to[name], device_id_type=MESH_ID)

        for name in ("x", "y", "core", "cross"):
            hello(name)
        pl.when(self.has_up)(lambda: hello("up"))
        pl.when(self.has_down)(lambda: hello("down"))
        pl.semaphore_wait(barrier, 4 + (6 - self.z) // 4 + (self.z + 3) // 4)


class Plan:
    FIELDS = (("kind", 16), ("unit", 9), ("t", 4), ("aux", 80), ("slot", 2), ("fresh", 2), ("next", 37))

    def __init__(self, per_turn):
        self.per_turn = per_turn
        self.steps = {}

    def fill(self, turn, steps):
        tiles = [index for index, step in enumerate(steps) if step[1] is not None]
        for index, (kind, unit, t, aux) in enumerate(steps):
            slot = fresh = following = 0
            if unit is not None:
                order = tiles.index(index)
                slot, fresh = order % 2, int(order == 0)
                if order + 1 < len(tiles):
                    later = steps[tiles[order + 1]]
                    following = 1 + later[1] * 4 + later[2]
            values = (kind, unit or 0, t, aux, slot, fresh, following)
            code, scale = 0, 1
            for (name, size), value in zip(self.FIELDS, values):
                assert 0 <= value < size
                code += scale * value
                scale *= size
            place = turn * self.per_turn + index * self.per_turn // len(steps)
            assert place not in self.steps
            self.steps[place] = code

    def read(self, place):
        code = jnp.int32(0)
        for where, value in self.steps.items():
            code = code + jnp.where(place == where, jnp.int32(value), jnp.int32(0))
        out = {}
        for name, size in self.FIELDS:
            out[name] = code % size
            code = code // size
        return out


def await_bytes(ref, sem):
    pltpu.make_async_copy(ref, ref, sem).wait()


def forward_kernel(
    shard_ref,
    x_ref,
    params_ref,
    position_ref,
    whole_ref,
    q_ref,
    pt_ref,
    stream_out_ref,
    qk_ref,
    v_ref,
    slope_ref,
    moved_ref,
    joined_ref,
    stream,
    xb,
    ptb,
    x_got,
    params_got,
    hidden_bias,
    qkb,
    vb,
    cols,
    slopeb,
    first_rows,
    total,
    wb,
    tile_sem,
    save_sem,
    kept_sem,
    peer_send,
    peer_recv,
    local_sem,
    send_sem,
    recv_sem,
    core_sem,
):
    at = Place()
    z, x, y, c = at.z, at.x, at.y, at.c
    share = shard_ref.shape[1]
    cut = (pl.ds(0, ROWS_A), pl.ds(ROWS_A, share - ROWS_A))
    kinds = {"up": 0, "down": 1, "x": 2, "y": 3, "core": 4}
    at.greet()

    def send(unit, colour, yy, zz, xx, kind, own=False):
        place = whole_ref.at[unit, yy, c, zz, xx, cut[colour]]
        pltpu.make_async_remote_copy(
            src_ref=shard_ref.at[unit, cut[colour]] if own else place,
            dst_ref=place,
            send_sem=send_sem.at[unit, colour, kinds[kind]],
            recv_sem=recv_sem.at[unit, colour, yy, zz, xx],
            device_id=at.to[kind],
            device_id_type=MESH_ID,
        ).start()

    def arrived(unit, colour, yy, zz, xx):
        await_bytes(
            whole_ref.at[unit, yy, c, zz, xx, cut[colour]], recv_sem.at[unit, colour, yy, zz, xx]
        )

    def own_copy(unit):
        return pltpu.make_async_copy(
            shard_ref.at[unit], whole_ref.at[unit, y, c, z, x], local_sem.at[unit]
        )

    def to_core(unit, part):
        if part == 2:
            place = whole_ref.at[unit, :, c, :, :, cut[1]]
        else:
            place = whole_ref.at[unit, y if part == 0 else at.far_y, c, :, :, cut[0]]
        return pltpu.make_async_remote_copy(
            src_ref=place,
            dst_ref=place,
            send_sem=send_sem.at[unit, part // 2, 4],
            recv_sem=core_sem.at[unit, part],
            device_id=at.to["core"],
            device_id_type=MESH_ID,
        )

    def from_z(unit, colour, step, yy):
        @pl.when(z >= step)
        def _():
            zz = z - step
            arrived(unit, colour, yy, zz, x)
            pl.when(at.has_up)(lambda: send(unit, colour, yy, zz, x, "up"))
            send(unit, colour, yy, zz, x, "x")
            if colour == 0:
                send(unit, colour, yy, zz, x, "y")

        @pl.when(z + step <= 3)
        def _():
            zz = z + step
            arrived(unit, colour, yy, zz, x)
            pl.when(at.has_down)(lambda: send(unit, colour, yy, zz, x, "down"))
            send(unit, colour, yy, zz, x, "x")
            if colour == 0:
                send(unit, colour, yy, zz, x, "y")

    def from_x(unit, step):
        def one(zz):
            arrived(unit, 0, y, zz, at.far_x)
            send(unit, 0, y, zz, at.far_x, "y")

        if step == 0:
            one(z)
        else:
            pl.when(z >= step)(lambda: one(z - step))
            pl.when(z + step <= 3)(lambda: one(z + step))

    def stage0(unit):
        own_copy(unit).start()
        pl.when(at.has_up)(lambda: send(unit, 0, y, z, x, "up", True))
        pl.when(at.has_down)(lambda: send(unit, 0, y, z, x, "down", True))
        send(unit, 1, y, z, x, "y", True)
        send(unit, 0, y, z, x, "x", True)
        pl.when(at.has_up)(lambda: send(unit, 1, y, z, x, "up", True))
        pl.when(at.has_down)(lambda: send(unit, 1, y, z, x, "down", True))
        send(unit, 0, y, z, x, "y", True)
        send(unit, 1, y, z, x, "x", True)

    def stage1(unit):
        from_z(unit, 0, 1, y)
        arrived(unit, 1, at.far_y, z, x)
        pl.when(at.has_up)(lambda: send(unit, 1, at.far_y, z, x, "up"))
        pl.when(at.has_down)(lambda: send(unit, 1, at.far_y, z, x, "down"))
        send(unit, 1, at.far_y, z, x, "x")
        from_z(unit, 1, 1, y)
        from_x(unit, 0)

    def stage2(unit):
        from_z(unit, 0, 2, y)
        from_z(unit, 1, 1, at.far_y)
        from_z(unit, 1, 2, y)
        from_x(unit, 1)

    def stage3(unit):
        from_z(unit, 0, 3, y)
        from_z(unit, 1, 2, at.far_y)
        from_z(unit, 1, 3, y)
        from_x(unit, 2)

    def stage4(unit):
        from_z(unit, 1, 3, at.far_y)
        from_x(unit, 3)
        own_copy(unit).wait()
        to_core(unit, 0).start()

    def stage5(unit):
        for zz in range(4):
            for xx in range(2):
                arrived(unit, 0, at.far_y, zz, xx)
        to_core(unit, 1).start()
        for zz in range(4):
            for yy in range(2):
                arrived(unit, 1, yy, zz, at.far_x)
        to_core(unit, 2).start()

    def stage6(unit):
        other = 1 - c
        await_bytes(whole_ref.at[unit, y, other, :, :, cut[0]], core_sem.at[unit, 0])
        await_bytes(whole_ref.at[unit, at.far_y, other, :, :, cut[0]], core_sem.at[unit, 1])
        await_bytes(whole_ref.at[unit, :, other, :, :, cut[1]], core_sem.at[unit, 2])
        for colour in range(2):
            rows = cut[colour]
            await_bytes(whole_ref.at[unit, :, c, :, :, rows], send_sem.at[unit, colour, 4])
            whole_x = whole_ref.at[unit, 0, c, :, 0, rows] if colour == 0 else None
            if colour == 0:
                await_bytes(whole_x, send_sem.at[unit, 0, 2])
                await_bytes(whole_ref.at[unit, 0, c, :, :, rows], send_sem.at[unit, 0, 3])
            else:
                await_bytes(whole_ref.at[unit, 0, c, :, :, rows], send_sem.at[unit, 1, 2])
                await_bytes(whole_ref.at[unit, 0, c, 0, 0, rows], send_sem.at[unit, 1, 3])
            for level in range(3):

                def ups(level=level):
                    if colour == 0:
                        ref = whole_ref.at[unit, 0, c, pl.ds(0, level + 1), 0, rows]
                    else:
                        ref = whole_ref.at[unit, :, c, pl.ds(0, level + 1), 0, rows]
                    return ref

                pl.when(z == level)(
                    lambda level=level: await_bytes(ups(level), send_sem.at[unit, colour, 0])
                )
                pl.when(z == 3 - level)(
                    lambda level=level: await_bytes(ups(level), send_sem.at[unit, colour, 1])
                )

    stages = (stage0, stage1, stage2, stage3, stage4, stage5, stage6)

    rows_all, width = x_ref.shape[1], x_ref.shape[2]
    half_rows = rows_all // 2
    scale = 1.0 / math.sqrt(HEAD)
    own_t = y * 2 + c

    def save_now(source, target):
        copy = pltpu.make_async_copy(source, target, save_sem.at[0])
        copy.start()
        copy.wait()

    peers = (("y", at.far_y * 2 + c), ("core", y * 2 + 1 - c), ("cross", at.far_y * 2 + 1 - c))

    def peer_copies(index):
        kind, t = peers[index]
        target = {"device_id": at.to[kind], "device_id_type": MESH_ID}
        return (
            pltpu.make_async_remote_copy(
                src_ref=params_ref,
                dst_ref=params_got.at[own_t],
                send_sem=peer_send.at[0, index],
                recv_sem=peer_recv.at[0, index],
                **target,
            ),
            pltpu.make_async_remote_copy(
                src_ref=x_ref.at[t],
                dst_ref=x_got.at[own_t],
                send_sem=peer_send.at[1, index],
                recv_sem=peer_recv.at[1, index],
                **target,
            ),
        )

    own_peer = (
        pltpu.make_async_copy(params_ref, params_got.at[own_t], peer_send.at[0, 3]),
        pltpu.make_async_copy(x_ref.at[own_t], x_got.at[own_t], peer_send.at[1, 3]),
    )
    for index in range(3):
        for copy in peer_copies(index):
            copy.start()
    for copy in own_peer:
        copy.start()

    def each(count, size, use):
        def one(step, carry):
            use(pl.ds(pl.multiple_of(step * size, size), size))
            return carry

        lax.fori_loop(0, count, one, 0)

    def tile_load(unit, t, slot):
        return pltpu.make_async_copy(whole_ref.at[unit, t // 2, t % 2], wb.at[slot], tile_sem.at[slot])

    def kept_copies(which, t):
        target = (10, 4, 1, 0)[which]
        copies = [
            pltpu.make_async_copy(cols.at[which, t], q_ref.at[target, t], kept_sem.at[which, t, 0])
        ]
        if which < 2:
            pairs = [(qkb.at[which, t], qk_ref.at[which, t]), (vb.at[which, t], v_ref.at[which, t])]
        else:
            pairs = [(slopeb.at[which - 2, t], slope_ref.at[which - 2, t])]
        for index, (source, target_ref) in enumerate(pairs):
            copies.append(
                pltpu.make_async_copy(source, target_ref, kept_sem.at[which, t, 1 + index])
            )
        return copies

    def do_spread(op):
        matrix = op["slot"]
        t, aux = op["t"], op["aux"]

        def multiply(rows):
            total[rows, :] = dot_plain(xb[rows, :], wb[matrix].reshape(C, WIDE))

        each(2, half_rows, multiply)
        quarter = rows_all // 4

        @pl.when(aux == 0)
        def _():
            def use(rows):
                first_rows[t, rows, :] = total[rows, width:]

            each(4, quarter, use)

        @pl.when((aux == 1) | (aux == 3))
        def _():
            def use(rows):
                qkb[(aux - 1) // 2, t, rows, :] = total[rows, :].astype(jnp.bfloat16)

            each(4, quarter, use)

        @pl.when((aux == 2) | (aux == 4))
        def _():
            def use(rows):
                vb[(aux - 2) // 2, t, rows, :] = total[rows, 0:width].astype(jnp.bfloat16)

            each(4, quarter, use)

        @pl.when((aux == 5) | (aux == 6))
        def _():
            half = aux - 5

            def use(rows):
                pre = total[rows, :] + hidden_bias[t, pl.ds(half, 1), :]
                below = 0.5 * (1.0 + lax.erf(pre * math.sqrt(0.5)))
                cols[2 + half, t, rows, :] = (pre * below).astype(jnp.bfloat16)
                density = jnp.exp(-0.5 * pre * pre) * (1.0 / math.sqrt(2.0 * math.pi))
                slopeb[half, t, rows, :] = (below + pre * density).astype(jnp.bfloat16)

            each(rows_all // 32, 32, use)
            for which in (2, 3):

                @pl.when(half == which - 2)
                def _(which=which):
                    for copy in kept_copies(which, t):
                        copy.start()

        @pl.when(aux == 7)
        def _():
            def use(rows):
                moved_ref[t, rows, :] = (total[rows, width:] + params_got[t, 12:13, :]).astype(
                    jnp.bfloat16
                )

            each(4, quarter, use)

    def do_collapse(op):
        def multiply(rows):
            stream[rows, :] += dot_rows(cols[op["aux"], op["t"], rows, :], wb[op["slot"]].reshape(C, WIDE))

        each(2, half_rows, multiply)

    def do_attention(op):
        block, t = op["aux"], op["t"]
        same = same_pixel(BLOCK)

        def write(place):
            for start in range(0, rows_all, BLOCK):
                here = slice(start, start + BLOCK)
                for head in range(width // HEAD):
                    low = head * HEAD
                    query = qkb[block, t, here, low : low + HEAD]
                    key = qkb[block, t, here, width + low : width + low + HEAD]
                    value = vb[block, t, here, low : low + HEAD]
                    probs = head_probs(query, key, same, scale).astype(jnp.bfloat16)
                    total[here, low : low + HEAD] = dot_plain(probs, value)

        write(0)
        for which in range(2):

            @pl.when(block == which)
            def _(which=which):
                own = slice(width, 2 * width) if which == 0 else slice(0, width)
                other = slice(0, width) if which == 0 else slice(width, 2 * width)

                def use(rows):
                    cols[which, t, rows, own] = total[rows, 0:width].astype(jnp.bfloat16)
                    cols[which, t, rows, other] = jnp.zeros((rows_all // 4, width), jnp.bfloat16)

                each(4, rows_all // 4, use)
                for copy in kept_copies(which, t):
                    copy.start()

    chunk = 4 * FRAMES

    def do_norm(op):
        layer = op["aux"]

        def use(rows):
            @pl.when(layer == 0)
            def _():
                for t in range(4):
                    stream[rows, t * width : (t + 1) * width] = first_rows[t, rows, :]

            values = stream[rows, :] + joined_ref[pl.ds(8 + layer, 1), :]
            stream[rows, :] = values
            centre = jnp.mean(values, axis=1, keepdims=True)
            offset = values - centre
            inverse = lax.rsqrt(jnp.mean(offset * offset, axis=1, keepdims=True) + 1e-05)
            normed = offset * inverse * joined_ref[pl.ds(1 + layer, 1), :]
            normed = normed + joined_ref[pl.ds(5 + layer, 1), :]
            added = jnp.where(layer < 2, position_ref[...], 0.0)
            normed = normed.reshape(chunk // FRAMES, FRAMES, C) + added[None]
            xb[rows, :] = normed.reshape(chunk, C).astype(jnp.bfloat16)

        each(rows_all // chunk, chunk, use)
        save_now(stream, stream_out_ref.at[layer])

    def do_turn(op):
        def one(step, carry):
            lanes = pl.ds(pl.multiple_of(step * 128, 128), 128)
            ptb[lanes, :] = xb[:, lanes].T
            return carry

        lax.fori_loop(0, C // 128, one, 0)
        save_now(ptb, pt_ref.at[op["aux"]])

    def do_last(op):
        def use(rows):
            xb[rows, :] = (stream[rows, :] + joined_ref[11:12, :]).astype(jnp.bfloat16)

        each(rows_all // chunk, chunk, use)

    def do_join(op):
        for index in range(3):
            for copy in peer_copies(index):
                copy.wait_recv()
        for copy in own_peer:
            copy.wait()
        for t in range(4):
            lanes = slice(t * width, (t + 1) * width)
            joined_ref[:, lanes] = params_got[t, 0:16, :]

            def use(rows, t=t, lanes=lanes):
                xb[rows, lanes] = x_got[t, rows, :]

            each(4, rows_all // 4, use)
            for half in range(2):
                for part in range(2):
                    row = 16 + 2 * half + part
                    hidden_bias[t, half : half + 1, part * width : (part + 1) * width] = params_got[
                        t, row : row + 1, :
                    ]

    works = (None, do_spread, do_collapse, do_attention, do_norm, do_turn, do_last, do_join)
    four = range(4)

    def spreads(unit, aux):
        return [(1, unit, t, aux) for t in four]

    def collapses(unit, aux):
        return [(2, unit, t, aux) for t in four]

    def attentions(aux):
        return [(3, None, t, aux) for t in four]

    count = len(stages)
    places = 2 * count
    plan = Plan(places)
    for ready, steps in {
        -4: [(7, None, 0, 0), (5, None, 0, 7)],
        1: spreads(1, 0) + [(4, None, 0, 0)] + spreads(0, 1) + spreads(1, 2),
        2: [(5, None, 0, 4)] + attentions(0),
        3: collapses(3, 0) + [(4, None, 0, 1)] + spreads(2, 3) + spreads(3, 4),
        4: [(5, None, 0, 3)] + attentions(1) + collapses(4, 1) + [(4, None, 0, 2)],
        5: [(5, None, 0, 1)] + spreads(5, 5),
        6: spreads(6, 6),
        7: collapses(7, 2),
        8: collapses(8, 3) + [(6, None, 0, 0)] + spreads(4, 7) + [(5, None, 0, 5)],
    }.items():
        plan.fill(ready + count - 1, steps)

    def do_step(place):
        op = plan.read(place)
        has_tile = (op["kind"] == 1) | (op["kind"] == 2)

        @pl.when(has_tile)
        def _():
            pl.when(op["fresh"] == 1)(lambda: tile_load(op["unit"], op["t"], op["slot"]).start())

            @pl.when(op["next"] > 0)
            def _():
                following = op["next"] - 1
                tile_load(following // 4, following % 4, 1 - op["slot"]).start()

            tile_load(op["unit"], op["t"], op["slot"]).wait()

        for kind in range(1, len(works)):

            @pl.when(op["kind"] == kind)
            def _(kind=kind):
                works[kind](op)

    def advance(now, carry):
        turn, place = now // count, now % count
        for number in range(count):
            unit = turn - number

            @pl.when((place == count - 1 - number) & (unit >= 0) & (unit < UNITS))
            def _(number=number, unit=unit):
                stages[number](unit)

        def two(step, carry):
            do_step(2 * now + step)
            return carry

        lax.fori_loop(0, 2, two, 0)
        return carry

    lax.fori_loop(0, (UNITS + count - 1) * count, advance, 0)
    for which in range(4):
        for t in range(4):
            for copy in kept_copies(which, t):
                copy.wait()
    for index in range(3):
        for copy in peer_copies(index):
            copy.wait_send()


def forward_all(shards, rows_in, params, position):
    units, share, wide = shards.shape
    rows, width = rows_in.shape[1], rows_in.shape[2]
    low = jnp.bfloat16
    anywhere, near = pl.BlockSpec(memory_space=pl.ANY), pl.BlockSpec(memory_space=pltpu.VMEM)
    return pl.pallas_call(
        forward_kernel,
        in_specs=[anywhere, anywhere, near, near],
        out_specs=[anywhere] * 7 + [near] * 2,
        out_shape=[
            jax.ShapeDtypeStruct((units, 2, 2, 4, 2, share, wide), low),
            jax.ShapeDtypeStruct((12, 4, rows, wide), low),
            jax.ShapeDtypeStruct((8, C, rows), low),
            jax.ShapeDtypeStruct((3, rows, C), jnp.float32),
            jax.ShapeDtypeStruct((2, 4, rows, wide), low),
            jax.ShapeDtypeStruct((2, 4, rows, width), low),
            jax.ShapeDtypeStruct((2, 4, rows, wide), low),
            jax.ShapeDtypeStruct((4, rows, width), low),
            jax.ShapeDtypeStruct((16, C), jnp.float32),
        ],
        scratch_shapes=[
            pltpu.VMEM((rows, C), jnp.float32),
            pltpu.VMEM((rows, C), low),
            pltpu.VMEM((C, rows), low),
            pltpu.VMEM((4, rows, width), low),
            pltpu.VMEM((4,) + params.shape, jnp.float32),
            pltpu.VMEM((4, 8, wide), jnp.float32),
            pltpu.VMEM((2, 4, rows, wide), low),
            pltpu.VMEM((2, 4, rows, width), low),
            pltpu.VMEM((4, 4, rows, wide), low),
            pltpu.VMEM((2, 4, rows, wide), low),
            pltpu.VMEM((4, rows, width), jnp.float32),
            pltpu.VMEM((rows, wide), jnp.float32),
            pltpu.VMEM((2, 4, 2, share, wide), low),
            pltpu.SemaphoreType.DMA((2,)),
            pltpu.SemaphoreType.DMA((1,)),
            pltpu.SemaphoreType.DMA((4, 4, 3)),
            pltpu.SemaphoreType.DMA((2, 4)),
            pltpu.SemaphoreType.DMA((2, 3)),
            pltpu.SemaphoreType.DMA((units,)),
            pltpu.SemaphoreType.DMA((units, 2, 5)),
            pltpu.SemaphoreType.DMA((units, 2, 2, 4, 2)),
            pltpu.SemaphoreType.DMA((units, 3)),
        ],
        compiler_params=pltpu.CompilerParams(
            collective_id=0, has_side_effects=True, vmem_limit_bytes=60 << 20
        ),
    )(shards, rows_in, params, position)


def backward_kernel(
    whole_ref,
    q_given,
    pt_given,
    streams_ref,
    qk_ref,
    v_ref,
    slope_ref,
    moved_ref,
    joined_ref,
    out_ref,
    q_ref,
    pt_ref,
    ptx_ref,
    qx_ref,
    got_ref,
    vec_ref,
    hidden_ref,
    p_buf,
    q_buf,
    dw,
    rya,
    rxa,
    rua,
    rda,
    rxb,
    rub,
    rdb,
    ryb,
    gs,
    gn,
    xb,
    ptb,
    wb,
    cb,
    av,
    datt,
    total,
    sb,
    ob,
    dn,
    load_sem,
    give_sem,
    take_sem,
    send_sem,
    recv_sem,
    tile_sem,
    aux_sem,
    route_sem,
    misc_sem,
    out_sem,
    peer_send,
    peer_recv,
):
    at = Place()
    z, x, y, c = at.z, at.x, at.y, at.c
    far_x, far_y = at.far_x, at.far_y
    share = out_ref.shape[1]
    row_a, row_b = pl.ds(0, ROWS_A), pl.ds(ROWS_A, share - ROWS_A)
    rows_all, width = got_ref.shape[1], got_ref.shape[2]
    half_rows = rows_all // 2
    count_p = pt_ref.shape[0]
    scale = 1.0 / math.sqrt(HEAD)
    own_t = y * 2 + c
    at.greet()

    def give_p(index, source=None):
        return pltpu.make_async_remote_copy(
            src_ref=pt_ref.at[index] if source is None else source,
            dst_ref=ptx_ref.at[index],
            send_sem=give_sem.at[index],
            recv_sem=take_sem.at[index],
            device_id=at.to["core"],
            device_id_type=MESH_ID,
        )

    def give_q(index, yy, source):
        return pltpu.make_async_remote_copy(
            src_ref=source,
            dst_ref=qx_ref.at[index, yy],
            send_sem=give_sem.at[count_p + 2 * index + yy],
            recv_sem=take_sem.at[count_p + 2 * index + yy],
            device_id=at.to["core"],
            device_id_type=MESH_ID,
        )

    def known_q(index, yy):
        source = moved_ref if index == 9 else q_ref.at[index]
        return give_q(index, yy, source.at[2 * yy + 1 - c])

    known = (0, 1, 4, 9, 10)
    known_p = (1, 5, 3, 4, 7)
    for index in known[:2]:
        for yy in range(2):
            known_q(index, yy).start()
    give_p(1).start()
    for index in known[2:]:
        for yy in range(2):
            known_q(index, yy).start()
    for index in known_p[1:]:
        give_p(index).start()
    moved_own = [
        pltpu.make_async_copy(
            moved_ref.at[2 * yy + c], q_ref.at[9, 2 * yy + c], misc_sem.at[yy]
        )
        for yy in range(2)
    ]
    for copy in moved_own:
        copy.start()

    def each(count, size, use):
        def one(step, carry):
            use(pl.ds(pl.multiple_of(step * size, size), size))
            return carry

        lax.fori_loop(0, count, one, 0)

    def aux_load(source, target, number):
        return pltpu.make_async_copy(source, target, aux_sem.at[number])

    def tile_load(unit, t, slot):
        return pltpu.make_async_copy(whole_ref.at[unit, t // 2, t % 2], wb.at[slot], tile_sem.at[slot])

    def route(source, index, t):
        yy = t // 2
        local = pltpu.make_async_copy(source, q_ref.at[index, t], route_sem.at[index, yy])

        def begin():
            pl.when(c == t % 2)(lambda: local.start())
            pl.when(c != t % 2)(lambda: give_q(index, yy, source).start())

        def wait():
            pl.when(c == t % 2)(lambda: local.wait())
            pl.when(c != t % 2)(lambda: give_q(index, yy, source).wait_send())

        return begin, wait

    chunk = 4 * FRAMES
    quarter = rows_all // 4

    def column_sum(row, values):
        vec_ref[pl.ds(row, 1), :] += jnp.sum(values, axis=0, keepdims=True)

    def do_spread(op):
        t, aux = op["t"], op["aux"]
        side = t % 2

        def slope_load():
            return aux_load(slope_ref.at[aux, t], cb.at[4], 0)

        def head_loads():
            return (
                aux_load(qk_ref.at[aux - 2, t], cb.at[4], 0),
                aux_load(v_ref.at[aux - 2, t], av, 1),
            )

        pl.when(aux < 2)(lambda: slope_load().start())

        @pl.when(aux >= 2)
        def _():
            for load in head_loads():
                load.start()

        def multiply(rows):
            total[rows, :] = dot_plain(xb[rows, :], wb[op["slot"]].reshape(C, WIDE))

        each(2, half_rows, multiply)

        @pl.when(aux < 2)
        def _():
            slope_load().wait()

            def use(rows):
                grad = total[rows, :] * cb[4, rows, :].astype(jnp.float32)
                hidden_ref[t, pl.ds(aux, 1), :] += jnp.sum(grad, axis=0, keepdims=True)
                cb[side, rows, :] = grad.astype(jnp.bfloat16)

            each(4, quarter, use)
            route(cb.at[side], 3 - aux, t)[0]()

        @pl.when(aux >= 2)
        def _():
            for load in head_loads():
                load.wait()

            for block in range(2):

                @pl.when(aux == 2 + block)
                def _(block=block):
                    low = width if block == 0 else 0

                    def use(rows):
                        datt[rows, :] = total[rows, low : low + width].astype(jnp.bfloat16)

                    each(4, quarter, use)

    def do_collapse(op):
        which, routed, t = op["aux"] % 5, op["aux"] // 5, op["t"]

        @pl.when(which == 4)
        def _():
            load = aux_load(moved_ref.at[t], cb.at[4], 0)
            load.start()
            load.wait()

        def multiply(rows):
            gn[rows, :] += dot_rows(cb[which, rows, :], wb[op["slot"]].reshape(C, WIDE))

        each(2, half_rows, multiply)
        pl.when(routed > 0)(lambda: route(cb.at[which], routed - 1, t)[1]())

    def do_attention(op):
        block, t = op["aux"], op["t"]
        side = t % 2
        same = same_pixel(BLOCK)
        for start in range(0, rows_all, BLOCK):
            here = slice(start, start + BLOCK)
            for head in range(width // HEAD):
                low = head * HEAD
                query = cb[4, here, low : low + HEAD]
                key = cb[4, here, width + low : width + low + HEAD]
                value = av[here, low : low + HEAD]
                grad = datt[here, low : low + HEAD]
                probs = head_probs(query, key, same, scale)
                grad_probs = dot_rows(grad, value)
                centred = jnp.sum(probs * grad_probs, axis=1, keepdims=True)
                grad_raw = (probs * (grad_probs - centred) * scale).astype(jnp.bfloat16)
                cb[side, here, low : low + HEAD] = dot_plain(grad_raw, key).astype(jnp.bfloat16)
                cb[side, here, width + low : width + low + HEAD] = dot_first(
                    grad_raw, query
                ).astype(jnp.bfloat16)
                cb[2 + side, here, low : low + HEAD] = dot_first(
                    probs.astype(jnp.bfloat16), grad
                ).astype(jnp.bfloat16)
        route(cb.at[side], 7 - 2 * block, t)[0]()
        route(cb.at[2 + side], 8 - 2 * block, t)[0]()

    def do_layer(op):
        layer = op["aux"]

        def load(step):
            rows = pl.ds(pl.multiple_of(step * chunk, chunk), chunk)
            return pltpu.make_async_copy(
                streams_ref.at[layer, rows], sb.at[step % 2], misc_sem.at[3 + step % 2]
            )

        def one(step, carry):
            pl.when(step + 1 < rows_all // chunk)(lambda: load(step + 1).start())
            load(step).wait()
            rows = pl.ds(pl.multiple_of(step * chunk, chunk), chunk)
            values = sb[step % 2]
            centre = jnp.mean(values, axis=1, keepdims=True)
            offset = values - centre
            inverse = lax.rsqrt(jnp.mean(offset * offset, axis=1, keepdims=True) + 1e-05)
            hat = offset * inverse
            grad = gn[rows, :]
            column_sum(layer, grad * hat)
            column_sum(3 + layer, grad)
            scaled = grad * joined_ref[pl.ds(1 + layer, 1), :]
            first = jnp.mean(scaled, axis=1, keepdims=True)
            second = jnp.mean(scaled * hat, axis=1, keepdims=True)
            result = gs[rows, :] + inverse * (scaled - first - hat * second)
            gs[rows, :] = result
            column_sum(6 + layer, result)
            xb[rows, :] = result.astype(jnp.bfloat16)
            gn[rows, :] = jnp.zeros((chunk, C), jnp.float32)
            return carry

        load(0).start()
        lax.fori_loop(0, rows_all // chunk, one, 0)

    def do_turn(op):
        index = op["aux"]

        def one(step, carry):
            lanes = pl.ds(pl.multiple_of(step * 128, 128), 128)
            ptb[lanes, :] = xb[:, lanes].T
            return carry

        lax.fori_loop(0, C // 128, one, 0)
        local = pltpu.make_async_copy(ptb, pt_ref.at[index], misc_sem.at[2])
        local.start()
        give_p(index, ptb).start()
        local.wait()
        give_p(index, ptb).wait_send()

    def do_first(op):
        def use(rows):
            values = gn[rows, :]
            gs[rows, :] = values
            column_sum(9, values)
            xb[rows, :] = values.astype(jnp.bfloat16)
            gn[rows, :] = jnp.zeros((chunk, C), jnp.float32)

        each(rows_all // chunk, chunk, use)

    def do_place(op):
        t = op["t"]
        side = t % 2
        for block in range(4):

            @pl.when(t == block)
            def _(block=block):
                def use(rows):
                    cb[side, rows, 0:width] = jnp.zeros((quarter, width), jnp.bfloat16)
                    cb[side, rows, width:] = xb[rows, block * width : (block + 1) * width]

                each(4, quarter, use)

        route(cb.at[side], 11, t)[0]()

    peers = (("y", far_y * 2 + c), ("core", y * 2 + 1 - c), ("cross", far_y * 2 + 1 - c))

    def peer_copy(index):
        kind, t = peers[index]
        return pltpu.make_async_remote_copy(
            src_ref=dn.at[t],
            dst_ref=got_ref.at[own_t],
            send_sem=peer_send.at[index],
            recv_sem=peer_recv.at[index],
            device_id=at.to[kind],
            device_id_type=MESH_ID,
        )

    own_peer = pltpu.make_async_copy(dn.at[own_t], got_ref.at[own_t], peer_send.at[3])

    def do_send(op):
        for t in range(4):

            def use(rows, t=t):
                dn[t, rows, :] = gn[rows, t * width : (t + 1) * width].astype(jnp.bfloat16)

            each(4, quarter, use)
        for index in range(3):
            peer_copy(index).start()
        own_peer.start()

    def do_moved(op):
        for copy in moved_own:
            copy.wait()

    works = (
        None,
        do_spread,
        do_collapse,
        do_attention,
        do_layer,
        do_turn,
        do_first,
        do_place,
        do_send,
        do_moved,
    )
    four = range(4)

    def feed(half):
        steps = []
        for t in four:
            steps += [(1, 7 + half, t, half), (2, 5 + half, t, t % 2 + 5 * (4 - half))]
        return steps

    def heads(block, t):
        return [
            (1, 3 + block, t, 2 + block),
            (3, None, t, block),
            (2, 2 * block, t, t % 2 + 5 * (8 - 2 * block)),
            (2, 2 * block + 1, t, 2 + t % 2 + 5 * (9 - 2 * block)),
        ]

    def inputs(t):
        return [(7, None, t, 0), (2, 1, t, t % 2 + 5 * 12)]

    stage_count = 6
    plan = Plan(2 * stage_count)
    for turn, steps in {
        -1: [(2, 4, t, 4) for t in four] + [(6, None, 0, 0), (5, None, 0, 0)],
        0: feed(1),
        1: feed(0),
        2: [(4, None, 0, 2), (5, None, 0, 2)] + heads(1, 0) + [(9, None, 0, 0)],
        3: heads(1, 1) + heads(1, 2),
        4: heads(1, 3),
        5: [(4, None, 0, 1), (5, None, 0, 6)] + heads(0, 0),
        6: heads(0, 1) + heads(0, 2) + heads(0, 3),
        7: [(4, None, 0, 0)] + inputs(0) + inputs(1) + inputs(2) + inputs(3),
        8: [(8, None, 0, 0)],
    }.items():
        plan.fill(turn + 1, steps)

    def do_step(place):
        op = plan.read(place)
        has_tile = (op["kind"] == 1) | (op["kind"] == 2)

        @pl.when(has_tile)
        def _():
            pl.when(op["fresh"] == 1)(lambda: tile_load(op["unit"], op["t"], op["slot"]).start())

            @pl.when(op["next"] > 0)
            def _():
                following = op["next"] - 1
                tile_load(following // 4, following % 4, 1 - op["slot"]).start()

            tile_load(op["unit"], op["t"], op["slot"]).wait()

        for kind in range(1, len(works)):

            @pl.when(op["kind"] == kind)
            def _(kind=kind):
                works[kind](op)

    vec_ref[...] = jnp.zeros_like(vec_ref)
    hidden_ref[...] = jnp.zeros_like(hidden_ref)

    def clear(rows):
        gn[rows, :] = jnp.zeros((chunk, C), jnp.float32)
        cb[2, rows, :] = jnp.zeros((chunk, WIDE), jnp.bfloat16)
        cb[3, rows, :] = jnp.zeros((chunk, WIDE), jnp.bfloat16)

    each(rows_all // chunk, chunk, clear)

    names = ["ya0", "ya1", "xa", "ua0", "ua1", "ua2", "da0", "da1", "da2"]
    names += ["xb0", "xb1", "ub0", "ub1", "ub2", "db0", "db1", "db2", "yb"]
    number = {name: index for index, name in enumerate(names)}

    class Slot:
        def __init__(self, turn):
            self.d, self.r = turn % SLOTS_IN_FLIGHT, turn % SLOTS_RECEIVED

    def copy(slot, name, src, dst, kind, shift=0):
        index = number[name] + shift
        return pltpu.make_async_remote_copy(
            src_ref=src,
            dst_ref=dst,
            send_sem=send_sem.at[slot.d, index],
            recv_sem=recv_sem.at[slot.r, index],
            device_id=at.to[kind],
            device_id_type=MESH_ID,
        )

    def ya(slot, part):
        side = far_x if part == 0 else x
        return copy(
            slot, f"ya{part}", dw.at[slot.d, far_y, :, side, row_a], rya.at[slot.r, part], "y"
        )

    def xa(slot):
        return copy(slot, "xa", dw.at[slot.d, y, :, far_x, row_a], rxa.at[slot.r], "x")

    def xb_copy(slot, part):
        return copy(
            slot, f"xb{part}", dw.at[slot.d, part, :, far_x, row_b], rxb.at[slot.r, part], "x"
        )

    def yb(slot):
        return copy(slot, "yb", dw.at[slot.d, far_y, z, x, row_b], ryb.at[slot.r], "y")

    def up(slot, colour, d):
        if colour == 0:
            return copy(
                slot, "ua0", dw.at[slot.d, y, d, x, row_a], rua.at[slot.r, d - 1], "up", d - 1
            )
        return copy(slot, "ub0", dw.at[slot.d, :, d, x, row_b], rub.at[slot.r, d - 1], "up", d - 1)

    def down(slot, colour, d):
        if colour == 0:
            return copy(slot, "da0", dw.at[slot.d, y, d, x, row_a], rda.at[slot.r, d], "down", d)
        return copy(slot, "db0", dw.at[slot.d, :, d, x, row_b], rdb.at[slot.r, d], "down", d)

    def add(place, got):
        total = place[...].astype(jnp.float32) + got[...].astype(jnp.float32)
        place[...] = total.astype(jnp.bfloat16)

    def products(slot, p_index, q_index, more):
        loads = [
            pltpu.make_async_copy(pt_ref.at[p_index], p_buf.at[0], load_sem.at[0]),
            pltpu.make_async_copy(ptx_ref.at[p_index], p_buf.at[1], load_sem.at[1]),
        ]
        for yy in range(2):
            loads += [
                pltpu.make_async_copy(
                    q_ref.at[q_index, 2 * yy + c], q_buf.at[0, yy], load_sem.at[2 + yy]
                ),
                pltpu.make_async_copy(
                    qx_ref.at[q_index, yy], q_buf.at[1, yy], load_sem.at[4 + yy]
                ),
            ]
        for load in loads:
            load.start()
        for load in loads:
            load.wait()

        def one(step, carry):
            side, zz = step // 4, step % 4
            yy = jnp.where(side == 0, far_y, y)
            rows = pl.ds(pl.multiple_of(zz * 2 * share, 2 * share), 2 * share)
            result = dot_plain(p_buf[0, rows, :], q_buf[0, yy]) + dot_plain(
                p_buf[1, rows, :], q_buf[1, yy]
            )
            result = result.reshape(2, share, WIDE)
            earlier = dw[slot.d, yy, zz].astype(jnp.float32)
            result = result + jnp.where(more == 1, earlier, 0.0)
            dw[slot.d, yy, zz] = result.astype(jnp.bfloat16)
            return carry

        lax.fori_loop(0, 8, one, 0)

    def take_p(index):
        await_bytes(ptx_ref.at[index], take_sem.at[index])

    def take_q(index):
        for yy in range(2):
            await_bytes(qx_ref.at[index, yy], take_sem.at[count_p + 2 * index + yy])

    def stage0(turn):
        slot = Slot(turn)
        p_index = (turn + turn // 5) // 2

        @pl.when((turn + turn // 5) % 2 == 0)
        def _():
            take_p(p_index)

        take_q(turn)
        mixed = (turn >= 4).astype(jnp.int32) * (1 - turn % 2)
        extra = (turn - 4) // 2

        @pl.when(mixed == 1)
        def _():
            take_p(5 + extra)
            take_q(UNITS + extra)

        def one_pass(more, carry):
            products(
                slot,
                jnp.where(more == 1, 5 + extra, p_index),
                jnp.where(more == 1, UNITS + extra, turn),
                more,
            )
            return carry

        lax.fori_loop(0, 1 + mixed, one_pass, 0)

        ya(slot, 0).start()
        xb_copy(slot, 0).start()
        ya(slot, 1).start()
        xb_copy(slot, 1).start()

    def z_step(slot, colour, step):
        @pl.when(z <= step - 1)
        def _():
            d = z + 4 - step

            @pl.when(z >= 1)
            def _():
                up(slot, colour, d).wait_recv()
                if colour == 0:
                    add(dw.at[slot.d, y, d, x, row_a], rua.at[slot.r, d - 1])
                else:
                    add(dw.at[slot.d, 0, d, x, row_b], rub.at[slot.r, d - 1, 0])
                    add(dw.at[slot.d, 1, d, x, row_b], rub.at[slot.r, d - 1, 1])

            up(slot, colour, d).start()

        @pl.when(3 - z <= step - 1)
        def _():
            d = z - 4 + step

            @pl.when(z <= 2)
            def _():
                down(slot, colour, d).wait_recv()
                if colour == 0:
                    add(dw.at[slot.d, y, d, x, row_a], rda.at[slot.r, d])
                else:
                    add(dw.at[slot.d, 0, d, x, row_b], rdb.at[slot.r, d, 0])
                    add(dw.at[slot.d, 1, d, x, row_b], rdb.at[slot.r, d, 1])

            down(slot, colour, d).start()

    def stage1(turn):
        slot = Slot(turn)
        for part in range(2):
            xb_copy(slot, part).wait_recv()
            for zz in range(4):
                add(dw.at[slot.d, part, zz, x, row_b], rxb.at[slot.r, part, zz])
        z_step(slot, 1, 1)
        ya(slot, 0).wait_recv()
        for zz in range(4):
            add(dw.at[slot.d, y, zz, far_x, row_a], rya.at[slot.r, 0, zz])
        xa(slot).start()
        ya(slot, 1).wait_recv()
        for zz in range(4):
            add(dw.at[slot.d, y, zz, x, row_a], rya.at[slot.r, 1, zz])

    def stage2(turn):
        slot = Slot(turn)
        z_step(slot, 1, 2)
        xa(slot).wait_recv()
        for zz in range(4):
            add(dw.at[slot.d, y, zz, x, row_a], rxa.at[slot.r, zz])
        z_step(slot, 0, 1)

    def stage3(turn):
        slot = Slot(turn)
        z_step(slot, 1, 3)
        z_step(slot, 0, 2)

    def stage4(turn):
        slot = Slot(turn)
        z_step(slot, 0, 3)

        @pl.when(z >= 1)
        def _():
            up(slot, 1, z).wait_recv()
            for yy in range(2):
                add(dw.at[slot.d, yy, z, x, row_b], rub.at[slot.r, z - 1, yy])

        @pl.when(z <= 2)
        def _():
            down(slot, 1, z).wait_recv()
            for yy in range(2):
                add(dw.at[slot.d, yy, z, x, row_b], rdb.at[slot.r, z, yy])

        yb(slot).start()

    def out_copy(turn):
        return pltpu.make_async_copy(ob.at[turn % 2], out_ref.at[turn], out_sem.at[turn % 2])

    def stage5(turn):
        slot = Slot(turn)
        side = turn % 2
        pl.when(turn >= 2)(lambda: out_copy(turn - 2).wait())
        ob[side, row_a, :] = dw[slot.d, y, z, x, row_a, :].astype(jnp.float32)

        @pl.when(z >= 1)
        def _():
            up(slot, 0, z).wait_recv()
            ob[side, row_a, :] += rua[slot.r, z - 1].astype(jnp.float32)

        @pl.when(z <= 2)
        def _():
            down(slot, 0, z).wait_recv()
            ob[side, row_a, :] += rda[slot.r, z].astype(jnp.float32)

        yb(slot).wait_recv()
        ob[side, row_b, :] = dw[slot.d, y, z, x, row_b, :].astype(jnp.float32) + ryb[
            slot.r
        ].astype(jnp.float32)
        out_copy(turn).start()

        ya(slot, 0).wait_send()
        ya(slot, 1).wait_send()
        xa(slot).wait_send()
        xb_copy(slot, 0).wait_send()
        xb_copy(slot, 1).wait_send()
        yb(slot).wait_send()
        for colour in range(2):
            for step in range(1, 4):

                @pl.when(z <= step - 1)
                def _(colour=colour, step=step):
                    up(slot, colour, z + 4 - step).wait_send()

                @pl.when(3 - z <= step - 1)
                def _(colour=colour, step=step):
                    down(slot, colour, z - 4 + step).wait_send()

    stages = (stage0, stage1, stage2, stage3, stage4, stage5)

    def advance(now, carry):
        for step in range(stage_count):
            turn = now // stage_count - 1 - step

            @pl.when((now % stage_count == step) & (turn >= 0) & (turn < UNITS))
            def _(step=step, turn=turn):
                stages[step](turn)

        def two(step, carry):
            do_step(2 * now + step)
            return carry

        lax.fori_loop(0, 2, two, 0)
        return carry

    lax.fori_loop(0, (UNITS + stage_count) * stage_count, advance, 0)
    out_copy(UNITS - 2).wait()
    out_copy(UNITS - 1).wait()
    for index in range(3):
        peer_copy(index).wait()
    own_peer.wait()
    for index in known:
        for yy in range(2):
            known_q(index, yy).wait_send()
    for index in known_p:
        give_p(index).wait_send()


def backward_all(whole, q_all, pt_all, streams, qk, values, slopes, moved_part, joined):
    share = whole.shape[5]
    count_p, unused, rows = pt_all.shape
    width = values.shape[3]
    low = jnp.bfloat16
    slots, taken, rest = SLOTS_IN_FLIGHT, SLOTS_RECEIVED, share - ROWS_A
    anywhere, near = pl.BlockSpec(memory_space=pl.ANY), pl.BlockSpec(memory_space=pltpu.VMEM)
    return pl.pallas_call(
        backward_kernel,
        in_specs=[anywhere] * 8 + [near],
        out_specs=[anywhere] * 6 + [near] * 2,
        out_shape=[
            jax.ShapeDtypeStruct((UNITS, share, WIDE), jnp.float32),
            jax.ShapeDtypeStruct(q_all.shape, low),
            jax.ShapeDtypeStruct(pt_all.shape, low),
            jax.ShapeDtypeStruct(pt_all.shape, low),
            jax.ShapeDtypeStruct((q_all.shape[0], 2, rows, WIDE), low),
            jax.ShapeDtypeStruct((4, rows, width), low),
            jax.ShapeDtypeStruct((16, C), jnp.float32),
            jax.ShapeDtypeStruct((4, 8, WIDE), jnp.float32),
        ],
        input_output_aliases={1: 1, 2: 2},
        scratch_shapes=[
            pltpu.VMEM((2, C, rows), low),
            pltpu.VMEM((2, 2, rows, WIDE), low),
            pltpu.VMEM((slots, 2, 4, 2, share, WIDE), low),
            pltpu.VMEM((taken, 2, 4, ROWS_A, WIDE), low),
            pltpu.VMEM((taken, 4, ROWS_A, WIDE), low),
            pltpu.VMEM((taken, 3, ROWS_A, WIDE), low),
            pltpu.VMEM((taken, 3, ROWS_A, WIDE), low),
            pltpu.VMEM((taken, 2, 4, rest, WIDE), low),
            pltpu.VMEM((taken, 3, 2, rest, WIDE), low),
            pltpu.VMEM((taken, 3, 2, rest, WIDE), low),
            pltpu.VMEM((taken, rest, WIDE), low),
            pltpu.VMEM((rows, C), jnp.float32),
            pltpu.VMEM((rows, C), jnp.float32),
            pltpu.VMEM((rows, C), low),
            pltpu.VMEM((C, rows), low),
            pltpu.VMEM((2, 4, 2, share, WIDE), low),
            pltpu.VMEM((5, rows, WIDE), low),
            pltpu.VMEM((rows, width), low),
            pltpu.VMEM((rows, width), low),
            pltpu.VMEM((rows, WIDE), jnp.float32),
            pltpu.VMEM((2, 4 * FRAMES, C), jnp.float32),
            pltpu.VMEM((2, share, WIDE), jnp.float32),
            pltpu.VMEM((4, rows, width), low),
            pltpu.SemaphoreType.DMA((6,)),
            pltpu.SemaphoreType.DMA((32,)),
            pltpu.SemaphoreType.DMA((32,)),
            pltpu.SemaphoreType.DMA((slots, 18)),
            pltpu.SemaphoreType.DMA((taken, 18)),
            pltpu.SemaphoreType.DMA((2,)),
            pltpu.SemaphoreType.DMA((4,)),
            pltpu.SemaphoreType.DMA((12, 2)),
            pltpu.SemaphoreType.DMA((5,)),
            pltpu.SemaphoreType.DMA((2,)),
            pltpu.SemaphoreType.DMA((4,)),
            pltpu.SemaphoreType.DMA((3,)),
        ],
        compiler_params=pltpu.CompilerParams(
            collective_id=1, has_side_effects=True, vmem_limit_bytes=63 << 20
        ),
    )(whole, q_all, pt_all, streams, qk, values, slopes, moved_part, joined)


def gather_plain(shards):
    units, share, wide = shards.shape
    whole = lax.all_gather(shards, MIXED, axis=1, tiled=True)
    return whole.reshape(units, lax.axis_size("tensor"), C, wide)


def reduce_plain(turned, parts):
    reduced = []
    for turn in range(UNITS):
        pairs = [(turned[(turn + turn // 5) // 2], parts[turn])]
        if turn in (4, 6, 8):
            extra = (turn - 4) // 2
            pairs.append((turned[5 + extra], parts[UNITS + extra]))
        whole = sum(
            jnp.einsum("kr,trn->tkn", left, right, preferred_element_type=jnp.float32)
            for left, right in pairs
        )
        whole = whole.astype(jnp.bfloat16).reshape(-1, whole.shape[2])
        reduced.append(
            lax.psum_scatter(whole, MIXED, scatter_dimension=0, tiled=True).astype(jnp.float32)
        )
    return jnp.stack(reduced, 0)


def by_pixels(values, tensor_size):
    slots, frames, width, pixels = values.shape
    own = pixels // tensor_size
    return jnp.transpose(values, (3, 0, 1, 2)).reshape(tensor_size, own * slots * frames, width)


def exchange(parts):
    return lax.all_to_all(parts, "tensor", 0, 0, tiled=True)


def back_to_channels(arrived, slots, pixels):
    width = arrived.shape[2]
    return jnp.transpose(arrived.reshape(pixels, slots, FRAMES, width), (1, 2, 3, 0))


def body(
    by_kernel,
    latent,
    clip_flags,
    cotangent,
    norm_gain,
    norm_shift,
    channel_bias,
    hidden_bias,
    weight_in,
    weight_qkv,
    weight_out,
    weight_up,
    weight_down,
    weight_proj,
):
    tensor_size = lax.axis_size("tensor")
    slots, frames, width, pixels = latent.shape
    share = weight_in.shape[0]
    hidden_width = hidden_bias.shape[0]
    flags = (clip_flags > 0)[:, None, None, None]

    wide = 2 * width

    shards = []
    side = jnp.concatenate
    for block in range(2):
        shards.append(weight_qkv[block, :, :2].reshape(share, wide))
        other = weight_in if block == 0 else weight_out[0].T
        shards.append(side([weight_qkv[block, :, 2], other], 1))
    shards.append(side([weight_out[1].T, weight_proj], 1))
    shards += [weight_up[:, :wide], weight_up[:, wide:]]
    down_turned = weight_down.T
    shards += [down_turned[:, :wide], down_turned[:, wide:]]
    shards = jnp.stack(shards, 0)
    params = jnp.zeros((24, width), jnp.float32)
    params = params.at[:13].set(side([norm_gain, norm_shift, channel_bias], 0))
    params = params.at[16:20].set(hidden_bias.reshape(4, width))

    start = latent.astype(jnp.float32)
    cot = cotangent.astype(jnp.float32)
    group_width = C // GROUPS
    grouped = start.reshape(slots, frames, width // group_width, group_width, pixels)
    group_centre = jnp.mean(grouped, axis=(1, 3, 4), keepdims=True)
    offset = grouped - group_centre
    group_inverse = lax.rsqrt(jnp.mean(offset * offset, axis=(1, 3, 4), keepdims=True) + 1e-06)
    group_hat = (offset * group_inverse).reshape(start.shape)
    normed = group_hat * norm_gain[0][:, None] + norm_shift[0][:, None]
    sent = by_pixels(normed.astype(jnp.bfloat16), tensor_size)
    rows = sent.shape[1]

    grad_moved_local = jnp.where(flags, cot, 0.0)
    bias_moved = jnp.sum(grad_moved_local, axis=(0, 1, 3))
    grad_moved = exchange(by_pixels(grad_moved_local.astype(jnp.bfloat16), tensor_size))

    empty = jnp.zeros((tensor_size, rows, width), jnp.bfloat16)
    moved_part = side([empty, grad_moved], 2)
    if by_kernel:
        whole, q_all, pt_all, streams, qk_all, v_all, slopes, moved, joined = forward_all(
            shards, sent, params, make_positions()
        )
        gains = joined[:4]
        reduced, q_all, pt_all, unused, unused, arrived_grad, sums, hidden_sums = backward_all(
            whole, q_all, pt_all, streams, qk_all, v_all, slopes, moved_part, joined
        )
        vectors = sums[:10]
        hidden_grad = hidden_sums[:, :2].reshape(tensor_size, 2 * wide)
    else:
        arrived = exchange(sent)
        inputs_in = jnp.transpose(arrived, (1, 0, 2)).reshape(rows, C)
        packed = lax.all_gather(params, "tensor", axis=0, tiled=False)
        joined = jnp.transpose(packed[:, :13], (1, 0, 2)).reshape(13, C)
        gains, shifts, biases = joined[:4], joined[4:8], joined[8:]
        hidden_full = packed[:, 16:20].reshape(tensor_size, 2 * wide)
        whole = gather_plain(shards)
        full_qk = (whole[0], whole[2])
        full_v = (whole[1, :, :, :width], whole[3, :, :, :width])
        full_in = whole[1, :, :, width:]
        full_out = (whole[3, :, :, width:], whole[4, :, :, :width])
        full_proj = whole[4, :, :, width:]
        full_up = (whole[5], whole[6])
        full_down = (whole[7], whole[8])

        def join(parts):
            return jnp.transpose(parts, (1, 0, 2)).reshape(rows, parts.shape[0] * parts.shape[2])

        stream = join(spread(inputs_in, full_in)) + biases[0]
        position = jnp.tile(make_positions(), (rows // FRAMES, 1))
        kept = []
        for block in range(2):
            hat, inverse = layer_stats(stream)
            lifted = (hat * gains[1 + block] + shifts[1 + block] + position).astype(jnp.bfloat16)
            qk = spread(lifted, full_qk[block]).astype(jnp.bfloat16)
            values = spread(lifted, full_v[block]).astype(jnp.bfloat16)
            attended = attend(qk, values)
            stream = stream + collapse(attended, full_out[block]) + biases[1 + block]
            kept.append((hat, inverse, lifted.T, qk, values, attended))
        hat_feed, inverse_feed = layer_stats(stream)
        inputs_up = (hat_feed * gains[3] + shifts[3]).astype(jnp.bfloat16)
        pre_act = [
            spread(inputs_up, full_up[half])
            + hidden_full[:, None, half * wide : half * wide + wide]
            for half in range(2)
        ]
        slopes = [
            jax.vjp(partial(jax.nn.gelu, approximate=False), pre)[1](jnp.ones_like(pre))[0]
            for pre in pre_act
        ]
        hidden = [jax.nn.gelu(pre, approximate=False).astype(jnp.bfloat16) for pre in pre_act]
        stream = stream + collapse(hidden[0], full_down[0]) + collapse(hidden[1], full_down[1])
        stream = stream + biases[3]
        inputs_proj = stream.astype(jnp.bfloat16)
        moved = spread(inputs_proj, full_proj) + biases[4].reshape(tensor_size, 1, width)
        moved = moved.astype(jnp.bfloat16)

        bias_grads = [None] * 4
        gain_grads = [None] * 3
        shift_grads = [None] * 3
        turned, parts = [None] * 8, [None] * 12
        turned[1], turned[5], turned[7] = inputs_up.T, inputs_proj.T, inputs_in.T
        parts[0], parts[1] = hidden[1], hidden[0]
        parts[9] = moved_part
        grad_stream = collapse(grad_moved, full_proj)
        bias_grads[3] = jnp.sum(grad_stream, 0)
        grad_low = grad_stream.astype(jnp.bfloat16)
        turned[0] = grad_low.T
        hidden_grads = [None, None]
        grad_normed = 0.0
        for half in (1, 0):
            grad_hidden = spread(grad_low, full_down[half])
            grad_pre = grad_hidden * slopes[half]
            hidden_grads[half] = jnp.sum(grad_pre, 1)
            parts[3 - half] = grad_pre.astype(jnp.bfloat16)
            grad_normed = grad_normed + collapse(parts[3 - half], full_up[half])
        hidden_grad = side(hidden_grads, 1)
        grad_layer, gain_grads[2], shift_grads[2] = layer_back(
            grad_normed, hat_feed, inverse_feed, gains[3]
        )
        grad_stream = grad_stream + grad_layer
        for block in (1, 0):
            hat, inverse, lifted_turned, qk, values, attended = kept[block]
            bias_grads[1 + block] = jnp.sum(grad_stream, 0)
            grad_low = grad_stream.astype(jnp.bfloat16)
            turned[2 if block == 1 else 6] = grad_low.T
            pair = [attended, empty] if block == 1 else [empty, attended]
            parts[4 if block == 1 else 10] = side(pair, 2)
            grad_attended = spread(grad_low, full_out[block]).astype(jnp.bfloat16)
            grad_qk, grad_values = attend_back(qk, values, grad_attended)
            turned[3 if block == 1 else 4] = lifted_turned
            parts[6 if block == 1 else 8] = side([grad_values, empty], 2)
            parts[5 if block == 1 else 7] = grad_qk
            grad_lifted = collapse(grad_qk, full_qk[block]) + collapse(grad_values, full_v[block])
            grad_layer, gain_grads[block], shift_grads[block] = layer_back(
                grad_lifted, hat, inverse, gains[1 + block]
            )
            grad_stream = grad_stream + grad_layer
        bias_grads[0] = jnp.sum(grad_stream, 0)
        grad_low = grad_stream.astype(jnp.bfloat16)
        grad_low_parts = jnp.transpose(grad_low.reshape(rows, tensor_size, width), (1, 0, 2))
        parts[11] = side([empty, grad_low_parts], 2)
        turned, parts = jnp.stack(turned, 0), jnp.stack(parts, 0)
        reduced = reduce_plain(turned, parts)
        grad_normed = collapse(grad_low_parts, full_in).astype(jnp.bfloat16)
        grad_normed = jnp.transpose(grad_normed.reshape(rows, tensor_size, width), (1, 0, 2))
        arrived_grad = exchange(grad_normed)
        vectors = jnp.stack(gain_grads + shift_grads + bias_grads, 0)

    moved_local = back_to_channels(exchange(moved), slots, pixels).astype(jnp.float32)
    output = jnp.where(flags, start + moved_local, start).astype(jnp.bfloat16)

    qkv_grads = [
        side([reduced[7 - 2 * block], reduced[8 - 2 * block, :, :width]], 1).reshape(share, 3, width)
        for block in range(2)
    ]
    out_grads = [reduced[6, :, width:].T, reduced[4, :, :width].T]
    in_grad, proj_grad = reduced[8, :, width:], reduced[4, :, width:]
    up_grad = side([reduced[3], reduced[2]], 1)
    down_grad = side([reduced[1], reduced[0]], 1)
    grad_normed = back_to_channels(arrived_grad, slots, pixels).astype(jnp.float32)
    scaled = grad_normed * norm_gain[0][:, None]
    scaled_groups = scaled.reshape(grouped.shape)
    hat_groups = group_hat.reshape(grouped.shape)
    first = jnp.mean(scaled_groups, axis=(1, 3, 4), keepdims=True)
    second = jnp.mean(scaled_groups * hat_groups, axis=(1, 3, 4), keepdims=True)
    grad_group = group_inverse * (scaled_groups - first - hat_groups * second)
    latent_grad = cot + grad_group.reshape(start.shape)
    group_gain_grad = jnp.sum(grad_normed * group_hat, axis=(0, 1, 3))
    group_shift_grad = jnp.sum(grad_normed, axis=(0, 1, 3))

    vectors = jnp.transpose(vectors.reshape(10, tensor_size, width), (1, 0, 2))
    vectors = jnp.concatenate([vectors.reshape(tensor_size, 10 * width), hidden_grad], 1)
    vectors = lax.psum_scatter(vectors, "tensor", scatter_dimension=0, tiled=False)
    sums = lax.psum(
        jnp.concatenate([vectors, group_gain_grad, group_shift_grad, bias_moved]), "dp"
    )
    channel_sums = sums[: 10 * width].reshape(10, width)
    hidden_bias_grad = sums[10 * width : 10 * width + hidden_width]
    local_sums = sums[10 * width + hidden_width :].reshape(3, width)
    gain_grad = jnp.concatenate([local_sums[0:1], channel_sums[0:3]], 0)
    shift_grad = jnp.concatenate([local_sums[1:2], channel_sums[3:6]], 0)
    channel_bias_grad = jnp.concatenate([channel_sums[6:10], local_sums[2:3]], 0)
    return (
        output,
        latent_grad,
        gain_grad,
        shift_grad,
        channel_bias_grad,
        hidden_bias_grad,
        in_grad,
        jnp.stack(qkv_grads, 0),
        jnp.stack(out_grads, 0),
        up_grad,
        down_grad.T,
        proj_grad,
    )


def solution(mesh):
    placed = (
        P("dp", None, "tensor", None),
        P("dp"),
        P("dp", None, "tensor", None),
        P(None, "tensor"),
        P(None, "tensor"),
        P(None, "tensor"),
        P("tensor"),
        P("dp", "tensor"),
        P(None, "dp", None, "tensor"),
        P(None, "tensor", "dp"),
        P("dp", "tensor"),
        P("tensor", "dp"),
        P("dp", "tensor"),
    )
    return jax.shard_map(
        partial(body, tuple(mesh.shape[name] for name in ("dp", "tensor")) == (8, 4)),
        mesh=mesh,
        in_specs=placed,
        out_specs=(
            P("dp", None, "tensor", None),
            P("dp", None, "tensor", None),
            P(None, "tensor"),
            P(None, "tensor"),
            P(None, "tensor"),
            P("tensor"),
            P("dp", "tensor"),
            P(None, "dp", None, "tensor"),
            P(None, "tensor", "dp"),
            P("dp", "tensor"),
            P("tensor", "dp"),
            P("dp", "tensor"),
        ),
        check_vma=False,
    )
```

```python
from functools import partial
import math

import jax
import jax.numpy as jnp
from jax import lax
from jax.experimental import pallas as pl
from jax.experimental.pallas import tpu as pltpu
from jax.sharding import PartitionSpec as P

C = 1280
GROUPS = 32
FRAMES = 16
HEAD = 160
BLOCK = 128
MIXED = ("tensor", "dp")


def spread(rows, weight):
    return jnp.einsum("rk,tkn->trn", rows, weight, preferred_element_type=jnp.float32)


def collapse(parts, weight):
    return jnp.einsum("trn,tkn->rk", parts, weight, preferred_element_type=jnp.float32)


def make_positions():
    channel_ids = jnp.arange(C)
    pair_rate = jnp.exp((channel_ids // 2).astype(jnp.float32) * (-2.0 * math.log(10000.0) / C))
    angles = jnp.arange(FRAMES).astype(jnp.float32)[:, None] * pair_rate[None, :]
    return jnp.where(channel_ids[None, :] % 2 == 0, jnp.sin(angles), jnp.cos(angles))


def layer_stats(stream):
    centre = jnp.mean(stream, axis=1, keepdims=True)
    offset = stream - centre
    inverse = lax.rsqrt(jnp.mean(offset * offset, axis=1, keepdims=True) + 1e-05)
    return offset * inverse, inverse


def layer_back(grad_out, normal_part, inverse, gain):
    scaled = grad_out * gain
    first = jnp.mean(scaled, axis=1, keepdims=True)
    second = jnp.mean(scaled * normal_part, axis=1, keepdims=True)
    grad_in = inverse * (scaled - first - normal_part * second)
    return grad_in, jnp.sum(grad_out * normal_part, 0), jnp.sum(grad_out, 0)


def dot_rows(left, right):
    return lax.dot_general(left, right, (((1,), (1,)), ((), ())), preferred_element_type=jnp.float32)


def dot_plain(left, right):
    return lax.dot_general(left, right, (((1,), (0,)), ((), ())), preferred_element_type=jnp.float32)


def dot_first(left, right):
    return lax.dot_general(left, right, (((0,), (0,)), ((), ())), preferred_element_type=jnp.float32)


def same_pixel(block):
    row = lax.broadcasted_iota(jnp.int32, (block, block), 0) // FRAMES
    col = lax.broadcasted_iota(jnp.int32, (block, block), 1) // FRAMES
    return row == col


def head_probs(query, key, same, scale):
    scores = jnp.where(same, dot_rows(query, key) * scale, -1e30)
    top = jnp.max(scores, axis=1, keepdims=True)
    weights = jnp.where(same, jnp.exp(scores - top), 0.0)
    return weights / jnp.sum(weights, axis=1, keepdims=True)


def attend_kernel(scale, qk_ref, v_ref, out_ref):
    rows, width = out_ref.shape[1], out_ref.shape[2]
    block = min(BLOCK, rows)
    same = same_pixel(block)
    for start in range(0, rows, block):
        for head in range(width // HEAD):
            here, low = slice(start, start + block), head * HEAD
            query = qk_ref[0, here, low : low + HEAD]
            key = qk_ref[0, here, width + low : width + low + HEAD]
            value = v_ref[0, here, low : low + HEAD]
            probs = head_probs(query, key, same, scale).astype(jnp.bfloat16)
            out_ref[0, here, low : low + HEAD] = dot_plain(probs, value).astype(jnp.bfloat16)


def part_spec(array):
    return pl.BlockSpec((1,) + array.shape[1:], lambda t: (t, 0, 0))


def attend(qk, values):
    return pl.pallas_call(
        partial(attend_kernel, 1.0 / math.sqrt(HEAD)),
        grid=(qk.shape[0],),
        in_specs=[part_spec(qk), part_spec(values)],
        out_specs=part_spec(values),
        out_shape=jax.ShapeDtypeStruct(values.shape, jnp.bfloat16),
        compiler_params=pltpu.CompilerParams(vmem_limit_bytes=32 << 20),
    )(qk, values)


def attend_back_kernel(scale, qk_ref, v_ref, grad_ref, dqk_ref, dv_ref):
    rows, width = grad_ref.shape[1], grad_ref.shape[2]
    block = min(BLOCK, rows)
    same = same_pixel(block)
    for start in range(0, rows, block):
        for head in range(width // HEAD):
            here, low = slice(start, start + block), head * HEAD
            query = qk_ref[0, here, low : low + HEAD]
            key = qk_ref[0, here, width + low : width + low + HEAD]
            value = v_ref[0, here, low : low + HEAD]
            grad = grad_ref[0, here, low : low + HEAD]
            probs = head_probs(query, key, same, scale)
            grad_probs = dot_rows(grad, value)
            centred = jnp.sum(probs * grad_probs, axis=1, keepdims=True)
            grad_raw = (probs * (grad_probs - centred) * scale).astype(jnp.bfloat16)
            dqk_ref[0, here, low : low + HEAD] = dot_plain(grad_raw, key).astype(jnp.bfloat16)
            dqk_ref[0, here, width + low : width + low + HEAD] = dot_first(grad_raw, query).astype(
                jnp.bfloat16
            )
            dv_ref[0, here, low : low + HEAD] = dot_first(probs.astype(jnp.bfloat16), grad).astype(
                jnp.bfloat16
            )


def attend_back(qk, values, grad):
    return pl.pallas_call(
        partial(attend_back_kernel, 1.0 / math.sqrt(HEAD)),
        grid=(qk.shape[0],),
        in_specs=[part_spec(qk), part_spec(values), part_spec(values)],
        out_specs=[part_spec(qk), part_spec(values)],
        out_shape=[
            jax.ShapeDtypeStruct(qk.shape, jnp.bfloat16),
            jax.ShapeDtypeStruct(values.shape, jnp.bfloat16),
        ],
        compiler_params=pltpu.CompilerParams(vmem_limit_bytes=32 << 20),
    )(qk, values, grad)


UNITS = 9
WIDE = 640
SLOTS_IN_FLIGHT = 6
SLOTS_RECEIVED = 4
ROWS_A = 96
MESH_ID = pl.DeviceIdType.MESH


class Place:
    def __init__(self):
        dp, tn = lax.axis_index("dp"), lax.axis_index("tensor")
        self.z, self.x = dp // 2, dp % 2
        self.y, self.c = tn // 2, tn % 2
        self.far_x, self.far_y = 1 - self.x, 1 - self.y
        self.to = {
            "x": (self.z * 2 + self.far_x, tn),
            "y": (dp, self.far_y * 2 + self.c),
            "core": (dp, self.y * 2 + 1 - self.c),
            "cross": (dp, self.far_y * 2 + 1 - self.c),
            "up": (dp + 2, tn),
            "down": (dp - 2, tn),
        }
        self.has_up = self.z < 3
        self.has_down = self.z > 0

    def greet(self):
        barrier = pltpu.get_barrier_semaphore()

        def hello(name):
            pl.semaphore_signal(barrier, inc=1, device_id=self.to[name], device_id_type=MESH_ID)

        for name in ("x", "y", "core", "cross"):
            hello(name)
        pl.when(self.has_up)(lambda: hello("up"))
        pl.when(self.has_down)(lambda: hello("down"))
        pl.semaphore_wait(barrier, 4 + (6 - self.z) // 4 + (self.z + 3) // 4)


class Plan:
    FIELDS = (
        ("kind", 16),
        ("unit", 16),
        ("t", 4),
        ("aux", 128),
        ("slot", 2),
        ("fresh", 2),
        ("next", 64),
        ("early", 32),
    )

    def __init__(self, per_turn, loads_early=False):
        self.per_turn, self.loads_early = per_turn, loads_early
        self.steps = {}

    def fill(self, turn, steps):
        tiles = [index for index, step in enumerate(steps) if step[1] is not None]
        early = {}
        for order, index in enumerate(tiles):
            if self.loads_early and steps[index][0] == 1:
                early[tiles[order - 1] if order else index] = 1 + steps[index][3] * 4 + steps[index][2]
        for index, (kind, unit, t, aux) in enumerate(steps):
            slot = fresh = following = 0
            if unit is not None:
                order = tiles.index(index)
                slot, fresh = order % 2, int(order == 0)
                if order + 1 < len(tiles):
                    later = steps[tiles[order + 1]]
                    following = 1 + later[1] * 4 + later[2]
            values = (kind, unit or 0, t, aux, slot, fresh, following, early.get(index, 0))
            code, scale = 0, 1
            for (name, size), value in zip(self.FIELDS, values):
                assert 0 <= value < size
                code += scale * value
                scale *= size
            place = turn * self.per_turn + index * self.per_turn // len(steps)
            assert place not in self.steps
            self.steps[place] = code

    def code(self, place):
        code = jnp.int32(0)
        for where, value in self.steps.items():
            code = jnp.where(place == where, jnp.int32(value), code)
        return code

    def fields(self, code):
        out = {}
        for name, size in self.FIELDS:
            out[name] = code % size
            code = code // size
        return out


def await_bytes(ref, sem):
    pltpu.make_async_copy(ref, ref, sem).wait()


def forward_kernel(
    shard_ref,
    x_ref,
    params_ref,
    position_ref,
    whole_ref,
    q_ref,
    pt_ref,
    stream_out_ref,
    qk_ref,
    v_ref,
    slope_ref,
    moved_ref,
    joined_ref,
    stream,
    xb,
    ptb,
    x_got,
    params_got,
    hidden_bias,
    qkb,
    vb,
    cols,
    slopeb,
    first_rows,
    total,
    wb,
    tile_sem,
    save_sem,
    kept_sem,
    peer_send,
    peer_recv,
    local_sem,
    send_sem,
    recv_sem,
    core_sem,
):
    at = Place()
    z, x, y, c = at.z, at.x, at.y, at.c
    share = shard_ref.shape[1]
    cut = (pl.ds(0, ROWS_A), pl.ds(ROWS_A, share - ROWS_A))
    kinds = {"up": 0, "down": 1, "x": 2, "y": 3, "core": 4}
    at.greet()

    def send(unit, colour, yy, zz, xx, kind, own=False):
        place = whole_ref.at[unit, yy, c, zz, xx, cut[colour]]
        pltpu.make_async_remote_copy(
            src_ref=shard_ref.at[unit, cut[colour]] if own else place,
            dst_ref=place,
            send_sem=send_sem.at[unit, colour, kinds[kind]],
            recv_sem=recv_sem.at[unit, colour, yy, zz, xx],
            device_id=at.to[kind],
            device_id_type=MESH_ID,
        ).start()

    def arrived(unit, colour, yy, zz, xx):
        await_bytes(
            whole_ref.at[unit, yy, c, zz, xx, cut[colour]], recv_sem.at[unit, colour, yy, zz, xx]
        )

    def own_copy(unit):
        return pltpu.make_async_copy(
            shard_ref.at[unit], whole_ref.at[unit, y, c, z, x], local_sem.at[unit]
        )

    def to_core(unit, part):
        if part == 2:
            place = whole_ref.at[unit, :, c, :, :, cut[1]]
        else:
            place = whole_ref.at[unit, y if part == 0 else at.far_y, c, :, :, cut[0]]
        return pltpu.make_async_remote_copy(
            src_ref=place,
            dst_ref=place,
            send_sem=send_sem.at[unit, part // 2, 4],
            recv_sem=core_sem.at[unit, part],
            device_id=at.to["core"],
            device_id_type=MESH_ID,
        )

    def from_z(unit, colour, step, yy):
        @pl.when(z >= step)
        def _():
            zz = z - step
            arrived(unit, colour, yy, zz, x)
            pl.when(at.has_up)(lambda: send(unit, colour, yy, zz, x, "up"))
            send(unit, colour, yy, zz, x, "x")
            if colour == 0:
                send(unit, colour, yy, zz, x, "y")

        @pl.when(z + step <= 3)
        def _():
            zz = z + step
            arrived(unit, colour, yy, zz, x)
            pl.when(at.has_down)(lambda: send(unit, colour, yy, zz, x, "down"))
            send(unit, colour, yy, zz, x, "x")
            if colour == 0:
                send(unit, colour, yy, zz, x, "y")

    def from_x(unit, step):
        def one(zz):
            arrived(unit, 0, y, zz, at.far_x)
            send(unit, 0, y, zz, at.far_x, "y")

        if step == 0:
            one(z)
        else:
            pl.when(z >= step)(lambda: one(z - step))
            pl.when(z + step <= 3)(lambda: one(z + step))

    def stage0(unit):
        own_copy(unit).start()
        pl.when(at.has_up)(lambda: send(unit, 0, y, z, x, "up", True))
        pl.when(at.has_down)(lambda: send(unit, 0, y, z, x, "down", True))
        send(unit, 1, y, z, x, "y", True)
        send(unit, 0, y, z, x, "x", True)
        pl.when(at.has_up)(lambda: send(unit, 1, y, z, x, "up", True))
        pl.when(at.has_down)(lambda: send(unit, 1, y, z, x, "down", True))
        send(unit, 0, y, z, x, "y", True)
        send(unit, 1, y, z, x, "x", True)

    def stage1(unit):
        from_z(unit, 0, 1, y)
        arrived(unit, 1, at.far_y, z, x)
        pl.when(at.has_up)(lambda: send(unit, 1, at.far_y, z, x, "up"))
        pl.when(at.has_down)(lambda: send(unit, 1, at.far_y, z, x, "down"))
        send(unit, 1, at.far_y, z, x, "x")
        from_z(unit, 1, 1, y)
        from_x(unit, 0)

    def stage2(unit):
        from_z(unit, 0, 2, y)
        from_z(unit, 1, 1, at.far_y)
        from_z(unit, 1, 2, y)
        from_x(unit, 1)

    def stage3(unit):
        from_z(unit, 0, 3, y)
        from_z(unit, 1, 2, at.far_y)
        from_z(unit, 1, 3, y)
        from_x(unit, 2)

    def stage4(unit):
        from_z(unit, 1, 3, at.far_y)
        from_x(unit, 3)
        own_copy(unit).wait()
        to_core(unit, 0).start()

    def stage5(unit):
        for zz in range(4):
            for xx in range(2):
                arrived(unit, 0, at.far_y, zz, xx)
        to_core(unit, 1).start()
        for zz in range(4):
            for yy in range(2):
                arrived(unit, 1, yy, zz, at.far_x)
        to_core(unit, 2).start()

    def stage6(unit):
        other = 1 - c
        await_bytes(whole_ref.at[unit, y, other, :, :, cut[0]], core_sem.at[unit, 0])
        await_bytes(whole_ref.at[unit, at.far_y, other, :, :, cut[0]], core_sem.at[unit, 1])
        await_bytes(whole_ref.at[unit, :, other, :, :, cut[1]], core_sem.at[unit, 2])
        for colour in range(2):
            rows = cut[colour]
            await_bytes(whole_ref.at[unit, :, c, :, :, rows], send_sem.at[unit, colour, 4])
            whole_x = whole_ref.at[unit, 0, c, :, 0, rows] if colour == 0 else None
            if colour == 0:
                await_bytes(whole_x, send_sem.at[unit, 0, 2])
                await_bytes(whole_ref.at[unit, 0, c, :, :, rows], send_sem.at[unit, 0, 3])
            else:
                await_bytes(whole_ref.at[unit, 0, c, :, :, rows], send_sem.at[unit, 1, 2])
                await_bytes(whole_ref.at[unit, 0, c, 0, 0, rows], send_sem.at[unit, 1, 3])
            for level in range(3):

                def ups(level=level):
                    if colour == 0:
                        ref = whole_ref.at[unit, 0, c, pl.ds(0, level + 1), 0, rows]
                    else:
                        ref = whole_ref.at[unit, :, c, pl.ds(0, level + 1), 0, rows]
                    return ref

                pl.when(z == level)(
                    lambda level=level: await_bytes(ups(level), send_sem.at[unit, colour, 0])
                )
                pl.when(z == 3 - level)(
                    lambda level=level: await_bytes(ups(level), send_sem.at[unit, colour, 1])
                )

    stages = (stage0, stage1, stage2, stage3, stage4, stage5, stage6)

    rows_all, width = x_ref.shape[1], x_ref.shape[2]
    half_rows = rows_all // 2
    scale = 1.0 / math.sqrt(HEAD)
    own_t = y * 2 + c

    def save_now(source, target):
        copy = pltpu.make_async_copy(source, target, save_sem.at[0])
        copy.start()
        copy.wait()

    peers = (("y", at.far_y * 2 + c), ("core", y * 2 + 1 - c), ("cross", at.far_y * 2 + 1 - c))

    def peer_copies(index):
        kind, t = peers[index]
        target = {"device_id": at.to[kind], "device_id_type": MESH_ID}
        return (
            pltpu.make_async_remote_copy(
                src_ref=params_ref,
                dst_ref=params_got.at[own_t],
                send_sem=peer_send.at[0, index],
                recv_sem=peer_recv.at[0, index],
                **target,
            ),
            pltpu.make_async_remote_copy(
                src_ref=x_ref.at[t],
                dst_ref=x_got.at[own_t],
                send_sem=peer_send.at[1, index],
                recv_sem=peer_recv.at[1, index],
                **target,
            ),
        )

    own_peer = (
        pltpu.make_async_copy(params_ref, params_got.at[own_t], peer_send.at[0, 3]),
        pltpu.make_async_copy(x_ref.at[own_t], x_got.at[own_t], peer_send.at[1, 3]),
    )
    for index in range(3):
        for copy in peer_copies(index):
            copy.start()
    for copy in own_peer:
        copy.start()

    def each(count, size, use):
        def one(step, carry):
            use(pl.ds(pl.multiple_of(step * size, size), size))
            return carry

        lax.fori_loop(0, count, one, 0)

    def tile_load(unit, t, slot):
        return pltpu.make_async_copy(whole_ref.at[unit, t // 2, t % 2], wb.at[slot], tile_sem.at[slot])

    def kept_copies(which, t):
        target = (10, 4, 1, 0)[which]
        copies = [
            pltpu.make_async_copy(cols.at[which, t], q_ref.at[target, t], kept_sem.at[which, t, 0])
        ]
        if which < 2:
            pairs = [(qkb.at[which, t], qk_ref.at[which, t]), (vb.at[which, t], v_ref.at[which, t])]
        else:
            pairs = [(slopeb.at[which - 2, t], slope_ref.at[which - 2, t])]
        for index, (source, target_ref) in enumerate(pairs):
            copies.append(
                pltpu.make_async_copy(source, target_ref, kept_sem.at[which, t, 1 + index])
            )
        return copies

    def do_spread(op):
        matrix = op["slot"]
        t, aux = op["t"], op["aux"]

        def multiply(rows):
            total[rows, :] = dot_plain(xb[rows, :], wb[matrix].reshape(C, WIDE))

        each(2, half_rows, multiply)
        quarter = rows_all // 4

        @pl.when(aux == 0)
        def _():
            def use(rows):
                first_rows[t, rows, :] = total[rows, width:]

            each(4, quarter, use)

        @pl.when((aux == 1) | (aux == 3))
        def _():
            def use(rows):
                qkb[(aux - 1) // 2, t, rows, :] = total[rows, :].astype(jnp.bfloat16)

            each(4, quarter, use)

        @pl.when((aux == 2) | (aux == 4))
        def _():
            def use(rows):
                vb[(aux - 2) // 2, t, rows, :] = total[rows, 0:width].astype(jnp.bfloat16)

            each(4, quarter, use)

        @pl.when((aux == 5) | (aux == 6))
        def _():
            half = aux - 5

            def use(rows):
                pre = total[rows, :] + hidden_bias[t, pl.ds(half, 1), :]
                below = 0.5 * (1.0 + lax.erf(pre * math.sqrt(0.5)))
                cols[2 + half, t, rows, :] = (pre * below).astype(jnp.bfloat16)
                density = jnp.exp(-0.5 * pre * pre) * (1.0 / math.sqrt(2.0 * math.pi))
                slopeb[half, t, rows, :] = (below + pre * density).astype(jnp.bfloat16)

            each(rows_all // 32, 32, use)
            for which in (2, 3):

                @pl.when(half == which - 2)
                def _(which=which):
                    for copy in kept_copies(which, t):
                        copy.start()

        @pl.when(aux == 7)
        def _():
            def use(rows):
                moved_ref[t, rows, :] = (total[rows, width:] + params_got[t, 12:13, :]).astype(
                    jnp.bfloat16
                )

            each(4, quarter, use)

    def do_collapse(op):
        def multiply(rows):
            stream[rows, :] += dot_rows(cols[op["aux"], op["t"], rows, :], wb[op["slot"]].reshape(C, WIDE))

        each(2, half_rows, multiply)

    def do_attention(op):
        block, t = op["aux"], op["t"]
        same = same_pixel(BLOCK)

        def write(place):
            for start in range(0, rows_all, BLOCK):
                here = slice(start, start + BLOCK)
                for head in range(width // HEAD):
                    low = head * HEAD
                    query = qkb[block, t, here, low : low + HEAD]
                    key = qkb[block, t, here, width + low : width + low + HEAD]
                    value = vb[block, t, here, low : low + HEAD]
                    probs = head_probs(query, key, same, scale).astype(jnp.bfloat16)
                    total[here, low : low + HEAD] = dot_plain(probs, value)

        write(0)
        for which in range(2):

            @pl.when(block == which)
            def _(which=which):
                own = slice(width, 2 * width) if which == 0 else slice(0, width)
                other = slice(0, width) if which == 0 else slice(width, 2 * width)

                def use(rows):
                    cols[which, t, rows, own] = total[rows, 0:width].astype(jnp.bfloat16)
                    cols[which, t, rows, other] = jnp.zeros((rows_all // 4, width), jnp.bfloat16)

                each(4, rows_all // 4, use)
                for copy in kept_copies(which, t):
                    copy.start()

    chunk = 4 * FRAMES

    def do_norm(op):
        layer = op["aux"]

        def use(rows):
            @pl.when(layer == 0)
            def _():
                for t in range(4):
                    stream[rows, t * width : (t + 1) * width] = first_rows[t, rows, :]

            values = stream[rows, :] + joined_ref[pl.ds(8 + layer, 1), :]
            stream[rows, :] = values
            centre = jnp.mean(values, axis=1, keepdims=True)
            offset = values - centre
            inverse = lax.rsqrt(jnp.mean(offset * offset, axis=1, keepdims=True) + 1e-05)
            normed = offset * inverse * joined_ref[pl.ds(1 + layer, 1), :]
            normed = normed + joined_ref[pl.ds(5 + layer, 1), :]
            added = jnp.where(layer < 2, position_ref[...], 0.0)
            normed = normed.reshape(chunk // FRAMES, FRAMES, C) + added[None]
            xb[rows, :] = normed.reshape(chunk, C).astype(jnp.bfloat16)

        each(rows_all // chunk, chunk, use)
        save_now(stream, stream_out_ref.at[layer])

    def do_turn(op):
        def one(step, carry):
            lanes = pl.ds(pl.multiple_of(step * 128, 128), 128)
            ptb[lanes, :] = xb[:, lanes].T
            return carry

        lax.fori_loop(0, C // 128, one, 0)
        save_now(ptb, pt_ref.at[op["aux"]])

    def do_last(op):
        def use(rows):
            xb[rows, :] = (stream[rows, :] + joined_ref[11:12, :]).astype(jnp.bfloat16)

        each(rows_all // chunk, chunk, use)

    def do_join(op):
        for index in range(3):
            for copy in peer_copies(index):
                copy.wait_recv()
        for copy in own_peer:
            copy.wait()
        for t in range(4):
            lanes = slice(t * width, (t + 1) * width)
            joined_ref[:, lanes] = params_got[t, 0:16, :]

            def use(rows, t=t, lanes=lanes):
                xb[rows, lanes] = x_got[t, rows, :]

            each(4, rows_all // 4, use)
            for half in range(2):
                for part in range(2):
                    row = 16 + 2 * half + part
                    hidden_bias[t, half : half + 1, part * width : (part + 1) * width] = params_got[
                        t, row : row + 1, :
                    ]

    works = (None, do_spread, do_collapse, do_attention, do_norm, do_turn, do_last, do_join)
    four = range(4)

    def spreads(unit, aux):
        return [(1, unit, t, aux) for t in four]

    def collapses(unit, aux):
        return [(2, unit, t, aux) for t in four]

    def attentions(aux):
        return [(3, None, t, aux) for t in four]

    count = len(stages)
    places = 2 * count
    plan = Plan(places)
    for ready, steps in {
        -4: [(7, None, 0, 0), (5, None, 0, 7)],
        1: spreads(1, 0) + [(4, None, 0, 0)] + spreads(0, 1) + spreads(1, 2),
        2: [(5, None, 0, 4)] + attentions(0),
        3: collapses(3, 0) + [(4, None, 0, 1)] + spreads(2, 3) + spreads(3, 4),
        4: [(5, None, 0, 3)] + attentions(1) + collapses(4, 1) + [(4, None, 0, 2)],
        5: [(5, None, 0, 1)] + spreads(5, 5),
        6: spreads(6, 6),
        7: collapses(7, 2),
        8: collapses(8, 3) + [(6, None, 0, 0)] + spreads(4, 7) + [(5, None, 0, 5)],
    }.items():
        plan.fill(ready + count - 1, steps)

    def do_step(place):
        code = plan.code(place)
        pl.when(code > 0)(lambda: do_filled(code))

    def do_filled(code):
        op = plan.fields(code)
        has_tile = (op["kind"] == 1) | (op["kind"] == 2)

        @pl.when(has_tile)
        def _():
            pl.when(op["fresh"] == 1)(lambda: tile_load(op["unit"], op["t"], op["slot"]).start())

            @pl.when(op["next"] > 0)
            def _():
                following = op["next"] - 1
                tile_load(following // 4, following % 4, 1 - op["slot"]).start()

            tile_load(op["unit"], op["t"], op["slot"]).wait()

        for kind in range(1, len(works)):

            @pl.when(op["kind"] == kind)
            def _(kind=kind):
                works[kind](op)

    def advance(turn, carry):
        def inner(place, carry):
            for number in range(count):
                unit = turn - number

                @pl.when((place == count - 1 - number) & (unit >= 0) & (unit < UNITS))
                def _(number=number, unit=unit):
                    stages[number](unit)

            def two(step, carry):
                do_step(2 * (turn * count + place) + step)
                return carry

            return lax.fori_loop(0, 2, two, carry)

        return lax.fori_loop(0, count, inner, carry)

    lax.fori_loop(0, UNITS + count - 1, advance, 0)
    for which in range(4):
        for t in range(4):
            for copy in kept_copies(which, t):
                copy.wait()
    for index in range(3):
        for copy in peer_copies(index):
            copy.wait_send()


def forward_all(shards, rows_in, params, position):
    units, share, wide = shards.shape
    rows, width = rows_in.shape[1], rows_in.shape[2]
    low = jnp.bfloat16
    anywhere, near = pl.BlockSpec(memory_space=pl.ANY), pl.BlockSpec(memory_space=pltpu.VMEM)
    return pl.pallas_call(
        forward_kernel,
        in_specs=[near, anywhere, near, near],
        out_specs=[anywhere] * 7 + [near] * 2,
        out_shape=[
            jax.ShapeDtypeStruct((units, 2, 2, 4, 2, share, wide), low),
            jax.ShapeDtypeStruct((12, 4, rows, wide), low),
            jax.ShapeDtypeStruct((8, C, rows), low),
            jax.ShapeDtypeStruct((3, rows, C), jnp.float32),
            jax.ShapeDtypeStruct((2, 4, rows, wide), low),
            jax.ShapeDtypeStruct((2, 4, rows, width), low),
            jax.ShapeDtypeStruct((2, 4, rows, wide), low),
            jax.ShapeDtypeStruct((4, rows, width), low),
            jax.ShapeDtypeStruct((16, C), jnp.float32),
        ],
        scratch_shapes=[
            pltpu.VMEM((rows, C), jnp.float32),
            pltpu.VMEM((rows, C), low),
            pltpu.VMEM((C, rows), low),
            pltpu.VMEM((4, rows, width), low),
            pltpu.VMEM((4,) + params.shape, jnp.float32),
            pltpu.VMEM((4, 8, wide), jnp.float32),
            pltpu.VMEM((2, 4, rows, wide), low),
            pltpu.VMEM((2, 4, rows, width), low),
            pltpu.VMEM((4, 4, rows, wide), low),
            pltpu.VMEM((2, 4, rows, wide), low),
            pltpu.VMEM((4, rows, width), jnp.float32),
            pltpu.VMEM((rows, wide), jnp.float32),
            pltpu.VMEM((2, 4, 2, share, wide), low),
            pltpu.SemaphoreType.DMA((2,)),
            pltpu.SemaphoreType.DMA((1,)),
            pltpu.SemaphoreType.DMA((4, 4, 3)),
            pltpu.SemaphoreType.DMA((2, 4)),
            pltpu.SemaphoreType.DMA((2, 3)),
            pltpu.SemaphoreType.DMA((units,)),
            pltpu.SemaphoreType.DMA((units, 2, 5)),
            pltpu.SemaphoreType.DMA((units, 2, 2, 4, 2)),
            pltpu.SemaphoreType.DMA((units, 3)),
        ],
        compiler_params=pltpu.CompilerParams(
            collective_id=0, has_side_effects=True, vmem_limit_bytes=60 << 20
        ),
    )(shards, rows_in, params, position)


def backward_kernel(
    whole_ref,
    q_given,
    pt_given,
    streams_ref,
    qk_ref,
    v_ref,
    slope_ref,
    moved_ref,
    joined_ref,
    out_ref,
    q_ref,
    pt_ref,
    ptx_ref,
    qx_ref,
    got_ref,
    vec_ref,
    hidden_ref,
    p_buf,
    q_buf,
    dw,
    rya,
    rxa,
    rua,
    rda,
    rxb,
    rub,
    rdb,
    ryb,
    gs,
    gn,
    xb,
    ptb,
    wb,
    cb,
    av,
    datt,
    total,
    sb,
    ob,
    dn,
    load_sem,
    give_sem,
    take_sem,
    send_sem,
    recv_sem,
    tile_sem,
    aux_sem,
    route_sem,
    misc_sem,
    out_sem,
    peer_send,
    peer_recv,
):
    at = Place()
    z, x, y, c = at.z, at.x, at.y, at.c
    far_x, far_y = at.far_x, at.far_y
    share = out_ref.shape[1]
    row_a, row_b = pl.ds(0, ROWS_A), pl.ds(ROWS_A, share - ROWS_A)
    rows_all, width = got_ref.shape[1], got_ref.shape[2]
    half_rows = rows_all // 2
    count_p = pt_ref.shape[0]
    scale = 1.0 / math.sqrt(HEAD)
    own_t = y * 2 + c
    at.greet()

    def give_p(index, source=None):
        return pltpu.make_async_remote_copy(
            src_ref=pt_ref.at[index] if source is None else source,
            dst_ref=ptx_ref.at[index],
            send_sem=give_sem.at[index],
            recv_sem=take_sem.at[index],
            device_id=at.to["core"],
            device_id_type=MESH_ID,
        )

    def give_q(index, yy, source):
        return pltpu.make_async_remote_copy(
            src_ref=source,
            dst_ref=qx_ref.at[index, yy],
            send_sem=give_sem.at[count_p + 2 * index + yy],
            recv_sem=take_sem.at[count_p + 2 * index + yy],
            device_id=at.to["core"],
            device_id_type=MESH_ID,
        )

    def known_q(index, yy):
        source = moved_ref if index == 9 else q_ref.at[index]
        return give_q(index, yy, source.at[2 * yy + 1 - c])

    known = (0, 1, 4, 9, 10)
    known_p = (1, 5, 3, 4, 7)
    for index in known[:2]:
        for yy in range(2):
            known_q(index, yy).start()
    give_p(1).start()
    for index in known[2:]:
        for yy in range(2):
            known_q(index, yy).start()
    for index in known_p[1:]:
        give_p(index).start()
    def each(count, size, use):
        def one(step, carry):
            use(pl.ds(pl.multiple_of(step * size, size), size))
            return carry

        lax.fori_loop(0, count, one, 0)

    def aux_load(source, target, number):
        return pltpu.make_async_copy(source, target, aux_sem.at[number])

    def tile_load(unit, t, slot):
        return pltpu.make_async_copy(whole_ref.at[unit, t // 2, t % 2], wb.at[slot], tile_sem.at[slot])

    def route(source, index, t):
        yy = t // 2
        local = pltpu.make_async_copy(source, q_ref.at[index, t], route_sem.at[index, yy])

        def begin():
            pl.when(c == t % 2)(lambda: local.start())
            pl.when(c != t % 2)(lambda: give_q(index, yy, source).start())

        def wait():
            pl.when(c == t % 2)(lambda: local.wait())
            pl.when(c != t % 2)(lambda: give_q(index, yy, source).wait_send())

        return begin, wait

    chunk = 4 * FRAMES
    quarter = rows_all // 4

    def column_sum(row, values):
        vec_ref[pl.ds(row, 1), :] += jnp.sum(values, axis=0, keepdims=True)

    def slope_load(aux, t):
        return aux_load(slope_ref.at[aux, t], cb.at[4], 0)

    def head_loads(aux, t):
        return (
            aux_load(qk_ref.at[aux - 2, t], cb.at[4], 0),
            aux_load(v_ref.at[aux - 2, t], av, 1),
        )

    def load_early(code):
        aux, t = code // 4, code % 4
        pl.when(aux < 2)(lambda: slope_load(aux, t).start())

        @pl.when(aux >= 2)
        def _():
            for load in head_loads(aux, t):
                load.start()

    def do_spread(op):
        t, aux = op["t"], op["aux"]
        side = t % 2

        def multiply(rows):
            total[rows, :] = dot_plain(xb[rows, :], wb[op["slot"]].reshape(C, WIDE))

        each(2, half_rows, multiply)

        @pl.when(aux < 2)
        def _():
            slope_load(aux, t).wait()

            def use(rows):
                grad = total[rows, :] * cb[4, rows, :].astype(jnp.float32)
                hidden_ref[t, pl.ds(aux, 1), :] += jnp.sum(grad, axis=0, keepdims=True)
                cb[side, rows, :] = grad.astype(jnp.bfloat16)

            each(4, quarter, use)
            route(cb.at[side], 3 - aux, t)[0]()

        @pl.when(aux >= 2)
        def _():
            for load in head_loads(aux, t):
                load.wait()

            for block in range(2):

                @pl.when(aux == 2 + block)
                def _(block=block):
                    low = width if block == 0 else 0

                    def use(rows):
                        datt[rows, :] = total[rows, low : low + width].astype(jnp.bfloat16)

                    each(4, quarter, use)

    def moved_own(t):
        return pltpu.make_async_copy(cb.at[4], q_ref.at[9, t], misc_sem.at[0])

    def do_collapse(op):
        which, routed, t = op["aux"] % 5, op["aux"] // 5, op["t"]

        @pl.when(which == 4)
        def _():
            load = aux_load(moved_ref.at[t], cb.at[4], 0)
            load.start()
            load.wait()
            pl.when(c == t % 2)(lambda: moved_own(t).start())

        def multiply(rows):
            gn[rows, :] += dot_rows(cb[which, rows, :], wb[op["slot"]].reshape(C, WIDE))

        each(2, half_rows, multiply)
        pl.when(routed > 0)(lambda: route(cb.at[which], routed - 1, t)[1]())
        pl.when((which == 4) & (c == t % 2))(lambda: moved_own(t).wait())

    def do_attention(op):
        block, t = op["aux"], op["t"]
        side = t % 2
        same = same_pixel(BLOCK)
        for start in range(0, rows_all, BLOCK):
            here = slice(start, start + BLOCK)
            for head in range(width // HEAD):
                low = head * HEAD
                query = cb[4, here, low : low + HEAD]
                key = cb[4, here, width + low : width + low + HEAD]
                value = av[here, low : low + HEAD]
                grad = datt[here, low : low + HEAD]
                probs = head_probs(query, key, same, scale)
                grad_probs = dot_rows(grad, value)
                centred = jnp.sum(probs * grad_probs, axis=1, keepdims=True)
                grad_raw = (probs * (grad_probs - centred) * scale).astype(jnp.bfloat16)
                cb[side, here, low : low + HEAD] = dot_plain(grad_raw, key).astype(jnp.bfloat16)
                cb[side, here, width + low : width + low + HEAD] = dot_first(
                    grad_raw, query
                ).astype(jnp.bfloat16)
                cb[2 + side, here, low : low + HEAD] = dot_first(
                    probs.astype(jnp.bfloat16), grad
                ).astype(jnp.bfloat16)
        route(cb.at[side], 7 - 2 * block, t)[0]()
        route(cb.at[2 + side], 8 - 2 * block, t)[0]()

    def do_layer(op):
        layer = op["aux"]

        def load(step):
            rows = pl.ds(pl.multiple_of(step * chunk, chunk), chunk)
            return pltpu.make_async_copy(
                streams_ref.at[layer, rows], sb.at[step % 2], misc_sem.at[3 + step % 2]
            )

        def one(step, carry):
            pl.when(step + 1 < rows_all // chunk)(lambda: load(step + 1).start())
            load(step).wait()
            rows = pl.ds(pl.multiple_of(step * chunk, chunk), chunk)
            values = sb[step % 2]
            centre = jnp.mean(values, axis=1, keepdims=True)
            offset = values - centre
            inverse = lax.rsqrt(jnp.mean(offset * offset, axis=1, keepdims=True) + 1e-05)
            hat = offset * inverse
            grad = gn[rows, :]
            column_sum(layer, grad * hat)
            column_sum(3 + layer, grad)
            scaled = grad * joined_ref[pl.ds(1 + layer, 1), :]
            first = jnp.mean(scaled, axis=1, keepdims=True)
            second = jnp.mean(scaled * hat, axis=1, keepdims=True)
            result = gs[rows, :] + inverse * (scaled - first - hat * second)
            gs[rows, :] = result
            column_sum(6 + layer, result)
            xb[rows, :] = result.astype(jnp.bfloat16)
            gn[rows, :] = jnp.zeros((chunk, C), jnp.float32)
            return carry

        load(0).start()
        lax.fori_loop(0, rows_all // chunk, one, 0)

    def do_turn(op):
        index = op["aux"]

        def one(step, carry):
            lanes = pl.ds(pl.multiple_of(step * 128, 128), 128)
            ptb[lanes, :] = xb[:, lanes].T
            return carry

        lax.fori_loop(0, C // 128, one, 0)
        turn_copy(index).start()
        give_p(index, ptb).start()

    def turn_copy(index):
        return pltpu.make_async_copy(ptb, pt_ref.at[index], misc_sem.at[2])

    def do_turned(op):
        turn_copy(op["aux"]).wait()
        give_p(op["aux"], ptb).wait_send()

    def do_first(op):
        def use(rows):
            values = gn[rows, :]
            gs[rows, :] = values
            column_sum(9, values)
            xb[rows, :] = values.astype(jnp.bfloat16)
            gn[rows, :] = jnp.zeros((chunk, C), jnp.float32)

        each(rows_all // chunk, chunk, use)

    def do_place(op):
        t = op["t"]
        side = t % 2
        for block in range(4):

            @pl.when(t == block)
            def _(block=block):
                def use(rows):
                    cb[side, rows, 0:width] = jnp.zeros((quarter, width), jnp.bfloat16)
                    cb[side, rows, width:] = xb[rows, block * width : (block + 1) * width]

                each(4, quarter, use)

        route(cb.at[side], 11, t)[0]()

    peers = (("y", far_y * 2 + c), ("core", y * 2 + 1 - c), ("cross", far_y * 2 + 1 - c))

    def peer_copy(index):
        kind, t = peers[index]
        return pltpu.make_async_remote_copy(
            src_ref=dn.at[t],
            dst_ref=got_ref.at[own_t],
            send_sem=peer_send.at[index],
            recv_sem=peer_recv.at[index],
            device_id=at.to[kind],
            device_id_type=MESH_ID,
        )

    own_peer = pltpu.make_async_copy(dn.at[own_t], got_ref.at[own_t], peer_send.at[3])

    def do_send(op):
        for t in range(4):

            def use(rows, t=t):
                dn[t, rows, :] = gn[rows, t * width : (t + 1) * width].astype(jnp.bfloat16)

            each(4, quarter, use)
        for index in range(3):
            peer_copy(index).start()
        own_peer.start()

    works = (
        None,
        do_spread,
        do_collapse,
        do_attention,
        do_layer,
        do_turn,
        do_first,
        do_place,
        do_send,
        do_turned,
    )
    four = range(4)

    def feed(half):
        steps = []
        for t in four:
            steps += [(1, 7 + half, t, half), (2, 5 + half, t, t % 2 + 5 * (4 - half))]
        return steps

    def heads(block, t):
        return [
            (1, 3 + block, t, 2 + block),
            (3, None, t, block),
            (2, 2 * block, t, t % 2 + 5 * (8 - 2 * block)),
            (2, 2 * block + 1, t, 2 + t % 2 + 5 * (9 - 2 * block)),
        ]

    def inputs(t):
        return [(7, None, t, 0), (2, 1, t, t % 2 + 5 * 12)]

    stage_count = 6
    plan = Plan(2 * stage_count, True)
    for turn, steps in {
        -1: [(2, 4, t, 4) for t in four] + [(6, None, 0, 0), (5, None, 0, 0), (9, None, 0, 0)],
        0: feed(1),
        1: feed(0),
        2: [(4, None, 0, 2), (5, None, 0, 2)] + heads(1, 0) + [(9, None, 0, 2)],
        3: heads(1, 1) + heads(1, 2),
        4: heads(1, 3),
        5: [(4, None, 0, 1), (5, None, 0, 6)] + heads(0, 0) + [(9, None, 0, 6)],
        6: heads(0, 1) + heads(0, 2) + heads(0, 3),
        7: [(4, None, 0, 0)] + inputs(0) + inputs(1) + inputs(2) + inputs(3),
        8: [(8, None, 0, 0)],
    }.items():
        plan.fill(turn + 1, steps)

    def do_step(place):
        code = plan.code(place)
        pl.when(code > 0)(lambda: do_filled(code))

    def do_filled(code):
        op = plan.fields(code)
        has_tile = (op["kind"] == 1) | (op["kind"] == 2)

        @pl.when(has_tile)
        def _():
            pl.when(op["fresh"] == 1)(lambda: tile_load(op["unit"], op["t"], op["slot"]).start())

            @pl.when(op["next"] > 0)
            def _():
                following = op["next"] - 1
                tile_load(following // 4, following % 4, 1 - op["slot"]).start()

            pl.when(op["early"] > 0)(lambda: load_early(op["early"] - 1))
            tile_load(op["unit"], op["t"], op["slot"]).wait()

        for kind in range(1, len(works)):

            @pl.when(op["kind"] == kind)
            def _(kind=kind):
                works[kind](op)

    vec_ref[...] = jnp.zeros_like(vec_ref)
    hidden_ref[...] = jnp.zeros_like(hidden_ref)

    def clear(rows):
        gn[rows, :] = jnp.zeros((chunk, C), jnp.float32)
        cb[2, rows, :] = jnp.zeros((chunk, WIDE), jnp.bfloat16)
        cb[3, rows, :] = jnp.zeros((chunk, WIDE), jnp.bfloat16)

    each(rows_all // chunk, chunk, clear)

    names = ["ya0", "ya1", "xa", "ua0", "ua1", "ua2", "da0", "da1", "da2"]
    names += ["xb0", "xb1", "ub0", "ub1", "ub2", "db0", "db1", "db2", "yb"]
    number = {name: index for index, name in enumerate(names)}

    class Slot:
        def __init__(self, turn):
            self.d, self.r = turn % SLOTS_IN_FLIGHT, turn % SLOTS_RECEIVED

    def copy(slot, name, src, dst, kind, shift=0):
        index = number[name] + shift
        return pltpu.make_async_remote_copy(
            src_ref=src,
            dst_ref=dst,
            send_sem=send_sem.at[slot.d, index],
            recv_sem=recv_sem.at[slot.r, index],
            device_id=at.to[kind],
            device_id_type=MESH_ID,
        )

    def ya(slot, part):
        side = far_x if part == 0 else x
        return copy(
            slot, f"ya{part}", dw.at[slot.d, far_y, :, side, row_a], rya.at[slot.r, part], "y"
        )

    def xa(slot):
        return copy(slot, "xa", dw.at[slot.d, y, :, far_x, row_a], rxa.at[slot.r], "x")

    def xb_copy(slot, part):
        return copy(
            slot, f"xb{part}", dw.at[slot.d, part, :, far_x, row_b], rxb.at[slot.r, part], "x"
        )

    def yb(slot):
        return copy(slot, "yb", dw.at[slot.d, far_y, z, x, row_b], ryb.at[slot.r], "y")

    def up(slot, colour, d):
        if colour == 0:
            return copy(
                slot, "ua0", dw.at[slot.d, y, d, x, row_a], rua.at[slot.r, d - 1], "up", d - 1
            )
        return copy(slot, "ub0", dw.at[slot.d, :, d, x, row_b], rub.at[slot.r, d - 1], "up", d - 1)

    def down(slot, colour, d):
        if colour == 0:
            return copy(slot, "da0", dw.at[slot.d, y, d, x, row_a], rda.at[slot.r, d], "down", d)
        return copy(slot, "db0", dw.at[slot.d, :, d, x, row_b], rdb.at[slot.r, d], "down", d)

    def add(place, got):
        total = place[...].astype(jnp.float32) + got[...].astype(jnp.float32)
        place[...] = total.astype(jnp.bfloat16)

    def product_loads(p_index, q_index):
        loads = [
            pltpu.make_async_copy(pt_ref.at[p_index], p_buf.at[0], load_sem.at[0]),
            pltpu.make_async_copy(ptx_ref.at[p_index], p_buf.at[1], load_sem.at[1]),
        ]
        for yy in range(2):
            loads += [
                pltpu.make_async_copy(
                    q_ref.at[q_index, 2 * yy + c], q_buf.at[0, yy], load_sem.at[2 + yy]
                ),
                pltpu.make_async_copy(
                    qx_ref.at[q_index, yy], q_buf.at[1, yy], load_sem.at[4 + yy]
                ),
            ]
        return loads

    def products(slot, p_index, q_index, more):
        for load in product_loads(p_index, q_index):
            load.wait()

        def one(step, carry):
            side, zz = step // 4, step % 4
            yy = jnp.where(side == 0, far_y, y)
            rows = pl.ds(pl.multiple_of(zz * 2 * share, 2 * share), 2 * share)
            result = dot_plain(p_buf[0, rows, :], q_buf[0, yy]) + dot_plain(
                p_buf[1, rows, :], q_buf[1, yy]
            )
            result = result.reshape(2, share, WIDE)
            earlier = dw[slot.d, yy, zz].astype(jnp.float32)
            result = result + jnp.where(more == 1, earlier, 0.0)
            dw[slot.d, yy, zz] = result.astype(jnp.bfloat16)
            return carry

        lax.fori_loop(0, 8, one, 0)

    def take_p(index):
        await_bytes(ptx_ref.at[index], take_sem.at[index])

    def take_q(index):
        for yy in range(2):
            await_bytes(qx_ref.at[index, yy], take_sem.at[count_p + 2 * index + yy])

    def prepare(turn):
        p_index = (turn + turn // 5) // 2

        @pl.when((turn + turn // 5) % 2 == 0)
        def _():
            take_p(p_index)

        take_q(turn)
        for load in product_loads(p_index, turn):
            load.start()

    def stage0(turn):
        slot = Slot(turn)
        p_index = (turn + turn // 5) // 2
        mixed = (turn >= 4).astype(jnp.int32) * (1 - turn % 2)
        extra = (turn - 4) // 2

        @pl.when(mixed == 1)
        def _():
            take_p(5 + extra)
            take_q(UNITS + extra)

        def one_pass(more, carry):
            @pl.when(more == 1)
            def _():
                for load in product_loads(5 + extra, UNITS + extra):
                    load.start()

            products(
                slot,
                jnp.where(more == 1, 5 + extra, p_index),
                jnp.where(more == 1, UNITS + extra, turn),
                more,
            )
            return carry

        lax.fori_loop(0, 1 + mixed, one_pass, 0)

        ya(slot, 0).start()
        xb_copy(slot, 0).start()
        ya(slot, 1).start()
        xb_copy(slot, 1).start()

    def z_step(slot, colour, step):
        @pl.when(z <= step - 1)
        def _():
            d = z + 4 - step

            @pl.when(z >= 1)
            def _():
                up(slot, colour, d).wait_recv()
                if colour == 0:
                    add(dw.at[slot.d, y, d, x, row_a], rua.at[slot.r, d - 1])
                else:
                    add(dw.at[slot.d, 0, d, x, row_b], rub.at[slot.r, d - 1, 0])
                    add(dw.at[slot.d, 1, d, x, row_b], rub.at[slot.r, d - 1, 1])

            up(slot, colour, d).start()

        @pl.when(3 - z <= step - 1)
        def _():
            d = z - 4 + step

            @pl.when(z <= 2)
            def _():
                down(slot, colour, d).wait_recv()
                if colour == 0:
                    add(dw.at[slot.d, y, d, x, row_a], rda.at[slot.r, d])
                else:
                    add(dw.at[slot.d, 0, d, x, row_b], rdb.at[slot.r, d, 0])
                    add(dw.at[slot.d, 1, d, x, row_b], rdb.at[slot.r, d, 1])

            down(slot, colour, d).start()

    def stage1(turn):
        slot = Slot(turn)
        for part in range(2):
            xb_copy(slot, part).wait_recv()
            for zz in range(4):
                add(dw.at[slot.d, part, zz, x, row_b], rxb.at[slot.r, part, zz])
        z_step(slot, 1, 1)
        ya(slot, 0).wait_recv()
        for zz in range(4):
            add(dw.at[slot.d, y, zz, far_x, row_a], rya.at[slot.r, 0, zz])
        xa(slot).start()
        ya(slot, 1).wait_recv()
        for zz in range(4):
            add(dw.at[slot.d, y, zz, x, row_a], rya.at[slot.r, 1, zz])

    def stage2(turn):
        slot = Slot(turn)
        z_step(slot, 1, 2)
        xa(slot).wait_recv()
        for zz in range(4):
            add(dw.at[slot.d, y, zz, x, row_a], rxa.at[slot.r, zz])
        z_step(slot, 0, 1)

    def stage3(turn):
        slot = Slot(turn)
        z_step(slot, 1, 3)
        z_step(slot, 0, 2)

    def stage4(turn):
        slot = Slot(turn)
        z_step(slot, 0, 3)

        @pl.when(z >= 1)
        def _():
            up(slot, 1, z).wait_recv()
            for yy in range(2):
                add(dw.at[slot.d, yy, z, x, row_b], rub.at[slot.r, z - 1, yy])

        @pl.when(z <= 2)
        def _():
            down(slot, 1, z).wait_recv()
            for yy in range(2):
                add(dw.at[slot.d, yy, z, x, row_b], rdb.at[slot.r, z, yy])

        yb(slot).start()

    def out_copy(turn):
        return pltpu.make_async_copy(ob.at[turn % 2], out_ref.at[turn], out_sem.at[turn % 2])

    def stage5(turn):
        slot = Slot(turn)
        side = turn % 2
        pl.when(turn >= 2)(lambda: out_copy(turn - 2).wait())
        ob[side, row_a, :] = dw[slot.d, y, z, x, row_a, :].astype(jnp.float32)

        @pl.when(z >= 1)
        def _():
            up(slot, 0, z).wait_recv()
            ob[side, row_a, :] += rua[slot.r, z - 1].astype(jnp.float32)

        @pl.when(z <= 2)
        def _():
            down(slot, 0, z).wait_recv()
            ob[side, row_a, :] += rda[slot.r, z].astype(jnp.float32)

        yb(slot).wait_recv()
        ob[side, row_b, :] = dw[slot.d, y, z, x, row_b, :].astype(jnp.float32) + ryb[
            slot.r
        ].astype(jnp.float32)
        out_copy(turn).start()

        ya(slot, 0).wait_send()
        ya(slot, 1).wait_send()
        xa(slot).wait_send()
        xb_copy(slot, 0).wait_send()
        xb_copy(slot, 1).wait_send()
        yb(slot).wait_send()
        for colour in range(2):
            for step in range(1, 4):

                @pl.when(z <= step - 1)
                def _(colour=colour, step=step):
                    up(slot, colour, z + 4 - step).wait_send()

                @pl.when(3 - z <= step - 1)
                def _(colour=colour, step=step):
                    down(slot, colour, z - 4 + step).wait_send()

    stages = (stage0, stage1, stage2, stage3, stage4, stage5)

    def advance(now, carry):
        def inner(place, carry):
            for spot, step in enumerate(range(stage_count)):
                turn = now - 1 - step

                @pl.when((place == spot) & (turn >= 0) & (turn < UNITS))
                def _(step=step, turn=turn):
                    stages[step](turn)

            def two(step, carry):
                do_step(2 * (now * stage_count + place) + step)
                return carry

            return lax.fori_loop(0, 2, two, carry)

        lax.fori_loop(0, stage_count, inner, 0)
        pl.when(now < UNITS)(lambda: prepare(now))
        return carry

    lax.fori_loop(0, UNITS + stage_count, advance, 0)
    out_copy(UNITS - 2).wait()
    out_copy(UNITS - 1).wait()
    for index in range(3):
        peer_copy(index).wait()
    own_peer.wait()
    for index in known:
        for yy in range(2):
            known_q(index, yy).wait_send()
    for index in known_p:
        give_p(index).wait_send()


def backward_all(whole, q_all, pt_all, streams, qk, values, slopes, moved_part, joined):
    share = whole.shape[5]
    count_p, unused, rows = pt_all.shape
    width = values.shape[3]
    low = jnp.bfloat16
    slots, taken, rest = SLOTS_IN_FLIGHT, SLOTS_RECEIVED, share - ROWS_A
    anywhere, near = pl.BlockSpec(memory_space=pl.ANY), pl.BlockSpec(memory_space=pltpu.VMEM)
    return pl.pallas_call(
        backward_kernel,
        in_specs=[anywhere] * 8 + [near],
        out_specs=[anywhere] * 6 + [near] * 2,
        out_shape=[
            jax.ShapeDtypeStruct((UNITS, share, WIDE), jnp.float32),
            jax.ShapeDtypeStruct(q_all.shape, low),
            jax.ShapeDtypeStruct(pt_all.shape, low),
            jax.ShapeDtypeStruct(pt_all.shape, low),
            jax.ShapeDtypeStruct((q_all.shape[0], 2, rows, WIDE), low),
            jax.ShapeDtypeStruct((4, rows, width), low),
            jax.ShapeDtypeStruct((16, C), jnp.float32),
            jax.ShapeDtypeStruct((4, 8, WIDE), jnp.float32),
        ],
        input_output_aliases={1: 1, 2: 2},
        scratch_shapes=[
            pltpu.VMEM((2, C, rows), low),
            pltpu.VMEM((2, 2, rows, WIDE), low),
            pltpu.VMEM((slots, 2, 4, 2, share, WIDE), low),
            pltpu.VMEM((taken, 2, 4, ROWS_A, WIDE), low),
            pltpu.VMEM((taken, 4, ROWS_A, WIDE), low),
            pltpu.VMEM((taken, 3, ROWS_A, WIDE), low),
            pltpu.VMEM((taken, 3, ROWS_A, WIDE), low),
            pltpu.VMEM((taken, 2, 4, rest, WIDE), low),
            pltpu.VMEM((taken, 3, 2, rest, WIDE), low),
            pltpu.VMEM((taken, 3, 2, rest, WIDE), low),
            pltpu.VMEM((taken, rest, WIDE), low),
            pltpu.VMEM((rows, C), jnp.float32),
            pltpu.VMEM((rows, C), jnp.float32),
            pltpu.VMEM((rows, C), low),
            pltpu.VMEM((C, rows), low),
            pltpu.VMEM((2, 4, 2, share, WIDE), low),
            pltpu.VMEM((5, rows, WIDE), low),
            pltpu.VMEM((rows, width), low),
            pltpu.VMEM((rows, width), low),
            pltpu.VMEM((rows, WIDE), jnp.float32),
            pltpu.VMEM((2, 4 * FRAMES, C), jnp.float32),
            pltpu.VMEM((2, share, WIDE), jnp.float32),
            pltpu.VMEM((4, rows, width), low),
            pltpu.SemaphoreType.DMA((6,)),
            pltpu.SemaphoreType.DMA((32,)),
            pltpu.SemaphoreType.DMA((32,)),
            pltpu.SemaphoreType.DMA((slots, 18)),
            pltpu.SemaphoreType.DMA((taken, 18)),
            pltpu.SemaphoreType.DMA((2,)),
            pltpu.SemaphoreType.DMA((4,)),
            pltpu.SemaphoreType.DMA((12, 2)),
            pltpu.SemaphoreType.DMA((5,)),
            pltpu.SemaphoreType.DMA((2,)),
            pltpu.SemaphoreType.DMA((4,)),
            pltpu.SemaphoreType.DMA((3,)),
        ],
        compiler_params=pltpu.CompilerParams(
            collective_id=1, has_side_effects=True, vmem_limit_bytes=63 << 20
        ),
    )(whole, q_all, pt_all, streams, qk, values, slopes, moved_part, joined)


def gather_plain(shards):
    units, share, wide = shards.shape
    whole = lax.all_gather(shards, MIXED, axis=1, tiled=True)
    return whole.reshape(units, lax.axis_size("tensor"), C, wide)


def reduce_plain(turned, parts):
    reduced = []
    for turn in range(UNITS):
        pairs = [(turned[(turn + turn // 5) // 2], parts[turn])]
        if turn in (4, 6, 8):
            extra = (turn - 4) // 2
            pairs.append((turned[5 + extra], parts[UNITS + extra]))
        whole = sum(
            jnp.einsum("kr,trn->tkn", left, right, preferred_element_type=jnp.float32)
            for left, right in pairs
        )
        whole = whole.astype(jnp.bfloat16).reshape(-1, whole.shape[2])
        reduced.append(
            lax.psum_scatter(whole, MIXED, scatter_dimension=0, tiled=True).astype(jnp.float32)
        )
    return jnp.stack(reduced, 0)


def by_pixels(values, tensor_size):
    slots, frames, width, pixels = values.shape
    own = pixels // tensor_size
    return jnp.transpose(values, (3, 0, 1, 2)).reshape(tensor_size, own * slots * frames, width)


def exchange(parts):
    return lax.all_to_all(parts, "tensor", 0, 0, tiled=True)


def back_to_channels(arrived, slots, pixels):
    width = arrived.shape[2]
    return jnp.transpose(arrived.reshape(pixels, slots, FRAMES, width), (1, 2, 3, 0))


def group_total(values):
    width = values.shape[0]
    size = C // GROUPS
    grouped = values.reshape(width // size, size, 1)
    summed = jnp.sum(grouped, axis=1, keepdims=True)
    return jnp.broadcast_to(summed, grouped.shape).reshape(width, 1)


def enter_kernel(
    latent_ref,
    cot_ref,
    flag_ref,
    gain_ref,
    shift_ref,
    in_ref,
    qkv_ref,
    out_ref,
    up_ref,
    down_ref,
    proj_ref,
    sent_ref,
    moved_ref,
    shards_ref,
    centre_ref,
    inverse_ref,
    bias_ref,
    rows_buf,
):
    frames, width, pixels = latent_ref.shape[1:]
    cells = frames * pixels * (C // GROUPS)
    shards_ref[0, :, 0:width] = qkv_ref[0, 0]
    shards_ref[0, :, width:] = qkv_ref[0, 1]
    shards_ref[1, :, 0:width] = qkv_ref[0, 2]
    shards_ref[1, :, width:] = in_ref[...]
    shards_ref[2, :, 0:width] = qkv_ref[1, 0]
    shards_ref[2, :, width:] = qkv_ref[1, 1]
    shards_ref[3, :, 0:width] = qkv_ref[1, 2]
    shards_ref[3, :, width:] = out_ref[0]
    shards_ref[4, :, 0:width] = out_ref[1]
    shards_ref[4, :, width:] = proj_ref[...]
    for half in range(2):
        lanes = slice(half * WIDE, (half + 1) * WIDE)
        shards_ref[5 + half] = up_ref[:, lanes]
        shards_ref[7 + half] = down_ref[:, lanes]

    def frame_sum(use):
        def one(f, carry):
            return carry + use(f)

        total = lax.fori_loop(0, frames, one, jnp.zeros((width, pixels), jnp.float32))
        return jnp.sum(total, axis=1, keepdims=True)

    def values(f):
        return latent_ref[0, f].astype(jnp.float32)

    centre = group_total(frame_sum(values)) / cells
    spread_sum = group_total(frame_sum(lambda f: (values(f) - centre) * (values(f) - centre)))
    inverse = lax.rsqrt(spread_sum / cells + 1e-06)
    centre_ref[...] = centre
    inverse_ref[...] = inverse
    flag = (flag_ref[0] > 0).astype(jnp.float32)

    def masked(f):
        return cot_ref[0, f].astype(jnp.float32) * flag

    bias_ref[...] = frame_sum(masked)
    own = pixels // 4 * frames

    def rows_of(use, target):
        def one(f, carry):
            block = use(f)
            for part in range(3):
                rows_buf[part, pl.ds(f, pixels, stride=frames), :] = block[
                    part * 128 : part * 128 + 128, :
                ].T
            return carry

        lax.fori_loop(0, frames, one, 0)

        def cast(step, carry):
            rows = pl.ds(pl.multiple_of(step * 128, 128), 128)
            t, inside = step // (own // 128), step % (own // 128)
            inner = pl.ds(pl.multiple_of(inside * 128, 128), 128)
            for part in range(3):
                low, high = part * 128, min(part * 128 + 128, width)
                target[t, inner, low:high] = rows_buf[part, rows, 0 : high - low].astype(
                    jnp.bfloat16
                )
            return carry

        lax.fori_loop(0, 4 * own // 128, cast, 0)

    def padded(block):
        return jnp.concatenate([block, jnp.zeros((384 - width, pixels), jnp.float32)], 0)

    gain, shift = gain_ref[...], shift_ref[...]
    rows_of(lambda f: padded((values(f) - centre) * inverse * gain + shift), sent_ref)
    rows_of(lambda f: padded(masked(f)), moved_ref)


def enter(latent, cotangent, flags, gain, shift, w_in, w_qkv, w_out, w_up, w_down, w_proj):
    slots, frames, width, pixels = latent.shape
    share, rows = w_in.shape[0], pixels // 4 * frames
    near = pl.BlockSpec(memory_space=pltpu.VMEM)
    column = jax.ShapeDtypeStruct((width, 1), jnp.float32)
    low = jnp.bfloat16
    return pl.pallas_call(
        enter_kernel,
        in_specs=[near, near, pl.BlockSpec(memory_space=pltpu.SMEM)] + [near] * 8,
        out_specs=[near] * 6,
        out_shape=[
            jax.ShapeDtypeStruct((4, rows, width), low),
            jax.ShapeDtypeStruct((4, rows, width), low),
            jax.ShapeDtypeStruct((UNITS, share, WIDE), low),
            column,
            column,
            column,
        ],
        scratch_shapes=[pltpu.VMEM((3, 4 * rows, 128), jnp.float32)],
        compiler_params=pltpu.CompilerParams(vmem_limit_bytes=48 << 20),
    )(
        latent,
        cotangent,
        flags,
        gain.reshape(width, 1),
        shift.reshape(width, 1),
        w_in,
        jnp.transpose(w_qkv, (0, 2, 1, 3)),
        jnp.transpose(w_out, (0, 2, 1)),
        w_up,
        w_down.T,
        w_proj,
    )


def leave_kernel(
    grad_ref,
    moved_ref,
    latent_ref,
    cot_ref,
    flag_ref,
    gain_ref,
    centre_ref,
    inverse_ref,
    reduced_ref,
    output_ref,
    latent_grad_ref,
    gain_grad_ref,
    shift_grad_ref,
    in_ref,
    qkv_ref,
    out_ref,
    up_ref,
    down_ref,
    proj_ref,
    rows_buf,
    turned,
):
    frames, width, pixels = latent_ref.shape[1:]
    cells = frames * pixels * (C // GROUPS)
    for block in range(2):
        for part in range(2):
            qkv_ref[block, part] = reduced_ref[7 - 2 * block, :, part * width : (part + 1) * width]
        qkv_ref[block, 2] = reduced_ref[8 - 2 * block, :, 0:width]
    in_ref[...] = reduced_ref[8, :, width:]
    out_ref[0] = reduced_ref[6, :, width:]
    out_ref[1] = reduced_ref[4, :, 0:width]
    proj_ref[...] = reduced_ref[4, :, width:]
    for half in range(2):
        lanes = slice(half * WIDE, (half + 1) * WIDE)
        up_ref[:, lanes] = reduced_ref[3 - half]
        down_ref[:, lanes] = reduced_ref[1 - half]

    own = pixels // 4 * frames

    def spread_rows(source):
        def cast(step, carry):
            rows = pl.ds(pl.multiple_of(step * 128, 128), 128)
            t, inside = step // (own // 128), step % (own // 128)
            inner = pl.ds(pl.multiple_of(inside * 128, 128), 128)
            for part in range(3):
                low, high = part * 128, min(part * 128 + 128, width)
                rows_buf[part, rows, 0 : high - low] = source[t, inner, low:high].astype(
                    jnp.float32
                )
            return carry

        lax.fori_loop(0, 4 * own // 128, cast, 0)

    def frame(f):
        rows = pl.ds(f, pixels, stride=frames)
        turned_parts = [rows_buf[part, rows, :].T for part in range(3)]
        return jnp.concatenate(turned_parts, 0)[0:width, :]

    def hat(f):
        return (latent_ref[0, f].astype(jnp.float32) - centre_ref[...]) * inverse_ref[...]

    flag = (flag_ref[0] > 0).astype(jnp.float32)
    rows_buf[...] = jnp.zeros_like(rows_buf)
    spread_rows(moved_ref)

    def finish(f, carry):
        start = latent_ref[0, f].astype(jnp.float32)
        output_ref[0, f] = (start + flag * frame(f)).astype(jnp.bfloat16)
        return carry

    lax.fori_loop(0, frames, finish, 0)
    spread_rows(grad_ref)
    zero = jnp.zeros((width, pixels), jnp.float32)

    def gather(f, carry):
        grad = frame(f)
        turned[f] = grad
        return carry[0] + grad * hat(f), carry[1] + grad

    by_gain, by_shift = lax.fori_loop(0, frames, gather, (zero, zero))
    gain_sum = jnp.sum(by_gain, axis=1, keepdims=True)
    shift_sum = jnp.sum(by_shift, axis=1, keepdims=True)
    gain_grad_ref[...] = gain_sum
    shift_grad_ref[...] = shift_sum
    gain = gain_ref[...]
    first = group_total(gain * shift_sum) / cells
    second = group_total(gain * gain_sum) / cells

    def back(f, carry):
        grad = inverse_ref[...] * (turned[f] * gain - first - hat(f) * second)
        latent_grad_ref[0, f] = cot_ref[0, f].astype(jnp.float32) + grad
        return carry

    lax.fori_loop(0, frames, back, 0)


def leave(grad, moved, latent, cotangent, flags, gain, centre, inverse, reduced):
    slots, frames, width, pixels = latent.shape
    rows, share = pixels // 4 * frames, reduced.shape[1]
    near = pl.BlockSpec(memory_space=pltpu.VMEM)
    real = jnp.float32
    column = jax.ShapeDtypeStruct((width, 1), real)
    made = pl.pallas_call(
        leave_kernel,
        in_specs=[near] * 4 + [pl.BlockSpec(memory_space=pltpu.SMEM)] + [near] * 4,
        out_specs=[near] * 10,
        out_shape=[
            jax.ShapeDtypeStruct(latent.shape, jnp.bfloat16),
            jax.ShapeDtypeStruct(latent.shape, real),
            column,
            column,
            jax.ShapeDtypeStruct((share, width), real),
            jax.ShapeDtypeStruct((2, 3, share, width), real),
            jax.ShapeDtypeStruct((2, share, width), real),
            jax.ShapeDtypeStruct((share, 2 * WIDE), real),
            jax.ShapeDtypeStruct((share, 2 * WIDE), real),
            jax.ShapeDtypeStruct((share, width), real),
        ],
        scratch_shapes=[
            pltpu.VMEM((3, 4 * rows, 128), real),
            pltpu.VMEM((frames, width, pixels), real),
        ],
        compiler_params=pltpu.CompilerParams(vmem_limit_bytes=56 << 20),
    )(
        grad,
        moved,
        latent,
        cotangent,
        flags,
        gain.reshape(width, 1),
        centre,
        inverse,
        reduced,
    )
    output, latent_grad, gain_grad, shift_grad, g_in, g_qkv, g_out, g_up, g_down, g_proj = made
    weights = (
        g_in,
        jnp.transpose(g_qkv, (0, 2, 1, 3)),
        jnp.transpose(g_out, (0, 2, 1)),
        g_up,
        g_down.T,
        g_proj,
    )
    return output, latent_grad, gain_grad.reshape(width), shift_grad.reshape(width), weights


def kernel_body(
    latent,
    clip_flags,
    cotangent,
    norm_gain,
    norm_shift,
    channel_bias,
    hidden_bias,
    weight_in,
    weight_qkv,
    weight_out,
    weight_up,
    weight_down,
    weight_proj,
):
    width = latent.shape[2]
    side = jnp.concatenate
    params = side([norm_gain, norm_shift, channel_bias, jnp.zeros((3, width), jnp.float32)], 0)
    params = side([params, hidden_bias.reshape(4, width), jnp.zeros((4, width), jnp.float32)], 0)
    sent, moved_sent, shards, centre, inverse, bias_moved = enter(
        latent,
        cotangent,
        clip_flags,
        norm_gain[0],
        norm_shift[0],
        weight_in,
        weight_qkv,
        weight_out,
        weight_up,
        weight_down,
        weight_proj,
    )
    grad_moved = exchange(moved_sent)
    moved_part = jnp.pad(grad_moved, ((0, 0), (0, 0), (width, 0)))
    whole, q_all, pt_all, streams, qk_all, v_all, slopes, moved, joined = forward_all(
        shards, sent, params, make_positions()
    )
    moved_back = exchange(moved)
    reduced, q_all, pt_all, unused, unused, grad_back, sums, hidden_sums = backward_all(
        whole, q_all, pt_all, streams, qk_all, v_all, slopes, moved_part, joined
    )
    output, latent_grad, group_gain, group_shift, weights = leave(
        grad_back,
        moved_back,
        latent,
        cotangent,
        clip_flags,
        norm_gain[0],
        centre,
        inverse,
        reduced,
    )
    vectors = jnp.transpose(sums[:10].reshape(10, 4, width), (1, 0, 2)).reshape(4, 10 * width)
    vectors = side([vectors, hidden_sums[:, :2].reshape(4, 2 * WIDE)], 1)
    vectors = jnp.sum(exchange(vectors), 0)
    local = side([vectors, group_gain, group_shift, bias_moved.reshape(width)])
    total = local
    count = lax.axis_size("dp")
    for bit in range(count.bit_length() - 1):
        total = total + lax.ppermute(total, "dp", [(i, i ^ (1 << bit)) for i in range(count)])
    channel, hidden_grad = total[: 10 * width].reshape(10, width), total[10 * width : 14 * width]
    group = total[14 * width :].reshape(3, width)
    return (
        output,
        latent_grad,
        side([group[0:1], channel[0:3]], 0),
        side([group[1:2], channel[3:6]], 0),
        side([channel[6:10], group[2:3]], 0),
        hidden_grad,
    ) + weights


def body(
    latent,
    clip_flags,
    cotangent,
    norm_gain,
    norm_shift,
    channel_bias,
    hidden_bias,
    weight_in,
    weight_qkv,
    weight_out,
    weight_up,
    weight_down,
    weight_proj,
):
    tensor_size = lax.axis_size("tensor")
    slots, frames, width, pixels = latent.shape
    share = weight_in.shape[0]
    hidden_width = hidden_bias.shape[0]
    flags = (clip_flags > 0)[:, None, None, None]

    wide = 2 * width

    shards = []
    side = jnp.concatenate
    for block in range(2):
        shards.append(weight_qkv[block, :, :2].reshape(share, wide))
        other = weight_in if block == 0 else weight_out[0].T
        shards.append(side([weight_qkv[block, :, 2], other], 1))
    shards.append(side([weight_out[1].T, weight_proj], 1))
    shards += [weight_up[:, :wide], weight_up[:, wide:]]
    down_turned = weight_down.T
    shards += [down_turned[:, :wide], down_turned[:, wide:]]
    shards = jnp.stack(shards, 0)
    params = jnp.zeros((24, width), jnp.float32)
    params = params.at[:13].set(side([norm_gain, norm_shift, channel_bias], 0))
    params = params.at[16:20].set(hidden_bias.reshape(4, width))

    start = latent.astype(jnp.float32)
    cot = cotangent.astype(jnp.float32)
    group_width = C // GROUPS
    grouped = start.reshape(slots, frames, width // group_width, group_width, pixels)
    group_centre = jnp.mean(grouped, axis=(1, 3, 4), keepdims=True)
    offset = grouped - group_centre
    group_inverse = lax.rsqrt(jnp.mean(offset * offset, axis=(1, 3, 4), keepdims=True) + 1e-06)
    group_hat = (offset * group_inverse).reshape(start.shape)
    normed = group_hat * norm_gain[0][:, None] + norm_shift[0][:, None]
    sent = by_pixels(normed.astype(jnp.bfloat16), tensor_size)
    rows = sent.shape[1]

    grad_moved_local = jnp.where(flags, cot, 0.0)
    bias_moved = jnp.sum(grad_moved_local, axis=(0, 1, 3))
    grad_moved = exchange(by_pixels(grad_moved_local.astype(jnp.bfloat16), tensor_size))

    empty = jnp.zeros((tensor_size, rows, width), jnp.bfloat16)
    moved_part = side([empty, grad_moved], 2)
    arrived = exchange(sent)
    inputs_in = jnp.transpose(arrived, (1, 0, 2)).reshape(rows, C)
    packed = lax.all_gather(params, "tensor", axis=0, tiled=False)
    joined = jnp.transpose(packed[:, :13], (1, 0, 2)).reshape(13, C)
    gains, shifts, biases = joined[:4], joined[4:8], joined[8:]
    hidden_full = packed[:, 16:20].reshape(tensor_size, 2 * wide)
    whole = gather_plain(shards)
    full_qk = (whole[0], whole[2])
    full_v = (whole[1, :, :, :width], whole[3, :, :, :width])
    full_in = whole[1, :, :, width:]
    full_out = (whole[3, :, :, width:], whole[4, :, :, :width])
    full_proj = whole[4, :, :, width:]
    full_up = (whole[5], whole[6])
    full_down = (whole[7], whole[8])

    def join(parts):
        return jnp.transpose(parts, (1, 0, 2)).reshape(rows, parts.shape[0] * parts.shape[2])

    stream = join(spread(inputs_in, full_in)) + biases[0]
    position = jnp.tile(make_positions(), (rows // FRAMES, 1))
    kept = []
    for block in range(2):
        hat, inverse = layer_stats(stream)
        lifted = (hat * gains[1 + block] + shifts[1 + block] + position).astype(jnp.bfloat16)
        qk = spread(lifted, full_qk[block]).astype(jnp.bfloat16)
        values = spread(lifted, full_v[block]).astype(jnp.bfloat16)
        attended = attend(qk, values)
        stream = stream + collapse(attended, full_out[block]) + biases[1 + block]
        kept.append((hat, inverse, lifted.T, qk, values, attended))
    hat_feed, inverse_feed = layer_stats(stream)
    inputs_up = (hat_feed * gains[3] + shifts[3]).astype(jnp.bfloat16)
    pre_act = [
        spread(inputs_up, full_up[half])
        + hidden_full[:, None, half * wide : half * wide + wide]
        for half in range(2)
    ]
    slopes = [
        jax.vjp(partial(jax.nn.gelu, approximate=False), pre)[1](jnp.ones_like(pre))[0]
        for pre in pre_act
    ]
    hidden = [jax.nn.gelu(pre, approximate=False).astype(jnp.bfloat16) for pre in pre_act]
    stream = stream + collapse(hidden[0], full_down[0]) + collapse(hidden[1], full_down[1])
    stream = stream + biases[3]
    inputs_proj = stream.astype(jnp.bfloat16)
    moved = spread(inputs_proj, full_proj) + biases[4].reshape(tensor_size, 1, width)
    moved = moved.astype(jnp.bfloat16)

    bias_grads = [None] * 4
    gain_grads = [None] * 3
    shift_grads = [None] * 3
    turned, parts = [None] * 8, [None] * 12
    turned[1], turned[5], turned[7] = inputs_up.T, inputs_proj.T, inputs_in.T
    parts[0], parts[1] = hidden[1], hidden[0]
    parts[9] = moved_part
    grad_stream = collapse(grad_moved, full_proj)
    bias_grads[3] = jnp.sum(grad_stream, 0)
    grad_low = grad_stream.astype(jnp.bfloat16)
    turned[0] = grad_low.T
    hidden_grads = [None, None]
    grad_normed = 0.0
    for half in (1, 0):
        grad_hidden = spread(grad_low, full_down[half])
        grad_pre = grad_hidden * slopes[half]
        hidden_grads[half] = jnp.sum(grad_pre, 1)
        parts[3 - half] = grad_pre.astype(jnp.bfloat16)
        grad_normed = grad_normed + collapse(parts[3 - half], full_up[half])
    hidden_grad = side(hidden_grads, 1)
    grad_layer, gain_grads[2], shift_grads[2] = layer_back(
        grad_normed, hat_feed, inverse_feed, gains[3]
    )
    grad_stream = grad_stream + grad_layer
    for block in (1, 0):
        hat, inverse, lifted_turned, qk, values, attended = kept[block]
        bias_grads[1 + block] = jnp.sum(grad_stream, 0)
        grad_low = grad_stream.astype(jnp.bfloat16)
        turned[2 if block == 1 else 6] = grad_low.T
        pair = [attended, empty] if block == 1 else [empty, attended]
        parts[4 if block == 1 else 10] = side(pair, 2)
        grad_attended = spread(grad_low, full_out[block]).astype(jnp.bfloat16)
        grad_qk, grad_values = attend_back(qk, values, grad_attended)
        turned[3 if block == 1 else 4] = lifted_turned
        parts[6 if block == 1 else 8] = side([grad_values, empty], 2)
        parts[5 if block == 1 else 7] = grad_qk
        grad_lifted = collapse(grad_qk, full_qk[block]) + collapse(grad_values, full_v[block])
        grad_layer, gain_grads[block], shift_grads[block] = layer_back(
            grad_lifted, hat, inverse, gains[1 + block]
        )
        grad_stream = grad_stream + grad_layer
    bias_grads[0] = jnp.sum(grad_stream, 0)
    grad_low = grad_stream.astype(jnp.bfloat16)
    grad_low_parts = jnp.transpose(grad_low.reshape(rows, tensor_size, width), (1, 0, 2))
    parts[11] = side([empty, grad_low_parts], 2)
    turned, parts = jnp.stack(turned, 0), jnp.stack(parts, 0)
    reduced = reduce_plain(turned, parts)
    grad_normed = collapse(grad_low_parts, full_in).astype(jnp.bfloat16)
    grad_normed = jnp.transpose(grad_normed.reshape(rows, tensor_size, width), (1, 0, 2))
    arrived_grad = exchange(grad_normed)
    vectors = jnp.stack(gain_grads + shift_grads + bias_grads, 0)

    moved_local = back_to_channels(exchange(moved), slots, pixels).astype(jnp.float32)
    output = jnp.where(flags, start + moved_local, start).astype(jnp.bfloat16)

    qkv_grads = [
        side([reduced[7 - 2 * block], reduced[8 - 2 * block, :, :width]], 1).reshape(share, 3, width)
        for block in range(2)
    ]
    out_grads = [reduced[6, :, width:].T, reduced[4, :, :width].T]
    in_grad, proj_grad = reduced[8, :, width:], reduced[4, :, width:]
    up_grad = side([reduced[3], reduced[2]], 1)
    down_grad = side([reduced[1], reduced[0]], 1)
    grad_normed = back_to_channels(arrived_grad, slots, pixels).astype(jnp.float32)
    scaled = grad_normed * norm_gain[0][:, None]
    scaled_groups = scaled.reshape(grouped.shape)
    hat_groups = group_hat.reshape(grouped.shape)
    first = jnp.mean(scaled_groups, axis=(1, 3, 4), keepdims=True)
    second = jnp.mean(scaled_groups * hat_groups, axis=(1, 3, 4), keepdims=True)
    grad_group = group_inverse * (scaled_groups - first - hat_groups * second)
    latent_grad = cot + grad_group.reshape(start.shape)
    group_gain_grad = jnp.sum(grad_normed * group_hat, axis=(0, 1, 3))
    group_shift_grad = jnp.sum(grad_normed, axis=(0, 1, 3))

    vectors = jnp.transpose(vectors.reshape(10, tensor_size, width), (1, 0, 2))
    vectors = jnp.concatenate([vectors.reshape(tensor_size, 10 * width), hidden_grad], 1)
    vectors = lax.psum_scatter(vectors, "tensor", scatter_dimension=0, tiled=False)
    sums = lax.psum(
        jnp.concatenate([vectors, group_gain_grad, group_shift_grad, bias_moved]), "dp"
    )
    channel_sums = sums[: 10 * width].reshape(10, width)
    hidden_bias_grad = sums[10 * width : 10 * width + hidden_width]
    local_sums = sums[10 * width + hidden_width :].reshape(3, width)
    gain_grad = jnp.concatenate([local_sums[0:1], channel_sums[0:3]], 0)
    shift_grad = jnp.concatenate([local_sums[1:2], channel_sums[3:6]], 0)
    channel_bias_grad = jnp.concatenate([channel_sums[6:10], local_sums[2:3]], 0)
    return (
        output,
        latent_grad,
        gain_grad,
        shift_grad,
        channel_bias_grad,
        hidden_bias_grad,
        in_grad,
        jnp.stack(qkv_grads, 0),
        jnp.stack(out_grads, 0),
        up_grad,
        down_grad.T,
        proj_grad,
    )


def solution(mesh):
    placed = (
        P("dp", None, "tensor", None),
        P("dp"),
        P("dp", None, "tensor", None),
        P(None, "tensor"),
        P(None, "tensor"),
        P(None, "tensor"),
        P("tensor"),
        P("dp", "tensor"),
        P(None, "dp", None, "tensor"),
        P(None, "tensor", "dp"),
        P("dp", "tensor"),
        P("tensor", "dp"),
        P("dp", "tensor"),
    )
    kernels_fit = (mesh.shape["dp"], mesh.shape["tensor"]) == (8, 4)
    return jax.shard_map(
        kernel_body if kernels_fit else body,
        mesh=mesh,
        in_specs=placed,
        out_specs=(
            P("dp", None, "tensor", None),
            P("dp", None, "tensor", None),
            P(None, "tensor"),
            P(None, "tensor"),
            P(None, "tensor"),
            P("tensor"),
            P("dp", "tensor"),
            P(None, "dp", None, "tensor"),
            P(None, "tensor", "dp"),
            P("dp", "tensor"),
            P("tensor", "dp"),
            P("dp", "tensor"),
        ),
        check_vma=False,
    )
```

```python
from functools import partial
import math

import jax
import jax.numpy as jnp
from jax import lax
from jax.experimental import pallas as pl
from jax.experimental.pallas import tpu as pltpu
from jax.sharding import PartitionSpec as P

C = 1280
GROUPS = 32
FRAMES = 16
HEAD = 160
BLOCK = 128
MIXED = ("tensor", "dp")


def spread(rows, weight):
    return jnp.einsum("rk,tkn->trn", rows, weight, preferred_element_type=jnp.float32)


def collapse(parts, weight):
    return jnp.einsum("trn,tkn->rk", parts, weight, preferred_element_type=jnp.float32)


def make_positions():
    channel_ids = jnp.arange(C)
    pair_rate = jnp.exp((channel_ids // 2).astype(jnp.float32) * (-2.0 * math.log(10000.0) / C))
    angles = jnp.arange(FRAMES).astype(jnp.float32)[:, None] * pair_rate[None, :]
    return jnp.where(channel_ids[None, :] % 2 == 0, jnp.sin(angles), jnp.cos(angles))


def layer_stats(stream):
    centre = jnp.mean(stream, axis=1, keepdims=True)
    offset = stream - centre
    inverse = lax.rsqrt(jnp.mean(offset * offset, axis=1, keepdims=True) + 1e-05)
    return offset * inverse, inverse


def layer_back(grad_out, normal_part, inverse, gain):
    scaled = grad_out * gain
    first = jnp.mean(scaled, axis=1, keepdims=True)
    second = jnp.mean(scaled * normal_part, axis=1, keepdims=True)
    grad_in = inverse * (scaled - first - normal_part * second)
    return grad_in, jnp.sum(grad_out * normal_part, 0), jnp.sum(grad_out, 0)


def dot_rows(left, right):
    return lax.dot_general(left, right, (((1,), (1,)), ((), ())), preferred_element_type=jnp.float32)


def dot_plain(left, right):
    return lax.dot_general(left, right, (((1,), (0,)), ((), ())), preferred_element_type=jnp.float32)


def dot_first(left, right):
    return lax.dot_general(left, right, (((0,), (0,)), ((), ())), preferred_element_type=jnp.float32)


def same_pixel(block):
    row = lax.broadcasted_iota(jnp.int32, (block, block), 0) // FRAMES
    col = lax.broadcasted_iota(jnp.int32, (block, block), 1) // FRAMES
    return row == col


def head_probs(query, key, same, scale):
    scores = jnp.where(same, dot_rows(query, key) * scale, -1e30)
    top = jnp.max(scores, axis=1, keepdims=True)
    weights = jnp.where(same, jnp.exp(scores - top), 0.0)
    return weights / jnp.sum(weights, axis=1, keepdims=True)


def attend_kernel(scale, qk_ref, v_ref, out_ref):
    rows, width = out_ref.shape[1], out_ref.shape[2]
    block = min(BLOCK, rows)
    same = same_pixel(block)
    for start in range(0, rows, block):
        for head in range(width // HEAD):
            here, low = slice(start, start + block), head * HEAD
            query = qk_ref[0, here, low : low + HEAD]
            key = qk_ref[0, here, width + low : width + low + HEAD]
            value = v_ref[0, here, low : low + HEAD]
            probs = head_probs(query, key, same, scale).astype(jnp.bfloat16)
            out_ref[0, here, low : low + HEAD] = dot_plain(probs, value).astype(jnp.bfloat16)


def part_spec(array):
    return pl.BlockSpec((1,) + array.shape[1:], lambda t: (t, 0, 0))


def attend(qk, values):
    return pl.pallas_call(
        partial(attend_kernel, 1.0 / math.sqrt(HEAD)),
        grid=(qk.shape[0],),
        in_specs=[part_spec(qk), part_spec(values)],
        out_specs=part_spec(values),
        out_shape=jax.ShapeDtypeStruct(values.shape, jnp.bfloat16),
        compiler_params=pltpu.CompilerParams(vmem_limit_bytes=32 << 20),
    )(qk, values)


def attend_back_kernel(scale, qk_ref, v_ref, grad_ref, dqk_ref, dv_ref):
    rows, width = grad_ref.shape[1], grad_ref.shape[2]
    block = min(BLOCK, rows)
    same = same_pixel(block)
    for start in range(0, rows, block):
        for head in range(width // HEAD):
            here, low = slice(start, start + block), head * HEAD
            query = qk_ref[0, here, low : low + HEAD]
            key = qk_ref[0, here, width + low : width + low + HEAD]
            value = v_ref[0, here, low : low + HEAD]
            grad = grad_ref[0, here, low : low + HEAD]
            probs = head_probs(query, key, same, scale)
            grad_probs = dot_rows(grad, value)
            centred = jnp.sum(probs * grad_probs, axis=1, keepdims=True)
            grad_raw = (probs * (grad_probs - centred) * scale).astype(jnp.bfloat16)
            dqk_ref[0, here, low : low + HEAD] = dot_plain(grad_raw, key).astype(jnp.bfloat16)
            dqk_ref[0, here, width + low : width + low + HEAD] = dot_first(grad_raw, query).astype(
                jnp.bfloat16
            )
            dv_ref[0, here, low : low + HEAD] = dot_first(probs.astype(jnp.bfloat16), grad).astype(
                jnp.bfloat16
            )


def attend_back(qk, values, grad):
    return pl.pallas_call(
        partial(attend_back_kernel, 1.0 / math.sqrt(HEAD)),
        grid=(qk.shape[0],),
        in_specs=[part_spec(qk), part_spec(values), part_spec(values)],
        out_specs=[part_spec(qk), part_spec(values)],
        out_shape=[
            jax.ShapeDtypeStruct(qk.shape, jnp.bfloat16),
            jax.ShapeDtypeStruct(values.shape, jnp.bfloat16),
        ],
        compiler_params=pltpu.CompilerParams(vmem_limit_bytes=32 << 20),
    )(qk, values, grad)


UNITS = 9
WIDE = 640
SLOTS_IN_FLIGHT = 6
SLOTS_RECEIVED = 4
ROWS_A = 96
MESH_ID = pl.DeviceIdType.MESH


class Place:
    def __init__(self):
        dp, tn = lax.axis_index("dp"), lax.axis_index("tensor")
        self.z, self.x = dp // 2, dp % 2
        self.y, self.c = tn // 2, tn % 2
        self.far_x, self.far_y = 1 - self.x, 1 - self.y
        self.to = {
            "x": (self.z * 2 + self.far_x, tn),
            "y": (dp, self.far_y * 2 + self.c),
            "core": (dp, self.y * 2 + 1 - self.c),
            "cross": (dp, self.far_y * 2 + 1 - self.c),
            "up": (dp + 2, tn),
            "down": (dp - 2, tn),
        }
        self.has_up = self.z < 3
        self.has_down = self.z > 0

    def greet(self):
        barrier = pltpu.get_barrier_semaphore()

        def hello(name):
            pl.semaphore_signal(barrier, inc=1, device_id=self.to[name], device_id_type=MESH_ID)

        for name in ("x", "y", "core", "cross"):
            hello(name)
        pl.when(self.has_up)(lambda: hello("up"))
        pl.when(self.has_down)(lambda: hello("down"))
        pl.semaphore_wait(barrier, 4 + (6 - self.z) // 4 + (self.z + 3) // 4)


class Plan:
    FIELDS = (
        ("kind", 16),
        ("unit", 16),
        ("t", 4),
        ("aux", 128),
        ("slot", 2),
        ("fresh", 2),
        ("next", 64),
        ("early", 32),
    )

    def __init__(self, per_turn, loads_early=False):
        self.per_turn, self.loads_early = per_turn, loads_early
        self.steps = {}

    def fill(self, turn, steps):
        tiles = [index for index, step in enumerate(steps) if step[1] is not None]
        early = {}
        for order, index in enumerate(tiles):
            if self.loads_early and steps[index][0] == 1:
                early[tiles[order - 1] if order else index] = 1 + steps[index][3] * 4 + steps[index][2]
        for index, (kind, unit, t, aux) in enumerate(steps):
            slot = fresh = following = 0
            if unit is not None:
                order = tiles.index(index)
                slot, fresh = order % 2, int(order == 0)
                if order + 1 < len(tiles):
                    later = steps[tiles[order + 1]]
                    following = 1 + later[1] * 4 + later[2]
            values = (kind, unit or 0, t, aux, slot, fresh, following, early.get(index, 0))
            code, scale = 0, 1
            for (name, size), value in zip(self.FIELDS, values):
                assert 0 <= value < size
                code += scale * value
                scale *= size
            place = turn * self.per_turn + index * self.per_turn // len(steps)
            assert place not in self.steps
            self.steps[place] = code

    def code(self, place):
        code = jnp.int32(0)
        for where, value in self.steps.items():
            code = jnp.where(place == where, jnp.int32(value), code)
        return code

    def fields(self, code):
        out = {}
        for name, size in self.FIELDS:
            out[name] = code % size
            code = code // size
        return out


def await_bytes(ref, sem):
    pltpu.make_async_copy(ref, ref, sem).wait()


def forward_kernel(
    shard_ref,
    x_ref,
    params_ref,
    position_ref,
    grad_ref,
    whole_ref,
    q_ref,
    pt_ref,
    stream_out_ref,
    qk_ref,
    v_ref,
    slope_ref,
    grad_got,
    moved_ref,
    joined_ref,
    stream,
    xb,
    ptb,
    x_got,
    params_got,
    hidden_bias,
    qkb,
    vb,
    cols,
    slopeb,
    first_rows,
    total,
    wb,
    tile_sem,
    save_sem,
    kept_sem,
    peer_send,
    peer_recv,
    local_sem,
    send_sem,
    recv_sem,
    core_sem,
):
    at = Place()
    z, x, y, c = at.z, at.x, at.y, at.c
    share = shard_ref.shape[1]
    cut = (pl.ds(0, ROWS_A), pl.ds(ROWS_A, share - ROWS_A))
    kinds = {"up": 0, "down": 1, "x": 2, "y": 3, "core": 4}
    at.greet()

    def send(unit, colour, yy, zz, xx, kind, own=False):
        place = whole_ref.at[unit, yy, c, zz, xx, cut[colour]]
        pltpu.make_async_remote_copy(
            src_ref=shard_ref.at[unit, cut[colour]] if own else place,
            dst_ref=place,
            send_sem=send_sem.at[unit, colour, kinds[kind]],
            recv_sem=recv_sem.at[unit, colour, yy, zz, xx],
            device_id=at.to[kind],
            device_id_type=MESH_ID,
        ).start()

    def arrived(unit, colour, yy, zz, xx):
        await_bytes(
            whole_ref.at[unit, yy, c, zz, xx, cut[colour]], recv_sem.at[unit, colour, yy, zz, xx]
        )

    def own_copy(unit):
        return pltpu.make_async_copy(
            shard_ref.at[unit], whole_ref.at[unit, y, c, z, x], local_sem.at[unit]
        )

    def to_core(unit, part):
        if part == 2:
            place = whole_ref.at[unit, :, c, :, :, cut[1]]
        else:
            place = whole_ref.at[unit, y if part == 0 else at.far_y, c, :, :, cut[0]]
        return pltpu.make_async_remote_copy(
            src_ref=place,
            dst_ref=place,
            send_sem=send_sem.at[unit, part // 2, 4],
            recv_sem=core_sem.at[unit, part],
            device_id=at.to["core"],
            device_id_type=MESH_ID,
        )

    def from_z(unit, colour, step, yy):
        @pl.when(z >= step)
        def _():
            zz = z - step
            arrived(unit, colour, yy, zz, x)
            pl.when(at.has_up)(lambda: send(unit, colour, yy, zz, x, "up"))
            send(unit, colour, yy, zz, x, "x")
            if colour == 0:
                send(unit, colour, yy, zz, x, "y")

        @pl.when(z + step <= 3)
        def _():
            zz = z + step
            arrived(unit, colour, yy, zz, x)
            pl.when(at.has_down)(lambda: send(unit, colour, yy, zz, x, "down"))
            send(unit, colour, yy, zz, x, "x")
            if colour == 0:
                send(unit, colour, yy, zz, x, "y")

    def from_x(unit, step):
        def one(zz):
            arrived(unit, 0, y, zz, at.far_x)
            send(unit, 0, y, zz, at.far_x, "y")

        if step == 0:
            one(z)
        else:
            pl.when(z >= step)(lambda: one(z - step))
            pl.when(z + step <= 3)(lambda: one(z + step))

    def stage0(unit):
        own_copy(unit).start()
        pl.when(at.has_up)(lambda: send(unit, 0, y, z, x, "up", True))
        pl.when(at.has_down)(lambda: send(unit, 0, y, z, x, "down", True))
        send(unit, 1, y, z, x, "y", True)
        send(unit, 0, y, z, x, "x", True)
        pl.when(at.has_up)(lambda: send(unit, 1, y, z, x, "up", True))
        pl.when(at.has_down)(lambda: send(unit, 1, y, z, x, "down", True))
        send(unit, 0, y, z, x, "y", True)
        send(unit, 1, y, z, x, "x", True)

    def stage1(unit):
        from_z(unit, 0, 1, y)
        arrived(unit, 1, at.far_y, z, x)
        pl.when(at.has_up)(lambda: send(unit, 1, at.far_y, z, x, "up"))
        pl.when(at.has_down)(lambda: send(unit, 1, at.far_y, z, x, "down"))
        send(unit, 1, at.far_y, z, x, "x")
        from_z(unit, 1, 1, y)
        from_x(unit, 0)

    def stage2(unit):
        from_z(unit, 0, 2, y)
        from_z(unit, 1, 1, at.far_y)
        from_z(unit, 1, 2, y)
        from_x(unit, 1)

    def stage3(unit):
        from_z(unit, 0, 3, y)
        from_z(unit, 1, 2, at.far_y)
        from_z(unit, 1, 3, y)
        from_x(unit, 2)

    def stage4(unit):
        from_z(unit, 1, 3, at.far_y)
        from_x(unit, 3)
        own_copy(unit).wait()
        to_core(unit, 0).start()

    def stage5(unit):
        for zz in range(4):
            for xx in range(2):
                arrived(unit, 0, at.far_y, zz, xx)
        to_core(unit, 1).start()
        for zz in range(4):
            for yy in range(2):
                arrived(unit, 1, yy, zz, at.far_x)
        to_core(unit, 2).start()

    def stage6(unit):
        other = 1 - c
        await_bytes(whole_ref.at[unit, y, other, :, :, cut[0]], core_sem.at[unit, 0])
        await_bytes(whole_ref.at[unit, at.far_y, other, :, :, cut[0]], core_sem.at[unit, 1])
        await_bytes(whole_ref.at[unit, :, other, :, :, cut[1]], core_sem.at[unit, 2])
        for colour in range(2):
            rows = cut[colour]
            await_bytes(whole_ref.at[unit, :, c, :, :, rows], send_sem.at[unit, colour, 4])
            whole_x = whole_ref.at[unit, 0, c, :, 0, rows] if colour == 0 else None
            if colour == 0:
                await_bytes(whole_x, send_sem.at[unit, 0, 2])
                await_bytes(whole_ref.at[unit, 0, c, :, :, rows], send_sem.at[unit, 0, 3])
            else:
                await_bytes(whole_ref.at[unit, 0, c, :, :, rows], send_sem.at[unit, 1, 2])
                await_bytes(whole_ref.at[unit, 0, c, 0, 0, rows], send_sem.at[unit, 1, 3])
            for level in range(3):

                def ups(level=level):
                    if colour == 0:
                        ref = whole_ref.at[unit, 0, c, pl.ds(0, level + 1), 0, rows]
                    else:
                        ref = whole_ref.at[unit, :, c, pl.ds(0, level + 1), 0, rows]
                    return ref

                pl.when(z == level)(
                    lambda level=level: await_bytes(ups(level), send_sem.at[unit, colour, 0])
                )
                pl.when(z == 3 - level)(
                    lambda level=level: await_bytes(ups(level), send_sem.at[unit, colour, 1])
                )

    stages = (stage0, stage1, stage2, stage3, stage4, stage5, stage6)

    rows_all, width = x_ref.shape[1], x_ref.shape[2]
    half_rows = rows_all // 2
    scale = 1.0 / math.sqrt(HEAD)
    own_t = y * 2 + c

    def save_now(source, target):
        copy = pltpu.make_async_copy(source, target, save_sem.at[0])
        copy.start()
        copy.wait()

    peers = (("y", at.far_y * 2 + c), ("core", y * 2 + 1 - c), ("cross", at.far_y * 2 + 1 - c))

    def peer_copies(index):
        kind, t = peers[index]
        target = {"device_id": at.to[kind], "device_id_type": MESH_ID}
        return (
            pltpu.make_async_remote_copy(
                src_ref=params_ref,
                dst_ref=params_got.at[own_t],
                send_sem=peer_send.at[0, index],
                recv_sem=peer_recv.at[0, index],
                **target,
            ),
            pltpu.make_async_remote_copy(
                src_ref=x_ref.at[t],
                dst_ref=x_got.at[own_t],
                send_sem=peer_send.at[1, index],
                recv_sem=peer_recv.at[1, index],
                **target,
            ),
            pltpu.make_async_remote_copy(
                src_ref=grad_ref.at[t],
                dst_ref=grad_got.at[own_t],
                send_sem=peer_send.at[2, index],
                recv_sem=peer_recv.at[2, index],
                **target,
            ),
        )

    own_peer = (
        pltpu.make_async_copy(params_ref, params_got.at[own_t], peer_send.at[0, 3]),
        pltpu.make_async_copy(x_ref.at[own_t], x_got.at[own_t], peer_send.at[1, 3]),
        pltpu.make_async_copy(grad_ref.at[own_t], grad_got.at[own_t], peer_send.at[2, 3]),
    )
    for index in range(3):
        for copy in peer_copies(index):
            copy.start()
    for copy in own_peer:
        copy.start()

    def each(count, size, use):
        def one(step, carry):
            use(pl.ds(pl.multiple_of(step * size, size), size))
            return carry

        lax.fori_loop(0, count, one, 0)

    def tile_load(unit, t, slot):
        return pltpu.make_async_copy(whole_ref.at[unit, t // 2, t % 2], wb.at[slot], tile_sem.at[slot])

    def kept_copies(which, t):
        target = (10, 4, 1, 0)[which]
        copies = [
            pltpu.make_async_copy(cols.at[which, t], q_ref.at[target, t], kept_sem.at[which, t, 0])
        ]
        if which < 2:
            pairs = [(qkb.at[which, t], qk_ref.at[which, t]), (vb.at[which, t], v_ref.at[which, t])]
        else:
            pairs = [(slopeb.at[which - 2, t], slope_ref.at[which - 2, t])]
        for index, (source, target_ref) in enumerate(pairs):
            copies.append(
                pltpu.make_async_copy(source, target_ref, kept_sem.at[which, t, 1 + index])
            )
        return copies

    def do_spread(op):
        matrix = op["slot"]
        t, aux = op["t"], op["aux"]

        def multiply(rows):
            total[rows, :] = dot_plain(xb[rows, :], wb[matrix].reshape(C, WIDE))

        each(2, half_rows, multiply)
        quarter = rows_all // 4

        @pl.when(aux == 0)
        def _():
            def use(rows):
                first_rows[t, rows, :] = total[rows, width:]

            each(4, quarter, use)

        @pl.when((aux == 1) | (aux == 3))
        def _():
            def use(rows):
                qkb[(aux - 1) // 2, t, rows, :] = total[rows, :].astype(jnp.bfloat16)

            each(4, quarter, use)

        @pl.when((aux == 2) | (aux == 4))
        def _():
            def use(rows):
                vb[(aux - 2) // 2, t, rows, :] = total[rows, 0:width].astype(jnp.bfloat16)

            each(4, quarter, use)

        @pl.when((aux == 5) | (aux == 6))
        def _():
            half = aux - 5

            def use(rows):
                pre = total[rows, :] + hidden_bias[t, pl.ds(half, 1), :]
                below = 0.5 * (1.0 + lax.erf(pre * math.sqrt(0.5)))
                cols[2 + half, t, rows, :] = (pre * below).astype(jnp.bfloat16)
                density = jnp.exp(-0.5 * pre * pre) * (1.0 / math.sqrt(2.0 * math.pi))
                slopeb[half, t, rows, :] = (below + pre * density).astype(jnp.bfloat16)

            each(rows_all // 32, 32, use)
            for which in (2, 3):

                @pl.when(half == which - 2)
                def _(which=which):
                    for copy in kept_copies(which, t):
                        copy.start()

        @pl.when(aux == 7)
        def _():
            def use(rows):
                moved_ref[t, rows, :] = (total[rows, width:] + params_got[t, 12:13, :]).astype(
                    jnp.bfloat16
                )

            each(4, quarter, use)

    def do_collapse(op):
        def multiply(rows):
            stream[rows, :] += dot_rows(cols[op["aux"], op["t"], rows, :], wb[op["slot"]].reshape(C, WIDE))

        each(2, half_rows, multiply)

    def do_attention(op):
        block, t = op["aux"], op["t"]
        same = same_pixel(BLOCK)

        def write(place):
            for start in range(0, rows_all, BLOCK):
                here = slice(start, start + BLOCK)
                for head in range(width // HEAD):
                    low = head * HEAD
                    query = qkb[block, t, here, low : low + HEAD]
                    key = qkb[block, t, here, width + low : width + low + HEAD]
                    value = vb[block, t, here, low : low + HEAD]
                    probs = head_probs(query, key, same, scale).astype(jnp.bfloat16)
                    total[here, low : low + HEAD] = dot_plain(probs, value)

        write(0)
        for which in range(2):

            @pl.when(block == which)
            def _(which=which):
                own = slice(width, 2 * width) if which == 0 else slice(0, width)
                other = slice(0, width) if which == 0 else slice(width, 2 * width)

                def use(rows):
                    cols[which, t, rows, own] = total[rows, 0:width].astype(jnp.bfloat16)
                    cols[which, t, rows, other] = jnp.zeros((rows_all // 4, width), jnp.bfloat16)

                each(4, rows_all // 4, use)
                for copy in kept_copies(which, t):
                    copy.start()

    chunk = 4 * FRAMES

    def do_norm(op):
        layer = op["aux"]

        def use(rows):
            @pl.when(layer == 0)
            def _():
                for t in range(4):
                    stream[rows, t * width : (t + 1) * width] = first_rows[t, rows, :]

            values = stream[rows, :] + joined_ref[pl.ds(8 + layer, 1), :]
            stream[rows, :] = values
            centre = jnp.mean(values, axis=1, keepdims=True)
            offset = values - centre
            inverse = lax.rsqrt(jnp.mean(offset * offset, axis=1, keepdims=True) + 1e-05)
            normed = offset * inverse * joined_ref[pl.ds(1 + layer, 1), :]
            normed = normed + joined_ref[pl.ds(5 + layer, 1), :]
            added = jnp.where(layer < 2, position_ref[...], 0.0)
            normed = normed.reshape(chunk // FRAMES, FRAMES, C) + added[None]
            xb[rows, :] = normed.reshape(chunk, C).astype(jnp.bfloat16)

        each(rows_all // chunk, chunk, use)
        save_now(stream, stream_out_ref.at[layer])

    def do_turn(op):
        def one(step, carry):
            lanes = pl.ds(pl.multiple_of(step * 128, 128), 128)
            ptb[lanes, :] = xb[:, lanes].T
            return carry

        lax.fori_loop(0, C // 128, one, 0)
        save_now(ptb, pt_ref.at[op["aux"]])

    def do_last(op):
        def use(rows):
            xb[rows, :] = (stream[rows, :] + joined_ref[11:12, :]).astype(jnp.bfloat16)

        each(rows_all // chunk, chunk, use)

    def do_join(op):
        for index in range(3):
            for copy in peer_copies(index)[:2]:
                copy.wait_recv()
        for copy in own_peer[:2]:
            copy.wait()
        for t in range(4):
            lanes = slice(t * width, (t + 1) * width)
            joined_ref[:, lanes] = params_got[t, 0:16, :]

            def use(rows, t=t, lanes=lanes):
                xb[rows, lanes] = x_got[t, rows, :]

            each(4, rows_all // 4, use)
            for half in range(2):
                for part in range(2):
                    row = 16 + 2 * half + part
                    hidden_bias[t, half : half + 1, part * width : (part + 1) * width] = params_got[
                        t, row : row + 1, :
                    ]

    works = (None, do_spread, do_collapse, do_attention, do_norm, do_turn, do_last, do_join)
    four = range(4)

    def spreads(unit, aux):
        return [(1, unit, t, aux) for t in four]

    def collapses(unit, aux):
        return [(2, unit, t, aux) for t in four]

    def attentions(aux):
        return [(3, None, t, aux) for t in four]

    count = len(stages)
    places = 2 * count
    plan = Plan(places)
    for ready, steps in {
        -4: [(7, None, 0, 0), (5, None, 0, 7)],
        1: spreads(1, 0) + [(4, None, 0, 0)] + spreads(0, 1) + spreads(1, 2),
        2: [(5, None, 0, 4)] + attentions(0),
        3: collapses(3, 0) + [(4, None, 0, 1)] + spreads(2, 3) + spreads(3, 4),
        4: [(5, None, 0, 3)] + attentions(1) + collapses(4, 1) + [(4, None, 0, 2)],
        5: [(5, None, 0, 1)] + spreads(5, 5),
        6: spreads(6, 6),
        7: collapses(7, 2),
        8: collapses(8, 3) + [(6, None, 0, 0)] + spreads(4, 7) + [(5, None, 0, 5)],
    }.items():
        plan.fill(ready + count - 1, steps)

    def do_step(place):
        code = plan.code(place)
        pl.when(code > 0)(lambda: do_filled(code))

    def do_filled(code):
        op = plan.fields(code)
        has_tile = (op["kind"] == 1) | (op["kind"] == 2)

        @pl.when(has_tile)
        def _():
            pl.when(op["fresh"] == 1)(lambda: tile_load(op["unit"], op["t"], op["slot"]).start())

            @pl.when(op["next"] > 0)
            def _():
                following = op["next"] - 1
                tile_load(following // 4, following % 4, 1 - op["slot"]).start()

            tile_load(op["unit"], op["t"], op["slot"]).wait()

        for kind in range(1, len(works)):

            @pl.when(op["kind"] == kind)
            def _(kind=kind):
                works[kind](op)

    def advance(turn, carry):
        def inner(place, carry):
            for number in range(count):
                unit = turn - number

                @pl.when((place == count - 1 - number) & (unit >= 0) & (unit < UNITS))
                def _(number=number, unit=unit):
                    stages[number](unit)

            def two(step, carry):
                do_step(2 * (turn * count + place) + step)
                return carry

            return lax.fori_loop(0, 2, two, carry)

        return lax.fori_loop(0, count, inner, carry)

    lax.fori_loop(0, UNITS + count - 1, advance, 0)
    for which in range(4):
        for t in range(4):
            for copy in kept_copies(which, t):
                copy.wait()
    for index in range(3):
        for copy in peer_copies(index):
            copy.wait_send()
        peer_copies(index)[2].wait_recv()
    own_peer[2].wait()


def forward_all(shards, rows_in, params, position, grad):
    units, share, wide = shards.shape
    rows, width = rows_in.shape[1], rows_in.shape[2]
    low = jnp.bfloat16
    anywhere, near = pl.BlockSpec(memory_space=pl.ANY), pl.BlockSpec(memory_space=pltpu.VMEM)
    return pl.pallas_call(
        forward_kernel,
        in_specs=[near, anywhere, near, near, near],
        out_specs=[anywhere] * 8 + [near] * 2,
        out_shape=[
            jax.ShapeDtypeStruct((units, 2, 2, 4, 2, share, wide), low),
            jax.ShapeDtypeStruct((12, 4, rows, wide), low),
            jax.ShapeDtypeStruct((8, C, rows), low),
            jax.ShapeDtypeStruct((3, rows, C), jnp.float32),
            jax.ShapeDtypeStruct((2, 4, rows, wide), low),
            jax.ShapeDtypeStruct((2, 4, rows, width), low),
            jax.ShapeDtypeStruct((2, 4, rows, wide), low),
            jax.ShapeDtypeStruct((4, rows, width), low),
            jax.ShapeDtypeStruct((4, rows, width), low),
            jax.ShapeDtypeStruct((16, C), jnp.float32),
        ],
        scratch_shapes=[
            pltpu.VMEM((rows, C), jnp.float32),
            pltpu.VMEM((rows, C), low),
            pltpu.VMEM((C, rows), low),
            pltpu.VMEM((4, rows, width), low),
            pltpu.VMEM((4,) + params.shape, jnp.float32),
            pltpu.VMEM((4, 8, wide), jnp.float32),
            pltpu.VMEM((2, 4, rows, wide), low),
            pltpu.VMEM((2, 4, rows, width), low),
            pltpu.VMEM((4, 4, rows, wide), low),
            pltpu.VMEM((2, 4, rows, wide), low),
            pltpu.VMEM((4, rows, width), jnp.float32),
            pltpu.VMEM((rows, wide), jnp.float32),
            pltpu.VMEM((2, 4, 2, share, wide), low),
            pltpu.SemaphoreType.DMA((2,)),
            pltpu.SemaphoreType.DMA((1,)),
            pltpu.SemaphoreType.DMA((4, 4, 3)),
            pltpu.SemaphoreType.DMA((3, 4)),
            pltpu.SemaphoreType.DMA((3, 3)),
            pltpu.SemaphoreType.DMA((units,)),
            pltpu.SemaphoreType.DMA((units, 2, 5)),
            pltpu.SemaphoreType.DMA((units, 2, 2, 4, 2)),
            pltpu.SemaphoreType.DMA((units, 3)),
        ],
        compiler_params=pltpu.CompilerParams(
            collective_id=0, has_side_effects=True, vmem_limit_bytes=60 << 20
        ),
    )(shards, rows_in, params, position, grad)


def backward_kernel(
    whole_ref,
    q_given,
    pt_given,
    streams_ref,
    qk_ref,
    v_ref,
    slope_ref,
    grad_ref,
    moved_ref,
    joined_ref,
    out_ref,
    q_ref,
    pt_ref,
    ptx_ref,
    qx_ref,
    got_ref,
    moved_got,
    vec_ref,
    hidden_ref,
    p_buf,
    q_buf,
    dw,
    rya,
    rxa,
    rua,
    rda,
    rxb,
    rub,
    rdb,
    ryb,
    gs,
    gn,
    xb,
    ptb,
    wb,
    cb,
    av,
    datt,
    total,
    sb,
    ob,
    dn,
    load_sem,
    give_sem,
    take_sem,
    send_sem,
    recv_sem,
    tile_sem,
    aux_sem,
    route_sem,
    misc_sem,
    out_sem,
    peer_send,
    peer_recv,
):
    at = Place()
    z, x, y, c = at.z, at.x, at.y, at.c
    far_x, far_y = at.far_x, at.far_y
    share = out_ref.shape[1]
    row_a, row_b = pl.ds(0, ROWS_A), pl.ds(ROWS_A, share - ROWS_A)
    rows_all, width = got_ref.shape[1], got_ref.shape[2]
    half_rows = rows_all // 2
    count_p = pt_ref.shape[0]
    scale = 1.0 / math.sqrt(HEAD)
    own_t = y * 2 + c
    at.greet()

    def give_p(index, source=None):
        return pltpu.make_async_remote_copy(
            src_ref=pt_ref.at[index] if source is None else source,
            dst_ref=ptx_ref.at[index],
            send_sem=give_sem.at[index],
            recv_sem=take_sem.at[index],
            device_id=at.to["core"],
            device_id_type=MESH_ID,
        )

    def give_q(index, yy, source):
        return pltpu.make_async_remote_copy(
            src_ref=source,
            dst_ref=qx_ref.at[index, yy],
            send_sem=give_sem.at[count_p + 2 * index + yy],
            recv_sem=take_sem.at[count_p + 2 * index + yy],
            device_id=at.to["core"],
            device_id_type=MESH_ID,
        )

    def known_q(index, yy):
        return give_q(index, yy, q_ref.at[index, 2 * yy + 1 - c])

    known = (0, 1, 4, 10)
    known_p = (1, 5, 3, 4, 7)
    for index in known[:2]:
        for yy in range(2):
            known_q(index, yy).start()
    give_p(1).start()
    for index in known[2:]:
        for yy in range(2):
            known_q(index, yy).start()
    for index in known_p[1:]:
        give_p(index).start()
    def each(count, size, use):
        def one(step, carry):
            use(pl.ds(pl.multiple_of(step * size, size), size))
            return carry

        lax.fori_loop(0, count, one, 0)

    def aux_load(source, target, number):
        return pltpu.make_async_copy(source, target, aux_sem.at[number])

    def tile_load(unit, t, slot):
        return pltpu.make_async_copy(whole_ref.at[unit, t // 2, t % 2], wb.at[slot], tile_sem.at[slot])

    def route(source, index, t):
        yy = t // 2
        local = pltpu.make_async_copy(source, q_ref.at[index, t], route_sem.at[index, yy])

        def begin():
            pl.when(c == t % 2)(lambda: local.start())
            pl.when(c != t % 2)(lambda: give_q(index, yy, source).start())

        def wait():
            pl.when(c == t % 2)(lambda: local.wait())
            pl.when(c != t % 2)(lambda: give_q(index, yy, source).wait_send())

        return begin, wait

    chunk = 4 * FRAMES
    quarter = rows_all // 4

    def column_sum(row, values):
        vec_ref[pl.ds(row, 1), :] += jnp.sum(values, axis=0, keepdims=True)

    def slope_load(aux, t):
        return aux_load(slope_ref.at[aux, t], cb.at[4], 0)

    def head_loads(aux, t):
        return (
            aux_load(qk_ref.at[aux - 2, t], cb.at[4], 0),
            aux_load(v_ref.at[aux - 2, t], av, 1),
        )

    def load_early(code):
        aux, t = code // 4, code % 4
        pl.when(aux < 2)(lambda: slope_load(aux, t).start())

        @pl.when(aux >= 2)
        def _():
            for load in head_loads(aux, t):
                load.start()

    def do_spread(op):
        t, aux = op["t"], op["aux"]
        side = t % 2

        def multiply(rows):
            total[rows, :] = dot_plain(xb[rows, :], wb[op["slot"]].reshape(C, WIDE))

        each(2, half_rows, multiply)

        @pl.when(aux < 2)
        def _():
            slope_load(aux, t).wait()

            def use(rows):
                grad = total[rows, :] * cb[4, rows, :].astype(jnp.float32)
                hidden_ref[t, pl.ds(aux, 1), :] += jnp.sum(grad, axis=0, keepdims=True)
                cb[side, rows, :] = grad.astype(jnp.bfloat16)

            each(4, quarter, use)
            route(cb.at[side], 3 - aux, t)[0]()

        @pl.when(aux >= 2)
        def _():
            for load in head_loads(aux, t):
                load.wait()

            for block in range(2):

                @pl.when(aux == 2 + block)
                def _(block=block):
                    low = width if block == 0 else 0

                    def use(rows):
                        datt[rows, :] = total[rows, low : low + width].astype(jnp.bfloat16)

                    each(4, quarter, use)

    def do_collapse(op):
        which, routed, t = op["aux"] % 5, op["aux"] // 5, op["t"]

        def multiply(rows):
            gn[rows, :] += dot_rows(cb[which, rows, :], wb[op["slot"]].reshape(C, WIDE))

        each(2, half_rows, multiply)
        pl.when(routed > 0)(lambda: route(cb.at[which], routed - 1, t)[1]())

    def do_attention(op):
        block, t = op["aux"], op["t"]
        side = t % 2
        same = same_pixel(BLOCK)
        for start in range(0, rows_all, BLOCK):
            here = slice(start, start + BLOCK)
            for head in range(width // HEAD):
                low = head * HEAD
                query = cb[4, here, low : low + HEAD]
                key = cb[4, here, width + low : width + low + HEAD]
                value = av[here, low : low + HEAD]
                grad = datt[here, low : low + HEAD]
                probs = head_probs(query, key, same, scale)
                grad_probs = dot_rows(grad, value)
                centred = jnp.sum(probs * grad_probs, axis=1, keepdims=True)
                grad_raw = (probs * (grad_probs - centred) * scale).astype(jnp.bfloat16)
                cb[side, here, low : low + HEAD] = dot_plain(grad_raw, key).astype(jnp.bfloat16)
                cb[side, here, width + low : width + low + HEAD] = dot_first(
                    grad_raw, query
                ).astype(jnp.bfloat16)
                cb[2 + side, here, low : low + HEAD] = dot_first(
                    probs.astype(jnp.bfloat16), grad
                ).astype(jnp.bfloat16)
        route(cb.at[side], 7 - 2 * block, t)[0]()
        route(cb.at[2 + side], 8 - 2 * block, t)[0]()

    def do_layer(op):
        layer = op["aux"]

        def load(step):
            rows = pl.ds(pl.multiple_of(step * chunk, chunk), chunk)
            return pltpu.make_async_copy(
                streams_ref.at[layer, rows], sb.at[step % 2], misc_sem.at[3 + step % 2]
            )

        def one(step, carry):
            pl.when(step + 1 < rows_all // chunk)(lambda: load(step + 1).start())
            load(step).wait()
            rows = pl.ds(pl.multiple_of(step * chunk, chunk), chunk)
            values = sb[step % 2]
            centre = jnp.mean(values, axis=1, keepdims=True)
            offset = values - centre
            inverse = lax.rsqrt(jnp.mean(offset * offset, axis=1, keepdims=True) + 1e-05)
            hat = offset * inverse
            grad = gn[rows, :]
            column_sum(layer, grad * hat)
            column_sum(3 + layer, grad)
            scaled = grad * joined_ref[pl.ds(1 + layer, 1), :]
            first = jnp.mean(scaled, axis=1, keepdims=True)
            second = jnp.mean(scaled * hat, axis=1, keepdims=True)
            result = gs[rows, :] + inverse * (scaled - first - hat * second)
            gs[rows, :] = result
            column_sum(6 + layer, result)
            xb[rows, :] = result.astype(jnp.bfloat16)
            gn[rows, :] = jnp.zeros((chunk, C), jnp.float32)
            return carry

        load(0).start()
        lax.fori_loop(0, rows_all // chunk, one, 0)

    def do_turn(op):
        index = op["aux"]

        def one(step, carry):
            lanes = pl.ds(pl.multiple_of(step * 128, 128), 128)
            ptb[lanes, :] = xb[:, lanes].T
            return carry

        lax.fori_loop(0, C // 128, one, 0)
        turn_copy(index).start()
        give_p(index, ptb).start()

    def turn_copy(index):
        return pltpu.make_async_copy(ptb, pt_ref.at[index], misc_sem.at[2])

    def do_turned(op):
        turn_copy(op["aux"]).wait()
        give_p(op["aux"], ptb).wait_send()

    def do_first(op):
        def use(rows):
            values = gn[rows, :]
            gs[rows, :] = values
            column_sum(9, values)
            xb[rows, :] = values.astype(jnp.bfloat16)
            gn[rows, :] = jnp.zeros((chunk, C), jnp.float32)

        each(rows_all // chunk, chunk, use)

    def do_place(op):
        t, aux = op["t"], op["aux"]
        side = t % 2

        @pl.when(aux == 1)
        def _():
            load = aux_load(grad_ref.at[t], datt, 0)
            load.start()
            load.wait()

            def use(rows):
                cb[side, rows, 0:width] = jnp.zeros((quarter, width), jnp.bfloat16)
                cb[side, rows, width:] = datt[rows, :]

            each(4, quarter, use)

        for block in range(4):

            @pl.when((aux == 0) & (t == block))
            def _(block=block):
                def use(rows):
                    cb[side, rows, 0:width] = jnp.zeros((quarter, width), jnp.bfloat16)
                    cb[side, rows, width:] = xb[rows, block * width : (block + 1) * width]

                each(4, quarter, use)

        route(cb.at[side], 11 - 2 * aux, t)[0]()

    peers = (("y", far_y * 2 + c), ("core", y * 2 + 1 - c), ("cross", far_y * 2 + 1 - c))

    def peer_copy(index):
        kind, t = peers[index]
        return pltpu.make_async_remote_copy(
            src_ref=dn.at[t],
            dst_ref=got_ref.at[own_t],
            send_sem=peer_send.at[0, index],
            recv_sem=peer_recv.at[0, index],
            device_id=at.to[kind],
            device_id_type=MESH_ID,
        )

    def moved_copy(index):
        kind, t = peers[index]
        return pltpu.make_async_remote_copy(
            src_ref=moved_ref.at[t],
            dst_ref=moved_got.at[own_t],
            send_sem=peer_send.at[1, index],
            recv_sem=peer_recv.at[1, index],
            device_id=at.to[kind],
            device_id_type=MESH_ID,
        )

    own_peer = pltpu.make_async_copy(dn.at[own_t], got_ref.at[own_t], peer_send.at[0, 3])
    own_moved = pltpu.make_async_copy(
        moved_ref.at[own_t], moved_got.at[own_t], peer_send.at[1, 3]
    )
    for index in range(3):
        moved_copy(index).start()
    own_moved.start()

    def do_send(op):
        for t in range(4):

            def use(rows, t=t):
                dn[t, rows, :] = gn[rows, t * width : (t + 1) * width].astype(jnp.bfloat16)

            each(4, quarter, use)
        for index in range(3):
            peer_copy(index).start()
        own_peer.start()

    works = (
        None,
        do_spread,
        do_collapse,
        do_attention,
        do_layer,
        do_turn,
        do_first,
        do_place,
        do_send,
        do_turned,
    )
    four = range(4)

    def feed(half):
        steps = []
        for t in four:
            steps += [(1, 7 + half, t, half), (2, 5 + half, t, t % 2 + 5 * (4 - half))]
        return steps

    def heads(block, t):
        return [
            (1, 3 + block, t, 2 + block),
            (3, None, t, block),
            (2, 2 * block, t, t % 2 + 5 * (8 - 2 * block)),
            (2, 2 * block + 1, t, 2 + t % 2 + 5 * (9 - 2 * block)),
        ]

    def inputs(t):
        return [(7, None, t, 0), (2, 1, t, t % 2 + 5 * 12)]

    def outputs(t):
        return [(7, None, t, 1), (2, 4, t, t % 2 + 5 * 10)]

    stage_count = 6
    plan = Plan(2 * stage_count, True)
    for turn, steps in {
        -1: outputs(0) + outputs(1) + outputs(2) + outputs(3) + [(6, None, 0, 0), (5, None, 0, 0), (9, None, 0, 0)],
        0: feed(1),
        1: feed(0),
        2: [(4, None, 0, 2), (5, None, 0, 2)] + heads(1, 0) + [(9, None, 0, 2)],
        3: heads(1, 1) + heads(1, 2),
        4: heads(1, 3),
        5: [(4, None, 0, 1), (5, None, 0, 6)] + heads(0, 0) + [(9, None, 0, 6)],
        6: heads(0, 1) + heads(0, 2) + heads(0, 3),
        7: [(4, None, 0, 0)] + inputs(0) + inputs(1) + inputs(2) + inputs(3),
        8: [(8, None, 0, 0)],
    }.items():
        plan.fill(turn + 1, steps)

    def do_step(place):
        code = plan.code(place)
        pl.when(code > 0)(lambda: do_filled(code))

    def do_filled(code):
        op = plan.fields(code)
        has_tile = (op["kind"] == 1) | (op["kind"] == 2)

        @pl.when(has_tile)
        def _():
            pl.when(op["fresh"] == 1)(lambda: tile_load(op["unit"], op["t"], op["slot"]).start())

            @pl.when(op["next"] > 0)
            def _():
                following = op["next"] - 1
                tile_load(following // 4, following % 4, 1 - op["slot"]).start()

            pl.when(op["early"] > 0)(lambda: load_early(op["early"] - 1))
            tile_load(op["unit"], op["t"], op["slot"]).wait()

        for kind in range(1, len(works)):

            @pl.when(op["kind"] == kind)
            def _(kind=kind):
                works[kind](op)

    vec_ref[...] = jnp.zeros_like(vec_ref)
    hidden_ref[...] = jnp.zeros_like(hidden_ref)

    def clear(rows):
        gn[rows, :] = jnp.zeros((chunk, C), jnp.float32)
        cb[2, rows, :] = jnp.zeros((chunk, WIDE), jnp.bfloat16)
        cb[3, rows, :] = jnp.zeros((chunk, WIDE), jnp.bfloat16)

    each(rows_all // chunk, chunk, clear)

    names = ["ya0", "ya1", "xa", "ua0", "ua1", "ua2", "da0", "da1", "da2"]
    names += ["xb0", "xb1", "ub0", "ub1", "ub2", "db0", "db1", "db2", "yb"]
    number = {name: index for index, name in enumerate(names)}

    class Slot:
        def __init__(self, turn):
            self.d, self.r = turn % SLOTS_IN_FLIGHT, turn % SLOTS_RECEIVED

    def copy(slot, name, src, dst, kind, shift=0):
        index = number[name] + shift
        return pltpu.make_async_remote_copy(
            src_ref=src,
            dst_ref=dst,
            send_sem=send_sem.at[slot.d, index],
            recv_sem=recv_sem.at[slot.r, index],
            device_id=at.to[kind],
            device_id_type=MESH_ID,
        )

    def ya(slot, part):
        side = far_x if part == 0 else x
        return copy(
            slot, f"ya{part}", dw.at[slot.d, far_y, :, side, row_a], rya.at[slot.r, part], "y"
        )

    def xa(slot):
        return copy(slot, "xa", dw.at[slot.d, y, :, far_x, row_a], rxa.at[slot.r], "x")

    def xb_copy(slot, part):
        return copy(
            slot, f"xb{part}", dw.at[slot.d, part, :, far_x, row_b], rxb.at[slot.r, part], "x"
        )

    def yb(slot):
        return copy(slot, "yb", dw.at[slot.d, far_y, z, x, row_b], ryb.at[slot.r], "y")

    def up(slot, colour, d):
        if colour == 0:
            return copy(
                slot, "ua0", dw.at[slot.d, y, d, x, row_a], rua.at[slot.r, d - 1], "up", d - 1
            )
        return copy(slot, "ub0", dw.at[slot.d, :, d, x, row_b], rub.at[slot.r, d - 1], "up", d - 1)

    def down(slot, colour, d):
        if colour == 0:
            return copy(slot, "da0", dw.at[slot.d, y, d, x, row_a], rda.at[slot.r, d], "down", d)
        return copy(slot, "db0", dw.at[slot.d, :, d, x, row_b], rdb.at[slot.r, d], "down", d)

    def add(place, got):
        total = place[...].astype(jnp.float32) + got[...].astype(jnp.float32)
        place[...] = total.astype(jnp.bfloat16)

    def product_loads(p_index, q_index):
        loads = [
            pltpu.make_async_copy(pt_ref.at[p_index], p_buf.at[0], load_sem.at[0]),
            pltpu.make_async_copy(ptx_ref.at[p_index], p_buf.at[1], load_sem.at[1]),
        ]
        for yy in range(2):
            loads += [
                pltpu.make_async_copy(
                    q_ref.at[q_index, 2 * yy + c], q_buf.at[0, yy], load_sem.at[2 + yy]
                ),
                pltpu.make_async_copy(
                    qx_ref.at[q_index, yy], q_buf.at[1, yy], load_sem.at[4 + yy]
                ),
            ]
        return loads

    def products(slot, p_index, q_index, mixed, more):
        for load in product_loads(p_index, q_index):
            load.wait()

        def one(step, carry):
            side, zz = step // 4, step % 4
            yy = jnp.where(side == 0, far_y, y)
            rows = pl.ds(pl.multiple_of(zz * 2 * share, 2 * share), 2 * share)

            def part(first, last):
                result = dot_plain(p_buf[0, rows, :], q_buf[0, yy, :, first:last])
                result = result + dot_plain(p_buf[1, rows, :], q_buf[1, yy, :, first:last])
                return result.reshape(2, share, last - first)

            @pl.when(mixed == 0)
            def _():
                dw[slot.d, yy, zz] = part(0, WIDE).astype(jnp.bfloat16)

            @pl.when((mixed == 1) & (more == 0))
            def _():
                dw[slot.d, yy, zz, :, :, 0:384] = part(0, 384).astype(jnp.bfloat16)

            @pl.when((mixed == 1) & (more == 1))
            def _():
                result = part(256, WIDE)
                shared = dw[slot.d, yy, zz, :, :, 256:384].astype(jnp.float32)
                shared = shared + result[:, :, 0:128]
                dw[slot.d, yy, zz, :, :, 256:384] = shared.astype(jnp.bfloat16)
                dw[slot.d, yy, zz, :, :, 384:] = result[:, :, 128:].astype(jnp.bfloat16)

            return carry

        lax.fori_loop(0, 8, one, 0)

    def take_p(index):
        await_bytes(ptx_ref.at[index], take_sem.at[index])

    def take_q(index):
        for yy in range(2):
            await_bytes(qx_ref.at[index, yy], take_sem.at[count_p + 2 * index + yy])

    def prepare(turn):
        p_index = (turn + turn // 5) // 2

        @pl.when((turn + turn // 5) % 2 == 0)
        def _():
            take_p(p_index)

        take_q(turn)
        for load in product_loads(p_index, turn):
            load.start()

    def stage0(turn):
        slot = Slot(turn)
        p_index = (turn + turn // 5) // 2
        mixed = (turn >= 4).astype(jnp.int32) * (1 - turn % 2)
        extra = (turn - 4) // 2

        @pl.when(mixed == 1)
        def _():
            take_p(5 + extra)
            take_q(UNITS + extra)

        def one_pass(more, carry):
            @pl.when(more == 1)
            def _():
                for load in product_loads(5 + extra, UNITS + extra):
                    load.start()

            products(
                slot,
                jnp.where(more == 1, 5 + extra, p_index),
                jnp.where(more == 1, UNITS + extra, turn),
                mixed,
                more,
            )
            return carry

        lax.fori_loop(0, 1 + mixed, one_pass, 0)

        ya(slot, 0).start()
        xb_copy(slot, 0).start()
        ya(slot, 1).start()
        xb_copy(slot, 1).start()

    def z_step(slot, colour, step):
        @pl.when(z <= step - 1)
        def _():
            d = z + 4 - step

            @pl.when(z >= 1)
            def _():
                up(slot, colour, d).wait_recv()
                if colour == 0:
                    add(dw.at[slot.d, y, d, x, row_a], rua.at[slot.r, d - 1])
                else:
                    add(dw.at[slot.d, 0, d, x, row_b], rub.at[slot.r, d - 1, 0])
                    add(dw.at[slot.d, 1, d, x, row_b], rub.at[slot.r, d - 1, 1])

            up(slot, colour, d).start()

        @pl.when(3 - z <= step - 1)
        def _():
            d = z - 4 + step

            @pl.when(z <= 2)
            def _():
                down(slot, colour, d).wait_recv()
                if colour == 0:
                    add(dw.at[slot.d, y, d, x, row_a], rda.at[slot.r, d])
                else:
                    add(dw.at[slot.d, 0, d, x, row_b], rdb.at[slot.r, d, 0])
                    add(dw.at[slot.d, 1, d, x, row_b], rdb.at[slot.r, d, 1])

            down(slot, colour, d).start()

    def stage1(turn):
        slot = Slot(turn)
        for part in range(2):
            xb_copy(slot, part).wait_recv()
            for zz in range(4):
                add(dw.at[slot.d, part, zz, x, row_b], rxb.at[slot.r, part, zz])
        z_step(slot, 1, 1)
        ya(slot, 0).wait_recv()
        for zz in range(4):
            add(dw.at[slot.d, y, zz, far_x, row_a], rya.at[slot.r, 0, zz])
        xa(slot).start()
        ya(slot, 1).wait_recv()
        for zz in range(4):
            add(dw.at[slot.d, y, zz, x, row_a], rya.at[slot.r, 1, zz])

    def stage2(turn):
        slot = Slot(turn)
        z_step(slot, 1, 2)
        xa(slot).wait_recv()
        for zz in range(4):
            add(dw.at[slot.d, y, zz, x, row_a], rxa.at[slot.r, zz])
        z_step(slot, 0, 1)

    def stage3(turn):
        slot = Slot(turn)
        z_step(slot, 1, 3)
        z_step(slot, 0, 2)

    def stage4(turn):
        slot = Slot(turn)
        z_step(slot, 0, 3)

        @pl.when(z >= 1)
        def _():
            up(slot, 1, z).wait_recv()
            for yy in range(2):
                add(dw.at[slot.d, yy, z, x, row_b], rub.at[slot.r, z - 1, yy])

        @pl.when(z <= 2)
        def _():
            down(slot, 1, z).wait_recv()
            for yy in range(2):
                add(dw.at[slot.d, yy, z, x, row_b], rdb.at[slot.r, z, yy])

        yb(slot).start()

    def out_copy(turn):
        return pltpu.make_async_copy(ob.at[turn % 2], out_ref.at[turn], out_sem.at[turn % 2])

    def stage5(turn):
        slot = Slot(turn)
        side = turn % 2
        pl.when(turn >= 2)(lambda: out_copy(turn - 2).wait())
        ob[side, row_a, :] = dw[slot.d, y, z, x, row_a, :].astype(jnp.float32)

        @pl.when(z >= 1)
        def _():
            up(slot, 0, z).wait_recv()
            ob[side, row_a, :] += rua[slot.r, z - 1].astype(jnp.float32)

        @pl.when(z <= 2)
        def _():
            down(slot, 0, z).wait_recv()
            ob[side, row_a, :] += rda[slot.r, z].astype(jnp.float32)

        yb(slot).wait_recv()
        ob[side, row_b, :] = dw[slot.d, y, z, x, row_b, :].astype(jnp.float32) + ryb[
            slot.r
        ].astype(jnp.float32)
        out_copy(turn).start()

        ya(slot, 0).wait_send()
        ya(slot, 1).wait_send()
        xa(slot).wait_send()
        xb_copy(slot, 0).wait_send()
        xb_copy(slot, 1).wait_send()
        yb(slot).wait_send()
        for colour in range(2):
            for step in range(1, 4):

                @pl.when(z <= step - 1)
                def _(colour=colour, step=step):
                    up(slot, colour, z + 4 - step).wait_send()

                @pl.when(3 - z <= step - 1)
                def _(colour=colour, step=step):
                    down(slot, colour, z - 4 + step).wait_send()

    stages = (stage0, stage1, stage2, stage3, stage4, stage5)

    def advance(now, carry):
        def inner(place, carry):
            for spot, step in enumerate(range(stage_count)):
                turn = now - 1 - step

                @pl.when((place == spot) & (turn >= 0) & (turn < UNITS))
                def _(step=step, turn=turn):
                    stages[step](turn)

            def two(step, carry):
                do_step(2 * (now * stage_count + place) + step)
                return carry

            return lax.fori_loop(0, 2, two, carry)

        lax.fori_loop(0, stage_count, inner, 0)
        pl.when(now < UNITS)(lambda: prepare(now))
        return carry

    lax.fori_loop(0, UNITS + stage_count, advance, 0)
    out_copy(UNITS - 2).wait()
    out_copy(UNITS - 1).wait()
    for index in range(3):
        peer_copy(index).wait()
        moved_copy(index).wait()
    own_peer.wait()
    own_moved.wait()
    for index in known:
        for yy in range(2):
            known_q(index, yy).wait_send()
    for index in known_p:
        give_p(index).wait_send()


def backward_all(whole, q_all, pt_all, streams, qk, values, slopes, grad, moved, joined):
    share = whole.shape[5]
    count_p, unused, rows = pt_all.shape
    width = values.shape[3]
    low = jnp.bfloat16
    slots, taken, rest = SLOTS_IN_FLIGHT, SLOTS_RECEIVED, share - ROWS_A
    anywhere, near = pl.BlockSpec(memory_space=pl.ANY), pl.BlockSpec(memory_space=pltpu.VMEM)
    return pl.pallas_call(
        backward_kernel,
        in_specs=[anywhere] * 9 + [near],
        out_specs=[anywhere] * 7 + [near] * 2,
        out_shape=[
            jax.ShapeDtypeStruct((UNITS, share, WIDE), jnp.float32),
            jax.ShapeDtypeStruct(q_all.shape, low),
            jax.ShapeDtypeStruct(pt_all.shape, low),
            jax.ShapeDtypeStruct(pt_all.shape, low),
            jax.ShapeDtypeStruct((q_all.shape[0], 2, rows, WIDE), low),
            jax.ShapeDtypeStruct((4, rows, width), low),
            jax.ShapeDtypeStruct((4, rows, width), low),
            jax.ShapeDtypeStruct((16, C), jnp.float32),
            jax.ShapeDtypeStruct((4, 8, WIDE), jnp.float32),
        ],
        input_output_aliases={1: 1, 2: 2},
        scratch_shapes=[
            pltpu.VMEM((2, C, rows), low),
            pltpu.VMEM((2, 2, rows, WIDE), low),
            pltpu.VMEM((slots, 2, 4, 2, share, WIDE), low),
            pltpu.VMEM((taken, 2, 4, ROWS_A, WIDE), low),
            pltpu.VMEM((taken, 4, ROWS_A, WIDE), low),
            pltpu.VMEM((taken, 3, ROWS_A, WIDE), low),
            pltpu.VMEM((taken, 3, ROWS_A, WIDE), low),
            pltpu.VMEM((taken, 2, 4, rest, WIDE), low),
            pltpu.VMEM((taken, 3, 2, rest, WIDE), low),
            pltpu.VMEM((taken, 3, 2, rest, WIDE), low),
            pltpu.VMEM((taken, rest, WIDE), low),
            pltpu.VMEM((rows, C), jnp.float32),
            pltpu.VMEM((rows, C), jnp.float32),
            pltpu.VMEM((rows, C), low),
            pltpu.VMEM((C, rows), low),
            pltpu.VMEM((2, 4, 2, share, WIDE), low),
            pltpu.VMEM((5, rows, WIDE), low),
            pltpu.VMEM((rows, width), low),
            pltpu.VMEM((rows, width), low),
            pltpu.VMEM((rows, WIDE), jnp.float32),
            pltpu.VMEM((2, 4 * FRAMES, C), jnp.float32),
            pltpu.VMEM((2, share, WIDE), jnp.float32),
            pltpu.VMEM((4, rows, width), low),
            pltpu.SemaphoreType.DMA((6,)),
            pltpu.SemaphoreType.DMA((32,)),
            pltpu.SemaphoreType.DMA((32,)),
            pltpu.SemaphoreType.DMA((slots, 18)),
            pltpu.SemaphoreType.DMA((taken, 18)),
            pltpu.SemaphoreType.DMA((2,)),
            pltpu.SemaphoreType.DMA((4,)),
            pltpu.SemaphoreType.DMA((12, 2)),
            pltpu.SemaphoreType.DMA((5,)),
            pltpu.SemaphoreType.DMA((2,)),
            pltpu.SemaphoreType.DMA((2, 4)),
            pltpu.SemaphoreType.DMA((2, 3)),
        ],
        compiler_params=pltpu.CompilerParams(
            collective_id=1, has_side_effects=True, vmem_limit_bytes=63 << 20
        ),
    )(whole, q_all, pt_all, streams, qk, values, slopes, grad, moved, joined)


def gather_plain(shards):
    units, share, wide = shards.shape
    whole = lax.all_gather(shards, MIXED, axis=1, tiled=True)
    return whole.reshape(units, lax.axis_size("tensor"), C, wide)


def reduce_plain(turned, parts):
    reduced = []
    for turn in range(UNITS):
        pairs = [(turned[(turn + turn // 5) // 2], parts[turn])]
        if turn in (4, 6, 8):
            extra = (turn - 4) // 2
            pairs.append((turned[5 + extra], parts[UNITS + extra]))
        whole = sum(
            jnp.einsum("kr,trn->tkn", left, right, preferred_element_type=jnp.float32)
            for left, right in pairs
        )
        whole = whole.astype(jnp.bfloat16).reshape(-1, whole.shape[2])
        reduced.append(
            lax.psum_scatter(whole, MIXED, scatter_dimension=0, tiled=True).astype(jnp.float32)
        )
    return jnp.stack(reduced, 0)


def by_pixels(values, tensor_size):
    slots, frames, width, pixels = values.shape
    own = pixels // tensor_size
    return jnp.transpose(values, (3, 0, 1, 2)).reshape(tensor_size, own * slots * frames, width)


def exchange(parts):
    return lax.all_to_all(parts, "tensor", 0, 0, tiled=True)


def back_to_channels(arrived, slots, pixels):
    width = arrived.shape[2]
    return jnp.transpose(arrived.reshape(pixels, slots, FRAMES, width), (1, 2, 3, 0))


def group_total(values):
    width = values.shape[0]
    size = C // GROUPS
    grouped = values.reshape(width // size, size, 1)
    summed = jnp.sum(grouped, axis=1, keepdims=True)
    return jnp.broadcast_to(summed, grouped.shape).reshape(width, 1)


def enter_kernel(
    latent_ref,
    cot_ref,
    flag_ref,
    gain_ref,
    shift_ref,
    in_ref,
    qkv_ref,
    out_ref,
    up_ref,
    down_ref,
    proj_ref,
    sent_ref,
    moved_ref,
    shards_ref,
    centre_ref,
    inverse_ref,
    bias_ref,
    rows_buf,
):
    frames, width, pixels = latent_ref.shape[1:]
    cells = frames * pixels * (C // GROUPS)
    shards_ref[0, :, 0:width] = qkv_ref[0, 0]
    shards_ref[0, :, width:] = qkv_ref[0, 1]
    shards_ref[1, :, 0:width] = qkv_ref[0, 2]
    shards_ref[1, :, width:] = in_ref[...]
    shards_ref[2, :, 0:width] = qkv_ref[1, 0]
    shards_ref[2, :, width:] = qkv_ref[1, 1]
    shards_ref[3, :, 0:width] = qkv_ref[1, 2]
    shards_ref[3, :, width:] = out_ref[0]
    shards_ref[4, :, 0:width] = out_ref[1]
    shards_ref[4, :, width:] = proj_ref[...]
    for half in range(2):
        lanes = slice(half * WIDE, (half + 1) * WIDE)
        shards_ref[5 + half] = up_ref[:, lanes]
        shards_ref[7 + half] = down_ref[:, lanes]

    def frame_sum(use):
        def one(f, carry):
            return carry + use(f)

        total = lax.fori_loop(0, frames, one, jnp.zeros((width, pixels), jnp.float32))
        return jnp.sum(total, axis=1, keepdims=True)

    def values(f):
        return latent_ref[0, f].astype(jnp.float32)

    centre = group_total(frame_sum(values)) / cells
    spread_sum = group_total(frame_sum(lambda f: (values(f) - centre) * (values(f) - centre)))
    inverse = lax.rsqrt(spread_sum / cells + 1e-06)
    centre_ref[...] = centre
    inverse_ref[...] = inverse
    flag = (flag_ref[0] > 0).astype(jnp.float32)

    def masked(f):
        return cot_ref[0, f].astype(jnp.float32) * flag

    bias_ref[...] = frame_sum(masked)
    own = pixels // 4 * frames

    def rows_of(use, target):
        def one(f, carry):
            block = use(f)
            for part in range(3):
                rows_buf[part, pl.ds(f, pixels, stride=frames), :] = block[
                    part * 128 : part * 128 + 128, :
                ].T
            return carry

        lax.fori_loop(0, frames, one, 0)

        def cast(step, carry):
            rows = pl.ds(pl.multiple_of(step * 128, 128), 128)
            t, inside = step // (own // 128), step % (own // 128)
            inner = pl.ds(pl.multiple_of(inside * 128, 128), 128)
            for part in range(3):
                low, high = part * 128, min(part * 128 + 128, width)
                target[t, inner, low:high] = rows_buf[part, rows, 0 : high - low].astype(
                    jnp.bfloat16
                )
            return carry

        lax.fori_loop(0, 4 * own // 128, cast, 0)

    def padded(block):
        return jnp.concatenate([block, jnp.zeros((384 - width, pixels), jnp.float32)], 0)

    gain, shift = gain_ref[...], shift_ref[...]
    rows_of(lambda f: padded((values(f) - centre) * inverse * gain + shift), sent_ref)
    rows_of(lambda f: padded(masked(f)), moved_ref)


def enter(latent, cotangent, flags, gain, shift, w_in, w_qkv, w_out, w_up, w_down, w_proj):
    slots, frames, width, pixels = latent.shape
    share, rows = w_in.shape[0], pixels // 4 * frames
    near = pl.BlockSpec(memory_space=pltpu.VMEM)
    column = jax.ShapeDtypeStruct((width, 1), jnp.float32)
    low = jnp.bfloat16
    return pl.pallas_call(
        enter_kernel,
        in_specs=[near, near, pl.BlockSpec(memory_space=pltpu.SMEM)] + [near] * 8,
        out_specs=[near] * 6,
        out_shape=[
            jax.ShapeDtypeStruct((4, rows, width), low),
            jax.ShapeDtypeStruct((4, rows, width), low),
            jax.ShapeDtypeStruct((UNITS, share, WIDE), low),
            column,
            column,
            column,
        ],
        scratch_shapes=[pltpu.VMEM((3, 4 * rows, 128), jnp.float32)],
        compiler_params=pltpu.CompilerParams(vmem_limit_bytes=48 << 20),
    )(
        latent,
        cotangent,
        flags,
        gain.reshape(width, 1),
        shift.reshape(width, 1),
        w_in,
        jnp.transpose(w_qkv, (0, 2, 1, 3)),
        jnp.transpose(w_out, (0, 2, 1)),
        w_up,
        w_down.T,
        w_proj,
    )


def leave_kernel(
    grad_ref,
    moved_ref,
    latent_ref,
    cot_ref,
    flag_ref,
    gain_ref,
    centre_ref,
    inverse_ref,
    reduced_ref,
    output_ref,
    latent_grad_ref,
    gain_grad_ref,
    shift_grad_ref,
    in_ref,
    qkv_ref,
    out_ref,
    up_ref,
    down_ref,
    proj_ref,
    rows_buf,
    turned,
):
    frames, width, pixels = latent_ref.shape[1:]
    cells = frames * pixels * (C // GROUPS)
    for block in range(2):
        for part in range(2):
            qkv_ref[block, part] = reduced_ref[7 - 2 * block, :, part * width : (part + 1) * width]
        qkv_ref[block, 2] = reduced_ref[8 - 2 * block, :, 0:width]
    in_ref[...] = reduced_ref[8, :, width:]
    out_ref[0] = reduced_ref[6, :, width:]
    out_ref[1] = reduced_ref[4, :, 0:width]
    proj_ref[...] = reduced_ref[4, :, width:]
    for half in range(2):
        lanes = slice(half * WIDE, (half + 1) * WIDE)
        up_ref[:, lanes] = reduced_ref[3 - half]
        down_ref[:, lanes] = reduced_ref[1 - half]

    own = pixels // 4 * frames

    def spread_rows(source):
        def cast(step, carry):
            rows = pl.ds(pl.multiple_of(step * 128, 128), 128)
            t, inside = step // (own // 128), step % (own // 128)
            inner = pl.ds(pl.multiple_of(inside * 128, 128), 128)
            for part in range(3):
                low, high = part * 128, min(part * 128 + 128, width)
                rows_buf[part, rows, 0 : high - low] = source[t, inner, low:high].astype(
                    jnp.float32
                )
            return carry

        lax.fori_loop(0, 4 * own // 128, cast, 0)

    def frame(f):
        rows = pl.ds(f, pixels, stride=frames)
        turned_parts = [rows_buf[part, rows, :].T for part in range(3)]
        return jnp.concatenate(turned_parts, 0)[0:width, :]

    def hat(f):
        return (latent_ref[0, f].astype(jnp.float32) - centre_ref[...]) * inverse_ref[...]

    flag = (flag_ref[0] > 0).astype(jnp.float32)
    rows_buf[...] = jnp.zeros_like(rows_buf)
    spread_rows(moved_ref)

    def finish(f, carry):
        start = latent_ref[0, f].astype(jnp.float32)
        output_ref[0, f] = (start + flag * frame(f)).astype(jnp.bfloat16)
        return carry

    lax.fori_loop(0, frames, finish, 0)
    spread_rows(grad_ref)
    zero = jnp.zeros((width, pixels), jnp.float32)

    def gather(f, carry):
        grad = frame(f)
        turned[f] = grad
        return carry[0] + grad * hat(f), carry[1] + grad

    by_gain, by_shift = lax.fori_loop(0, frames, gather, (zero, zero))
    gain_sum = jnp.sum(by_gain, axis=1, keepdims=True)
    shift_sum = jnp.sum(by_shift, axis=1, keepdims=True)
    gain_grad_ref[...] = gain_sum
    shift_grad_ref[...] = shift_sum
    gain = gain_ref[...]
    first = group_total(gain * shift_sum) / cells
    second = group_total(gain * gain_sum) / cells

    def back(f, carry):
        grad = inverse_ref[...] * (turned[f] * gain - first - hat(f) * second)
        latent_grad_ref[0, f] = cot_ref[0, f].astype(jnp.float32) + grad
        return carry

    lax.fori_loop(0, frames, back, 0)


def leave(grad, moved, latent, cotangent, flags, gain, centre, inverse, reduced):
    slots, frames, width, pixels = latent.shape
    rows, share = pixels // 4 * frames, reduced.shape[1]
    near = pl.BlockSpec(memory_space=pltpu.VMEM)
    real = jnp.float32
    column = jax.ShapeDtypeStruct((width, 1), real)
    made = pl.pallas_call(
        leave_kernel,
        in_specs=[near] * 4 + [pl.BlockSpec(memory_space=pltpu.SMEM)] + [near] * 4,
        out_specs=[near] * 10,
        out_shape=[
            jax.ShapeDtypeStruct(latent.shape, jnp.bfloat16),
            jax.ShapeDtypeStruct(latent.shape, real),
            column,
            column,
            jax.ShapeDtypeStruct((share, width), real),
            jax.ShapeDtypeStruct((2, 3, share, width), real),
            jax.ShapeDtypeStruct((2, share, width), real),
            jax.ShapeDtypeStruct((share, 2 * WIDE), real),
            jax.ShapeDtypeStruct((share, 2 * WIDE), real),
            jax.ShapeDtypeStruct((share, width), real),
        ],
        scratch_shapes=[
            pltpu.VMEM((3, 4 * rows, 128), real),
            pltpu.VMEM((frames, width, pixels), real),
        ],
        compiler_params=pltpu.CompilerParams(vmem_limit_bytes=56 << 20),
    )(
        grad,
        moved,
        latent,
        cotangent,
        flags,
        gain.reshape(width, 1),
        centre,
        inverse,
        reduced,
    )
    output, latent_grad, gain_grad, shift_grad, g_in, g_qkv, g_out, g_up, g_down, g_proj = made
    weights = (
        g_in,
        jnp.transpose(g_qkv, (0, 2, 1, 3)),
        jnp.transpose(g_out, (0, 2, 1)),
        g_up,
        g_down.T,
        g_proj,
    )
    return output, latent_grad, gain_grad.reshape(width), shift_grad.reshape(width), weights


def kernel_body(
    latent,
    clip_flags,
    cotangent,
    norm_gain,
    norm_shift,
    channel_bias,
    hidden_bias,
    weight_in,
    weight_qkv,
    weight_out,
    weight_up,
    weight_down,
    weight_proj,
):
    width = latent.shape[2]
    side = jnp.concatenate
    params = side([norm_gain, norm_shift, channel_bias, jnp.zeros((3, width), jnp.float32)], 0)
    params = side([params, hidden_bias.reshape(4, width), jnp.zeros((4, width), jnp.float32)], 0)
    sent, moved_sent, shards, centre, inverse, bias_moved = enter(
        latent,
        cotangent,
        clip_flags,
        norm_gain[0],
        norm_shift[0],
        weight_in,
        weight_qkv,
        weight_out,
        weight_up,
        weight_down,
        weight_proj,
    )
    whole, q_all, pt_all, streams, qk_all, v_all, slopes, grad, moved, joined = forward_all(
        shards, sent, params, make_positions(), moved_sent
    )
    reduced, q_all, pt_all, unused, unused, grad_back, moved_back, sums, hidden_sums = backward_all(
        whole, q_all, pt_all, streams, qk_all, v_all, slopes, grad, moved, joined
    )
    output, latent_grad, group_gain, group_shift, weights = leave(
        grad_back,
        moved_back,
        latent,
        cotangent,
        clip_flags,
        norm_gain[0],
        centre,
        inverse,
        reduced,
    )
    vectors = jnp.transpose(sums[:10].reshape(10, 4, width), (1, 0, 2)).reshape(4, 10 * width)
    vectors = side([vectors, hidden_sums[:, :2].reshape(4, 2 * WIDE)], 1)
    vectors = jnp.sum(exchange(vectors), 0)
    local = side([vectors, group_gain, group_shift, bias_moved.reshape(width)])
    total = local
    count = lax.axis_size("dp")
    for bit in range(count.bit_length() - 1):
        total = total + lax.ppermute(total, "dp", [(i, i ^ (1 << bit)) for i in range(count)])
    channel, hidden_grad = total[: 10 * width].reshape(10, width), total[10 * width : 14 * width]
    group = total[14 * width :].reshape(3, width)
    return (
        output,
        latent_grad,
        side([group[0:1], channel[0:3]], 0),
        side([group[1:2], channel[3:6]], 0),
        side([channel[6:10], group[2:3]], 0),
        hidden_grad,
    ) + weights


def body(
    latent,
    clip_flags,
    cotangent,
    norm_gain,
    norm_shift,
    channel_bias,
    hidden_bias,
    weight_in,
    weight_qkv,
    weight_out,
    weight_up,
    weight_down,
    weight_proj,
):
    tensor_size = lax.axis_size("tensor")
    slots, frames, width, pixels = latent.shape
    share = weight_in.shape[0]
    hidden_width = hidden_bias.shape[0]
    flags = (clip_flags > 0)[:, None, None, None]

    wide = 2 * width

    shards = []
    side = jnp.concatenate
    for block in range(2):
        shards.append(weight_qkv[block, :, :2].reshape(share, wide))
        other = weight_in if block == 0 else weight_out[0].T
        shards.append(side([weight_qkv[block, :, 2], other], 1))
    shards.append(side([weight_out[1].T, weight_proj], 1))
    shards += [weight_up[:, :wide], weight_up[:, wide:]]
    down_turned = weight_down.T
    shards += [down_turned[:, :wide], down_turned[:, wide:]]
    shards = jnp.stack(shards, 0)
    params = jnp.zeros((24, width), jnp.float32)
    params = params.at[:13].set(side([norm_gain, norm_shift, channel_bias], 0))
    params = params.at[16:20].set(hidden_bias.reshape(4, width))

    start = latent.astype(jnp.float32)
    cot = cotangent.astype(jnp.float32)
    group_width = C // GROUPS
    grouped = start.reshape(slots, frames, width // group_width, group_width, pixels)
    group_centre = jnp.mean(grouped, axis=(1, 3, 4), keepdims=True)
    offset = grouped - group_centre
    group_inverse = lax.rsqrt(jnp.mean(offset * offset, axis=(1, 3, 4), keepdims=True) + 1e-06)
    group_hat = (offset * group_inverse).reshape(start.shape)
    normed = group_hat * norm_gain[0][:, None] + norm_shift[0][:, None]
    sent = by_pixels(normed.astype(jnp.bfloat16), tensor_size)
    rows = sent.shape[1]

    grad_moved_local = jnp.where(flags, cot, 0.0)
    bias_moved = jnp.sum(grad_moved_local, axis=(0, 1, 3))
    grad_moved = exchange(by_pixels(grad_moved_local.astype(jnp.bfloat16), tensor_size))

    empty = jnp.zeros((tensor_size, rows, width), jnp.bfloat16)
    moved_part = side([empty, grad_moved], 2)
    arrived = exchange(sent)
    inputs_in = jnp.transpose(arrived, (1, 0, 2)).reshape(rows, C)
    packed = lax.all_gather(params, "tensor", axis=0, tiled=False)
    joined = jnp.transpose(packed[:, :13], (1, 0, 2)).reshape(13, C)
    gains, shifts, biases = joined[:4], joined[4:8], joined[8:]
    hidden_full = packed[:, 16:20].reshape(tensor_size, 2 * wide)
    whole = gather_plain(shards)
    full_qk = (whole[0], whole[2])
    full_v = (whole[1, :, :, :width], whole[3, :, :, :width])
    full_in = whole[1, :, :, width:]
    full_out = (whole[3, :, :, width:], whole[4, :, :, :width])
    full_proj = whole[4, :, :, width:]
    full_up = (whole[5], whole[6])
    full_down = (whole[7], whole[8])

    def join(parts):
        return jnp.transpose(parts, (1, 0, 2)).reshape(rows, parts.shape[0] * parts.shape[2])

    stream = join(spread(inputs_in, full_in)) + biases[0]
    position = jnp.tile(make_positions(), (rows // FRAMES, 1))
    kept = []
    for block in range(2):
        hat, inverse = layer_stats(stream)
        lifted = (hat * gains[1 + block] + shifts[1 + block] + position).astype(jnp.bfloat16)
        qk = spread(lifted, full_qk[block]).astype(jnp.bfloat16)
        values = spread(lifted, full_v[block]).astype(jnp.bfloat16)
        attended = attend(qk, values)
        stream = stream + collapse(attended, full_out[block]) + biases[1 + block]
        kept.append((hat, inverse, lifted.T, qk, values, attended))
    hat_feed, inverse_feed = layer_stats(stream)
    inputs_up = (hat_feed * gains[3] + shifts[3]).astype(jnp.bfloat16)
    pre_act = [
        spread(inputs_up, full_up[half])
        + hidden_full[:, None, half * wide : half * wide + wide]
        for half in range(2)
    ]
    slopes = [
        jax.vjp(partial(jax.nn.gelu, approximate=False), pre)[1](jnp.ones_like(pre))[0]
        for pre in pre_act
    ]
    hidden = [jax.nn.gelu(pre, approximate=False).astype(jnp.bfloat16) for pre in pre_act]
    stream = stream + collapse(hidden[0], full_down[0]) + collapse(hidden[1], full_down[1])
    stream = stream + biases[3]
    inputs_proj = stream.astype(jnp.bfloat16)
    moved = spread(inputs_proj, full_proj) + biases[4].reshape(tensor_size, 1, width)
    moved = moved.astype(jnp.bfloat16)

    bias_grads = [None] * 4
    gain_grads = [None] * 3
    shift_grads = [None] * 3
    turned, parts = [None] * 8, [None] * 12
    turned[1], turned[5], turned[7] = inputs_up.T, inputs_proj.T, inputs_in.T
    parts[0], parts[1] = hidden[1], hidden[0]
    parts[9] = moved_part
    grad_stream = collapse(grad_moved, full_proj)
    bias_grads[3] = jnp.sum(grad_stream, 0)
    grad_low = grad_stream.astype(jnp.bfloat16)
    turned[0] = grad_low.T
    hidden_grads = [None, None]
    grad_normed = 0.0
    for half in (1, 0):
        grad_hidden = spread(grad_low, full_down[half])
        grad_pre = grad_hidden * slopes[half]
        hidden_grads[half] = jnp.sum(grad_pre, 1)
        parts[3 - half] = grad_pre.astype(jnp.bfloat16)
        grad_normed = grad_normed + collapse(parts[3 - half], full_up[half])
    hidden_grad = side(hidden_grads, 1)
    grad_layer, gain_grads[2], shift_grads[2] = layer_back(
        grad_normed, hat_feed, inverse_feed, gains[3]
    )
    grad_stream = grad_stream + grad_layer
    for block in (1, 0):
        hat, inverse, lifted_turned, qk, values, attended = kept[block]
        bias_grads[1 + block] = jnp.sum(grad_stream, 0)
        grad_low = grad_stream.astype(jnp.bfloat16)
        turned[2 if block == 1 else 6] = grad_low.T
        pair = [attended, empty] if block == 1 else [empty, attended]
        parts[4 if block == 1 else 10] = side(pair, 2)
        grad_attended = spread(grad_low, full_out[block]).astype(jnp.bfloat16)
        grad_qk, grad_values = attend_back(qk, values, grad_attended)
        turned[3 if block == 1 else 4] = lifted_turned
        parts[6 if block == 1 else 8] = side([grad_values, empty], 2)
        parts[5 if block == 1 else 7] = grad_qk
        grad_lifted = collapse(grad_qk, full_qk[block]) + collapse(grad_values, full_v[block])
        grad_layer, gain_grads[block], shift_grads[block] = layer_back(
            grad_lifted, hat, inverse, gains[1 + block]
        )
        grad_stream = grad_stream + grad_layer
    bias_grads[0] = jnp.sum(grad_stream, 0)
    grad_low = grad_stream.astype(jnp.bfloat16)
    grad_low_parts = jnp.transpose(grad_low.reshape(rows, tensor_size, width), (1, 0, 2))
    parts[11] = side([empty, grad_low_parts], 2)
    turned, parts = jnp.stack(turned, 0), jnp.stack(parts, 0)
    reduced = reduce_plain(turned, parts)
    grad_normed = collapse(grad_low_parts, full_in).astype(jnp.bfloat16)
    grad_normed = jnp.transpose(grad_normed.reshape(rows, tensor_size, width), (1, 0, 2))
    arrived_grad = exchange(grad_normed)
    vectors = jnp.stack(gain_grads + shift_grads + bias_grads, 0)

    moved_local = back_to_channels(exchange(moved), slots, pixels).astype(jnp.float32)
    output = jnp.where(flags, start + moved_local, start).astype(jnp.bfloat16)

    qkv_grads = [
        side([reduced[7 - 2 * block], reduced[8 - 2 * block, :, :width]], 1).reshape(share, 3, width)
        for block in range(2)
    ]
    out_grads = [reduced[6, :, width:].T, reduced[4, :, :width].T]
    in_grad, proj_grad = reduced[8, :, width:], reduced[4, :, width:]
    up_grad = side([reduced[3], reduced[2]], 1)
    down_grad = side([reduced[1], reduced[0]], 1)
    grad_normed = back_to_channels(arrived_grad, slots, pixels).astype(jnp.float32)
    scaled = grad_normed * norm_gain[0][:, None]
    scaled_groups = scaled.reshape(grouped.shape)
    hat_groups = group_hat.reshape(grouped.shape)
    first = jnp.mean(scaled_groups, axis=(1, 3, 4), keepdims=True)
    second = jnp.mean(scaled_groups * hat_groups, axis=(1, 3, 4), keepdims=True)
    grad_group = group_inverse * (scaled_groups - first - hat_groups * second)
    latent_grad = cot + grad_group.reshape(start.shape)
    group_gain_grad = jnp.sum(grad_normed * group_hat, axis=(0, 1, 3))
    group_shift_grad = jnp.sum(grad_normed, axis=(0, 1, 3))

    vectors = jnp.transpose(vectors.reshape(10, tensor_size, width), (1, 0, 2))
    vectors = jnp.concatenate([vectors.reshape(tensor_size, 10 * width), hidden_grad], 1)
    vectors = lax.psum_scatter(vectors, "tensor", scatter_dimension=0, tiled=False)
    sums = lax.psum(
        jnp.concatenate([vectors, group_gain_grad, group_shift_grad, bias_moved]), "dp"
    )
    channel_sums = sums[: 10 * width].reshape(10, width)
    hidden_bias_grad = sums[10 * width : 10 * width + hidden_width]
    local_sums = sums[10 * width + hidden_width :].reshape(3, width)
    gain_grad = jnp.concatenate([local_sums[0:1], channel_sums[0:3]], 0)
    shift_grad = jnp.concatenate([local_sums[1:2], channel_sums[3:6]], 0)
    channel_bias_grad = jnp.concatenate([channel_sums[6:10], local_sums[2:3]], 0)
    return (
        output,
        latent_grad,
        gain_grad,
        shift_grad,
        channel_bias_grad,
        hidden_bias_grad,
        in_grad,
        jnp.stack(qkv_grads, 0),
        jnp.stack(out_grads, 0),
        up_grad,
        down_grad.T,
        proj_grad,
    )


def solution(mesh):
    placed = (
        P("dp", None, "tensor", None),
        P("dp"),
        P("dp", None, "tensor", None),
        P(None, "tensor"),
        P(None, "tensor"),
        P(None, "tensor"),
        P("tensor"),
        P("dp", "tensor"),
        P(None, "dp", None, "tensor"),
        P(None, "tensor", "dp"),
        P("dp", "tensor"),
        P("tensor", "dp"),
        P("dp", "tensor"),
    )
    kernels_fit = (mesh.shape["dp"], mesh.shape["tensor"]) == (8, 4)
    return jax.shard_map(
        kernel_body if kernels_fit else body,
        mesh=mesh,
        in_specs=placed,
        out_specs=(
            P("dp", None, "tensor", None),
            P("dp", None, "tensor", None),
            P(None, "tensor"),
            P(None, "tensor"),
            P(None, "tensor"),
            P("tensor"),
            P("dp", "tensor"),
            P(None, "dp", None, "tensor"),
            P(None, "tensor", "dp"),
            P("dp", "tensor"),
            P("tensor", "dp"),
            P("dp", "tensor"),
        ),
        check_vma=False,
    )
```

```python
from functools import partial
import math

import jax
import jax.numpy as jnp
from jax import lax
from jax.experimental import pallas as pl
from jax.experimental.pallas import tpu as pltpu
from jax.sharding import PartitionSpec as P

C = 1280
GROUPS = 32
FRAMES = 16
HEAD = 160
BLOCK = 128
MIXED = ("tensor", "dp")


def spread(rows, weight):
    return jnp.einsum("rk,tkn->trn", rows, weight, preferred_element_type=jnp.float32)


def collapse(parts, weight):
    return jnp.einsum("trn,tkn->rk", parts, weight, preferred_element_type=jnp.float32)


def make_positions():
    channel_ids = jnp.arange(C)
    pair_rate = jnp.exp((channel_ids // 2).astype(jnp.float32) * (-2.0 * math.log(10000.0) / C))
    angles = jnp.arange(FRAMES).astype(jnp.float32)[:, None] * pair_rate[None, :]
    return jnp.where(channel_ids[None, :] % 2 == 0, jnp.sin(angles), jnp.cos(angles))


def layer_stats(stream):
    centre = jnp.mean(stream, axis=1, keepdims=True)
    offset = stream - centre
    inverse = lax.rsqrt(jnp.mean(offset * offset, axis=1, keepdims=True) + 1e-05)
    return offset * inverse, inverse


def layer_back(grad_out, normal_part, inverse, gain):
    scaled = grad_out * gain
    first = jnp.mean(scaled, axis=1, keepdims=True)
    second = jnp.mean(scaled * normal_part, axis=1, keepdims=True)
    grad_in = inverse * (scaled - first - normal_part * second)
    return grad_in, jnp.sum(grad_out * normal_part, 0), jnp.sum(grad_out, 0)


def dot_rows(left, right):
    return lax.dot_general(left, right, (((1,), (1,)), ((), ())), preferred_element_type=jnp.float32)


def dot_plain(left, right):
    return lax.dot_general(left, right, (((1,), (0,)), ((), ())), preferred_element_type=jnp.float32)


def dot_first(left, right):
    return lax.dot_general(left, right, (((0,), (0,)), ((), ())), preferred_element_type=jnp.float32)


def same_pixel(block):
    row = lax.broadcasted_iota(jnp.int32, (block, block), 0) // FRAMES
    col = lax.broadcasted_iota(jnp.int32, (block, block), 1) // FRAMES
    return row == col


def head_probs(query, key, same, scale):
    scores = jnp.where(same, dot_rows(query, key) * scale, -1e30)
    top = jnp.max(scores, axis=1, keepdims=True)
    weights = jnp.where(same, jnp.exp(scores - top), 0.0)
    return weights / jnp.sum(weights, axis=1, keepdims=True)


def attend_kernel(scale, qk_ref, v_ref, out_ref):
    rows, width = out_ref.shape[1], out_ref.shape[2]
    block = min(BLOCK, rows)
    same = same_pixel(block)
    for start in range(0, rows, block):
        for head in range(width // HEAD):
            here, low = slice(start, start + block), head * HEAD
            query = qk_ref[0, here, low : low + HEAD]
            key = qk_ref[0, here, width + low : width + low + HEAD]
            value = v_ref[0, here, low : low + HEAD]
            probs = head_probs(query, key, same, scale).astype(jnp.bfloat16)
            out_ref[0, here, low : low + HEAD] = dot_plain(probs, value).astype(jnp.bfloat16)


def part_spec(array):
    return pl.BlockSpec((1,) + array.shape[1:], lambda t: (t, 0, 0))


def attend(qk, values):
    return pl.pallas_call(
        partial(attend_kernel, 1.0 / math.sqrt(HEAD)),
        grid=(qk.shape[0],),
        in_specs=[part_spec(qk), part_spec(values)],
        out_specs=part_spec(values),
        out_shape=jax.ShapeDtypeStruct(values.shape, jnp.bfloat16),
        compiler_params=pltpu.CompilerParams(vmem_limit_bytes=32 << 20),
    )(qk, values)


def attend_back_kernel(scale, qk_ref, v_ref, grad_ref, dqk_ref, dv_ref):
    rows, width = grad_ref.shape[1], grad_ref.shape[2]
    block = min(BLOCK, rows)
    same = same_pixel(block)
    for start in range(0, rows, block):
        for head in range(width // HEAD):
            here, low = slice(start, start + block), head * HEAD
            query = qk_ref[0, here, low : low + HEAD]
            key = qk_ref[0, here, width + low : width + low + HEAD]
            value = v_ref[0, here, low : low + HEAD]
            grad = grad_ref[0, here, low : low + HEAD]
            probs = head_probs(query, key, same, scale)
            grad_probs = dot_rows(grad, value)
            centred = jnp.sum(probs * grad_probs, axis=1, keepdims=True)
            grad_raw = (probs * (grad_probs - centred) * scale).astype(jnp.bfloat16)
            dqk_ref[0, here, low : low + HEAD] = dot_plain(grad_raw, key).astype(jnp.bfloat16)
            dqk_ref[0, here, width + low : width + low + HEAD] = dot_first(grad_raw, query).astype(
                jnp.bfloat16
            )
            dv_ref[0, here, low : low + HEAD] = dot_first(probs.astype(jnp.bfloat16), grad).astype(
                jnp.bfloat16
            )


def attend_back(qk, values, grad):
    return pl.pallas_call(
        partial(attend_back_kernel, 1.0 / math.sqrt(HEAD)),
        grid=(qk.shape[0],),
        in_specs=[part_spec(qk), part_spec(values), part_spec(values)],
        out_specs=[part_spec(qk), part_spec(values)],
        out_shape=[
            jax.ShapeDtypeStruct(qk.shape, jnp.bfloat16),
            jax.ShapeDtypeStruct(values.shape, jnp.bfloat16),
        ],
        compiler_params=pltpu.CompilerParams(vmem_limit_bytes=32 << 20),
    )(qk, values, grad)


UNITS = 9
WIDE = 640
SLOTS_IN_FLIGHT = 6
SLOTS_RECEIVED = 4
AHEAD = 4
ROWS_A = 96
MESH_ID = pl.DeviceIdType.MESH


class Place:
    def __init__(self):
        dp, tn = lax.axis_index("dp"), lax.axis_index("tensor")
        self.z, self.x = dp // 2, dp % 2
        self.y, self.c = tn // 2, tn % 2
        self.far_x, self.far_y = 1 - self.x, 1 - self.y
        self.to = {
            "x": (self.z * 2 + self.far_x, tn),
            "y": (dp, self.far_y * 2 + self.c),
            "core": (dp, self.y * 2 + 1 - self.c),
            "cross": (dp, self.far_y * 2 + 1 - self.c),
            "up": (dp + 2, tn),
            "down": (dp - 2, tn),
        }
        self.has_up = self.z < 3
        self.has_down = self.z > 0

    def greet(self):
        barrier = pltpu.get_barrier_semaphore()

        def hello(name):
            pl.semaphore_signal(barrier, inc=1, device_id=self.to[name], device_id_type=MESH_ID)

        for name in ("x", "y", "core", "cross"):
            hello(name)
        pl.when(self.has_up)(lambda: hello("up"))
        pl.when(self.has_down)(lambda: hello("down"))
        pl.semaphore_wait(barrier, 4 + (6 - self.z) // 4 + (self.z + 3) // 4)


class Plan:
    FIELDS = (
        ("kind", 16),
        ("unit", 16),
        ("t", 4),
        ("aux", 128),
        ("slot", 2),
        ("fresh", 2),
        ("next", 64),
        ("early", 32),
    )

    def __init__(self, per_turn, loads_early=False):
        self.per_turn, self.loads_early = per_turn, loads_early
        self.steps = {}

    def fill(self, turn, steps):
        tiles = [index for index, step in enumerate(steps) if step[1] is not None]
        early = {}
        for order, index in enumerate(tiles):
            if self.loads_early and steps[index][0] == 1:
                early[tiles[order - 1] if order else index] = 1 + steps[index][3] * 4 + steps[index][2]
        for index, (kind, unit, t, aux) in enumerate(steps):
            slot = fresh = following = 0
            if unit is not None:
                order = tiles.index(index)
                slot, fresh = order % 2, int(order == 0)
                if order + 1 < len(tiles):
                    later = steps[tiles[order + 1]]
                    following = 1 + later[1] * 4 + later[2]
            values = (kind, unit or 0, t, aux, slot, fresh, following, early.get(index, 0))
            code, scale = 0, 1
            for (name, size), value in zip(self.FIELDS, values):
                assert 0 <= value < size
                code += scale * value
                scale *= size
            place = turn * self.per_turn + index * self.per_turn // len(steps)
            assert place not in self.steps
            self.steps[place] = code

    def code(self, place):
        code = jnp.int32(0)
        for where, value in self.steps.items():
            code = jnp.where(place == where, jnp.int32(value), code)
        return code

    def fields(self, code):
        out = {}
        for name, size in self.FIELDS:
            out[name] = code % size
            code = code // size
        return out


def await_bytes(ref, sem):
    pltpu.make_async_copy(ref, ref, sem).wait()


def forward_kernel(
    shard_ref,
    x_ref,
    params_ref,
    position_ref,
    grad_ref,
    whole_ref,
    q_ref,
    pt_ref,
    stream_out_ref,
    qk_ref,
    v_ref,
    slope_ref,
    grad_got,
    moved_ref,
    joined_ref,
    stream,
    xb,
    ptb,
    x_got,
    params_got,
    hidden_bias,
    qkb,
    vb,
    cols,
    slopeb,
    first_rows,
    total,
    wb,
    tile_sem,
    save_sem,
    kept_sem,
    peer_send,
    peer_recv,
    local_sem,
    send_sem,
    recv_sem,
    core_sem,
):
    at = Place()
    z, x, y, c = at.z, at.x, at.y, at.c
    share = shard_ref.shape[1]
    cut = (pl.ds(0, ROWS_A), pl.ds(ROWS_A, share - ROWS_A))
    kinds = {"up": 0, "down": 1, "x": 2, "y": 3, "core": 4}
    at.greet()

    def send(unit, colour, yy, zz, xx, kind, own=False):
        place = whole_ref.at[unit, yy, c, zz, xx, cut[colour]]
        pltpu.make_async_remote_copy(
            src_ref=shard_ref.at[unit, cut[colour]] if own else place,
            dst_ref=place,
            send_sem=send_sem.at[unit, colour, kinds[kind]],
            recv_sem=recv_sem.at[unit, colour, yy, zz, xx],
            device_id=at.to[kind],
            device_id_type=MESH_ID,
        ).start()

    def arrived(unit, colour, yy, zz, xx):
        await_bytes(
            whole_ref.at[unit, yy, c, zz, xx, cut[colour]], recv_sem.at[unit, colour, yy, zz, xx]
        )

    def own_copy(unit):
        return pltpu.make_async_copy(
            shard_ref.at[unit], whole_ref.at[unit, y, c, z, x], local_sem.at[unit]
        )

    def to_core(unit, part):
        if part == 2:
            place = whole_ref.at[unit, :, c, :, :, cut[1]]
        else:
            place = whole_ref.at[unit, y if part == 0 else at.far_y, c, :, :, cut[0]]
        return pltpu.make_async_remote_copy(
            src_ref=place,
            dst_ref=place,
            send_sem=send_sem.at[unit, part // 2, 4],
            recv_sem=core_sem.at[unit, part],
            device_id=at.to["core"],
            device_id_type=MESH_ID,
        )

    def from_z(unit, colour, step, yy):
        @pl.when(z >= step)
        def _():
            zz = z - step
            arrived(unit, colour, yy, zz, x)
            pl.when(at.has_up)(lambda: send(unit, colour, yy, zz, x, "up"))
            send(unit, colour, yy, zz, x, "x")
            if colour == 0:
                send(unit, colour, yy, zz, x, "y")

        @pl.when(z + step <= 3)
        def _():
            zz = z + step
            arrived(unit, colour, yy, zz, x)
            pl.when(at.has_down)(lambda: send(unit, colour, yy, zz, x, "down"))
            send(unit, colour, yy, zz, x, "x")
            if colour == 0:
                send(unit, colour, yy, zz, x, "y")

    def from_x(unit, step):
        def one(zz):
            arrived(unit, 0, y, zz, at.far_x)
            send(unit, 0, y, zz, at.far_x, "y")

        if step == 0:
            one(z)
        else:
            pl.when(z >= step)(lambda: one(z - step))
            pl.when(z + step <= 3)(lambda: one(z + step))

    def stage0(unit):
        own_copy(unit).start()
        pl.when(at.has_up)(lambda: send(unit, 0, y, z, x, "up", True))
        pl.when(at.has_down)(lambda: send(unit, 0, y, z, x, "down", True))
        send(unit, 1, y, z, x, "y", True)
        send(unit, 0, y, z, x, "x", True)
        pl.when(at.has_up)(lambda: send(unit, 1, y, z, x, "up", True))
        pl.when(at.has_down)(lambda: send(unit, 1, y, z, x, "down", True))
        send(unit, 0, y, z, x, "y", True)
        send(unit, 1, y, z, x, "x", True)

    def stage1(unit):
        from_z(unit, 0, 1, y)
        arrived(unit, 1, at.far_y, z, x)
        pl.when(at.has_up)(lambda: send(unit, 1, at.far_y, z, x, "up"))
        pl.when(at.has_down)(lambda: send(unit, 1, at.far_y, z, x, "down"))
        send(unit, 1, at.far_y, z, x, "x")
        from_z(unit, 1, 1, y)
        from_x(unit, 0)

    def stage2(unit):
        from_z(unit, 0, 2, y)
        from_z(unit, 1, 1, at.far_y)
        from_z(unit, 1, 2, y)
        from_x(unit, 1)

    def stage3(unit):
        from_z(unit, 0, 3, y)
        from_z(unit, 1, 2, at.far_y)
        from_z(unit, 1, 3, y)
        from_x(unit, 2)

    def stage4(unit):
        from_z(unit, 1, 3, at.far_y)
        from_x(unit, 3)
        own_copy(unit).wait()
        to_core(unit, 0).start()

    def stage5(unit):
        for zz in range(4):
            for xx in range(2):
                arrived(unit, 0, at.far_y, zz, xx)
        to_core(unit, 1).start()
        for zz in range(4):
            for yy in range(2):
                arrived(unit, 1, yy, zz, at.far_x)
        to_core(unit, 2).start()

    def stage6(unit):
        other = 1 - c
        await_bytes(whole_ref.at[unit, y, other, :, :, cut[0]], core_sem.at[unit, 0])
        await_bytes(whole_ref.at[unit, at.far_y, other, :, :, cut[0]], core_sem.at[unit, 1])
        await_bytes(whole_ref.at[unit, :, other, :, :, cut[1]], core_sem.at[unit, 2])
        for colour in range(2):
            rows = cut[colour]
            await_bytes(whole_ref.at[unit, :, c, :, :, rows], send_sem.at[unit, colour, 4])
            whole_x = whole_ref.at[unit, 0, c, :, 0, rows] if colour == 0 else None
            if colour == 0:
                await_bytes(whole_x, send_sem.at[unit, 0, 2])
                await_bytes(whole_ref.at[unit, 0, c, :, :, rows], send_sem.at[unit, 0, 3])
            else:
                await_bytes(whole_ref.at[unit, 0, c, :, :, rows], send_sem.at[unit, 1, 2])
                await_bytes(whole_ref.at[unit, 0, c, 0, 0, rows], send_sem.at[unit, 1, 3])
            for level in range(3):

                def ups(level=level):
                    if colour == 0:
                        ref = whole_ref.at[unit, 0, c, pl.ds(0, level + 1), 0, rows]
                    else:
                        ref = whole_ref.at[unit, :, c, pl.ds(0, level + 1), 0, rows]
                    return ref

                pl.when(z == level)(
                    lambda level=level: await_bytes(ups(level), send_sem.at[unit, colour, 0])
                )
                pl.when(z == 3 - level)(
                    lambda level=level: await_bytes(ups(level), send_sem.at[unit, colour, 1])
                )

    stages = (stage0, stage1, stage2, stage3, stage4, stage5, stage6)

    rows_all, width = x_ref.shape[1], x_ref.shape[2]
    half_rows = rows_all // 2
    scale = 1.0 / math.sqrt(HEAD)
    own_t = y * 2 + c

    def save_now(source, target):
        copy = pltpu.make_async_copy(source, target, save_sem.at[0])
        copy.start()
        copy.wait()

    peers = (("y", at.far_y * 2 + c), ("core", y * 2 + 1 - c), ("cross", at.far_y * 2 + 1 - c))

    def peer_copies(index):
        kind, t = peers[index]
        target = {"device_id": at.to[kind], "device_id_type": MESH_ID}
        return (
            pltpu.make_async_remote_copy(
                src_ref=params_ref,
                dst_ref=params_got.at[own_t],
                send_sem=peer_send.at[0, index],
                recv_sem=peer_recv.at[0, index],
                **target,
            ),
            pltpu.make_async_remote_copy(
                src_ref=x_ref.at[t],
                dst_ref=x_got.at[own_t],
                send_sem=peer_send.at[1, index],
                recv_sem=peer_recv.at[1, index],
                **target,
            ),
            pltpu.make_async_remote_copy(
                src_ref=grad_ref.at[t],
                dst_ref=grad_got.at[own_t],
                send_sem=peer_send.at[2, index],
                recv_sem=peer_recv.at[2, index],
                **target,
            ),
        )

    own_peer = (
        pltpu.make_async_copy(params_ref, params_got.at[own_t], peer_send.at[0, 3]),
        pltpu.make_async_copy(x_ref.at[own_t], x_got.at[own_t], peer_send.at[1, 3]),
        pltpu.make_async_copy(grad_ref.at[own_t], grad_got.at[own_t], peer_send.at[2, 3]),
    )
    for index in range(3):
        for copy in peer_copies(index):
            copy.start()
    for copy in own_peer:
        copy.start()

    def each(count, size, use):
        def one(step, carry):
            use(pl.ds(pl.multiple_of(step * size, size), size))
            return carry

        lax.fori_loop(0, count, one, 0)

    def tile_load(unit, t, slot):
        return pltpu.make_async_copy(whole_ref.at[unit, t // 2, t % 2], wb.at[slot], tile_sem.at[slot])

    def kept_copies(which, t):
        target = (10, 4, 1, 0)[which]
        copies = [
            pltpu.make_async_copy(cols.at[which, t], q_ref.at[target, t], kept_sem.at[which, t, 0])
        ]
        if which < 2:
            pairs = [(qkb.at[which, t], qk_ref.at[which, t]), (vb.at[which, t], v_ref.at[which, t])]
        else:
            pairs = [(slopeb.at[which - 2, t], slope_ref.at[which - 2, t])]
        for index, (source, target_ref) in enumerate(pairs):
            copies.append(
                pltpu.make_async_copy(source, target_ref, kept_sem.at[which, t, 1 + index])
            )
        return copies

    def do_spread(op):
        matrix = op["slot"]
        t, aux = op["t"], op["aux"]

        def multiply(rows):
            total[rows, :] = dot_plain(xb[rows, :], wb[matrix].reshape(C, WIDE))

        each(2, half_rows, multiply)
        quarter = rows_all // 4

        @pl.when(aux == 0)
        def _():
            def use(rows):
                first_rows[t, rows, :] = total[rows, width:]

            each(4, quarter, use)

        @pl.when((aux == 1) | (aux == 3))
        def _():
            def use(rows):
                qkb[(aux - 1) // 2, t, rows, :] = total[rows, :].astype(jnp.bfloat16)

            each(4, quarter, use)

        @pl.when((aux == 2) | (aux == 4))
        def _():
            def use(rows):
                vb[(aux - 2) // 2, t, rows, :] = total[rows, 0:width].astype(jnp.bfloat16)

            each(4, quarter, use)

        @pl.when((aux == 5) | (aux == 6))
        def _():
            half = aux - 5

            def use(rows):
                pre = total[rows, :] + hidden_bias[t, pl.ds(half, 1), :]
                below = 0.5 * (1.0 + lax.erf(pre * math.sqrt(0.5)))
                cols[2 + half, t, rows, :] = (pre * below).astype(jnp.bfloat16)
                density = jnp.exp(-0.5 * pre * pre) * (1.0 / math.sqrt(2.0 * math.pi))
                slopeb[half, t, rows, :] = (below + pre * density).astype(jnp.bfloat16)

            each(rows_all // 32, 32, use)
            for which in (2, 3):

                @pl.when(half == which - 2)
                def _(which=which):
                    for copy in kept_copies(which, t):
                        copy.start()

        @pl.when(aux == 7)
        def _():
            def use(rows):
                moved_ref[t, rows, :] = (total[rows, width:] + params_got[t, 12:13, :]).astype(
                    jnp.bfloat16
                )

            each(4, quarter, use)

    def do_collapse(op):
        def multiply(rows):
            stream[rows, :] += dot_rows(cols[op["aux"], op["t"], rows, :], wb[op["slot"]].reshape(C, WIDE))

        each(2, half_rows, multiply)

    def do_attention(op):
        block, t = op["aux"], op["t"]
        same = same_pixel(BLOCK)

        def write(place):
            for start in range(0, rows_all, BLOCK):
                here = slice(start, start + BLOCK)
                for head in range(width // HEAD):
                    low = head * HEAD
                    query = qkb[block, t, here, low : low + HEAD]
                    key = qkb[block, t, here, width + low : width + low + HEAD]
                    value = vb[block, t, here, low : low + HEAD]
                    probs = head_probs(query, key, same, scale).astype(jnp.bfloat16)
                    total[here, low : low + HEAD] = dot_plain(probs, value)

        write(0)
        for which in range(2):

            @pl.when(block == which)
            def _(which=which):
                own = slice(width, 2 * width) if which == 0 else slice(0, width)
                other = slice(0, width) if which == 0 else slice(width, 2 * width)

                def use(rows):
                    cols[which, t, rows, own] = total[rows, 0:width].astype(jnp.bfloat16)
                    cols[which, t, rows, other] = jnp.zeros((rows_all // 4, width), jnp.bfloat16)

                each(4, rows_all // 4, use)
                for copy in kept_copies(which, t):
                    copy.start()

    chunk = 4 * FRAMES

    def do_norm(op):
        layer = op["aux"]

        def use(rows):
            @pl.when(layer == 0)
            def _():
                for t in range(4):
                    stream[rows, t * width : (t + 1) * width] = first_rows[t, rows, :]

            values = stream[rows, :] + joined_ref[pl.ds(8 + layer, 1), :]
            stream[rows, :] = values
            centre = jnp.mean(values, axis=1, keepdims=True)
            offset = values - centre
            inverse = lax.rsqrt(jnp.mean(offset * offset, axis=1, keepdims=True) + 1e-05)
            normed = offset * inverse * joined_ref[pl.ds(1 + layer, 1), :]
            normed = normed + joined_ref[pl.ds(5 + layer, 1), :]
            added = jnp.where(layer < 2, position_ref[...], 0.0)
            normed = normed.reshape(chunk // FRAMES, FRAMES, C) + added[None]
            xb[rows, :] = normed.reshape(chunk, C).astype(jnp.bfloat16)

        each(rows_all // chunk, chunk, use)
        save_now(stream, stream_out_ref.at[layer])

    def do_turn(op):
        def one(step, carry):
            lanes = pl.ds(pl.multiple_of(step * 128, 128), 128)
            ptb[lanes, :] = xb[:, lanes].T
            return carry

        lax.fori_loop(0, C // 128, one, 0)
        save_now(ptb, pt_ref.at[op["aux"]])

    def do_last(op):
        def use(rows):
            xb[rows, :] = (stream[rows, :] + joined_ref[11:12, :]).astype(jnp.bfloat16)

        each(rows_all // chunk, chunk, use)

    def do_join(op):
        for index in range(3):
            for copy in peer_copies(index)[:2]:
                copy.wait_recv()
        for copy in own_peer[:2]:
            copy.wait()
        for t in range(4):
            lanes = slice(t * width, (t + 1) * width)
            joined_ref[:, lanes] = params_got[t, 0:16, :]

            def use(rows, t=t, lanes=lanes):
                xb[rows, lanes] = x_got[t, rows, :]

            each(4, rows_all // 4, use)
            for half in range(2):
                for part in range(2):
                    row = 16 + 2 * half + part
                    hidden_bias[t, half : half + 1, part * width : (part + 1) * width] = params_got[
                        t, row : row + 1, :
                    ]

    works = (None, do_spread, do_collapse, do_attention, do_norm, do_turn, do_last, do_join)
    four = range(4)

    def spreads(unit, aux):
        return [(1, unit, t, aux) for t in four]

    def collapses(unit, aux):
        return [(2, unit, t, aux) for t in four]

    def attentions(aux):
        return [(3, None, t, aux) for t in four]

    count = len(stages)
    places = 2 * count
    plan = Plan(places)
    for ready, steps in {
        -4: [(7, None, 0, 0), (5, None, 0, 7)],
        1: spreads(1, 0) + [(4, None, 0, 0)] + spreads(0, 1) + spreads(1, 2),
        2: [(5, None, 0, 4)] + attentions(0),
        3: collapses(3, 0) + [(4, None, 0, 1)] + spreads(2, 3) + spreads(3, 4),
        4: [(5, None, 0, 3)] + attentions(1) + collapses(4, 1) + [(4, None, 0, 2)],
        5: [(5, None, 0, 1)] + spreads(5, 5),
        6: spreads(6, 6),
        7: collapses(7, 2),
        8: collapses(8, 3) + [(6, None, 0, 0)] + spreads(4, 7) + [(5, None, 0, 5)],
    }.items():
        plan.fill(ready + count - 1, steps)

    def do_step(place):
        code = plan.code(place)
        pl.when(code > 0)(lambda: do_filled(code))

    def do_filled(code):
        op = plan.fields(code)
        has_tile = (op["kind"] == 1) | (op["kind"] == 2)

        @pl.when(has_tile)
        def _():
            pl.when(op["fresh"] == 1)(lambda: tile_load(op["unit"], op["t"], op["slot"]).start())

            @pl.when(op["next"] > 0)
            def _():
                following = op["next"] - 1
                tile_load(following // 4, following % 4, 1 - op["slot"]).start()

            tile_load(op["unit"], op["t"], op["slot"]).wait()

        for kind in range(1, len(works)):

            @pl.when(op["kind"] == kind)
            def _(kind=kind):
                works[kind](op)

    def advance(turn, carry):
        def inner(place, carry):
            for spot, number in enumerate((count - 1, 0) + tuple(range(count - 2, 0, -1))):
                unit = turn - number + (AHEAD if number == 0 else 0)
                if number == 0:

                    @pl.when((place == spot) & (turn == 0))
                    def _():
                        def begin(unit, carry):
                            stage0(unit)
                            return carry

                        lax.fori_loop(0, AHEAD, begin, 0)

                @pl.when((place == spot) & (unit >= 0) & (unit < UNITS))
                def _(number=number, unit=unit):
                    stages[number](unit)

            def two(step, carry):
                do_step(2 * (turn * count + place) + step)
                return carry

            return lax.fori_loop(0, 2, two, carry)

        return lax.fori_loop(0, count, inner, carry)

    lax.fori_loop(0, UNITS + count - 1, advance, 0)
    for which in range(4):
        for t in range(4):
            for copy in kept_copies(which, t):
                copy.wait()
    for index in range(3):
        for copy in peer_copies(index):
            copy.wait_send()
        peer_copies(index)[2].wait_recv()
    own_peer[2].wait()


def forward_all(shards, rows_in, params, position, grad):
    units, share, wide = shards.shape
    rows, width = rows_in.shape[1], rows_in.shape[2]
    low = jnp.bfloat16
    anywhere, near = pl.BlockSpec(memory_space=pl.ANY), pl.BlockSpec(memory_space=pltpu.VMEM)
    return pl.pallas_call(
        forward_kernel,
        in_specs=[near, anywhere, near, near, near],
        out_specs=[anywhere] * 8 + [near] * 2,
        out_shape=[
            jax.ShapeDtypeStruct((units, 2, 2, 4, 2, share, wide), low),
            jax.ShapeDtypeStruct((12, 4, rows, wide), low),
            jax.ShapeDtypeStruct((8, C, rows), low),
            jax.ShapeDtypeStruct((3, rows, C), jnp.float32),
            jax.ShapeDtypeStruct((2, 4, rows, wide), low),
            jax.ShapeDtypeStruct((2, 4, rows, width), low),
            jax.ShapeDtypeStruct((2, 4, rows, wide), low),
            jax.ShapeDtypeStruct((4, rows, width), low),
            jax.ShapeDtypeStruct((4, rows, width), low),
            jax.ShapeDtypeStruct((16, C), jnp.float32),
        ],
        scratch_shapes=[
            pltpu.VMEM((rows, C), jnp.float32),
            pltpu.VMEM((rows, C), low),
            pltpu.VMEM((C, rows), low),
            pltpu.VMEM((4, rows, width), low),
            pltpu.VMEM((4,) + params.shape, jnp.float32),
            pltpu.VMEM((4, 8, wide), jnp.float32),
            pltpu.VMEM((2, 4, rows, wide), low),
            pltpu.VMEM((2, 4, rows, width), low),
            pltpu.VMEM((4, 4, rows, wide), low),
            pltpu.VMEM((2, 4, rows, wide), low),
            pltpu.VMEM((4, rows, width), jnp.float32),
            pltpu.VMEM((rows, wide), jnp.float32),
            pltpu.VMEM((2, 4, 2, share, wide), low),
            pltpu.SemaphoreType.DMA((2,)),
            pltpu.SemaphoreType.DMA((1,)),
            pltpu.SemaphoreType.DMA((4, 4, 3)),
            pltpu.SemaphoreType.DMA((3, 4)),
            pltpu.SemaphoreType.DMA((3, 3)),
            pltpu.SemaphoreType.DMA((units,)),
            pltpu.SemaphoreType.DMA((units, 2, 5)),
            pltpu.SemaphoreType.DMA((units, 2, 2, 4, 2)),
            pltpu.SemaphoreType.DMA((units, 3)),
        ],
        compiler_params=pltpu.CompilerParams(
            collective_id=0, has_side_effects=True, vmem_limit_bytes=60 << 20
        ),
    )(shards, rows_in, params, position, grad)


def backward_kernel(
    whole_ref,
    q_given,
    pt_given,
    streams_ref,
    qk_ref,
    v_ref,
    slope_ref,
    grad_ref,
    moved_ref,
    joined_ref,
    out_ref,
    q_ref,
    pt_ref,
    ptx_ref,
    qx_ref,
    got_ref,
    moved_got,
    vec_ref,
    hidden_ref,
    p_buf,
    q_buf,
    dw,
    rya,
    rxa,
    rua,
    rda,
    rxb,
    rub,
    rdb,
    ryb,
    gs,
    gn,
    xb,
    ptb,
    wb,
    cb,
    av,
    datt,
    total,
    sb,
    ob,
    dn,
    load_sem,
    give_sem,
    take_sem,
    send_sem,
    recv_sem,
    tile_sem,
    aux_sem,
    route_sem,
    misc_sem,
    out_sem,
    peer_send,
    peer_recv,
):
    at = Place()
    z, x, y, c = at.z, at.x, at.y, at.c
    far_x, far_y = at.far_x, at.far_y
    share = out_ref.shape[1]
    row_a, row_b = pl.ds(0, ROWS_A), pl.ds(ROWS_A, share - ROWS_A)
    rows_all, width = got_ref.shape[1], got_ref.shape[2]
    half_rows = rows_all // 2
    count_p = pt_ref.shape[0]
    scale = 1.0 / math.sqrt(HEAD)
    own_t = y * 2 + c
    at.greet()

    def give_p(index, source=None):
        return pltpu.make_async_remote_copy(
            src_ref=pt_ref.at[index] if source is None else source,
            dst_ref=ptx_ref.at[index],
            send_sem=give_sem.at[index],
            recv_sem=take_sem.at[index],
            device_id=at.to["core"],
            device_id_type=MESH_ID,
        )

    def give_q(index, yy, source):
        return pltpu.make_async_remote_copy(
            src_ref=source,
            dst_ref=qx_ref.at[index, yy],
            send_sem=give_sem.at[count_p + 2 * index + yy],
            recv_sem=take_sem.at[count_p + 2 * index + yy],
            device_id=at.to["core"],
            device_id_type=MESH_ID,
        )

    def known_q(index, yy):
        return give_q(index, yy, q_ref.at[index, 2 * yy + 1 - c])

    known = (0, 1, 4, 10)
    known_p = (1, 5, 3, 4, 7)
    for index in known[:2]:
        for yy in range(2):
            known_q(index, yy).start()
    give_p(1).start()
    for index in known[2:]:
        for yy in range(2):
            known_q(index, yy).start()
    for index in known_p[1:]:
        give_p(index).start()
    def each(count, size, use):
        def one(step, carry):
            use(pl.ds(pl.multiple_of(step * size, size), size))
            return carry

        lax.fori_loop(0, count, one, 0)

    def aux_load(source, target, number):
        return pltpu.make_async_copy(source, target, aux_sem.at[number])

    def tile_load(unit, t, slot):
        return pltpu.make_async_copy(whole_ref.at[unit, t // 2, t % 2], wb.at[slot], tile_sem.at[slot])

    def route(source, index, t):
        yy = t // 2
        local = pltpu.make_async_copy(source, q_ref.at[index, t], route_sem.at[index, yy])

        def begin():
            pl.when(c == t % 2)(lambda: local.start())
            pl.when(c != t % 2)(lambda: give_q(index, yy, source).start())

        def wait():
            pl.when(c == t % 2)(lambda: local.wait())
            pl.when(c != t % 2)(lambda: give_q(index, yy, source).wait_send())

        return begin, wait

    chunk = 4 * FRAMES
    quarter = rows_all // 4

    def column_sum(row, values):
        vec_ref[pl.ds(row, 1), :] += jnp.sum(values, axis=0, keepdims=True)

    def slope_load(aux, t):
        return aux_load(slope_ref.at[aux, t], cb.at[4], 0)

    def head_loads(aux, t):
        return (
            aux_load(qk_ref.at[aux - 2, t], cb.at[4], 0),
            aux_load(v_ref.at[aux - 2, t], av, 1),
        )

    def load_early(code):
        aux, t = code // 4, code % 4
        pl.when(aux < 2)(lambda: slope_load(aux, t).start())

        @pl.when(aux >= 2)
        def _():
            for load in head_loads(aux, t):
                load.start()

    def do_spread(op):
        t, aux = op["t"], op["aux"]
        side = t % 2

        def multiply(rows):
            total[rows, :] = dot_plain(xb[rows, :], wb[op["slot"]].reshape(C, WIDE))

        each(2, half_rows, multiply)

        @pl.when(aux < 2)
        def _():
            slope_load(aux, t).wait()

            def use(rows):
                grad = total[rows, :] * cb[4, rows, :].astype(jnp.float32)
                hidden_ref[t, pl.ds(aux, 1), :] += jnp.sum(grad, axis=0, keepdims=True)
                cb[side, rows, :] = grad.astype(jnp.bfloat16)

            each(4, quarter, use)
            route(cb.at[side], 3 - aux, t)[0]()

        @pl.when(aux >= 2)
        def _():
            for load in head_loads(aux, t):
                load.wait()

            for block in range(2):

                @pl.when(aux == 2 + block)
                def _(block=block):
                    low = width if block == 0 else 0

                    def use(rows):
                        datt[rows, :] = total[rows, low : low + width].astype(jnp.bfloat16)

                    each(4, quarter, use)

    def do_collapse(op):
        which, routed, t = op["aux"] % 5, op["aux"] // 5, op["t"]

        def multiply(rows):
            gn[rows, :] += dot_rows(cb[which, rows, :], wb[op["slot"]].reshape(C, WIDE))

        each(2, half_rows, multiply)
        pl.when(routed > 0)(lambda: route(cb.at[which], routed - 1, t)[1]())

    def do_attention(op):
        block, t = op["aux"], op["t"]
        side = t % 2
        same = same_pixel(BLOCK)
        for start in range(0, rows_all, BLOCK):
            here = slice(start, start + BLOCK)
            for head in range(width // HEAD):
                low = head * HEAD
                query = cb[4, here, low : low + HEAD]
                key = cb[4, here, width + low : width + low + HEAD]
                value = av[here, low : low + HEAD]
                grad = datt[here, low : low + HEAD]
                probs = head_probs(query, key, same, scale)
                grad_probs = dot_rows(grad, value)
                centred = jnp.sum(probs * grad_probs, axis=1, keepdims=True)
                grad_raw = (probs * (grad_probs - centred) * scale).astype(jnp.bfloat16)
                cb[side, here, low : low + HEAD] = dot_plain(grad_raw, key).astype(jnp.bfloat16)
                cb[side, here, width + low : width + low + HEAD] = dot_first(
                    grad_raw, query
                ).astype(jnp.bfloat16)
                cb[2 + side, here, low : low + HEAD] = dot_first(
                    probs.astype(jnp.bfloat16), grad
                ).astype(jnp.bfloat16)
        route(cb.at[side], 7 - 2 * block, t)[0]()
        route(cb.at[2 + side], 8 - 2 * block, t)[0]()

    def do_layer(op):
        layer = op["aux"]

        def load(step):
            rows = pl.ds(pl.multiple_of(step * chunk, chunk), chunk)
            return pltpu.make_async_copy(
                streams_ref.at[layer, rows], sb.at[step % 2], misc_sem.at[3 + step % 2]
            )

        def one(step, carry):
            pl.when(step + 1 < rows_all // chunk)(lambda: load(step + 1).start())
            load(step).wait()
            rows = pl.ds(pl.multiple_of(step * chunk, chunk), chunk)
            values = sb[step % 2]
            centre = jnp.mean(values, axis=1, keepdims=True)
            offset = values - centre
            inverse = lax.rsqrt(jnp.mean(offset * offset, axis=1, keepdims=True) + 1e-05)
            hat = offset * inverse
            grad = gn[rows, :]
            column_sum(layer, grad * hat)
            column_sum(3 + layer, grad)
            scaled = grad * joined_ref[pl.ds(1 + layer, 1), :]
            first = jnp.mean(scaled, axis=1, keepdims=True)
            second = jnp.mean(scaled * hat, axis=1, keepdims=True)
            result = gs[rows, :] + inverse * (scaled - first - hat * second)
            gs[rows, :] = result
            column_sum(6 + layer, result)
            xb[rows, :] = result.astype(jnp.bfloat16)
            gn[rows, :] = jnp.zeros((chunk, C), jnp.float32)
            return carry

        load(0).start()
        lax.fori_loop(0, rows_all // chunk, one, 0)

    def do_turn(op):
        index = op["aux"]

        def one(step, carry):
            lanes = pl.ds(pl.multiple_of(step * 128, 128), 128)
            ptb[lanes, :] = xb[:, lanes].T
            return carry

        lax.fori_loop(0, C // 128, one, 0)
        turn_copy(index).start()
        give_p(index, ptb).start()

    def turn_copy(index):
        return pltpu.make_async_copy(ptb, pt_ref.at[index], misc_sem.at[2])

    def do_turned(op):
        turn_copy(op["aux"]).wait()
        give_p(op["aux"], ptb).wait_send()

    def do_first(op):
        def use(rows):
            values = gn[rows, :]
            gs[rows, :] = values
            column_sum(9, values)
            xb[rows, :] = values.astype(jnp.bfloat16)
            gn[rows, :] = jnp.zeros((chunk, C), jnp.float32)

        each(rows_all // chunk, chunk, use)

    def do_place(op):
        t, aux = op["t"], op["aux"]
        side = t % 2

        @pl.when(aux == 1)
        def _():
            load = aux_load(grad_ref.at[t], datt, 0)
            load.start()
            load.wait()

            def use(rows):
                cb[side, rows, 0:width] = jnp.zeros((quarter, width), jnp.bfloat16)
                cb[side, rows, width:] = datt[rows, :]

            each(4, quarter, use)

        for block in range(4):

            @pl.when((aux == 0) & (t == block))
            def _(block=block):
                def use(rows):
                    cb[side, rows, 0:width] = jnp.zeros((quarter, width), jnp.bfloat16)
                    cb[side, rows, width:] = xb[rows, block * width : (block + 1) * width]

                each(4, quarter, use)

        route(cb.at[side], 11 - 2 * aux, t)[0]()

    peers = (("y", far_y * 2 + c), ("core", y * 2 + 1 - c), ("cross", far_y * 2 + 1 - c))

    def peer_copy(index):
        kind, t = peers[index]
        return pltpu.make_async_remote_copy(
            src_ref=dn.at[t],
            dst_ref=got_ref.at[own_t],
            send_sem=peer_send.at[0, index],
            recv_sem=peer_recv.at[0, index],
            device_id=at.to[kind],
            device_id_type=MESH_ID,
        )

    def moved_copy(index):
        kind, t = peers[index]
        return pltpu.make_async_remote_copy(
            src_ref=moved_ref.at[t],
            dst_ref=moved_got.at[own_t],
            send_sem=peer_send.at[1, index],
            recv_sem=peer_recv.at[1, index],
            device_id=at.to[kind],
            device_id_type=MESH_ID,
        )

    own_peer = pltpu.make_async_copy(dn.at[own_t], got_ref.at[own_t], peer_send.at[0, 3])
    own_moved = pltpu.make_async_copy(
        moved_ref.at[own_t], moved_got.at[own_t], peer_send.at[1, 3]
    )
    for index in range(3):
        moved_copy(index).start()
    own_moved.start()

    def do_send(op):
        for t in range(4):

            def use(rows, t=t):
                dn[t, rows, :] = gn[rows, t * width : (t + 1) * width].astype(jnp.bfloat16)

            each(4, quarter, use)
        for index in range(3):
            peer_copy(index).start()
        own_peer.start()

    works = (
        None,
        do_spread,
        do_collapse,
        do_attention,
        do_layer,
        do_turn,
        do_first,
        do_place,
        do_send,
        do_turned,
    )
    four = range(4)

    def feed(half):
        steps = []
        for t in four:
            steps += [(1, 7 + half, t, half), (2, 5 + half, t, t % 2 + 5 * (4 - half))]
        return steps

    def heads(block, t):
        return [
            (1, 3 + block, t, 2 + block),
            (3, None, t, block),
            (2, 2 * block, t, t % 2 + 5 * (8 - 2 * block)),
            (2, 2 * block + 1, t, 2 + t % 2 + 5 * (9 - 2 * block)),
        ]

    def inputs(t):
        return [(7, None, t, 0), (2, 1, t, t % 2 + 5 * 12)]

    def outputs(t):
        return [(7, None, t, 1), (2, 4, t, t % 2 + 5 * 10)]

    stage_count = 6
    plan = Plan(2 * stage_count, True)
    for turn, steps in {
        -1: outputs(0) + outputs(1) + outputs(2) + outputs(3) + [(6, None, 0, 0), (5, None, 0, 0), (9, None, 0, 0)],
        0: feed(1),
        1: feed(0),
        2: [(4, None, 0, 2), (5, None, 0, 2)] + heads(1, 0) + [(9, None, 0, 2)],
        3: heads(1, 1) + heads(1, 2),
        4: heads(1, 3),
        5: [(4, None, 0, 1), (5, None, 0, 6)] + heads(0, 0) + [(9, None, 0, 6)],
        6: heads(0, 1) + heads(0, 2) + heads(0, 3),
        7: [(4, None, 0, 0)] + inputs(0) + inputs(1) + inputs(2) + inputs(3),
        8: [(8, None, 0, 0)],
    }.items():
        plan.fill(turn + 1, steps)

    def do_step(place):
        code = plan.code(place)
        pl.when(code > 0)(lambda: do_filled(code))

    def do_filled(code):
        op = plan.fields(code)
        has_tile = (op["kind"] == 1) | (op["kind"] == 2)

        @pl.when(has_tile)
        def _():
            pl.when(op["fresh"] == 1)(lambda: tile_load(op["unit"], op["t"], op["slot"]).start())

            @pl.when(op["next"] > 0)
            def _():
                following = op["next"] - 1
                tile_load(following // 4, following % 4, 1 - op["slot"]).start()

            pl.when(op["early"] > 0)(lambda: load_early(op["early"] - 1))
            tile_load(op["unit"], op["t"], op["slot"]).wait()

        for kind in range(1, len(works)):

            @pl.when(op["kind"] == kind)
            def _(kind=kind):
                works[kind](op)

    vec_ref[...] = jnp.zeros_like(vec_ref)
    hidden_ref[...] = jnp.zeros_like(hidden_ref)

    def clear(rows):
        gn[rows, :] = jnp.zeros((chunk, C), jnp.float32)
        cb[2, rows, :] = jnp.zeros((chunk, WIDE), jnp.bfloat16)
        cb[3, rows, :] = jnp.zeros((chunk, WIDE), jnp.bfloat16)

    each(rows_all // chunk, chunk, clear)

    names = ["ya0", "ya1", "xa", "ua0", "ua1", "ua2", "da0", "da1", "da2"]
    names += ["xb0", "xb1", "ub0", "ub1", "ub2", "db0", "db1", "db2", "yb"]
    number = {name: index for index, name in enumerate(names)}

    class Slot:
        def __init__(self, turn):
            self.d, self.r = turn % SLOTS_IN_FLIGHT, turn % SLOTS_RECEIVED

    def copy(slot, name, src, dst, kind, shift=0):
        index = number[name] + shift
        return pltpu.make_async_remote_copy(
            src_ref=src,
            dst_ref=dst,
            send_sem=send_sem.at[slot.d, index],
            recv_sem=recv_sem.at[slot.r, index],
            device_id=at.to[kind],
            device_id_type=MESH_ID,
        )

    def ya(slot, part):
        side = far_x if part == 0 else x
        return copy(
            slot, f"ya{part}", dw.at[slot.d, far_y, :, side, row_a], rya.at[slot.r, part], "y"
        )

    def xa(slot):
        return copy(slot, "xa", dw.at[slot.d, y, :, far_x, row_a], rxa.at[slot.r], "x")

    def xb_copy(slot, part):
        return copy(
            slot, f"xb{part}", dw.at[slot.d, part, :, far_x, row_b], rxb.at[slot.r, part], "x"
        )

    def yb(slot):
        return copy(slot, "yb", dw.at[slot.d, far_y, z, x, row_b], ryb.at[slot.r], "y")

    def up(slot, colour, d):
        if colour == 0:
            return copy(
                slot, "ua0", dw.at[slot.d, y, d, x, row_a], rua.at[slot.r, d - 1], "up", d - 1
            )
        return copy(slot, "ub0", dw.at[slot.d, :, d, x, row_b], rub.at[slot.r, d - 1], "up", d - 1)

    def down(slot, colour, d):
        if colour == 0:
            return copy(slot, "da0", dw.at[slot.d, y, d, x, row_a], rda.at[slot.r, d], "down", d)
        return copy(slot, "db0", dw.at[slot.d, :, d, x, row_b], rdb.at[slot.r, d], "down", d)

    def add(place, got):
        total = place[...].astype(jnp.float32) + got[...].astype(jnp.float32)
        place[...] = total.astype(jnp.bfloat16)

    def product_loads(p_index, q_index):
        loads = [
            pltpu.make_async_copy(pt_ref.at[p_index], p_buf.at[0], load_sem.at[0]),
            pltpu.make_async_copy(ptx_ref.at[p_index], p_buf.at[1], load_sem.at[1]),
        ]
        for yy in range(2):
            loads += [
                pltpu.make_async_copy(
                    q_ref.at[q_index, 2 * yy + c], q_buf.at[0, yy], load_sem.at[2 + yy]
                ),
                pltpu.make_async_copy(
                    qx_ref.at[q_index, yy], q_buf.at[1, yy], load_sem.at[4 + yy]
                ),
            ]
        return loads

    def products(slot, p_index, q_index, mixed, more):
        for load in product_loads(p_index, q_index):
            load.wait()

        def one(step, carry):
            side, zz = step // 4, step % 4
            yy = jnp.where(side == 0, far_y, y)
            rows = pl.ds(pl.multiple_of(zz * 2 * share, 2 * share), 2 * share)

            def part(first, last):
                result = dot_plain(p_buf[0, rows, :], q_buf[0, yy, :, first:last])
                result = result + dot_plain(p_buf[1, rows, :], q_buf[1, yy, :, first:last])
                return result.reshape(2, share, last - first)

            @pl.when(mixed == 0)
            def _():
                dw[slot.d, yy, zz] = part(0, WIDE).astype(jnp.bfloat16)

            @pl.when((mixed == 1) & (more == 0))
            def _():
                dw[slot.d, yy, zz, :, :, 0:384] = part(0, 384).astype(jnp.bfloat16)

            @pl.when((mixed == 1) & (more == 1))
            def _():
                result = part(256, WIDE)
                shared = dw[slot.d, yy, zz, :, :, 256:384].astype(jnp.float32)
                shared = shared + result[:, :, 0:128]
                dw[slot.d, yy, zz, :, :, 256:384] = shared.astype(jnp.bfloat16)
                dw[slot.d, yy, zz, :, :, 384:] = result[:, :, 128:].astype(jnp.bfloat16)

            return carry

        lax.fori_loop(0, 8, one, 0)

    def take_p(index):
        await_bytes(ptx_ref.at[index], take_sem.at[index])

    def take_q(index):
        for yy in range(2):
            await_bytes(qx_ref.at[index, yy], take_sem.at[count_p + 2 * index + yy])

    def prepare(turn):
        p_index = (turn + turn // 5) // 2

        @pl.when((turn + turn // 5) % 2 == 0)
        def _():
            take_p(p_index)

        take_q(turn)
        for load in product_loads(p_index, turn):
            load.start()

    def stage0(turn):
        slot = Slot(turn)
        p_index = (turn + turn // 5) // 2
        mixed = (turn >= 4).astype(jnp.int32) * (1 - turn % 2)
        extra = (turn - 4) // 2

        @pl.when(mixed == 1)
        def _():
            take_p(5 + extra)
            take_q(UNITS + extra)

        def one_pass(more, carry):
            @pl.when(more == 1)
            def _():
                for load in product_loads(5 + extra, UNITS + extra):
                    load.start()

            products(
                slot,
                jnp.where(more == 1, 5 + extra, p_index),
                jnp.where(more == 1, UNITS + extra, turn),
                mixed,
                more,
            )
            return carry

        lax.fori_loop(0, 1 + mixed, one_pass, 0)

        ya(slot, 0).start()
        xb_copy(slot, 0).start()
        ya(slot, 1).start()
        xb_copy(slot, 1).start()

    def z_step(slot, colour, step):
        @pl.when(z <= step - 1)
        def _():
            d = z + 4 - step

            @pl.when(z >= 1)
            def _():
                up(slot, colour, d).wait_recv()
                if colour == 0:
                    add(dw.at[slot.d, y, d, x, row_a], rua.at[slot.r, d - 1])
                else:
                    add(dw.at[slot.d, 0, d, x, row_b], rub.at[slot.r, d - 1, 0])
                    add(dw.at[slot.d, 1, d, x, row_b], rub.at[slot.r, d - 1, 1])

            up(slot, colour, d).start()

        @pl.when(3 - z <= step - 1)
        def _():
            d = z - 4 + step

            @pl.when(z <= 2)
            def _():
                down(slot, colour, d).wait_recv()
                if colour == 0:
                    add(dw.at[slot.d, y, d, x, row_a], rda.at[slot.r, d])
                else:
                    add(dw.at[slot.d, 0, d, x, row_b], rdb.at[slot.r, d, 0])
                    add(dw.at[slot.d, 1, d, x, row_b], rdb.at[slot.r, d, 1])

            down(slot, colour, d).start()

    def stage1(turn):
        slot = Slot(turn)
        for part in range(2):
            xb_copy(slot, part).wait_recv()
            for zz in range(4):
                add(dw.at[slot.d, part, zz, x, row_b], rxb.at[slot.r, part, zz])
        z_step(slot, 1, 1)
        ya(slot, 0).wait_recv()
        for zz in range(4):
            add(dw.at[slot.d, y, zz, far_x, row_a], rya.at[slot.r, 0, zz])
        xa(slot).start()
        ya(slot, 1).wait_recv()
        for zz in range(4):
            add(dw.at[slot.d, y, zz, x, row_a], rya.at[slot.r, 1, zz])

    def stage2(turn):
        slot = Slot(turn)
        z_step(slot, 1, 2)
        xa(slot).wait_recv()
        for zz in range(4):
            add(dw.at[slot.d, y, zz, x, row_a], rxa.at[slot.r, zz])
        z_step(slot, 0, 1)

    def stage3(turn):
        slot = Slot(turn)
        z_step(slot, 1, 3)
        z_step(slot, 0, 2)

    def stage4(turn):
        slot = Slot(turn)
        z_step(slot, 0, 3)

        @pl.when(z >= 1)
        def _():
            up(slot, 1, z).wait_recv()
            for yy in range(2):
                add(dw.at[slot.d, yy, z, x, row_b], rub.at[slot.r, z - 1, yy])

        @pl.when(z <= 2)
        def _():
            down(slot, 1, z).wait_recv()
            for yy in range(2):
                add(dw.at[slot.d, yy, z, x, row_b], rdb.at[slot.r, z, yy])

        yb(slot).start()

    def out_copy(turn):
        return pltpu.make_async_copy(ob.at[turn % 2], out_ref.at[turn], out_sem.at[turn % 2])

    def stage5(turn):
        slot = Slot(turn)
        side = turn % 2
        pl.when(turn >= 2)(lambda: out_copy(turn - 2).wait())
        ob[side, row_a, :] = dw[slot.d, y, z, x, row_a, :].astype(jnp.float32)

        @pl.when(z >= 1)
        def _():
            up(slot, 0, z).wait_recv()
            ob[side, row_a, :] += rua[slot.r, z - 1].astype(jnp.float32)

        @pl.when(z <= 2)
        def _():
            down(slot, 0, z).wait_recv()
            ob[side, row_a, :] += rda[slot.r, z].astype(jnp.float32)

        yb(slot).wait_recv()
        ob[side, row_b, :] = dw[slot.d, y, z, x, row_b, :].astype(jnp.float32) + ryb[
            slot.r
        ].astype(jnp.float32)
        out_copy(turn).start()

        ya(slot, 0).wait_send()
        ya(slot, 1).wait_send()
        xa(slot).wait_send()
        xb_copy(slot, 0).wait_send()
        xb_copy(slot, 1).wait_send()
        yb(slot).wait_send()
        for colour in range(2):
            for step in range(1, 4):

                @pl.when(z <= step - 1)
                def _(colour=colour, step=step):
                    up(slot, colour, z + 4 - step).wait_send()

                @pl.when(3 - z <= step - 1)
                def _(colour=colour, step=step):
                    down(slot, colour, z - 4 + step).wait_send()

    stages = (stage0, stage1, stage2, stage3, stage4, stage5)

    def advance(now, carry):
        def inner(place, carry):
            for spot, step in enumerate(range(stage_count)):
                turn = now - 1 - step

                @pl.when((place == spot) & (turn >= 0) & (turn < UNITS))
                def _(step=step, turn=turn):
                    stages[step](turn)

            def two(step, carry):
                do_step(2 * (now * stage_count + place) + step)
                return carry

            return lax.fori_loop(0, 2, two, carry)

        lax.fori_loop(0, stage_count, inner, 0)
        pl.when(now < UNITS)(lambda: prepare(now))
        return carry

    lax.fori_loop(0, UNITS + stage_count, advance, 0)
    out_copy(UNITS - 2).wait()
    out_copy(UNITS - 1).wait()
    for index in range(3):
        peer_copy(index).wait()
        moved_copy(index).wait()
    own_peer.wait()
    own_moved.wait()
    for index in known:
        for yy in range(2):
            known_q(index, yy).wait_send()
    for index in known_p:
        give_p(index).wait_send()


def backward_all(whole, q_all, pt_all, streams, qk, values, slopes, grad, moved, joined):
    share = whole.shape[5]
    count_p, unused, rows = pt_all.shape
    width = values.shape[3]
    low = jnp.bfloat16
    slots, taken, rest = SLOTS_IN_FLIGHT, SLOTS_RECEIVED, share - ROWS_A
    anywhere, near = pl.BlockSpec(memory_space=pl.ANY), pl.BlockSpec(memory_space=pltpu.VMEM)
    return pl.pallas_call(
        backward_kernel,
        in_specs=[anywhere] * 9 + [near],
        out_specs=[anywhere] * 7 + [near] * 2,
        out_shape=[
            jax.ShapeDtypeStruct((UNITS, share, WIDE), jnp.float32),
            jax.ShapeDtypeStruct(q_all.shape, low),
            jax.ShapeDtypeStruct(pt_all.shape, low),
            jax.ShapeDtypeStruct(pt_all.shape, low),
            jax.ShapeDtypeStruct((q_all.shape[0], 2, rows, WIDE), low),
            jax.ShapeDtypeStruct((4, rows, width), low),
            jax.ShapeDtypeStruct((4, rows, width), low),
            jax.ShapeDtypeStruct((16, C), jnp.float32),
            jax.ShapeDtypeStruct((4, 8, WIDE), jnp.float32),
        ],
        input_output_aliases={1: 1, 2: 2},
        scratch_shapes=[
            pltpu.VMEM((2, C, rows), low),
            pltpu.VMEM((2, 2, rows, WIDE), low),
            pltpu.VMEM((slots, 2, 4, 2, share, WIDE), low),
            pltpu.VMEM((taken, 2, 4, ROWS_A, WIDE), low),
            pltpu.VMEM((taken, 4, ROWS_A, WIDE), low),
            pltpu.VMEM((taken, 3, ROWS_A, WIDE), low),
            pltpu.VMEM((taken, 3, ROWS_A, WIDE), low),
            pltpu.VMEM((taken, 2, 4, rest, WIDE), low),
            pltpu.VMEM((taken, 3, 2, rest, WIDE), low),
            pltpu.VMEM((taken, 3, 2, rest, WIDE), low),
            pltpu.VMEM((taken, rest, WIDE), low),
            pltpu.VMEM((rows, C), jnp.float32),
            pltpu.VMEM((rows, C), jnp.float32),
            pltpu.VMEM((rows, C), low),
            pltpu.VMEM((C, rows), low),
            pltpu.VMEM((2, 4, 2, share, WIDE), low),
            pltpu.VMEM((5, rows, WIDE), low),
            pltpu.VMEM((rows, width), low),
            pltpu.VMEM((rows, width), low),
            pltpu.VMEM((rows, WIDE), jnp.float32),
            pltpu.VMEM((2, 4 * FRAMES, C), jnp.float32),
            pltpu.VMEM((2, share, WIDE), jnp.float32),
            pltpu.VMEM((4, rows, width), low),
            pltpu.SemaphoreType.DMA((6,)),
            pltpu.SemaphoreType.DMA((32,)),
            pltpu.SemaphoreType.DMA((32,)),
            pltpu.SemaphoreType.DMA((slots, 18)),
            pltpu.SemaphoreType.DMA((taken, 18)),
            pltpu.SemaphoreType.DMA((2,)),
            pltpu.SemaphoreType.DMA((4,)),
            pltpu.SemaphoreType.DMA((12, 2)),
            pltpu.SemaphoreType.DMA((5,)),
            pltpu.SemaphoreType.DMA((2,)),
            pltpu.SemaphoreType.DMA((2, 4)),
            pltpu.SemaphoreType.DMA((2, 3)),
        ],
        compiler_params=pltpu.CompilerParams(
            collective_id=1, has_side_effects=True, vmem_limit_bytes=63 << 20
        ),
    )(whole, q_all, pt_all, streams, qk, values, slopes, grad, moved, joined)


def gather_plain(shards):
    units, share, wide = shards.shape
    whole = lax.all_gather(shards, MIXED, axis=1, tiled=True)
    return whole.reshape(units, lax.axis_size("tensor"), C, wide)


def reduce_plain(turned, parts):
    reduced = []
    for turn in range(UNITS):
        pairs = [(turned[(turn + turn // 5) // 2], parts[turn])]
        if turn in (4, 6, 8):
            extra = (turn - 4) // 2
            pairs.append((turned[5 + extra], parts[UNITS + extra]))
        whole = sum(
            jnp.einsum("kr,trn->tkn", left, right, preferred_element_type=jnp.float32)
            for left, right in pairs
        )
        whole = whole.astype(jnp.bfloat16).reshape(-1, whole.shape[2])
        reduced.append(
            lax.psum_scatter(whole, MIXED, scatter_dimension=0, tiled=True).astype(jnp.float32)
        )
    return jnp.stack(reduced, 0)


def by_pixels(values, tensor_size):
    slots, frames, width, pixels = values.shape
    own = pixels // tensor_size
    return jnp.transpose(values, (3, 0, 1, 2)).reshape(tensor_size, own * slots * frames, width)


def exchange(parts):
    return lax.all_to_all(parts, "tensor", 0, 0, tiled=True)


def back_to_channels(arrived, slots, pixels):
    width = arrived.shape[2]
    return jnp.transpose(arrived.reshape(pixels, slots, FRAMES, width), (1, 2, 3, 0))


def group_total(values):
    width = values.shape[0]
    size = C // GROUPS
    grouped = values.reshape(width // size, size, 1)
    summed = jnp.sum(grouped, axis=1, keepdims=True)
    return jnp.broadcast_to(summed, grouped.shape).reshape(width, 1)


def enter_kernel(
    latent_ref,
    cot_ref,
    flag_ref,
    gain_ref,
    shift_ref,
    in_ref,
    qkv_ref,
    out_ref,
    up_ref,
    down_ref,
    proj_ref,
    sent_ref,
    moved_ref,
    shards_ref,
    centre_ref,
    inverse_ref,
    bias_ref,
    rows_buf,
):
    frames, width, pixels = latent_ref.shape[1:]
    cells = frames * pixels * (C // GROUPS)
    shards_ref[0, :, 0:width] = qkv_ref[0, 0]
    shards_ref[0, :, width:] = qkv_ref[0, 1]
    shards_ref[1, :, 0:width] = qkv_ref[0, 2]
    shards_ref[1, :, width:] = in_ref[...]
    shards_ref[2, :, 0:width] = qkv_ref[1, 0]
    shards_ref[2, :, width:] = qkv_ref[1, 1]
    shards_ref[3, :, 0:width] = qkv_ref[1, 2]
    shards_ref[3, :, width:] = out_ref[0]
    shards_ref[4, :, 0:width] = out_ref[1]
    shards_ref[4, :, width:] = proj_ref[...]
    for half in range(2):
        lanes = slice(half * WIDE, (half + 1) * WIDE)
        shards_ref[5 + half] = up_ref[:, lanes]
        shards_ref[7 + half] = down_ref[:, lanes]

    def frame_sum(use):
        def one(f, carry):
            return carry + use(f)

        total = lax.fori_loop(0, frames, one, jnp.zeros((width, pixels), jnp.float32))
        return jnp.sum(total, axis=1, keepdims=True)

    def values(f):
        return latent_ref[0, f].astype(jnp.float32)

    centre = group_total(frame_sum(values)) / cells
    spread_sum = group_total(frame_sum(lambda f: (values(f) - centre) * (values(f) - centre)))
    inverse = lax.rsqrt(spread_sum / cells + 1e-06)
    centre_ref[...] = centre
    inverse_ref[...] = inverse
    flag = (flag_ref[0] > 0).astype(jnp.float32)

    def masked(f):
        return cot_ref[0, f].astype(jnp.float32) * flag

    bias_ref[...] = frame_sum(masked)
    own = pixels // 4 * frames

    def rows_of(use, target):
        def one(f, carry):
            block = use(f)
            for part in range(3):
                rows_buf[part, pl.ds(f, pixels, stride=frames), :] = block[
                    part * 128 : part * 128 + 128, :
                ].T
            return carry

        lax.fori_loop(0, frames, one, 0)

        def cast(step, carry):
            rows = pl.ds(pl.multiple_of(step * 128, 128), 128)
            t, inside = step // (own // 128), step % (own // 128)
            inner = pl.ds(pl.multiple_of(inside * 128, 128), 128)
            for part in range(3):
                low, high = part * 128, min(part * 128 + 128, width)
                target[t, inner, low:high] = rows_buf[part, rows, 0 : high - low].astype(
                    jnp.bfloat16
                )
            return carry

        lax.fori_loop(0, 4 * own // 128, cast, 0)

    def padded(block):
        return jnp.concatenate([block, jnp.zeros((384 - width, pixels), jnp.float32)], 0)

    gain, shift = gain_ref[...], shift_ref[...]
    rows_of(lambda f: padded((values(f) - centre) * inverse * gain + shift), sent_ref)
    rows_of(lambda f: padded(masked(f)), moved_ref)


def enter(latent, cotangent, flags, gain, shift, w_in, w_qkv, w_out, w_up, w_down, w_proj):
    slots, frames, width, pixels = latent.shape
    share, rows = w_in.shape[0], pixels // 4 * frames
    near = pl.BlockSpec(memory_space=pltpu.VMEM)
    column = jax.ShapeDtypeStruct((width, 1), jnp.float32)
    low = jnp.bfloat16
    return pl.pallas_call(
        enter_kernel,
        in_specs=[near, near, pl.BlockSpec(memory_space=pltpu.SMEM)] + [near] * 8,
        out_specs=[near] * 6,
        out_shape=[
            jax.ShapeDtypeStruct((4, rows, width), low),
            jax.ShapeDtypeStruct((4, rows, width), low),
            jax.ShapeDtypeStruct((UNITS, share, WIDE), low),
            column,
            column,
            column,
        ],
        scratch_shapes=[pltpu.VMEM((3, 4 * rows, 128), jnp.float32)],
        compiler_params=pltpu.CompilerParams(vmem_limit_bytes=48 << 20),
    )(
        latent,
        cotangent,
        flags,
        gain.reshape(width, 1),
        shift.reshape(width, 1),
        w_in,
        jnp.transpose(w_qkv, (0, 2, 1, 3)),
        jnp.transpose(w_out, (0, 2, 1)),
        w_up,
        w_down.T,
        w_proj,
    )


def leave_kernel(
    grad_ref,
    moved_ref,
    latent_ref,
    cot_ref,
    flag_ref,
    gain_ref,
    centre_ref,
    inverse_ref,
    reduced_ref,
    output_ref,
    latent_grad_ref,
    gain_grad_ref,
    shift_grad_ref,
    in_ref,
    qkv_ref,
    out_ref,
    up_ref,
    down_ref,
    proj_ref,
    rows_buf,
    turned,
):
    frames, width, pixels = latent_ref.shape[1:]
    cells = frames * pixels * (C // GROUPS)
    for block in range(2):
        for part in range(2):
            qkv_ref[block, part] = reduced_ref[7 - 2 * block, :, part * width : (part + 1) * width]
        qkv_ref[block, 2] = reduced_ref[8 - 2 * block, :, 0:width]
    in_ref[...] = reduced_ref[8, :, width:]
    out_ref[0] = reduced_ref[6, :, width:]
    out_ref[1] = reduced_ref[4, :, 0:width]
    proj_ref[...] = reduced_ref[4, :, width:]
    for half in range(2):
        lanes = slice(half * WIDE, (half + 1) * WIDE)
        up_ref[:, lanes] = reduced_ref[3 - half]
        down_ref[:, lanes] = reduced_ref[1 - half]

    own = pixels // 4 * frames

    def spread_rows(source):
        def cast(step, carry):
            rows = pl.ds(pl.multiple_of(step * 128, 128), 128)
            t, inside = step // (own // 128), step % (own // 128)
            inner = pl.ds(pl.multiple_of(inside * 128, 128), 128)
            for part in range(3):
                low, high = part * 128, min(part * 128 + 128, width)
                rows_buf[part, rows, 0 : high - low] = source[t, inner, low:high].astype(
                    jnp.float32
                )
            return carry

        lax.fori_loop(0, 4 * own // 128, cast, 0)

    def frame(f):
        rows = pl.ds(f, pixels, stride=frames)
        turned_parts = [rows_buf[part, rows, :].T for part in range(3)]
        return jnp.concatenate(turned_parts, 0)[0:width, :]

    def hat(f):
        return (latent_ref[0, f].astype(jnp.float32) - centre_ref[...]) * inverse_ref[...]

    flag = (flag_ref[0] > 0).astype(jnp.float32)
    rows_buf[...] = jnp.zeros_like(rows_buf)
    spread_rows(moved_ref)

    def finish(f, carry):
        start = latent_ref[0, f].astype(jnp.float32)
        output_ref[0, f] = (start + flag * frame(f)).astype(jnp.bfloat16)
        return carry

    lax.fori_loop(0, frames, finish, 0)
    spread_rows(grad_ref)
    zero = jnp.zeros((width, pixels), jnp.float32)

    def gather(f, carry):
        grad = frame(f)
        turned[f] = grad
        return carry[0] + grad * hat(f), carry[1] + grad

    by_gain, by_shift = lax.fori_loop(0, frames, gather, (zero, zero))
    gain_sum = jnp.sum(by_gain, axis=1, keepdims=True)
    shift_sum = jnp.sum(by_shift, axis=1, keepdims=True)
    gain_grad_ref[...] = gain_sum
    shift_grad_ref[...] = shift_sum
    gain = gain_ref[...]
    first = group_total(gain * shift_sum) / cells
    second = group_total(gain * gain_sum) / cells

    def back(f, carry):
        grad = inverse_ref[...] * (turned[f] * gain - first - hat(f) * second)
        latent_grad_ref[0, f] = cot_ref[0, f].astype(jnp.float32) + grad
        return carry

    lax.fori_loop(0, frames, back, 0)


def leave(grad, moved, latent, cotangent, flags, gain, centre, inverse, reduced):
    slots, frames, width, pixels = latent.shape
    rows, share = pixels // 4 * frames, reduced.shape[1]
    near = pl.BlockSpec(memory_space=pltpu.VMEM)
    real = jnp.float32
    column = jax.ShapeDtypeStruct((width, 1), real)
    made = pl.pallas_call(
        leave_kernel,
        in_specs=[near] * 4 + [pl.BlockSpec(memory_space=pltpu.SMEM)] + [near] * 4,
        out_specs=[near] * 10,
        out_shape=[
            jax.ShapeDtypeStruct(latent.shape, jnp.bfloat16),
            jax.ShapeDtypeStruct(latent.shape, real),
            column,
            column,
            jax.ShapeDtypeStruct((share, width), real),
            jax.ShapeDtypeStruct((2, 3, share, width), real),
            jax.ShapeDtypeStruct((2, share, width), real),
            jax.ShapeDtypeStruct((share, 2 * WIDE), real),
            jax.ShapeDtypeStruct((share, 2 * WIDE), real),
            jax.ShapeDtypeStruct((share, width), real),
        ],
        scratch_shapes=[
            pltpu.VMEM((3, 4 * rows, 128), real),
            pltpu.VMEM((frames, width, pixels), real),
        ],
        compiler_params=pltpu.CompilerParams(vmem_limit_bytes=56 << 20),
    )(
        grad,
        moved,
        latent,
        cotangent,
        flags,
        gain.reshape(width, 1),
        centre,
        inverse,
        reduced,
    )
    output, latent_grad, gain_grad, shift_grad, g_in, g_qkv, g_out, g_up, g_down, g_proj = made
    weights = (
        g_in,
        jnp.transpose(g_qkv, (0, 2, 1, 3)),
        jnp.transpose(g_out, (0, 2, 1)),
        g_up,
        g_down.T,
        g_proj,
    )
    return output, latent_grad, gain_grad.reshape(width), shift_grad.reshape(width), weights


def kernel_body(
    latent,
    clip_flags,
    cotangent,
    norm_gain,
    norm_shift,
    channel_bias,
    hidden_bias,
    weight_in,
    weight_qkv,
    weight_out,
    weight_up,
    weight_down,
    weight_proj,
):
    width = latent.shape[2]
    side = jnp.concatenate
    params = side([norm_gain, norm_shift, channel_bias, jnp.zeros((3, width), jnp.float32)], 0)
    params = side([params, hidden_bias.reshape(4, width), jnp.zeros((4, width), jnp.float32)], 0)
    sent, moved_sent, shards, centre, inverse, bias_moved = enter(
        latent,
        cotangent,
        clip_flags,
        norm_gain[0],
        norm_shift[0],
        weight_in,
        weight_qkv,
        weight_out,
        weight_up,
        weight_down,
        weight_proj,
    )
    whole, q_all, pt_all, streams, qk_all, v_all, slopes, grad, moved, joined = forward_all(
        shards, sent, params, make_positions(), moved_sent
    )
    reduced, q_all, pt_all, unused, unused, grad_back, moved_back, sums, hidden_sums = backward_all(
        whole, q_all, pt_all, streams, qk_all, v_all, slopes, grad, moved, joined
    )
    output, latent_grad, group_gain, group_shift, weights = leave(
        grad_back,
        moved_back,
        latent,
        cotangent,
        clip_flags,
        norm_gain[0],
        centre,
        inverse,
        reduced,
    )
    vectors = jnp.transpose(sums[:10].reshape(10, 4, width), (1, 0, 2)).reshape(4, 10 * width)
    vectors = side([vectors, hidden_sums[:, :2].reshape(4, 2 * WIDE)], 1)
    vectors = jnp.sum(exchange(vectors), 0)
    local = side([vectors, group_gain, group_shift, bias_moved.reshape(width)])
    total = local
    count = lax.axis_size("dp")
    for bit in range(count.bit_length() - 1):
        total = total + lax.ppermute(total, "dp", [(i, i ^ (1 << bit)) for i in range(count)])
    channel, hidden_grad = total[: 10 * width].reshape(10, width), total[10 * width : 14 * width]
    group = total[14 * width :].reshape(3, width)
    return (
        output,
        latent_grad,
        side([group[0:1], channel[0:3]], 0),
        side([group[1:2], channel[3:6]], 0),
        side([channel[6:10], group[2:3]], 0),
        hidden_grad,
    ) + weights


def body(
    latent,
    clip_flags,
    cotangent,
    norm_gain,
    norm_shift,
    channel_bias,
    hidden_bias,
    weight_in,
    weight_qkv,
    weight_out,
    weight_up,
    weight_down,
    weight_proj,
):
    tensor_size = lax.axis_size("tensor")
    slots, frames, width, pixels = latent.shape
    share = weight_in.shape[0]
    hidden_width = hidden_bias.shape[0]
    flags = (clip_flags > 0)[:, None, None, None]

    wide = 2 * width

    shards = []
    side = jnp.concatenate
    for block in range(2):
        shards.append(weight_qkv[block, :, :2].reshape(share, wide))
        other = weight_in if block == 0 else weight_out[0].T
        shards.append(side([weight_qkv[block, :, 2], other], 1))
    shards.append(side([weight_out[1].T, weight_proj], 1))
    shards += [weight_up[:, :wide], weight_up[:, wide:]]
    down_turned = weight_down.T
    shards += [down_turned[:, :wide], down_turned[:, wide:]]
    shards = jnp.stack(shards, 0)
    params = jnp.zeros((24, width), jnp.float32)
    params = params.at[:13].set(side([norm_gain, norm_shift, channel_bias], 0))
    params = params.at[16:20].set(hidden_bias.reshape(4, width))

    start = latent.astype(jnp.float32)
    cot = cotangent.astype(jnp.float32)
    group_width = C // GROUPS
    grouped = start.reshape(slots, frames, width // group_width, group_width, pixels)
    group_centre = jnp.mean(grouped, axis=(1, 3, 4), keepdims=True)
    offset = grouped - group_centre
    group_inverse = lax.rsqrt(jnp.mean(offset * offset, axis=(1, 3, 4), keepdims=True) + 1e-06)
    group_hat = (offset * group_inverse).reshape(start.shape)
    normed = group_hat * norm_gain[0][:, None] + norm_shift[0][:, None]
    sent = by_pixels(normed.astype(jnp.bfloat16), tensor_size)
    rows = sent.shape[1]

    grad_moved_local = jnp.where(flags, cot, 0.0)
    bias_moved = jnp.sum(grad_moved_local, axis=(0, 1, 3))
    grad_moved = exchange(by_pixels(grad_moved_local.astype(jnp.bfloat16), tensor_size))

    empty = jnp.zeros((tensor_size, rows, width), jnp.bfloat16)
    moved_part = side([empty, grad_moved], 2)
    arrived = exchange(sent)
    inputs_in = jnp.transpose(arrived, (1, 0, 2)).reshape(rows, C)
    packed = lax.all_gather(params, "tensor", axis=0, tiled=False)
    joined = jnp.transpose(packed[:, :13], (1, 0, 2)).reshape(13, C)
    gains, shifts, biases = joined[:4], joined[4:8], joined[8:]
    hidden_full = packed[:, 16:20].reshape(tensor_size, 2 * wide)
    whole = gather_plain(shards)
    full_qk = (whole[0], whole[2])
    full_v = (whole[1, :, :, :width], whole[3, :, :, :width])
    full_in = whole[1, :, :, width:]
    full_out = (whole[3, :, :, width:], whole[4, :, :, :width])
    full_proj = whole[4, :, :, width:]
    full_up = (whole[5], whole[6])
    full_down = (whole[7], whole[8])

    def join(parts):
        return jnp.transpose(parts, (1, 0, 2)).reshape(rows, parts.shape[0] * parts.shape[2])

    stream = join(spread(inputs_in, full_in)) + biases[0]
    position = jnp.tile(make_positions(), (rows // FRAMES, 1))
    kept = []
    for block in range(2):
        hat, inverse = layer_stats(stream)
        lifted = (hat * gains[1 + block] + shifts[1 + block] + position).astype(jnp.bfloat16)
        qk = spread(lifted, full_qk[block]).astype(jnp.bfloat16)
        values = spread(lifted, full_v[block]).astype(jnp.bfloat16)
        attended = attend(qk, values)
        stream = stream + collapse(attended, full_out[block]) + biases[1 + block]
        kept.append((hat, inverse, lifted.T, qk, values, attended))
    hat_feed, inverse_feed = layer_stats(stream)
    inputs_up = (hat_feed * gains[3] + shifts[3]).astype(jnp.bfloat16)
    pre_act = [
        spread(inputs_up, full_up[half])
        + hidden_full[:, None, half * wide : half * wide + wide]
        for half in range(2)
    ]
    slopes = [
        jax.vjp(partial(jax.nn.gelu, approximate=False), pre)[1](jnp.ones_like(pre))[0]
        for pre in pre_act
    ]
    hidden = [jax.nn.gelu(pre, approximate=False).astype(jnp.bfloat16) for pre in pre_act]
    stream = stream + collapse(hidden[0], full_down[0]) + collapse(hidden[1], full_down[1])
    stream = stream + biases[3]
    inputs_proj = stream.astype(jnp.bfloat16)
    moved = spread(inputs_proj, full_proj) + biases[4].reshape(tensor_size, 1, width)
    moved = moved.astype(jnp.bfloat16)

    bias_grads = [None] * 4
    gain_grads = [None] * 3
    shift_grads = [None] * 3
    turned, parts = [None] * 8, [None] * 12
    turned[1], turned[5], turned[7] = inputs_up.T, inputs_proj.T, inputs_in.T
    parts[0], parts[1] = hidden[1], hidden[0]
    parts[9] = moved_part
    grad_stream = collapse(grad_moved, full_proj)
    bias_grads[3] = jnp.sum(grad_stream, 0)
    grad_low = grad_stream.astype(jnp.bfloat16)
    turned[0] = grad_low.T
    hidden_grads = [None, None]
    grad_normed = 0.0
    for half in (1, 0):
        grad_hidden = spread(grad_low, full_down[half])
        grad_pre = grad_hidden * slopes[half]
        hidden_grads[half] = jnp.sum(grad_pre, 1)
        parts[3 - half] = grad_pre.astype(jnp.bfloat16)
        grad_normed = grad_normed + collapse(parts[3 - half], full_up[half])
    hidden_grad = side(hidden_grads, 1)
    grad_layer, gain_grads[2], shift_grads[2] = layer_back(
        grad_normed, hat_feed, inverse_feed, gains[3]
    )
    grad_stream = grad_stream + grad_layer
    for block in (1, 0):
        hat, inverse, lifted_turned, qk, values, attended = kept[block]
        bias_grads[1 + block] = jnp.sum(grad_stream, 0)
        grad_low = grad_stream.astype(jnp.bfloat16)
        turned[2 if block == 1 else 6] = grad_low.T
        pair = [attended, empty] if block == 1 else [empty, attended]
        parts[4 if block == 1 else 10] = side(pair, 2)
        grad_attended = spread(grad_low, full_out[block]).astype(jnp.bfloat16)
        grad_qk, grad_values = attend_back(qk, values, grad_attended)
        turned[3 if block == 1 else 4] = lifted_turned
        parts[6 if block == 1 else 8] = side([grad_values, empty], 2)
        parts[5 if block == 1 else 7] = grad_qk
        grad_lifted = collapse(grad_qk, full_qk[block]) + collapse(grad_values, full_v[block])
        grad_layer, gain_grads[block], shift_grads[block] = layer_back(
            grad_lifted, hat, inverse, gains[1 + block]
        )
        grad_stream = grad_stream + grad_layer
    bias_grads[0] = jnp.sum(grad_stream, 0)
    grad_low = grad_stream.astype(jnp.bfloat16)
    grad_low_parts = jnp.transpose(grad_low.reshape(rows, tensor_size, width), (1, 0, 2))
    parts[11] = side([empty, grad_low_parts], 2)
    turned, parts = jnp.stack(turned, 0), jnp.stack(parts, 0)
    reduced = reduce_plain(turned, parts)
    grad_normed = collapse(grad_low_parts, full_in).astype(jnp.bfloat16)
    grad_normed = jnp.transpose(grad_normed.reshape(rows, tensor_size, width), (1, 0, 2))
    arrived_grad = exchange(grad_normed)
    vectors = jnp.stack(gain_grads + shift_grads + bias_grads, 0)

    moved_local = back_to_channels(exchange(moved), slots, pixels).astype(jnp.float32)
    output = jnp.where(flags, start + moved_local, start).astype(jnp.bfloat16)

    qkv_grads = [
        side([reduced[7 - 2 * block], reduced[8 - 2 * block, :, :width]], 1).reshape(share, 3, width)
        for block in range(2)
    ]
    out_grads = [reduced[6, :, width:].T, reduced[4, :, :width].T]
    in_grad, proj_grad = reduced[8, :, width:], reduced[4, :, width:]
    up_grad = side([reduced[3], reduced[2]], 1)
    down_grad = side([reduced[1], reduced[0]], 1)
    grad_normed = back_to_channels(arrived_grad, slots, pixels).astype(jnp.float32)
    scaled = grad_normed * norm_gain[0][:, None]
    scaled_groups = scaled.reshape(grouped.shape)
    hat_groups = group_hat.reshape(grouped.shape)
    first = jnp.mean(scaled_groups, axis=(1, 3, 4), keepdims=True)
    second = jnp.mean(scaled_groups * hat_groups, axis=(1, 3, 4), keepdims=True)
    grad_group = group_inverse * (scaled_groups - first - hat_groups * second)
    latent_grad = cot + grad_group.reshape(start.shape)
    group_gain_grad = jnp.sum(grad_normed * group_hat, axis=(0, 1, 3))
    group_shift_grad = jnp.sum(grad_normed, axis=(0, 1, 3))

    vectors = jnp.transpose(vectors.reshape(10, tensor_size, width), (1, 0, 2))
    vectors = jnp.concatenate([vectors.reshape(tensor_size, 10 * width), hidden_grad], 1)
    vectors = lax.psum_scatter(vectors, "tensor", scatter_dimension=0, tiled=False)
    sums = lax.psum(
        jnp.concatenate([vectors, group_gain_grad, group_shift_grad, bias_moved]), "dp"
    )
    channel_sums = sums[: 10 * width].reshape(10, width)
    hidden_bias_grad = sums[10 * width : 10 * width + hidden_width]
    local_sums = sums[10 * width + hidden_width :].reshape(3, width)
    gain_grad = jnp.concatenate([local_sums[0:1], channel_sums[0:3]], 0)
    shift_grad = jnp.concatenate([local_sums[1:2], channel_sums[3:6]], 0)
    channel_bias_grad = jnp.concatenate([channel_sums[6:10], local_sums[2:3]], 0)
    return (
        output,
        latent_grad,
        gain_grad,
        shift_grad,
        channel_bias_grad,
        hidden_bias_grad,
        in_grad,
        jnp.stack(qkv_grads, 0),
        jnp.stack(out_grads, 0),
        up_grad,
        down_grad.T,
        proj_grad,
    )


def solution(mesh):
    placed = (
        P("dp", None, "tensor", None),
        P("dp"),
        P("dp", None, "tensor", None),
        P(None, "tensor"),
        P(None, "tensor"),
        P(None, "tensor"),
        P("tensor"),
        P("dp", "tensor"),
        P(None, "dp", None, "tensor"),
        P(None, "tensor", "dp"),
        P("dp", "tensor"),
        P("tensor", "dp"),
        P("dp", "tensor"),
    )
    kernels_fit = (mesh.shape["dp"], mesh.shape["tensor"]) == (8, 4)
    return jax.shard_map(
        kernel_body if kernels_fit else body,
        mesh=mesh,
        in_specs=placed,
        out_specs=(
            P("dp", None, "tensor", None),
            P("dp", None, "tensor", None),
            P(None, "tensor"),
            P(None, "tensor"),
            P(None, "tensor"),
            P("tensor"),
            P("dp", "tensor"),
            P(None, "dp", None, "tensor"),
            P(None, "tensor", "dp"),
            P("dp", "tensor"),
            P("tensor", "dp"),
            P("dp", "tensor"),
        ),
        check_vma=False,
    )
```

```python
from functools import partial
import math

import jax
import jax.numpy as jnp
from jax import lax
from jax.experimental import pallas as pl
from jax.experimental.pallas import tpu as pltpu
from jax.sharding import PartitionSpec as P

C = 1280
GROUPS = 32
FRAMES = 16
HEAD = 160
BLOCK = 128
MIXED = ("tensor", "dp")


def spread(rows, weight):
    return jnp.einsum("rk,tkn->trn", rows, weight, preferred_element_type=jnp.float32)


def collapse(parts, weight):
    return jnp.einsum("trn,tkn->rk", parts, weight, preferred_element_type=jnp.float32)


def make_positions():
    channel_ids = jnp.arange(C)
    pair_rate = jnp.exp((channel_ids // 2).astype(jnp.float32) * (-2.0 * math.log(10000.0) / C))
    angles = jnp.arange(FRAMES).astype(jnp.float32)[:, None] * pair_rate[None, :]
    return jnp.where(channel_ids[None, :] % 2 == 0, jnp.sin(angles), jnp.cos(angles))


def layer_stats(stream):
    centre = jnp.mean(stream, axis=1, keepdims=True)
    offset = stream - centre
    inverse = lax.rsqrt(jnp.mean(offset * offset, axis=1, keepdims=True) + 1e-05)
    return offset * inverse, inverse


def layer_back(grad_out, normal_part, inverse, gain):
    scaled = grad_out * gain
    first = jnp.mean(scaled, axis=1, keepdims=True)
    second = jnp.mean(scaled * normal_part, axis=1, keepdims=True)
    grad_in = inverse * (scaled - first - normal_part * second)
    return grad_in, jnp.sum(grad_out * normal_part, 0), jnp.sum(grad_out, 0)


def dot_rows(left, right):
    return lax.dot_general(left, right, (((1,), (1,)), ((), ())), preferred_element_type=jnp.float32)


def dot_plain(left, right):
    return lax.dot_general(left, right, (((1,), (0,)), ((), ())), preferred_element_type=jnp.float32)


def dot_first(left, right):
    return lax.dot_general(left, right, (((0,), (0,)), ((), ())), preferred_element_type=jnp.float32)


def same_pixel(block):
    row = lax.broadcasted_iota(jnp.int32, (block, block), 0) // FRAMES
    col = lax.broadcasted_iota(jnp.int32, (block, block), 1) // FRAMES
    return row == col


def head_probs(query, key, same, scale):
    scores = jnp.where(same, dot_rows(query, key) * scale, -1e30)
    top = jnp.max(scores, axis=1, keepdims=True)
    weights = jnp.where(same, jnp.exp(scores - top), 0.0)
    return weights / jnp.sum(weights, axis=1, keepdims=True)


def attend_kernel(scale, qk_ref, v_ref, out_ref):
    rows, width = out_ref.shape[1], out_ref.shape[2]
    block = min(BLOCK, rows)
    same = same_pixel(block)
    for start in range(0, rows, block):
        for head in range(width // HEAD):
            here, low = slice(start, start + block), head * HEAD
            query = qk_ref[0, here, low : low + HEAD]
            key = qk_ref[0, here, width + low : width + low + HEAD]
            value = v_ref[0, here, low : low + HEAD]
            probs = head_probs(query, key, same, scale).astype(jnp.bfloat16)
            out_ref[0, here, low : low + HEAD] = dot_plain(probs, value).astype(jnp.bfloat16)


def part_spec(array):
    return pl.BlockSpec((1,) + array.shape[1:], lambda t: (t, 0, 0))


def attend(qk, values):
    return pl.pallas_call(
        partial(attend_kernel, 1.0 / math.sqrt(HEAD)),
        grid=(qk.shape[0],),
        in_specs=[part_spec(qk), part_spec(values)],
        out_specs=part_spec(values),
        out_shape=jax.ShapeDtypeStruct(values.shape, jnp.bfloat16),
        compiler_params=pltpu.CompilerParams(vmem_limit_bytes=32 << 20),
    )(qk, values)


def attend_back_kernel(scale, qk_ref, v_ref, grad_ref, dqk_ref, dv_ref):
    rows, width = grad_ref.shape[1], grad_ref.shape[2]
    block = min(BLOCK, rows)
    same = same_pixel(block)
    for start in range(0, rows, block):
        for head in range(width // HEAD):
            here, low = slice(start, start + block), head * HEAD
            query = qk_ref[0, here, low : low + HEAD]
            key = qk_ref[0, here, width + low : width + low + HEAD]
            value = v_ref[0, here, low : low + HEAD]
            grad = grad_ref[0, here, low : low + HEAD]
            probs = head_probs(query, key, same, scale)
            grad_probs = dot_rows(grad, value)
            centred = jnp.sum(probs * grad_probs, axis=1, keepdims=True)
            grad_raw = (probs * (grad_probs - centred) * scale).astype(jnp.bfloat16)
            dqk_ref[0, here, low : low + HEAD] = dot_plain(grad_raw, key).astype(jnp.bfloat16)
            dqk_ref[0, here, width + low : width + low + HEAD] = dot_first(grad_raw, query).astype(
                jnp.bfloat16
            )
            dv_ref[0, here, low : low + HEAD] = dot_first(probs.astype(jnp.bfloat16), grad).astype(
                jnp.bfloat16
            )


def attend_back(qk, values, grad):
    return pl.pallas_call(
        partial(attend_back_kernel, 1.0 / math.sqrt(HEAD)),
        grid=(qk.shape[0],),
        in_specs=[part_spec(qk), part_spec(values), part_spec(values)],
        out_specs=[part_spec(qk), part_spec(values)],
        out_shape=[
            jax.ShapeDtypeStruct(qk.shape, jnp.bfloat16),
            jax.ShapeDtypeStruct(values.shape, jnp.bfloat16),
        ],
        compiler_params=pltpu.CompilerParams(vmem_limit_bytes=32 << 20),
    )(qk, values, grad)


UNITS = 9
WIDE = 640
SLOTS_IN_FLIGHT = 6
SLOTS_RECEIVED = 4
AHEAD = 4
ROWS_A = 96
MESH_ID = pl.DeviceIdType.MESH


class Place:
    def __init__(self):
        dp, tn = lax.axis_index("dp"), lax.axis_index("tensor")
        self.z, self.x = dp // 2, dp % 2
        self.y, self.c = tn // 2, tn % 2
        self.far_x, self.far_y = 1 - self.x, 1 - self.y
        self.to = {
            "x": (self.z * 2 + self.far_x, tn),
            "y": (dp, self.far_y * 2 + self.c),
            "core": (dp, self.y * 2 + 1 - self.c),
            "cross": (dp, self.far_y * 2 + 1 - self.c),
            "up": (dp + 2, tn),
            "down": (dp - 2, tn),
        }
        self.has_up = self.z < 3
        self.has_down = self.z > 0

    def greet(self):
        barrier = pltpu.get_barrier_semaphore()

        def hello(name):
            pl.semaphore_signal(barrier, inc=1, device_id=self.to[name], device_id_type=MESH_ID)

        for name in ("x", "y", "core", "cross"):
            hello(name)
        pl.when(self.has_up)(lambda: hello("up"))
        pl.when(self.has_down)(lambda: hello("down"))
        pl.semaphore_wait(barrier, 4 + (6 - self.z) // 4 + (self.z + 3) // 4)


class Plan:
    FIELDS = (
        ("kind", 16),
        ("unit", 16),
        ("t", 4),
        ("aux", 128),
        ("slot", 2),
        ("fresh", 2),
        ("next", 64),
        ("early", 32),
    )

    def __init__(self, per_turn, loads_early=False):
        self.per_turn, self.loads_early = per_turn, loads_early
        self.steps = {}

    def fill(self, turn, steps):
        tiles = [index for index, step in enumerate(steps) if step[1] is not None]
        early = {}
        for order, index in enumerate(tiles):
            if self.loads_early and steps[index][0] == 1:
                early[tiles[order - 1] if order else index] = 1 + steps[index][3] * 4 + steps[index][2]
        for index, (kind, unit, t, aux) in enumerate(steps):
            slot = fresh = following = 0
            if unit is not None:
                order = tiles.index(index)
                slot, fresh = order % 2, int(order == 0)
                if order + 1 < len(tiles):
                    later = steps[tiles[order + 1]]
                    following = 1 + later[1] * 4 + later[2]
            values = (kind, unit or 0, t, aux, slot, fresh, following, early.get(index, 0))
            code, scale = 0, 1
            for (name, size), value in zip(self.FIELDS, values):
                assert 0 <= value < size
                code += scale * value
                scale *= size
            place = turn * self.per_turn + index * self.per_turn // len(steps)
            assert place not in self.steps
            self.steps[place] = code

    def code(self, place):
        code = jnp.int32(0)
        for where, value in self.steps.items():
            code = jnp.where(place == where, jnp.int32(value), code)
        return code

    def fields(self, code):
        out = {}
        for name, size in self.FIELDS:
            out[name] = code % size
            code = code // size
        return out


def await_bytes(ref, sem):
    pltpu.make_async_copy(ref, ref, sem).wait()


def forward_kernel(
    shard_ref,
    x_ref,
    params_ref,
    position_ref,
    grad_ref,
    whole_ref,
    q_ref,
    pt_ref,
    stream_out_ref,
    qk_ref,
    v_ref,
    slope_ref,
    grad_got,
    moved_ref,
    joined_ref,
    stream,
    xb,
    ptb,
    x_got,
    params_got,
    hidden_bias,
    qkb,
    vb,
    cols,
    slopeb,
    first_rows,
    total,
    wb,
    tile_sem,
    save_sem,
    kept_sem,
    peer_send,
    peer_recv,
    local_sem,
    send_sem,
    recv_sem,
    core_sem,
):
    at = Place()
    z, x, y, c = at.z, at.x, at.y, at.c
    share = shard_ref.shape[1]
    cut = (pl.ds(0, ROWS_A), pl.ds(ROWS_A, share - ROWS_A))
    kinds = {"up": 0, "down": 1, "x": 2, "y": 3, "core": 4}
    at.greet()

    def send(unit, colour, yy, zz, xx, kind, own=False):
        place = whole_ref.at[unit, yy, c, zz, xx, cut[colour]]
        pltpu.make_async_remote_copy(
            src_ref=shard_ref.at[unit, cut[colour]] if own else place,
            dst_ref=place,
            send_sem=send_sem.at[unit, colour, kinds[kind]],
            recv_sem=recv_sem.at[unit, colour, yy, zz, xx],
            device_id=at.to[kind],
            device_id_type=MESH_ID,
        ).start()

    def arrived(unit, colour, yy, zz, xx):
        await_bytes(
            whole_ref.at[unit, yy, c, zz, xx, cut[colour]], recv_sem.at[unit, colour, yy, zz, xx]
        )

    def own_copy(unit):
        return pltpu.make_async_copy(
            shard_ref.at[unit], whole_ref.at[unit, y, c, z, x], local_sem.at[unit]
        )

    def to_core(unit, part):
        if part == 2:
            place = whole_ref.at[unit, :, c, :, :, cut[1]]
        else:
            place = whole_ref.at[unit, y if part == 0 else at.far_y, c, :, :, cut[0]]
        return pltpu.make_async_remote_copy(
            src_ref=place,
            dst_ref=place,
            send_sem=send_sem.at[unit, part // 2, 4],
            recv_sem=core_sem.at[unit, part],
            device_id=at.to["core"],
            device_id_type=MESH_ID,
        )

    def from_z(unit, colour, step, yy):
        @pl.when(z >= step)
        def _():
            zz = z - step
            arrived(unit, colour, yy, zz, x)
            pl.when(at.has_up)(lambda: send(unit, colour, yy, zz, x, "up"))
            send(unit, colour, yy, zz, x, "x")
            if colour == 0:
                send(unit, colour, yy, zz, x, "y")

        @pl.when(z + step <= 3)
        def _():
            zz = z + step
            arrived(unit, colour, yy, zz, x)
            pl.when(at.has_down)(lambda: send(unit, colour, yy, zz, x, "down"))
            send(unit, colour, yy, zz, x, "x")
            if colour == 0:
                send(unit, colour, yy, zz, x, "y")

    def from_x(unit, step):
        def one(zz):
            arrived(unit, 0, y, zz, at.far_x)
            send(unit, 0, y, zz, at.far_x, "y")

        if step == 0:
            one(z)
        else:
            pl.when(z >= step)(lambda: one(z - step))
            pl.when(z + step <= 3)(lambda: one(z + step))

    def stage0(unit):
        own_copy(unit).start()
        pl.when(at.has_up)(lambda: send(unit, 0, y, z, x, "up", True))
        pl.when(at.has_down)(lambda: send(unit, 0, y, z, x, "down", True))
        send(unit, 1, y, z, x, "y", True)
        send(unit, 0, y, z, x, "x", True)
        pl.when(at.has_up)(lambda: send(unit, 1, y, z, x, "up", True))
        pl.when(at.has_down)(lambda: send(unit, 1, y, z, x, "down", True))
        send(unit, 0, y, z, x, "y", True)
        send(unit, 1, y, z, x, "x", True)

    def stage1(unit):
        from_z(unit, 0, 1, y)
        arrived(unit, 1, at.far_y, z, x)
        pl.when(at.has_up)(lambda: send(unit, 1, at.far_y, z, x, "up"))
        pl.when(at.has_down)(lambda: send(unit, 1, at.far_y, z, x, "down"))
        send(unit, 1, at.far_y, z, x, "x")
        from_z(unit, 1, 1, y)
        from_x(unit, 0)

    def stage2(unit):
        from_z(unit, 0, 2, y)
        from_z(unit, 1, 1, at.far_y)
        from_z(unit, 1, 2, y)
        from_x(unit, 1)

    def stage3(unit):
        from_z(unit, 0, 3, y)
        from_z(unit, 1, 2, at.far_y)
        from_z(unit, 1, 3, y)
        from_x(unit, 2)

    def stage4(unit):
        from_z(unit, 1, 3, at.far_y)
        from_x(unit, 3)
        own_copy(unit).wait()
        to_core(unit, 0).start()

    def stage5(unit):
        for zz in range(4):
            for xx in range(2):
                arrived(unit, 0, at.far_y, zz, xx)
        to_core(unit, 1).start()
        for zz in range(4):
            for yy in range(2):
                arrived(unit, 1, yy, zz, at.far_x)
        to_core(unit, 2).start()

    def stage6(unit):
        other = 1 - c
        await_bytes(whole_ref.at[unit, y, other, :, :, cut[0]], core_sem.at[unit, 0])
        await_bytes(whole_ref.at[unit, at.far_y, other, :, :, cut[0]], core_sem.at[unit, 1])
        await_bytes(whole_ref.at[unit, :, other, :, :, cut[1]], core_sem.at[unit, 2])
        for colour in range(2):
            rows = cut[colour]
            await_bytes(whole_ref.at[unit, :, c, :, :, rows], send_sem.at[unit, colour, 4])
            whole_x = whole_ref.at[unit, 0, c, :, 0, rows] if colour == 0 else None
            if colour == 0:
                await_bytes(whole_x, send_sem.at[unit, 0, 2])
                await_bytes(whole_ref.at[unit, 0, c, :, :, rows], send_sem.at[unit, 0, 3])
            else:
                await_bytes(whole_ref.at[unit, 0, c, :, :, rows], send_sem.at[unit, 1, 2])
                await_bytes(whole_ref.at[unit, 0, c, 0, 0, rows], send_sem.at[unit, 1, 3])
            for level in range(3):

                def ups(level=level):
                    if colour == 0:
                        ref = whole_ref.at[unit, 0, c, pl.ds(0, level + 1), 0, rows]
                    else:
                        ref = whole_ref.at[unit, :, c, pl.ds(0, level + 1), 0, rows]
                    return ref

                pl.when(z == level)(
                    lambda level=level: await_bytes(ups(level), send_sem.at[unit, colour, 0])
                )
                pl.when(z == 3 - level)(
                    lambda level=level: await_bytes(ups(level), send_sem.at[unit, colour, 1])
                )

    stages = (stage0, stage1, stage2, stage3, stage4, stage5, stage6)

    rows_all, width = x_ref.shape[1], x_ref.shape[2]
    half_rows = rows_all // 2
    scale = 1.0 / math.sqrt(HEAD)
    own_t = y * 2 + c

    def save_now(source, target):
        copy = pltpu.make_async_copy(source, target, save_sem.at[0])
        copy.start()
        copy.wait()

    peers = (("y", at.far_y * 2 + c), ("core", y * 2 + 1 - c), ("cross", at.far_y * 2 + 1 - c))

    def peer_copies(index):
        kind, t = peers[index]
        target = {"device_id": at.to[kind], "device_id_type": MESH_ID}
        return (
            pltpu.make_async_remote_copy(
                src_ref=params_ref,
                dst_ref=params_got.at[own_t],
                send_sem=peer_send.at[0, index],
                recv_sem=peer_recv.at[0, index],
                **target,
            ),
            pltpu.make_async_remote_copy(
                src_ref=x_ref.at[t],
                dst_ref=x_got.at[own_t],
                send_sem=peer_send.at[1, index],
                recv_sem=peer_recv.at[1, index],
                **target,
            ),
            pltpu.make_async_remote_copy(
                src_ref=grad_ref.at[t],
                dst_ref=grad_got.at[own_t],
                send_sem=peer_send.at[2, index],
                recv_sem=peer_recv.at[2, index],
                **target,
            ),
        )

    own_peer = (
        pltpu.make_async_copy(params_ref, params_got.at[own_t], peer_send.at[0, 3]),
        pltpu.make_async_copy(x_ref.at[own_t], x_got.at[own_t], peer_send.at[1, 3]),
        pltpu.make_async_copy(grad_ref.at[own_t], grad_got.at[own_t], peer_send.at[2, 3]),
    )
    for index in range(3):
        for copy in peer_copies(index):
            copy.start()
    for copy in own_peer:
        copy.start()

    def each(count, size, use):
        def one(step, carry):
            use(pl.ds(pl.multiple_of(step * size, size), size))
            return carry

        lax.fori_loop(0, count, one, 0)

    def tile_load(unit, t, slot):
        return pltpu.make_async_copy(whole_ref.at[unit, t // 2, t % 2], wb.at[slot], tile_sem.at[slot])

    def kept_copies(which, t):
        target = (10, 4, 1, 0)[which]
        copies = [
            pltpu.make_async_copy(cols.at[which, t], q_ref.at[target, t], kept_sem.at[which, t, 0])
        ]
        if which < 2:
            pairs = [(qkb.at[which, t], qk_ref.at[which, t]), (vb.at[which, t], v_ref.at[which, t])]
        else:
            pairs = [(slopeb.at[which - 2, t], slope_ref.at[which - 2, t])]
        for index, (source, target_ref) in enumerate(pairs):
            copies.append(
                pltpu.make_async_copy(source, target_ref, kept_sem.at[which, t, 1 + index])
            )
        return copies

    def do_spread(op):
        matrix = op["slot"]
        t, aux = op["t"], op["aux"]

        def multiply(rows):
            total[rows, :] = dot_plain(xb[rows, :], wb[matrix].reshape(C, WIDE))

        each(2, half_rows, multiply)
        quarter = rows_all // 4

        @pl.when(aux == 0)
        def _():
            def use(rows):
                first_rows[t, rows, :] = total[rows, width:]

            each(4, quarter, use)

        @pl.when((aux == 1) | (aux == 3))
        def _():
            def use(rows):
                qkb[(aux - 1) // 2, t, rows, :] = total[rows, :].astype(jnp.bfloat16)

            each(4, quarter, use)

        @pl.when((aux == 2) | (aux == 4))
        def _():
            def use(rows):
                vb[(aux - 2) // 2, t, rows, :] = total[rows, 0:width].astype(jnp.bfloat16)

            each(4, quarter, use)

        @pl.when((aux == 5) | (aux == 6))
        def _():
            half = aux - 5

            def use(rows):
                pre = total[rows, :] + hidden_bias[t, pl.ds(half, 1), :]
                below = 0.5 * (1.0 + lax.erf(pre * math.sqrt(0.5)))
                cols[2 + half, t, rows, :] = (pre * below).astype(jnp.bfloat16)
                density = jnp.exp(-0.5 * pre * pre) * (1.0 / math.sqrt(2.0 * math.pi))
                slopeb[half, t, rows, :] = (below + pre * density).astype(jnp.bfloat16)

            each(rows_all // 32, 32, use)
            for which in (2, 3):

                @pl.when(half == which - 2)
                def _(which=which):
                    for copy in kept_copies(which, t):
                        copy.start()

        @pl.when(aux == 7)
        def _():
            def use(rows):
                moved_ref[t, rows, :] = (total[rows, width:] + params_got[t, 12:13, :]).astype(
                    jnp.bfloat16
                )

            each(4, quarter, use)

    def do_collapse(op):
        def multiply(rows):
            stream[rows, :] += dot_rows(cols[op["aux"], op["t"], rows, :], wb[op["slot"]].reshape(C, WIDE))

        each(2, half_rows, multiply)

    def do_attention(op):
        block, t = op["aux"], op["t"]
        same = same_pixel(BLOCK)

        def write(place):
            for start in range(0, rows_all, BLOCK):
                here = slice(start, start + BLOCK)
                for head in range(width // HEAD):
                    low = head * HEAD
                    query = qkb[block, t, here, low : low + HEAD]
                    key = qkb[block, t, here, width + low : width + low + HEAD]
                    value = vb[block, t, here, low : low + HEAD]
                    probs = head_probs(query, key, same, scale).astype(jnp.bfloat16)
                    total[here, low : low + HEAD] = dot_plain(probs, value)

        write(0)
        for which in range(2):

            @pl.when(block == which)
            def _(which=which):
                own = slice(width, 2 * width) if which == 0 else slice(0, width)
                other = slice(0, width) if which == 0 else slice(width, 2 * width)

                def use(rows):
                    cols[which, t, rows, own] = total[rows, 0:width].astype(jnp.bfloat16)
                    cols[which, t, rows, other] = jnp.zeros((rows_all // 4, width), jnp.bfloat16)

                each(4, rows_all // 4, use)
                for copy in kept_copies(which, t):
                    copy.start()

    chunk = 4 * FRAMES

    def do_norm(op):
        layer = op["aux"]

        def use(rows):
            @pl.when(layer == 0)
            def _():
                for t in range(4):
                    stream[rows, t * width : (t + 1) * width] = first_rows[t, rows, :]

            values = stream[rows, :] + joined_ref[pl.ds(8 + layer, 1), :]
            stream[rows, :] = values
            centre = jnp.mean(values, axis=1, keepdims=True)
            offset = values - centre
            inverse = lax.rsqrt(jnp.mean(offset * offset, axis=1, keepdims=True) + 1e-05)
            normed = offset * inverse * joined_ref[pl.ds(1 + layer, 1), :]
            normed = normed + joined_ref[pl.ds(5 + layer, 1), :]
            added = jnp.where(layer < 2, position_ref[...], 0.0)
            normed = normed.reshape(chunk // FRAMES, FRAMES, C) + added[None]
            xb[rows, :] = normed.reshape(chunk, C).astype(jnp.bfloat16)

        each(rows_all // chunk, chunk, use)
        save_now(stream, stream_out_ref.at[layer])

    def do_turn(op):
        def one(step, carry):
            lanes = pl.ds(pl.multiple_of(step * 128, 128), 128)
            ptb[lanes, :] = xb[:, lanes].T
            return carry

        lax.fori_loop(0, C // 128, one, 0)
        save_now(ptb, pt_ref.at[op["aux"]])

    def do_last(op):
        def use(rows):
            xb[rows, :] = (stream[rows, :] + joined_ref[11:12, :]).astype(jnp.bfloat16)

        each(rows_all // chunk, chunk, use)

    def do_join(op):
        for index in range(3):
            for copy in peer_copies(index)[:2]:
                copy.wait_recv()
        for copy in own_peer[:2]:
            copy.wait()
        for t in range(4):
            lanes = slice(t * width, (t + 1) * width)
            joined_ref[:, lanes] = params_got[t, 0:16, :]

            def use(rows, t=t, lanes=lanes):
                xb[rows, lanes] = x_got[t, rows, :]

            each(4, rows_all // 4, use)
            for half in range(2):
                for part in range(2):
                    row = 16 + 2 * half + part
                    hidden_bias[t, half : half + 1, part * width : (part + 1) * width] = params_got[
                        t, row : row + 1, :
                    ]

    works = (None, do_spread, do_collapse, do_attention, do_norm, do_turn, do_last, do_join)
    four = range(4)

    def spreads(unit, aux):
        return [(1, unit, t, aux) for t in four]

    def collapses(unit, aux):
        return [(2, unit, t, aux) for t in four]

    def attentions(aux):
        return [(3, None, t, aux) for t in four]

    count = len(stages)
    places = 2 * count
    plan = Plan(places)
    for ready, steps in {
        -4: [(7, None, 0, 0), (5, None, 0, 7)],
        1: spreads(1, 0) + [(4, None, 0, 0)] + spreads(0, 1) + spreads(1, 2),
        2: [(5, None, 0, 4)] + attentions(0),
        3: collapses(3, 0) + [(4, None, 0, 1)] + spreads(2, 3) + spreads(3, 4),
        4: [(5, None, 0, 3)] + attentions(1) + collapses(4, 1) + [(4, None, 0, 2)],
        5: [(5, None, 0, 1)] + spreads(5, 5),
        6: spreads(6, 6),
        7: collapses(7, 2),
        8: collapses(8, 3) + [(6, None, 0, 0)] + spreads(4, 7) + [(5, None, 0, 5)],
    }.items():
        plan.fill(ready + count - 1, steps)

    def do_step(place):
        code = plan.code(place)
        pl.when(code > 0)(lambda: do_filled(code))

    def do_filled(code):
        op = plan.fields(code)
        has_tile = (op["kind"] == 1) | (op["kind"] == 2)

        @pl.when(has_tile)
        def _():
            pl.when(op["fresh"] == 1)(lambda: tile_load(op["unit"], op["t"], op["slot"]).start())

            @pl.when(op["next"] > 0)
            def _():
                following = op["next"] - 1
                tile_load(following // 4, following % 4, 1 - op["slot"]).start()

            tile_load(op["unit"], op["t"], op["slot"]).wait()

        for kind in range(1, len(works)):

            @pl.when(op["kind"] == kind)
            def _(kind=kind):
                works[kind](op)

    def advance(turn, carry):
        def inner(place, carry):
            for spot, number in enumerate((count - 1, 0) + tuple(range(count - 2, 0, -1))):
                unit = turn - number + (AHEAD if number == 0 else 0)
                if number == 0:

                    @pl.when((place == spot) & (turn == 0))
                    def _():
                        def begin(unit, carry):
                            stage0(unit)
                            return carry

                        lax.fori_loop(0, AHEAD, begin, 0)

                @pl.when((place == spot) & (unit >= 0) & (unit < UNITS))
                def _(number=number, unit=unit):
                    stages[number](unit)

            def two(step, carry):
                do_step(2 * (turn * count + place) + step)
                return carry

            return lax.fori_loop(0, 2, two, carry)

        return lax.fori_loop(0, count, inner, carry)

    lax.fori_loop(0, UNITS + count - 1, advance, 0)
    for which in range(4):
        for t in range(4):
            for copy in kept_copies(which, t):
                copy.wait()
    for index in range(3):
        for copy in peer_copies(index):
            copy.wait_send()
        peer_copies(index)[2].wait_recv()
    own_peer[2].wait()


def forward_all(shards, rows_in, params, position, grad):
    units, share, wide = shards.shape
    rows, width = rows_in.shape[1], rows_in.shape[2]
    low = jnp.bfloat16
    anywhere, near = pl.BlockSpec(memory_space=pl.ANY), pl.BlockSpec(memory_space=pltpu.VMEM)
    return pl.pallas_call(
        forward_kernel,
        in_specs=[near, anywhere, near, near, near],
        out_specs=[anywhere] * 8 + [near] * 2,
        out_shape=[
            jax.ShapeDtypeStruct((units, 2, 2, 4, 2, share, wide), low),
            jax.ShapeDtypeStruct((12, 4, rows, wide), low),
            jax.ShapeDtypeStruct((8, C, rows), low),
            jax.ShapeDtypeStruct((3, rows, C), jnp.float32),
            jax.ShapeDtypeStruct((2, 4, rows, wide), low),
            jax.ShapeDtypeStruct((2, 4, rows, width), low),
            jax.ShapeDtypeStruct((2, 4, rows, wide), low),
            jax.ShapeDtypeStruct((4, rows, width), low),
            jax.ShapeDtypeStruct((4, rows, width), low),
            jax.ShapeDtypeStruct((16, C), jnp.float32),
        ],
        scratch_shapes=[
            pltpu.VMEM((rows, C), jnp.float32),
            pltpu.VMEM((rows, C), low),
            pltpu.VMEM((C, rows), low),
            pltpu.VMEM((4, rows, width), low),
            pltpu.VMEM((4,) + params.shape, jnp.float32),
            pltpu.VMEM((4, 8, wide), jnp.float32),
            pltpu.VMEM((2, 4, rows, wide), low),
            pltpu.VMEM((2, 4, rows, width), low),
            pltpu.VMEM((4, 4, rows, wide), low),
            pltpu.VMEM((2, 4, rows, wide), low),
            pltpu.VMEM((4, rows, width), jnp.float32),
            pltpu.VMEM((rows, wide), jnp.float32),
            pltpu.VMEM((2, 4, 2, share, wide), low),
            pltpu.SemaphoreType.DMA((2,)),
            pltpu.SemaphoreType.DMA((1,)),
            pltpu.SemaphoreType.DMA((4, 4, 3)),
            pltpu.SemaphoreType.DMA((3, 4)),
            pltpu.SemaphoreType.DMA((3, 3)),
            pltpu.SemaphoreType.DMA((units,)),
            pltpu.SemaphoreType.DMA((units, 2, 5)),
            pltpu.SemaphoreType.DMA((units, 2, 2, 4, 2)),
            pltpu.SemaphoreType.DMA((units, 3)),
        ],
        compiler_params=pltpu.CompilerParams(
            collective_id=0, has_side_effects=True, vmem_limit_bytes=60 << 20
        ),
    )(shards, rows_in, params, position, grad)


def backward_kernel(
    whole_ref,
    q_given,
    pt_given,
    streams_ref,
    qk_ref,
    v_ref,
    slope_ref,
    grad_ref,
    moved_ref,
    joined_ref,
    out_ref,
    q_ref,
    pt_ref,
    ptx_ref,
    qx_ref,
    got_ref,
    moved_got,
    vec_ref,
    hidden_ref,
    p_buf,
    q_buf,
    dw,
    rya,
    rxa,
    rua,
    rda,
    rxb,
    rub,
    rdb,
    ryb,
    gs,
    gn,
    xb,
    ptb,
    wb,
    cb,
    av,
    datt,
    total,
    sb,
    ob,
    dn,
    load_sem,
    give_sem,
    take_sem,
    send_sem,
    recv_sem,
    tile_sem,
    aux_sem,
    route_sem,
    misc_sem,
    out_sem,
    peer_send,
    peer_recv,
):
    at = Place()
    z, x, y, c = at.z, at.x, at.y, at.c
    far_x, far_y = at.far_x, at.far_y
    share = out_ref.shape[1]
    row_a, row_b = pl.ds(0, ROWS_A), pl.ds(ROWS_A, share - ROWS_A)
    rows_all, width = got_ref.shape[1], got_ref.shape[2]
    half_rows = rows_all // 2
    count_p = pt_ref.shape[0]
    scale = 1.0 / math.sqrt(HEAD)
    own_t = y * 2 + c
    at.greet()

    def give_p(index, source=None):
        return pltpu.make_async_remote_copy(
            src_ref=pt_ref.at[index] if source is None else source,
            dst_ref=ptx_ref.at[index],
            send_sem=give_sem.at[index],
            recv_sem=take_sem.at[index],
            device_id=at.to["core"],
            device_id_type=MESH_ID,
        )

    def give_q(index, yy, source):
        return pltpu.make_async_remote_copy(
            src_ref=source,
            dst_ref=qx_ref.at[index, yy],
            send_sem=give_sem.at[count_p + 2 * index + yy],
            recv_sem=take_sem.at[count_p + 2 * index + yy],
            device_id=at.to["core"],
            device_id_type=MESH_ID,
        )

    def known_q(index, yy):
        return give_q(index, yy, q_ref.at[index, 2 * yy + 1 - c])

    known = (0, 1, 4, 10)
    known_p = (1, 5, 3, 4, 7)
    for index in known[:2]:
        for yy in range(2):
            known_q(index, yy).start()
    give_p(1).start()

    def give_rest():
        for index in known[2:]:
            for yy in range(2):
                known_q(index, yy).start()
        for index in known_p[1:]:
            give_p(index).start()

    def each(count, size, use):
        def one(step, carry):
            use(pl.ds(pl.multiple_of(step * size, size), size))
            return carry

        lax.fori_loop(0, count, one, 0)

    def aux_load(source, target, number):
        return pltpu.make_async_copy(source, target, aux_sem.at[number])

    def tile_load(unit, t, slot):
        return pltpu.make_async_copy(whole_ref.at[unit, t // 2, t % 2], wb.at[slot], tile_sem.at[slot])

    def route(source, index, t):
        yy = t // 2
        local = pltpu.make_async_copy(source, q_ref.at[index, t], route_sem.at[index, yy])

        def begin():
            pl.when(c == t % 2)(lambda: local.start())
            pl.when(c != t % 2)(lambda: give_q(index, yy, source).start())

        def wait():
            pl.when(c == t % 2)(lambda: local.wait())
            pl.when(c != t % 2)(lambda: give_q(index, yy, source).wait_send())

        return begin, wait

    chunk = 4 * FRAMES
    quarter = rows_all // 4

    def column_sum(row, values):
        vec_ref[pl.ds(row, 1), :] += jnp.sum(values, axis=0, keepdims=True)

    def slope_load(aux, t):
        return aux_load(slope_ref.at[aux, t], cb.at[4], 0)

    def head_loads(aux, t):
        return (
            aux_load(qk_ref.at[aux - 2, t], cb.at[4], 0),
            aux_load(v_ref.at[aux - 2, t], av, 1),
        )

    def load_early(code):
        aux, t = code // 4, code % 4
        pl.when(aux < 2)(lambda: slope_load(aux, t).start())

        @pl.when(aux >= 2)
        def _():
            for load in head_loads(aux, t):
                load.start()

    def do_spread(op):
        t, aux = op["t"], op["aux"]
        side = t % 2

        def multiply(rows):
            total[rows, :] = dot_plain(xb[rows, :], wb[op["slot"]].reshape(C, WIDE))

        each(2, half_rows, multiply)

        @pl.when(aux < 2)
        def _():
            slope_load(aux, t).wait()

            def use(rows):
                grad = total[rows, :] * cb[4, rows, :].astype(jnp.float32)
                hidden_ref[t, pl.ds(aux, 1), :] += jnp.sum(grad, axis=0, keepdims=True)
                cb[side, rows, :] = grad.astype(jnp.bfloat16)

            each(4, quarter, use)
            route(cb.at[side], 3 - aux, t)[0]()

        @pl.when(aux >= 2)
        def _():
            for load in head_loads(aux, t):
                load.wait()

            for block in range(2):

                @pl.when(aux == 2 + block)
                def _(block=block):
                    low = width if block == 0 else 0

                    def use(rows):
                        datt[rows, :] = total[rows, low : low + width].astype(jnp.bfloat16)

                    each(4, quarter, use)

    def do_collapse(op):
        which, routed, t = op["aux"] % 5, op["aux"] // 5, op["t"]

        def multiply(rows):
            gn[rows, :] += dot_rows(cb[which, rows, :], wb[op["slot"]].reshape(C, WIDE))

        each(2, half_rows, multiply)
        pl.when(routed > 0)(lambda: route(cb.at[which], routed - 1, t)[1]())

    def do_attention(op):
        block, t = op["aux"], op["t"]
        side = t % 2
        same = same_pixel(BLOCK)
        for start in range(0, rows_all, BLOCK):
            here = slice(start, start + BLOCK)
            for head in range(width // HEAD):
                low = head * HEAD
                query = cb[4, here, low : low + HEAD]
                key = cb[4, here, width + low : width + low + HEAD]
                value = av[here, low : low + HEAD]
                grad = datt[here, low : low + HEAD]
                probs = head_probs(query, key, same, scale)
                grad_probs = dot_rows(grad, value)
                centred = jnp.sum(probs * grad_probs, axis=1, keepdims=True)
                grad_raw = (probs * (grad_probs - centred) * scale).astype(jnp.bfloat16)
                cb[side, here, low : low + HEAD] = dot_plain(grad_raw, key).astype(jnp.bfloat16)
                cb[side, here, width + low : width + low + HEAD] = dot_first(
                    grad_raw, query
                ).astype(jnp.bfloat16)
                cb[2 + side, here, low : low + HEAD] = dot_first(
                    probs.astype(jnp.bfloat16), grad
                ).astype(jnp.bfloat16)
        route(cb.at[side], 7 - 2 * block, t)[0]()
        route(cb.at[2 + side], 8 - 2 * block, t)[0]()

    def do_layer(op):
        layer = op["aux"]

        def load(step):
            rows = pl.ds(pl.multiple_of(step * chunk, chunk), chunk)
            return pltpu.make_async_copy(
                streams_ref.at[layer, rows], sb.at[step % 2], misc_sem.at[3 + step % 2]
            )

        def one(step, carry):
            pl.when(step + 1 < rows_all // chunk)(lambda: load(step + 1).start())
            load(step).wait()
            rows = pl.ds(pl.multiple_of(step * chunk, chunk), chunk)
            values = sb[step % 2]
            centre = jnp.mean(values, axis=1, keepdims=True)
            offset = values - centre
            inverse = lax.rsqrt(jnp.mean(offset * offset, axis=1, keepdims=True) + 1e-05)
            hat = offset * inverse
            grad = gn[rows, :]
            column_sum(layer, grad * hat)
            column_sum(3 + layer, grad)
            scaled = grad * joined_ref[pl.ds(1 + layer, 1), :]
            first = jnp.mean(scaled, axis=1, keepdims=True)
            second = jnp.mean(scaled * hat, axis=1, keepdims=True)
            result = gs[rows, :] + inverse * (scaled - first - hat * second)
            gs[rows, :] = result
            column_sum(6 + layer, result)
            xb[rows, :] = result.astype(jnp.bfloat16)
            gn[rows, :] = jnp.zeros((chunk, C), jnp.float32)
            return carry

        load(0).start()
        lax.fori_loop(0, rows_all // chunk, one, 0)

    def do_turn(op):
        index = op["aux"]

        def one(step, carry):
            lanes = pl.ds(pl.multiple_of(step * 128, 128), 128)
            ptb[lanes, :] = xb[:, lanes].T
            return carry

        lax.fori_loop(0, C // 128, one, 0)
        turn_copy(index).start()
        give_p(index, ptb).start()

    def turn_copy(index):
        return pltpu.make_async_copy(ptb, pt_ref.at[index], misc_sem.at[2])

    def do_turned(op):
        turn_copy(op["aux"]).wait()
        give_p(op["aux"], ptb).wait_send()

    def do_first(op):
        def use(rows):
            values = gn[rows, :]
            gs[rows, :] = values
            column_sum(9, values)
            xb[rows, :] = values.astype(jnp.bfloat16)
            gn[rows, :] = jnp.zeros((chunk, C), jnp.float32)

        each(rows_all // chunk, chunk, use)

    def do_place(op):
        t, aux = op["t"], op["aux"]
        side = t % 2

        @pl.when(aux == 1)
        def _():
            load = aux_load(grad_ref.at[t], datt, 0)
            load.start()
            load.wait()

            def use(rows):
                cb[side, rows, 0:width] = jnp.zeros((quarter, width), jnp.bfloat16)
                cb[side, rows, width:] = datt[rows, :]

            each(4, quarter, use)

        for block in range(4):

            @pl.when((aux == 0) & (t == block))
            def _(block=block):
                def use(rows):
                    cb[side, rows, 0:width] = jnp.zeros((quarter, width), jnp.bfloat16)
                    cb[side, rows, width:] = xb[rows, block * width : (block + 1) * width]

                each(4, quarter, use)

        route(cb.at[side], 11 - 2 * aux, t)[0]()

    peers = (("y", far_y * 2 + c), ("core", y * 2 + 1 - c), ("cross", far_y * 2 + 1 - c))

    def peer_copy(index):
        kind, t = peers[index]
        return pltpu.make_async_remote_copy(
            src_ref=dn.at[t],
            dst_ref=got_ref.at[own_t],
            send_sem=peer_send.at[0, index],
            recv_sem=peer_recv.at[0, index],
            device_id=at.to[kind],
            device_id_type=MESH_ID,
        )

    def moved_copy(index):
        kind, t = peers[index]
        return pltpu.make_async_remote_copy(
            src_ref=moved_ref.at[t],
            dst_ref=moved_got.at[own_t],
            send_sem=peer_send.at[1, index],
            recv_sem=peer_recv.at[1, index],
            device_id=at.to[kind],
            device_id_type=MESH_ID,
        )

    own_peer = pltpu.make_async_copy(dn.at[own_t], got_ref.at[own_t], peer_send.at[0, 3])
    own_moved = pltpu.make_async_copy(
        moved_ref.at[own_t], moved_got.at[own_t], peer_send.at[1, 3]
    )
    for index in range(3):
        moved_copy(index).start()
    own_moved.start()

    def do_send(op):
        for t in range(4):

            def use(rows, t=t):
                dn[t, rows, :] = gn[rows, t * width : (t + 1) * width].astype(jnp.bfloat16)

            each(4, quarter, use)
        for index in range(3):
            peer_copy(index).start()
        own_peer.start()

    works = (
        None,
        do_spread,
        do_collapse,
        do_attention,
        do_layer,
        do_turn,
        do_first,
        do_place,
        do_send,
        do_turned,
    )
    four = range(4)

    def feed(half):
        steps = []
        for t in four:
            steps += [(1, 7 + half, t, half), (2, 5 + half, t, t % 2 + 5 * (4 - half))]
        return steps

    def heads(block, t):
        return [
            (1, 3 + block, t, 2 + block),
            (3, None, t, block),
            (2, 2 * block, t, t % 2 + 5 * (8 - 2 * block)),
            (2, 2 * block + 1, t, 2 + t % 2 + 5 * (9 - 2 * block)),
        ]

    def inputs(t):
        return [(7, None, t, 0), (2, 1, t, t % 2 + 5 * 12)]

    def outputs(t):
        return [(7, None, t, 1), (2, 4, t, t % 2 + 5 * 10)]

    stage_count = 6
    plan = Plan(2 * stage_count, True)
    for turn, steps in {
        -1: outputs(0) + outputs(1) + outputs(2) + outputs(3) + [(6, None, 0, 0), (5, None, 0, 0), (9, None, 0, 0)],
        0: feed(1),
        1: feed(0),
        2: [(4, None, 0, 2), (5, None, 0, 2)] + heads(1, 0) + [(9, None, 0, 2)],
        3: heads(1, 1) + heads(1, 2),
        4: heads(1, 3),
        5: [(4, None, 0, 1), (5, None, 0, 6)] + heads(0, 0) + [(9, None, 0, 6)],
        6: heads(0, 1) + heads(0, 2) + heads(0, 3),
        7: [(4, None, 0, 0)] + inputs(0) + inputs(1) + inputs(2) + inputs(3),
        8: [(8, None, 0, 0)],
    }.items():
        plan.fill(turn + 1, steps)

    def do_step(place):
        code = plan.code(place)
        pl.when(code > 0)(lambda: do_filled(code))

    def do_filled(code):
        op = plan.fields(code)
        has_tile = (op["kind"] == 1) | (op["kind"] == 2)

        @pl.when(has_tile)
        def _():
            pl.when(op["fresh"] == 1)(lambda: tile_load(op["unit"], op["t"], op["slot"]).start())

            @pl.when(op["next"] > 0)
            def _():
                following = op["next"] - 1
                tile_load(following // 4, following % 4, 1 - op["slot"]).start()

            pl.when(op["early"] > 0)(lambda: load_early(op["early"] - 1))
            tile_load(op["unit"], op["t"], op["slot"]).wait()

        for kind in range(1, len(works)):

            @pl.when(op["kind"] == kind)
            def _(kind=kind):
                works[kind](op)

    vec_ref[...] = jnp.zeros_like(vec_ref)
    hidden_ref[...] = jnp.zeros_like(hidden_ref)

    def clear(rows):
        gn[rows, :] = jnp.zeros((chunk, C), jnp.float32)
        cb[2, rows, :] = jnp.zeros((chunk, WIDE), jnp.bfloat16)
        cb[3, rows, :] = jnp.zeros((chunk, WIDE), jnp.bfloat16)

    each(rows_all // chunk, chunk, clear)

    names = ["ya0", "ya1", "xa", "ua0", "ua1", "ua2", "da0", "da1", "da2"]
    names += ["xb0", "xb1", "ub0", "ub1", "ub2", "db0", "db1", "db2", "yb"]
    number = {name: index for index, name in enumerate(names)}

    class Slot:
        def __init__(self, turn):
            self.d, self.r = turn % SLOTS_IN_FLIGHT, turn % SLOTS_RECEIVED

    def copy(slot, name, src, dst, kind, shift=0):
        index = number[name] + shift
        return pltpu.make_async_remote_copy(
            src_ref=src,
            dst_ref=dst,
            send_sem=send_sem.at[slot.d, index],
            recv_sem=recv_sem.at[slot.r, index],
            device_id=at.to[kind],
            device_id_type=MESH_ID,
        )

    def ya(slot, part):
        side = far_x if part == 0 else x
        return copy(
            slot, f"ya{part}", dw.at[slot.d, far_y, :, side, row_a], rya.at[slot.r, part], "y"
        )

    def xa(slot):
        return copy(slot, "xa", dw.at[slot.d, y, :, far_x, row_a], rxa.at[slot.r], "x")

    def xb_copy(slot, part):
        return copy(
            slot, f"xb{part}", dw.at[slot.d, part, :, far_x, row_b], rxb.at[slot.r, part], "x"
        )

    def yb(slot):
        return copy(slot, "yb", dw.at[slot.d, far_y, z, x, row_b], ryb.at[slot.r], "y")

    def up(slot, colour, d):
        if colour == 0:
            return copy(
                slot, "ua0", dw.at[slot.d, y, d, x, row_a], rua.at[slot.r, d - 1], "up", d - 1
            )
        return copy(slot, "ub0", dw.at[slot.d, :, d, x, row_b], rub.at[slot.r, d - 1], "up", d - 1)

    def down(slot, colour, d):
        if colour == 0:
            return copy(slot, "da0", dw.at[slot.d, y, d, x, row_a], rda.at[slot.r, d], "down", d)
        return copy(slot, "db0", dw.at[slot.d, :, d, x, row_b], rdb.at[slot.r, d], "down", d)

    def add(place, got):
        total = place[...].astype(jnp.float32) + got[...].astype(jnp.float32)
        place[...] = total.astype(jnp.bfloat16)

    def product_loads(p_index, q_index):
        loads = [
            pltpu.make_async_copy(pt_ref.at[p_index], p_buf.at[0], load_sem.at[0]),
            pltpu.make_async_copy(ptx_ref.at[p_index], p_buf.at[1], load_sem.at[1]),
        ]
        for yy in range(2):
            loads += [
                pltpu.make_async_copy(
                    q_ref.at[q_index, 2 * yy + c], q_buf.at[0, yy], load_sem.at[2 + yy]
                ),
                pltpu.make_async_copy(
                    qx_ref.at[q_index, yy], q_buf.at[1, yy], load_sem.at[4 + yy]
                ),
            ]
        return loads

    def products(slot, p_index, q_index, mixed, more):
        for load in product_loads(p_index, q_index):
            load.wait()

        def one(step, carry):
            side, zz = step // 4, step % 4
            yy = jnp.where(side == 0, far_y, y)
            rows = pl.ds(pl.multiple_of(zz * 2 * share, 2 * share), 2 * share)

            def part(first, last):
                result = dot_plain(p_buf[0, rows, :], q_buf[0, yy, :, first:last])
                result = result + dot_plain(p_buf[1, rows, :], q_buf[1, yy, :, first:last])
                return result.reshape(2, share, last - first)

            @pl.when(mixed == 0)
            def _():
                dw[slot.d, yy, zz] = part(0, WIDE).astype(jnp.bfloat16)

            @pl.when((mixed == 1) & (more == 0))
            def _():
                dw[slot.d, yy, zz, :, :, 0:384] = part(0, 384).astype(jnp.bfloat16)

            @pl.when((mixed == 1) & (more == 1))
            def _():
                result = part(256, WIDE)
                shared = dw[slot.d, yy, zz, :, :, 256:384].astype(jnp.float32)
                shared = shared + result[:, :, 0:128]
                dw[slot.d, yy, zz, :, :, 256:384] = shared.astype(jnp.bfloat16)
                dw[slot.d, yy, zz, :, :, 384:] = result[:, :, 128:].astype(jnp.bfloat16)

            return carry

        lax.fori_loop(0, 8, one, 0)

    def take_p(index):
        await_bytes(ptx_ref.at[index], take_sem.at[index])

    def take_q(index):
        for yy in range(2):
            await_bytes(qx_ref.at[index, yy], take_sem.at[count_p + 2 * index + yy])

    def prepare(turn):
        p_index = (turn + turn // 5) // 2

        @pl.when((turn + turn // 5) % 2 == 0)
        def _():
            take_p(p_index)

        take_q(turn)
        for load in product_loads(p_index, turn):
            load.start()

    def stage0(turn):
        slot = Slot(turn)
        p_index = (turn + turn // 5) // 2
        mixed = (turn >= 4).astype(jnp.int32) * (1 - turn % 2)
        extra = (turn - 4) // 2

        @pl.when(mixed == 1)
        def _():
            take_p(5 + extra)
            take_q(UNITS + extra)

        def one_pass(more, carry):
            @pl.when(more == 1)
            def _():
                for load in product_loads(5 + extra, UNITS + extra):
                    load.start()

            products(
                slot,
                jnp.where(more == 1, 5 + extra, p_index),
                jnp.where(more == 1, UNITS + extra, turn),
                mixed,
                more,
            )
            return carry

        lax.fori_loop(0, 1 + mixed, one_pass, 0)

        ya(slot, 0).start()
        xb_copy(slot, 0).start()
        ya(slot, 1).start()
        xb_copy(slot, 1).start()

    def z_step(slot, colour, step):
        @pl.when(z <= step - 1)
        def _():
            d = z + 4 - step

            @pl.when(z >= 1)
            def _():
                up(slot, colour, d).wait_recv()
                if colour == 0:
                    add(dw.at[slot.d, y, d, x, row_a], rua.at[slot.r, d - 1])
                else:
                    add(dw.at[slot.d, 0, d, x, row_b], rub.at[slot.r, d - 1, 0])
                    add(dw.at[slot.d, 1, d, x, row_b], rub.at[slot.r, d - 1, 1])

            up(slot, colour, d).start()

        @pl.when(3 - z <= step - 1)
        def _():
            d = z - 4 + step

            @pl.when(z <= 2)
            def _():
                down(slot, colour, d).wait_recv()
                if colour == 0:
                    add(dw.at[slot.d, y, d, x, row_a], rda.at[slot.r, d])
                else:
                    add(dw.at[slot.d, 0, d, x, row_b], rdb.at[slot.r, d, 0])
                    add(dw.at[slot.d, 1, d, x, row_b], rdb.at[slot.r, d, 1])

            down(slot, colour, d).start()

    def stage1(turn):
        slot = Slot(turn)
        for part in range(2):
            xb_copy(slot, part).wait_recv()
            for zz in range(4):
                add(dw.at[slot.d, part, zz, x, row_b], rxb.at[slot.r, part, zz])
        z_step(slot, 1, 1)
        ya(slot, 0).wait_recv()
        for zz in range(4):
            add(dw.at[slot.d, y, zz, far_x, row_a], rya.at[slot.r, 0, zz])
        xa(slot).start()
        ya(slot, 1).wait_recv()
        for zz in range(4):
            add(dw.at[slot.d, y, zz, x, row_a], rya.at[slot.r, 1, zz])

    def stage2(turn):
        slot = Slot(turn)
        z_step(slot, 1, 2)
        xa(slot).wait_recv()
        for zz in range(4):
            add(dw.at[slot.d, y, zz, x, row_a], rxa.at[slot.r, zz])
        z_step(slot, 0, 1)

    def stage3(turn):
        slot = Slot(turn)
        z_step(slot, 1, 3)
        z_step(slot, 0, 2)

    def stage4(turn):
        slot = Slot(turn)
        z_step(slot, 0, 3)

        @pl.when(z >= 1)
        def _():
            up(slot, 1, z).wait_recv()
            for yy in range(2):
                add(dw.at[slot.d, yy, z, x, row_b], rub.at[slot.r, z - 1, yy])

        @pl.when(z <= 2)
        def _():
            down(slot, 1, z).wait_recv()
            for yy in range(2):
                add(dw.at[slot.d, yy, z, x, row_b], rdb.at[slot.r, z, yy])

        yb(slot).start()

    def out_copy(turn):
        return pltpu.make_async_copy(ob.at[turn % 2], out_ref.at[turn], out_sem.at[turn % 2])

    def stage5(turn):
        slot = Slot(turn)
        side = turn % 2
        pl.when(turn >= 2)(lambda: out_copy(turn - 2).wait())
        ob[side, row_a, :] = dw[slot.d, y, z, x, row_a, :].astype(jnp.float32)

        @pl.when(z >= 1)
        def _():
            up(slot, 0, z).wait_recv()
            ob[side, row_a, :] += rua[slot.r, z - 1].astype(jnp.float32)

        @pl.when(z <= 2)
        def _():
            down(slot, 0, z).wait_recv()
            ob[side, row_a, :] += rda[slot.r, z].astype(jnp.float32)

        yb(slot).wait_recv()
        ob[side, row_b, :] = dw[slot.d, y, z, x, row_b, :].astype(jnp.float32) + ryb[
            slot.r
        ].astype(jnp.float32)
        out_copy(turn).start()

        ya(slot, 0).wait_send()
        ya(slot, 1).wait_send()
        xa(slot).wait_send()
        xb_copy(slot, 0).wait_send()
        xb_copy(slot, 1).wait_send()
        yb(slot).wait_send()
        for colour in range(2):
            for step in range(1, 4):

                @pl.when(z <= step - 1)
                def _(colour=colour, step=step):
                    up(slot, colour, z + 4 - step).wait_send()

                @pl.when(3 - z <= step - 1)
                def _(colour=colour, step=step):
                    down(slot, colour, z - 4 + step).wait_send()

    stages = (stage0, stage1, stage2, stage3, stage4, stage5)

    def advance(now, carry):
        def inner(place, carry):
            for spot, step in enumerate(range(stage_count)):
                turn = now - 1 - step

                @pl.when((place == spot) & (turn >= 0) & (turn < UNITS))
                def _(step=step, turn=turn):
                    stages[step](turn)

            def two(step, carry):
                do_step(2 * (now * stage_count + place) + step)
                return carry

            return lax.fori_loop(0, 2, two, carry)

        pl.when(now == 1)(give_rest)
        lax.fori_loop(0, stage_count, inner, 0)
        pl.when(now < UNITS)(lambda: prepare(now))
        return carry

    lax.fori_loop(0, UNITS + stage_count, advance, 0)
    out_copy(UNITS - 2).wait()
    out_copy(UNITS - 1).wait()
    for index in range(3):
        peer_copy(index).wait()
        moved_copy(index).wait()
    own_peer.wait()
    own_moved.wait()
    for index in known:
        for yy in range(2):
            known_q(index, yy).wait_send()
    for index in known_p:
        give_p(index).wait_send()


def backward_all(whole, q_all, pt_all, streams, qk, values, slopes, grad, moved, joined):
    share = whole.shape[5]
    count_p, unused, rows = pt_all.shape
    width = values.shape[3]
    low = jnp.bfloat16
    slots, taken, rest = SLOTS_IN_FLIGHT, SLOTS_RECEIVED, share - ROWS_A
    anywhere, near = pl.BlockSpec(memory_space=pl.ANY), pl.BlockSpec(memory_space=pltpu.VMEM)
    return pl.pallas_call(
        backward_kernel,
        in_specs=[anywhere] * 9 + [near],
        out_specs=[anywhere] * 7 + [near] * 2,
        out_shape=[
            jax.ShapeDtypeStruct((UNITS, share, WIDE), jnp.float32),
            jax.ShapeDtypeStruct(q_all.shape, low),
            jax.ShapeDtypeStruct(pt_all.shape, low),
            jax.ShapeDtypeStruct(pt_all.shape, low),
            jax.ShapeDtypeStruct((q_all.shape[0], 2, rows, WIDE), low),
            jax.ShapeDtypeStruct((4, rows, width), low),
            jax.ShapeDtypeStruct((4, rows, width), low),
            jax.ShapeDtypeStruct((16, C), jnp.float32),
            jax.ShapeDtypeStruct((4, 8, WIDE), jnp.float32),
        ],
        input_output_aliases={1: 1, 2: 2},
        scratch_shapes=[
            pltpu.VMEM((2, C, rows), low),
            pltpu.VMEM((2, 2, rows, WIDE), low),
            pltpu.VMEM((slots, 2, 4, 2, share, WIDE), low),
            pltpu.VMEM((taken, 2, 4, ROWS_A, WIDE), low),
            pltpu.VMEM((taken, 4, ROWS_A, WIDE), low),
            pltpu.VMEM((taken, 3, ROWS_A, WIDE), low),
            pltpu.VMEM((taken, 3, ROWS_A, WIDE), low),
            pltpu.VMEM((taken, 2, 4, rest, WIDE), low),
            pltpu.VMEM((taken, 3, 2, rest, WIDE), low),
            pltpu.VMEM((taken, 3, 2, rest, WIDE), low),
            pltpu.VMEM((taken, rest, WIDE), low),
            pltpu.VMEM((rows, C), jnp.float32),
            pltpu.VMEM((rows, C), jnp.float32),
            pltpu.VMEM((rows, C), low),
            pltpu.VMEM((C, rows), low),
            pltpu.VMEM((2, 4, 2, share, WIDE), low),
            pltpu.VMEM((5, rows, WIDE), low),
            pltpu.VMEM((rows, width), low),
            pltpu.VMEM((rows, width), low),
            pltpu.VMEM((rows, WIDE), jnp.float32),
            pltpu.VMEM((2, 4 * FRAMES, C), jnp.float32),
            pltpu.VMEM((2, share, WIDE), jnp.float32),
            pltpu.VMEM((4, rows, width), low),
            pltpu.SemaphoreType.DMA((6,)),
            pltpu.SemaphoreType.DMA((32,)),
            pltpu.SemaphoreType.DMA((32,)),
            pltpu.SemaphoreType.DMA((slots, 18)),
            pltpu.SemaphoreType.DMA((taken, 18)),
            pltpu.SemaphoreType.DMA((2,)),
            pltpu.SemaphoreType.DMA((4,)),
            pltpu.SemaphoreType.DMA((12, 2)),
            pltpu.SemaphoreType.DMA((5,)),
            pltpu.SemaphoreType.DMA((2,)),
            pltpu.SemaphoreType.DMA((2, 4)),
            pltpu.SemaphoreType.DMA((2, 3)),
        ],
        compiler_params=pltpu.CompilerParams(
            collective_id=1, has_side_effects=True, vmem_limit_bytes=63 << 20
        ),
    )(whole, q_all, pt_all, streams, qk, values, slopes, grad, moved, joined)


def gather_plain(shards):
    units, share, wide = shards.shape
    whole = lax.all_gather(shards, MIXED, axis=1, tiled=True)
    return whole.reshape(units, lax.axis_size("tensor"), C, wide)


def reduce_plain(turned, parts):
    reduced = []
    for turn in range(UNITS):
        pairs = [(turned[(turn + turn // 5) // 2], parts[turn])]
        if turn in (4, 6, 8):
            extra = (turn - 4) // 2
            pairs.append((turned[5 + extra], parts[UNITS + extra]))
        whole = sum(
            jnp.einsum("kr,trn->tkn", left, right, preferred_element_type=jnp.float32)
            for left, right in pairs
        )
        whole = whole.astype(jnp.bfloat16).reshape(-1, whole.shape[2])
        reduced.append(
            lax.psum_scatter(whole, MIXED, scatter_dimension=0, tiled=True).astype(jnp.float32)
        )
    return jnp.stack(reduced, 0)


def by_pixels(values, tensor_size):
    slots, frames, width, pixels = values.shape
    own = pixels // tensor_size
    return jnp.transpose(values, (3, 0, 1, 2)).reshape(tensor_size, own * slots * frames, width)


def exchange(parts):
    return lax.all_to_all(parts, "tensor", 0, 0, tiled=True)


def back_to_channels(arrived, slots, pixels):
    width = arrived.shape[2]
    return jnp.transpose(arrived.reshape(pixels, slots, FRAMES, width), (1, 2, 3, 0))


def group_total(values):
    width = values.shape[0]
    size = C // GROUPS
    grouped = values.reshape(width // size, size, 1)
    summed = jnp.sum(grouped, axis=1, keepdims=True)
    return jnp.broadcast_to(summed, grouped.shape).reshape(width, 1)


def enter_kernel(
    latent_ref,
    cot_ref,
    flag_ref,
    gain_ref,
    shift_ref,
    in_ref,
    qkv_ref,
    out_ref,
    up_ref,
    down_ref,
    proj_ref,
    sent_ref,
    moved_ref,
    shards_ref,
    centre_ref,
    inverse_ref,
    bias_ref,
    rows_buf,
):
    frames, width, pixels = latent_ref.shape[1:]
    cells = frames * pixels * (C // GROUPS)
    shards_ref[0, :, 0:width] = qkv_ref[0, 0]
    shards_ref[0, :, width:] = qkv_ref[0, 1]
    shards_ref[1, :, 0:width] = qkv_ref[0, 2]
    shards_ref[1, :, width:] = in_ref[...]
    shards_ref[2, :, 0:width] = qkv_ref[1, 0]
    shards_ref[2, :, width:] = qkv_ref[1, 1]
    shards_ref[3, :, 0:width] = qkv_ref[1, 2]
    shards_ref[3, :, width:] = out_ref[0]
    shards_ref[4, :, 0:width] = out_ref[1]
    shards_ref[4, :, width:] = proj_ref[...]
    for half in range(2):
        lanes = slice(half * WIDE, (half + 1) * WIDE)
        shards_ref[5 + half] = up_ref[:, lanes]
        shards_ref[7 + half] = down_ref[:, lanes]

    def frame_sum(use):
        def one(f, carry):
            return carry + use(f)

        total = lax.fori_loop(0, frames, one, jnp.zeros((width, pixels), jnp.float32))
        return jnp.sum(total, axis=1, keepdims=True)

    def values(f):
        return latent_ref[0, f].astype(jnp.float32)

    centre = group_total(frame_sum(values)) / cells
    spread_sum = group_total(frame_sum(lambda f: (values(f) - centre) * (values(f) - centre)))
    inverse = lax.rsqrt(spread_sum / cells + 1e-06)
    centre_ref[...] = centre
    inverse_ref[...] = inverse
    flag = (flag_ref[0] > 0).astype(jnp.float32)

    def masked(f):
        return cot_ref[0, f].astype(jnp.float32) * flag

    bias_ref[...] = frame_sum(masked)
    own = pixels // 4 * frames

    def rows_of(use, target):
        def one(f, carry):
            block = use(f)
            for part in range(3):
                rows_buf[part, pl.ds(f, pixels, stride=frames), :] = block[
                    part * 128 : part * 128 + 128, :
                ].T
            return carry

        lax.fori_loop(0, frames, one, 0)

        def cast(step, carry):
            rows = pl.ds(pl.multiple_of(step * 128, 128), 128)
            t, inside = step // (own // 128), step % (own // 128)
            inner = pl.ds(pl.multiple_of(inside * 128, 128), 128)
            for part in range(3):
                low, high = part * 128, min(part * 128 + 128, width)
                target[t, inner, low:high] = rows_buf[part, rows, 0 : high - low].astype(
                    jnp.bfloat16
                )
            return carry

        lax.fori_loop(0, 4 * own // 128, cast, 0)

    def padded(block):
        return jnp.concatenate([block, jnp.zeros((384 - width, pixels), jnp.float32)], 0)

    gain, shift = gain_ref[...], shift_ref[...]
    rows_of(lambda f: padded((values(f) - centre) * inverse * gain + shift), sent_ref)
    rows_of(lambda f: padded(masked(f)), moved_ref)


def enter(latent, cotangent, flags, gain, shift, w_in, w_qkv, w_out, w_up, w_down, w_proj):
    slots, frames, width, pixels = latent.shape
    share, rows = w_in.shape[0], pixels // 4 * frames
    near = pl.BlockSpec(memory_space=pltpu.VMEM)
    column = jax.ShapeDtypeStruct((width, 1), jnp.float32)
    low = jnp.bfloat16
    return pl.pallas_call(
        enter_kernel,
        in_specs=[near, near, pl.BlockSpec(memory_space=pltpu.SMEM)] + [near] * 8,
        out_specs=[near] * 6,
        out_shape=[
            jax.ShapeDtypeStruct((4, rows, width), low),
            jax.ShapeDtypeStruct((4, rows, width), low),
            jax.ShapeDtypeStruct((UNITS, share, WIDE), low),
            column,
            column,
            column,
        ],
        scratch_shapes=[pltpu.VMEM((3, 4 * rows, 128), jnp.float32)],
        compiler_params=pltpu.CompilerParams(vmem_limit_bytes=48 << 20),
    )(
        latent,
        cotangent,
        flags,
        gain.reshape(width, 1),
        shift.reshape(width, 1),
        w_in,
        jnp.transpose(w_qkv, (0, 2, 1, 3)),
        jnp.transpose(w_out, (0, 2, 1)),
        w_up,
        w_down.T,
        w_proj,
    )


def leave_kernel(
    grad_ref,
    moved_ref,
    latent_ref,
    cot_ref,
    flag_ref,
    gain_ref,
    centre_ref,
    inverse_ref,
    reduced_ref,
    output_ref,
    latent_grad_ref,
    gain_grad_ref,
    shift_grad_ref,
    in_ref,
    qkv_ref,
    out_ref,
    up_ref,
    down_ref,
    proj_ref,
    rows_buf,
    turned,
):
    frames, width, pixels = latent_ref.shape[1:]
    cells = frames * pixels * (C // GROUPS)
    for block in range(2):
        for part in range(2):
            qkv_ref[block, part] = reduced_ref[7 - 2 * block, :, part * width : (part + 1) * width]
        qkv_ref[block, 2] = reduced_ref[8 - 2 * block, :, 0:width]
    in_ref[...] = reduced_ref[8, :, width:]
    out_ref[0] = reduced_ref[6, :, width:]
    out_ref[1] = reduced_ref[4, :, 0:width]
    proj_ref[...] = reduced_ref[4, :, width:]
    for half in range(2):
        lanes = slice(half * WIDE, (half + 1) * WIDE)
        up_ref[:, lanes] = reduced_ref[3 - half]
        down_ref[:, lanes] = reduced_ref[1 - half]

    own = pixels // 4 * frames

    def spread_rows(source):
        def cast(step, carry):
            rows = pl.ds(pl.multiple_of(step * 128, 128), 128)
            t, inside = step // (own // 128), step % (own // 128)
            inner = pl.ds(pl.multiple_of(inside * 128, 128), 128)
            for part in range(3):
                low, high = part * 128, min(part * 128 + 128, width)
                rows_buf[part, rows, 0 : high - low] = source[t, inner, low:high].astype(
                    jnp.float32
                )
            return carry

        lax.fori_loop(0, 4 * own // 128, cast, 0)

    def frame(f):
        rows = pl.ds(f, pixels, stride=frames)
        turned_parts = [rows_buf[part, rows, :].T for part in range(3)]
        return jnp.concatenate(turned_parts, 0)[0:width, :]

    def hat(f):
        return (latent_ref[0, f].astype(jnp.float32) - centre_ref[...]) * inverse_ref[...]

    flag = (flag_ref[0] > 0).astype(jnp.float32)
    rows_buf[...] = jnp.zeros_like(rows_buf)
    spread_rows(moved_ref)

    def finish(f, carry):
        start = latent_ref[0, f].astype(jnp.float32)
        output_ref[0, f] = (start + flag * frame(f)).astype(jnp.bfloat16)
        return carry

    lax.fori_loop(0, frames, finish, 0)
    spread_rows(grad_ref)
    zero = jnp.zeros((width, pixels), jnp.float32)

    def gather(f, carry):
        grad = frame(f)
        turned[f] = grad
        return carry[0] + grad * hat(f), carry[1] + grad

    by_gain, by_shift = lax.fori_loop(0, frames, gather, (zero, zero))
    gain_sum = jnp.sum(by_gain, axis=1, keepdims=True)
    shift_sum = jnp.sum(by_shift, axis=1, keepdims=True)
    gain_grad_ref[...] = gain_sum
    shift_grad_ref[...] = shift_sum
    gain = gain_ref[...]
    first = group_total(gain * shift_sum) / cells
    second = group_total(gain * gain_sum) / cells

    def back(f, carry):
        grad = inverse_ref[...] * (turned[f] * gain - first - hat(f) * second)
        latent_grad_ref[0, f] = cot_ref[0, f].astype(jnp.float32) + grad
        return carry

    lax.fori_loop(0, frames, back, 0)


def leave(grad, moved, latent, cotangent, flags, gain, centre, inverse, reduced):
    slots, frames, width, pixels = latent.shape
    rows, share = pixels // 4 * frames, reduced.shape[1]
    near = pl.BlockSpec(memory_space=pltpu.VMEM)
    real = jnp.float32
    column = jax.ShapeDtypeStruct((width, 1), real)
    made = pl.pallas_call(
        leave_kernel,
        in_specs=[near] * 4 + [pl.BlockSpec(memory_space=pltpu.SMEM)] + [near] * 4,
        out_specs=[near] * 10,
        out_shape=[
            jax.ShapeDtypeStruct(latent.shape, jnp.bfloat16),
            jax.ShapeDtypeStruct(latent.shape, real),
            column,
            column,
            jax.ShapeDtypeStruct((share, width), real),
            jax.ShapeDtypeStruct((2, 3, share, width), real),
            jax.ShapeDtypeStruct((2, share, width), real),
            jax.ShapeDtypeStruct((share, 2 * WIDE), real),
            jax.ShapeDtypeStruct((share, 2 * WIDE), real),
            jax.ShapeDtypeStruct((share, width), real),
        ],
        scratch_shapes=[
            pltpu.VMEM((3, 4 * rows, 128), real),
            pltpu.VMEM((frames, width, pixels), real),
        ],
        compiler_params=pltpu.CompilerParams(vmem_limit_bytes=56 << 20),
    )(
        grad,
        moved,
        latent,
        cotangent,
        flags,
        gain.reshape(width, 1),
        centre,
        inverse,
        reduced,
    )
    output, latent_grad, gain_grad, shift_grad, g_in, g_qkv, g_out, g_up, g_down, g_proj = made
    weights = (
        g_in,
        jnp.transpose(g_qkv, (0, 2, 1, 3)),
        jnp.transpose(g_out, (0, 2, 1)),
        g_up,
        g_down.T,
        g_proj,
    )
    return output, latent_grad, gain_grad.reshape(width), shift_grad.reshape(width), weights


def kernel_body(
    latent,
    clip_flags,
    cotangent,
    norm_gain,
    norm_shift,
    channel_bias,
    hidden_bias,
    weight_in,
    weight_qkv,
    weight_out,
    weight_up,
    weight_down,
    weight_proj,
):
    width = latent.shape[2]
    side = jnp.concatenate
    params = side([norm_gain, norm_shift, channel_bias, jnp.zeros((3, width), jnp.float32)], 0)
    params = side([params, hidden_bias.reshape(4, width), jnp.zeros((4, width), jnp.float32)], 0)
    sent, moved_sent, shards, centre, inverse, bias_moved = enter(
        latent,
        cotangent,
        clip_flags,
        norm_gain[0],
        norm_shift[0],
        weight_in,
        weight_qkv,
        weight_out,
        weight_up,
        weight_down,
        weight_proj,
    )
    whole, q_all, pt_all, streams, qk_all, v_all, slopes, grad, moved, joined = forward_all(
        shards, sent, params, make_positions(), moved_sent
    )
    reduced, q_all, pt_all, unused, unused, grad_back, moved_back, sums, hidden_sums = backward_all(
        whole, q_all, pt_all, streams, qk_all, v_all, slopes, grad, moved, joined
    )
    output, latent_grad, group_gain, group_shift, weights = leave(
        grad_back,
        moved_back,
        latent,
        cotangent,
        clip_flags,
        norm_gain[0],
        centre,
        inverse,
        reduced,
    )
    vectors = jnp.transpose(sums[:10].reshape(10, 4, width), (1, 0, 2)).reshape(4, 10 * width)
    vectors = side([vectors, hidden_sums[:, :2].reshape(4, 2 * WIDE)], 1)
    vectors = jnp.sum(exchange(vectors), 0)
    local = side([vectors, group_gain, group_shift, bias_moved.reshape(width)])
    total = local
    count = lax.axis_size("dp")
    for bit in range(count.bit_length() - 1):
        total = total + lax.ppermute(total, "dp", [(i, i ^ (1 << bit)) for i in range(count)])
    channel, hidden_grad = total[: 10 * width].reshape(10, width), total[10 * width : 14 * width]
    group = total[14 * width :].reshape(3, width)
    return (
        output,
        latent_grad,
        side([group[0:1], channel[0:3]], 0),
        side([group[1:2], channel[3:6]], 0),
        side([channel[6:10], group[2:3]], 0),
        hidden_grad,
    ) + weights


def body(
    latent,
    clip_flags,
    cotangent,
    norm_gain,
    norm_shift,
    channel_bias,
    hidden_bias,
    weight_in,
    weight_qkv,
    weight_out,
    weight_up,
    weight_down,
    weight_proj,
):
    tensor_size = lax.axis_size("tensor")
    slots, frames, width, pixels = latent.shape
    share = weight_in.shape[0]
    hidden_width = hidden_bias.shape[0]
    flags = (clip_flags > 0)[:, None, None, None]

    wide = 2 * width

    shards = []
    side = jnp.concatenate
    for block in range(2):
        shards.append(weight_qkv[block, :, :2].reshape(share, wide))
        other = weight_in if block == 0 else weight_out[0].T
        shards.append(side([weight_qkv[block, :, 2], other], 1))
    shards.append(side([weight_out[1].T, weight_proj], 1))
    shards += [weight_up[:, :wide], weight_up[:, wide:]]
    down_turned = weight_down.T
    shards += [down_turned[:, :wide], down_turned[:, wide:]]
    shards = jnp.stack(shards, 0)
    params = jnp.zeros((24, width), jnp.float32)
    params = params.at[:13].set(side([norm_gain, norm_shift, channel_bias], 0))
    params = params.at[16:20].set(hidden_bias.reshape(4, width))

    start = latent.astype(jnp.float32)
    cot = cotangent.astype(jnp.float32)
    group_width = C // GROUPS
    grouped = start.reshape(slots, frames, width // group_width, group_width, pixels)
    group_centre = jnp.mean(grouped, axis=(1, 3, 4), keepdims=True)
    offset = grouped - group_centre
    group_inverse = lax.rsqrt(jnp.mean(offset * offset, axis=(1, 3, 4), keepdims=True) + 1e-06)
    group_hat = (offset * group_inverse).reshape(start.shape)
    normed = group_hat * norm_gain[0][:, None] + norm_shift[0][:, None]
    sent = by_pixels(normed.astype(jnp.bfloat16), tensor_size)
    rows = sent.shape[1]

    grad_moved_local = jnp.where(flags, cot, 0.0)
    bias_moved = jnp.sum(grad_moved_local, axis=(0, 1, 3))
    grad_moved = exchange(by_pixels(grad_moved_local.astype(jnp.bfloat16), tensor_size))

    empty = jnp.zeros((tensor_size, rows, width), jnp.bfloat16)
    moved_part = side([empty, grad_moved], 2)
    arrived = exchange(sent)
    inputs_in = jnp.transpose(arrived, (1, 0, 2)).reshape(rows, C)
    packed = lax.all_gather(params, "tensor", axis=0, tiled=False)
    joined = jnp.transpose(packed[:, :13], (1, 0, 2)).reshape(13, C)
    gains, shifts, biases = joined[:4], joined[4:8], joined[8:]
    hidden_full = packed[:, 16:20].reshape(tensor_size, 2 * wide)
    whole = gather_plain(shards)
    full_qk = (whole[0], whole[2])
    full_v = (whole[1, :, :, :width], whole[3, :, :, :width])
    full_in = whole[1, :, :, width:]
    full_out = (whole[3, :, :, width:], whole[4, :, :, :width])
    full_proj = whole[4, :, :, width:]
    full_up = (whole[5], whole[6])
    full_down = (whole[7], whole[8])

    def join(parts):
        return jnp.transpose(parts, (1, 0, 2)).reshape(rows, parts.shape[0] * parts.shape[2])

    stream = join(spread(inputs_in, full_in)) + biases[0]
    position = jnp.tile(make_positions(), (rows // FRAMES, 1))
    kept = []
    for block in range(2):
        hat, inverse = layer_stats(stream)
        lifted = (hat * gains[1 + block] + shifts[1 + block] + position).astype(jnp.bfloat16)
        qk = spread(lifted, full_qk[block]).astype(jnp.bfloat16)
        values = spread(lifted, full_v[block]).astype(jnp.bfloat16)
        attended = attend(qk, values)
        stream = stream + collapse(attended, full_out[block]) + biases[1 + block]
        kept.append((hat, inverse, lifted.T, qk, values, attended))
    hat_feed, inverse_feed = layer_stats(stream)
    inputs_up = (hat_feed * gains[3] + shifts[3]).astype(jnp.bfloat16)
    pre_act = [
        spread(inputs_up, full_up[half])
        + hidden_full[:, None, half * wide : half * wide + wide]
        for half in range(2)
    ]
    slopes = [
        jax.vjp(partial(jax.nn.gelu, approximate=False), pre)[1](jnp.ones_like(pre))[0]
        for pre in pre_act
    ]
    hidden = [jax.nn.gelu(pre, approximate=False).astype(jnp.bfloat16) for pre in pre_act]
    stream = stream + collapse(hidden[0], full_down[0]) + collapse(hidden[1], full_down[1])
    stream = stream + biases[3]
    inputs_proj = stream.astype(jnp.bfloat16)
    moved = spread(inputs_proj, full_proj) + biases[4].reshape(tensor_size, 1, width)
    moved = moved.astype(jnp.bfloat16)

    bias_grads = [None] * 4
    gain_grads = [None] * 3
    shift_grads = [None] * 3
    turned, parts = [None] * 8, [None] * 12
    turned[1], turned[5], turned[7] = inputs_up.T, inputs_proj.T, inputs_in.T
    parts[0], parts[1] = hidden[1], hidden[0]
    parts[9] = moved_part
    grad_stream = collapse(grad_moved, full_proj)
    bias_grads[3] = jnp.sum(grad_stream, 0)
    grad_low = grad_stream.astype(jnp.bfloat16)
    turned[0] = grad_low.T
    hidden_grads = [None, None]
    grad_normed = 0.0
    for half in (1, 0):
        grad_hidden = spread(grad_low, full_down[half])
        grad_pre = grad_hidden * slopes[half]
        hidden_grads[half] = jnp.sum(grad_pre, 1)
        parts[3 - half] = grad_pre.astype(jnp.bfloat16)
        grad_normed = grad_normed + collapse(parts[3 - half], full_up[half])
    hidden_grad = side(hidden_grads, 1)
    grad_layer, gain_grads[2], shift_grads[2] = layer_back(
        grad_normed, hat_feed, inverse_feed, gains[3]
    )
    grad_stream = grad_stream + grad_layer
    for block in (1, 0):
        hat, inverse, lifted_turned, qk, values, attended = kept[block]
        bias_grads[1 + block] = jnp.sum(grad_stream, 0)
        grad_low = grad_stream.astype(jnp.bfloat16)
        turned[2 if block == 1 else 6] = grad_low.T
        pair = [attended, empty] if block == 1 else [empty, attended]
        parts[4 if block == 1 else 10] = side(pair, 2)
        grad_attended = spread(grad_low, full_out[block]).astype(jnp.bfloat16)
        grad_qk, grad_values = attend_back(qk, values, grad_attended)
        turned[3 if block == 1 else 4] = lifted_turned
        parts[6 if block == 1 else 8] = side([grad_values, empty], 2)
        parts[5 if block == 1 else 7] = grad_qk
        grad_lifted = collapse(grad_qk, full_qk[block]) + collapse(grad_values, full_v[block])
        grad_layer, gain_grads[block], shift_grads[block] = layer_back(
            grad_lifted, hat, inverse, gains[1 + block]
        )
        grad_stream = grad_stream + grad_layer
    bias_grads[0] = jnp.sum(grad_stream, 0)
    grad_low = grad_stream.astype(jnp.bfloat16)
    grad_low_parts = jnp.transpose(grad_low.reshape(rows, tensor_size, width), (1, 0, 2))
    parts[11] = side([empty, grad_low_parts], 2)
    turned, parts = jnp.stack(turned, 0), jnp.stack(parts, 0)
    reduced = reduce_plain(turned, parts)
    grad_normed = collapse(grad_low_parts, full_in).astype(jnp.bfloat16)
    grad_normed = jnp.transpose(grad_normed.reshape(rows, tensor_size, width), (1, 0, 2))
    arrived_grad = exchange(grad_normed)
    vectors = jnp.stack(gain_grads + shift_grads + bias_grads, 0)

    moved_local = back_to_channels(exchange(moved), slots, pixels).astype(jnp.float32)
    output = jnp.where(flags, start + moved_local, start).astype(jnp.bfloat16)

    qkv_grads = [
        side([reduced[7 - 2 * block], reduced[8 - 2 * block, :, :width]], 1).reshape(share, 3, width)
        for block in range(2)
    ]
    out_grads = [reduced[6, :, width:].T, reduced[4, :, :width].T]
    in_grad, proj_grad = reduced[8, :, width:], reduced[4, :, width:]
    up_grad = side([reduced[3], reduced[2]], 1)
    down_grad = side([reduced[1], reduced[0]], 1)
    grad_normed = back_to_channels(arrived_grad, slots, pixels).astype(jnp.float32)
    scaled = grad_normed * norm_gain[0][:, None]
    scaled_groups = scaled.reshape(grouped.shape)
    hat_groups = group_hat.reshape(grouped.shape)
    first = jnp.mean(scaled_groups, axis=(1, 3, 4), keepdims=True)
    second = jnp.mean(scaled_groups * hat_groups, axis=(1, 3, 4), keepdims=True)
    grad_group = group_inverse * (scaled_groups - first - hat_groups * second)
    latent_grad = cot + grad_group.reshape(start.shape)
    group_gain_grad = jnp.sum(grad_normed * group_hat, axis=(0, 1, 3))
    group_shift_grad = jnp.sum(grad_normed, axis=(0, 1, 3))

    vectors = jnp.transpose(vectors.reshape(10, tensor_size, width), (1, 0, 2))
    vectors = jnp.concatenate([vectors.reshape(tensor_size, 10 * width), hidden_grad], 1)
    vectors = lax.psum_scatter(vectors, "tensor", scatter_dimension=0, tiled=False)
    sums = lax.psum(
        jnp.concatenate([vectors, group_gain_grad, group_shift_grad, bias_moved]), "dp"
    )
    channel_sums = sums[: 10 * width].reshape(10, width)
    hidden_bias_grad = sums[10 * width : 10 * width + hidden_width]
    local_sums = sums[10 * width + hidden_width :].reshape(3, width)
    gain_grad = jnp.concatenate([local_sums[0:1], channel_sums[0:3]], 0)
    shift_grad = jnp.concatenate([local_sums[1:2], channel_sums[3:6]], 0)
    channel_bias_grad = jnp.concatenate([channel_sums[6:10], local_sums[2:3]], 0)
    return (
        output,
        latent_grad,
        gain_grad,
        shift_grad,
        channel_bias_grad,
        hidden_bias_grad,
        in_grad,
        jnp.stack(qkv_grads, 0),
        jnp.stack(out_grads, 0),
        up_grad,
        down_grad.T,
        proj_grad,
    )


def solution(mesh):
    placed = (
        P("dp", None, "tensor", None),
        P("dp"),
        P("dp", None, "tensor", None),
        P(None, "tensor"),
        P(None, "tensor"),
        P(None, "tensor"),
        P("tensor"),
        P("dp", "tensor"),
        P(None, "dp", None, "tensor"),
        P(None, "tensor", "dp"),
        P("dp", "tensor"),
        P("tensor", "dp"),
        P("dp", "tensor"),
    )
    kernels_fit = (mesh.shape["dp"], mesh.shape["tensor"]) == (8, 4)
    return jax.shard_map(
        kernel_body if kernels_fit else body,
        mesh=mesh,
        in_specs=placed,
        out_specs=(
            P("dp", None, "tensor", None),
            P("dp", None, "tensor", None),
            P(None, "tensor"),
            P(None, "tensor"),
            P(None, "tensor"),
            P("tensor"),
            P("dp", "tensor"),
            P(None, "dp", None, "tensor"),
            P(None, "tensor", "dp"),
            P("dp", "tensor"),
            P("tensor", "dp"),
            P("dp", "tensor"),
        ),
        check_vma=False,
    )
```
